32 devices in a mesh: dp: 4 (over x, core), fsdp: 8 (over z, y).
Axes of the slice: x: 2, y: 2, z: 4, core: 2. Of those that a mesh axis runs over, the one named last changes fastest.
Arguments:
- images: bfloat16 [32, 197, 768], P(('dp', 'fsdp')), may hold values from -6 to 6
- image_cot: bfloat16 [32, 197, 768], P(('dp', 'fsdp')), may hold values from -6 to 6
- captions: bfloat16 [32, 512, 768], P(('dp', 'fsdp')), may hold values from -6 to 6
- caption_cot: bfloat16 [32, 512, 768], P(('dp', 'fsdp')), may hold values from -6 to 6
- lengths: int32 [32, 8], P(('dp', 'fsdp')), may hold values from 1 to 256, 448 in all within a row
- w_qkv: bfloat16 [2, 768, 2304], P(None, 'fsdp'), may hold values from -0.21875 to 0.21875
- w_out: bfloat16 [2, 768, 768], P(None, 'fsdp'), may hold values from -0.875 to 0.875
- w_up: bfloat16 [2, 768, 3072], P(None, 'fsdp'), may hold values from -0.21875 to 0.21875
- w_down: bfloat16 [2, 3072, 768], P(None, 'fsdp'), may hold values from -0.109375 to 0.109375
- gains: bfloat16 [2, 2, 768], P(None, None, 'fsdp'), may hold values from 0.5 to 1.5
- biases: bfloat16 [2, 6, 768], P(None, None, 'fsdp'), may hold values from -2.5 to 2.5
- b_up: bfloat16 [2, 3072], P(None, 'fsdp'), may hold values from -2.5 to 2.5
Outputs:
- image_out: bfloat16 [32, 197, 768], P(('dp', 'fsdp'))
- caption_out: bfloat16 [32, 512, 768], P(('dp', 'fsdp'))
- image_grad: float32 [32, 197, 768], P(('dp', 'fsdp'))
- caption_grad: float32 [32, 512, 768], P(('dp', 'fsdp'))
- grad_qkv: float32 [2, 768, 2304], P(None, 'fsdp')
- grad_out: float32 [2, 768, 768], P(None, 'fsdp')
- grad_up: float32 [2, 768, 3072], P(None, 'fsdp')
- grad_down: float32 [2, 3072, 768], P(None, 'fsdp')
- grad_gains: float32 [2, 2, 768], P(None, None, 'fsdp')
- grad_biases: float32 [2, 6, 768], P(None, None, 'fsdp')
- grad_bup: float32 [2, 3072], P(None, 'fsdp')
The draws below stay inside these ranges and needn't reach their ends.
Inputs may be any that keep to these rules, and one draw needn't show every extreme that they name: The 8 lengths of each packed row sum to 448; the rest of the row is padding.
All inputs are finite; a program needn't handle non-finite values.
Results may differ from the reference program's by a relative error of at most 0.014.
Values may be sent and summed in bfloat16 or wider, within the bound.
A program may use at most 192 MiB of HBM per device.

```python
import math
import jax
import jax.numpy as jnp
import numpy as np
from jax import lax

D = 768
HEAD = 64
FF = 3072
IMG_ROWS = 197
TXT_LEN = 512
CAPS = 8
IMAGES = 32
CAPTIONS = 32


def level_of(rng, extent, cuts, least, high):
    loudness, own = 1.0, jax.random.fold_in(rng, 6)
    for axis_at, parts in cuts:
        draws = jnp.exp(jax.random.uniform(jax.random.fold_in(own, axis_at), (parts,), jnp.float32, least / len(cuts), high / len(cuts)))
        loudness = loudness * jnp.repeat(draws, extent[axis_at] // parts).reshape([-1 if axis == axis_at else 1 for axis in range(len(extent))])
    return loudness


def profile(number_of, total, bound, slope):
    weights = [(1 << 20) // math.isqrt(standing ** slope) + 1 for standing in range(2, number_of + 1)]
    surplus, given = total - bound - (number_of - 1), [1] * (number_of - 1)
    while surplus > 0:
        candidates = [i for i in range(number_of - 1) if given[i] < bound]
        whole, budget = sum([weights[i] for i in candidates]), surplus
        for i in candidates:
            addition = min(bound - given[i], max(1, budget * weights[i] // whole), surplus)
            given[i] = given[i] + addition
            surplus = surplus - addition
    return np.array([bound] + given)


def uneven_parts(key, count, total, bound, skew):
    if count == 2:
        one = jax.random.randint(key, (), max(1, total - bound), min(bound, total - 1) + 1)
        return jnp.stack([one, total - one])
    sizes = jnp.asarray(profile(count, total, bound, skew), jnp.int32)
    couples = (count - 1) // 2
    giver, receiver = sizes[1:1 + 2 * couples:2], sizes[2:2 + 2 * couples:2]
    slack = jnp.minimum(giver - 1, bound - receiver)
    passed = jax.random.randint(jax.random.fold_in(key, 1), (couples,), 0, 1 << 20) % (slack + 1)
    sizes = sizes.at[1:1 + 2 * couples:2].set(giver - passed).at[2:2 + 2 * couples:2].set(receiver + passed)
    return sizes[jax.random.permutation(jax.random.fold_in(key, 2), count)]


def bell_draw(stream_key, dims, scale, bound, cuts=(), kind=jnp.bfloat16):
    entries = scale * jax.random.normal(stream_key, dims, jnp.float32)
    if cuts:
        entries = entries * level_of(stream_key, dims, cuts, -0.22, 0.18)
    return jnp.clip(entries, -bound, bound).astype(kind)


def setup_inputs(seed: int = 0) -> dict:
    arg_keys = jax.random.split(jax.random.key(seed), 13)
    images = bell_draw(arg_keys[0], (IMAGES, IMG_ROWS, D), 1.0, 6.0, ((0, 32),))
    image_cot = bell_draw(arg_keys[1], (IMAGES, IMG_ROWS, D), 1.0, 6.0, ((0, 32),))
    captions = bell_draw(arg_keys[2], (CAPTIONS, TXT_LEN, D), 1.0, 6.0, ((0, 32),))
    caption_cot = bell_draw(arg_keys[3], (CAPTIONS, TXT_LEN, D), 1.0, 6.0, ((0, 32),))
    lengths = jax.vmap(lambda own: uneven_parts(own, CAPS, TXT_LEN * 7 // 8, TXT_LEN // 2, 2))(jax.random.split(arg_keys[4], CAPTIONS)).reshape((CAPTIONS, CAPS)).astype(jnp.int32)
    w_qkv = bell_draw(arg_keys[5], (2, D, 3 * D), D ** -0.5, 0.21875, ((1, 8),))
    w_out = bell_draw(arg_keys[6], (2, D, D), (D // 16) ** -0.5, 0.875, ((1, 8),))
    w_up = bell_draw(arg_keys[7], (2, D, FF), D ** -0.5, 0.21875, ((1, 8),))
    w_down = bell_draw(arg_keys[8], (2, FF, D), FF ** -0.5, 0.109375, ((1, 8),))
    gains = jnp.clip(1.0 + 0.1 * jax.random.normal(arg_keys[9], (2, 2, D), jnp.float32), 0.5, 1.5).astype(jnp.bfloat16)
    biases = bell_draw(arg_keys[10], (2, 6, D), 0.3, 2.5, ((2, 8),))
    b_up = bell_draw(arg_keys[11], (2, FF), 0.3, 2.5, ((1, 8),))
    return dict(images=images, image_cot=image_cot, captions=captions, caption_cot=caption_cot, lengths=lengths, w_qkv=w_qkv, w_out=w_out, w_up=w_up, w_down=w_down, gains=gains, biases=biases, b_up=b_up)


@jax.custom_vjp
def low(v):
    return lax.optimization_barrier(v.astype(jnp.bfloat16)).astype(jnp.float32)

@jax.custom_vjp
def low_back(v):
    return v

def low_keep(v):
    return (low(v), None)

def low_pass(kept, grad):
    return (grad,)

def back_keep(v):
    return (v, None)

def back_low(kept, grad):
    return (low(grad),)
low.defvjp(low_keep, low_pass)
low_back.defvjp(back_keep, back_low)
highest = lax.Precision.HIGHEST

def normed(values, gain, shift):
    center = values - lax.optimization_barrier(jnp.mean(values, axis=-1, keepdims=True))
    spread = lax.optimization_barrier(jnp.mean(center * center, axis=-1, keepdims=True))
    return center * lax.rsqrt(spread + 1e-05) * gain + shift

def segment_ids(lengths, seq_len):
    bounds = jnp.cumsum(lengths, axis=-1)
    positions = jnp.arange(seq_len, dtype=jnp.int32)
    return lax.optimization_barrier(jnp.sum((positions[None, :, None] >= bounds[:, None, :]).astype(jnp.int32), axis=-1))

def attend(pieces):
    queries, keys_all, values_all, segment = pieces
    length = queries.shape[0]
    heads_q = queries.reshape(length, -1, HEAD)
    heads_k = keys_all.reshape(length, -1, HEAD)
    heads_v = values_all.reshape(length, -1, HEAD)
    scores = jnp.einsum('qhd,khd->hqk', heads_q, heads_k, precision=highest)
    scores = low_back(scores)
    same = (segment[:, None] == segment[None, :])[None]
    scores = jnp.where(same, scores, -1e+30)
    largest = lax.optimization_barrier(jnp.max(scores, axis=-1, keepdims=True))
    raised = jnp.exp(scores - largest)
    attn_weights = raised / lax.optimization_barrier(jnp.sum(raised, axis=-1, keepdims=True))
    mixed = jnp.einsum('hqk,khd->qhd', low(attn_weights), heads_v, precision=highest)
    return mixed.reshape(length, -1)

def block(inputs, params, segment):
    qkv_weight, out_weight, up_weight, down_weight, gains, biases, up_bias = params
    width = inputs.shape[-1]
    normed_a = low(normed(inputs, gains[0], biases[0]))
    project = jnp.einsum('bld,de->ble', normed_a, qkv_weight, precision=highest)
    queries = low_back(low((project[..., :width] + biases[2]) * HEAD ** (-0.5)))
    keys_all = low_back(low(project[..., width:2 * width]))
    values_all = low_back(low(project[..., 2 * width:] + biases[3]))
    mixed = lax.map(jax.checkpoint(attend), (queries, keys_all, values_all, segment))
    mixed = low_back(low(mixed))
    branch = jnp.einsum('bld,de->ble', mixed, out_weight, precision=highest) + biases[4]
    hidden = inputs + low_back(branch)
    normed_c = low(normed(hidden, gains[1], biases[1]))
    before = low_back(jnp.einsum('bld,df->blf', normed_c, up_weight, precision=highest) + up_bias)
    activated = low(jax.nn.gelu(before, approximate=False))
    return hidden + jnp.einsum('blf,fd->bld', activated, down_weight, precision=highest) + biases[5]

def reference(images, image_cot, captions, caption_cot, lengths, w_qkv, w_out, w_up, w_down, gains, biases, b_up):
    params = tuple((member.astype(jnp.float32) for member in (w_qkv, w_out, w_up, w_down, gains, biases, b_up)))
    image_seg = jnp.zeros((images.shape[0], IMG_ROWS), jnp.int32)
    caption_seg = segment_ids(lengths, TXT_LEN)

    def forward(image_in, caption_in, *weights):
        first = block(image_in, tuple((member[0] for member in weights)), image_seg)
        second = block(caption_in, tuple((member[1] for member in weights)), caption_seg)
        return (first, second)
    outputs, backward = jax.vjp(forward, images.astype(jnp.float32), captions.astype(jnp.float32), *params)
    gradients = backward((image_cot.astype(jnp.float32), caption_cot.astype(jnp.float32)))
    return (outputs[0].astype(jnp.bfloat16), outputs[1].astype(jnp.bfloat16), gradients[0], gradients[1], gradients[2], gradients[3], gradients[4], gradients[5], gradients[6], gradients[7], gradients[8])
```

```python
import functools

import jax
import jax.numpy as jnp
from jax import lax
from jax.experimental import pallas as pl
from jax.experimental.pallas import tpu as pltpu
from jax.sharding import PartitionSpec as P

HEAD = 64

MESH = pl.DeviceIdType.MESH
UP, DOWN, YWAY, XWAY, CORE, COREY, COREX = range(7)


class Place:
    def __init__(self, line):
        dp, fs = lax.axis_index("dp"), lax.axis_index("fsdp")
        self.line = line
        self.dp, self.fs = dp, fs
        self.x, self.c = dp // 2, dp % 2
        self.z, self.y = fs // 2, fs % 2
        self.up = (dp, fs + 2)
        self.down = (dp, fs - 2)
        self.yway = (dp, self.z * 2 + 1 - self.y)
        self.xway = ((1 - self.x) * 2 + self.c, fs)
        self.core = (self.x * 2 + 1 - self.c, fs)
        self.has_up = self.z + 1 < line
        self.has_down = self.z > 0

    def greet(self):
        barrier = pltpu.get_barrier_semaphore()
        total = 0
        for step in range(1, 2 * self.line):
            other = lax.rem(self.fs + step, 2 * self.line)
            pl.semaphore_signal(barrier, inc=1, device_id=(self.dp, other), device_id_type=MESH)
            total += 1
        for step in range(1, 4):
            other = lax.rem(self.dp + step, 4)
            pl.semaphore_signal(barrier, inc=1, device_id=(other, self.fs), device_id_type=MESH)
            total += 1
        pl.semaphore_wait(barrier, total)


def remote(src, dst, send, recv, device):
    return pltpu.make_async_remote_copy(
        src_ref=src, dst_ref=dst, send_sem=send, recv_sem=recv, device_id=device, device_id_type=MESH
    )


class Gather:
    def __init__(self, at, place, own, full, send, recv, near):
        self.at, self.place, self.own, self.full = at, place, own, full
        self.send, self.recv, self.near = send, recv, near
        self.rows = own.shape[0]
        self.deep = self.rows // 2
        self.half = own.shape[1] // 2

    def rows_of(self, block, y, c):
        start = (block * 2 + y) * self.rows + c * self.deep
        return pl.ds(pl.multiple_of(start, 16), self.deep)

    def cols_of(self, x):
        return pl.ds(pl.multiple_of(x * self.half, 128), self.half)

    def copy(self, kind, block):
        p, s, r = self.place, self.send.at[self.at, kind, block], None
        if kind in (UP, DOWN):
            ref = self.full.at[self.rows_of(block, p.y, p.c)]
            return remote(ref, ref, s, self.recv.at[self.at, UP, block], p.up if kind == UP else p.down)
        if kind == YWAY:
            ref = self.full.at[self.rows_of(block, p.y, p.c), self.cols_of(p.x)]
            return remote(ref, ref, s, self.recv.at[self.at, kind, block], p.yway)
        if kind == XWAY:
            ref = self.full.at[self.rows_of(block, 1 - p.y, p.c), self.cols_of(p.x)]
            return remote(ref, ref, s, self.recv.at[self.at, kind, block], p.xway)
        if kind == CORE:
            ref = self.full.at[self.rows_of(block, p.y, p.c)]
        elif kind == COREY:
            ref = self.full.at[self.rows_of(block, 1 - p.y, p.c), self.cols_of(p.x)]
        else:
            ref = self.full.at[self.rows_of(block, 1 - p.y, p.c), self.cols_of(1 - p.x)]
        return remote(ref, ref, s, self.recv.at[self.at, kind, block], p.core)

    def landed(self, kind, block):
        p, s = self.place, self.send.at[self.at, kind, block]
        r = self.recv.at[self.at, kind, block]
        if kind == UP:
            ref = self.full.at[self.rows_of(block, p.y, p.c)]
        elif kind == YWAY:
            ref = self.full.at[self.rows_of(block, 1 - p.y, p.c), self.cols_of(p.x)]
        elif kind == XWAY:
            ref = self.full.at[self.rows_of(block, 1 - p.y, p.c), self.cols_of(1 - p.x)]
        elif kind == CORE:
            ref = self.full.at[self.rows_of(block, p.y, 1 - p.c)]
        elif kind == COREY:
            ref = self.full.at[self.rows_of(block, 1 - p.y, 1 - p.c), self.cols_of(p.x)]
        else:
            ref = self.full.at[self.rows_of(block, 1 - p.y, 1 - p.c), self.cols_of(1 - p.x)]
        return remote(ref, ref, s, r, p.core)

    def own_copy(self):
        start = pl.multiple_of(self.place.fs * self.rows, 16)
        return pltpu.make_async_copy(self.own, self.full.at[pl.ds(start, self.rows)], self.near.at[self.at])

    def first(self):
        p = self.place
        self.own_copy().start()
        mine = self.own.at[pl.ds(pl.multiple_of(p.c * self.deep, 16), self.deep)]
        there = self.full.at[self.rows_of(p.z, p.y, p.c)]

        def out(kind, device):
            return remote(mine, there, self.send.at[self.at, kind, p.z], self.recv.at[self.at, UP, p.z], device)

        pl.when(p.has_up)(lambda: out(UP, p.up).start())
        pl.when(p.has_down)(lambda: out(DOWN, p.down).start())
        cols = self.cols_of(p.x)
        remote(
            mine.at[:, cols],
            there.at[:, cols],
            self.send.at[self.at, YWAY, p.z],
            self.recv.at[self.at, YWAY, p.z],
            p.yway,
        ).start()

    def line_step(self, k):
        p = self.place

        def pass_on(block, kind, more):
            self.landed(UP, block).wait_recv()
            pl.when(more)(lambda: self.copy(kind, block).start())
            self.copy(YWAY, block).start()
            self.copy(CORE, block).start()

        pl.when(p.z - k >= 0)(lambda: pass_on(p.z - k, UP, p.has_up))
        pl.when(p.z + k < p.line)(lambda: pass_on(p.z + k, DOWN, p.has_down))

    def near_blocks(self, k, body):
        p = self.place
        if k == 0:
            body(p.z)
            return
        pl.when(p.z - k >= 0)(lambda: body(p.z - k))
        pl.when(p.z + k < p.line)(lambda: body(p.z + k))

    def y_step(self, k):
        def body(block):
            self.landed(YWAY, block).wait_recv()
            self.copy(XWAY, block).start()
            self.copy(COREY, block).start()

        self.near_blocks(k, body)

    def x_step(self, k):
        def body(block):
            self.landed(XWAY, block).wait_recv()
            self.copy(COREX, block).start()

        self.near_blocks(k, body)

    def stage(self, j):
        line = self.place.line
        if j == 0:
            self.first()
        if 1 <= j < line:
            self.line_step(j)
        if 1 <= j <= line:
            self.y_step(j - 1)
        if 2 <= j <= line + 1:
            self.x_step(j - 2)

    def arrive(self):
        p = self.place
        self.own_copy().wait()

        def body(block, carry):
            pl.when(block != p.z)(lambda: self.landed(CORE, block).wait_recv())
            self.landed(COREY, block).wait_recv()
            self.landed(COREX, block).wait_recv()
            return carry

        lax.fori_loop(0, p.line, body, 0)

    def drain(self):
        p = self.place

        def body(block, carry):
            pl.when(p.has_up & (block <= p.z))(lambda: self.copy(UP, block).wait_send())
            pl.when(p.has_down & (block >= p.z))(lambda: self.copy(DOWN, block).wait_send())
            pl.when(block != p.z)(lambda: self.copy(CORE, block).wait_send())
            for kind in (YWAY, XWAY, COREY, COREX):
                self.copy(kind, block).wait_send()
            return carry

        lax.fori_loop(0, p.line, body, 0)


GATHER_STAGES = 2


def gather_kernel(line, order, *refs):
    owned, small, fulls, small_all = refs[:4], refs[4], refs[5:13], refs[13]
    send, recv, near, small_send, small_recv = refs[14:]
    place = Place(line)
    place.greet()
    smalls = []
    for step in range(1, 2 * line):
        other = lax.rem(place.fs + step, 2 * line)
        smalls.append(
            remote(small, small_all.at[place.fs], small_send.at[step], small_recv.at[place.fs], (place.dp, other))
        )
        smalls[-1].start()
    kept = pltpu.make_async_copy(small, small_all.at[place.fs], small_send.at[0])
    kept.start()
    units = [
        Gather(at, place, owned[which].at[layer], fulls[layer * 4 + which], send, recv, near)
        for at, (layer, which) in enumerate(order)
    ]
    stages = line + GATHER_STAGES
    for slot in range(len(units) + stages - 1):
        for j in range(stages):
            if 0 <= slot - j < len(units):
                units[slot - j].stage(j)
    for unit in units:
        unit.arrive()
    for unit in units:
        unit.drain()
    kept.wait()
    for step in range(1, 2 * line):
        other = lax.rem(place.fs + step, 2 * line)
        smalls[step - 1].wait_send()
        remote(
            small, small_all.at[other], small_send.at[step], small_recv.at[other], (place.dp, other)
        ).wait_recv()


def gather_all(line, owned, small):
    width = [ref.shape for ref in owned]
    outs = [
        jax.ShapeDtypeStruct((2 * line * width[which][1], width[which][2]), owned[which].dtype)
        for layer in range(2)
        for which in range(4)
    ]
    outs.append(jax.ShapeDtypeStruct((2 * line, *small.shape), small.dtype))
    order = [(layer, which) for layer in range(2) for which in range(4)]
    anywhere = pl.BlockSpec(memory_space=pl.ANY)
    return pl.pallas_call(
        functools.partial(gather_kernel, line, order),
        out_shape=outs,
        in_specs=[anywhere] * 5,
        out_specs=[anywhere] * 9,
        scratch_shapes=[
            pltpu.SemaphoreType.DMA((8, 7, line)),
            pltpu.SemaphoreType.DMA((8, 7, line)),
            pltpu.SemaphoreType.DMA((8,)),
            pltpu.SemaphoreType.DMA((2 * line,)),
            pltpu.SemaphoreType.DMA((2 * line,)),
        ],
        compiler_params=pltpu.CompilerParams(collective_id=0, has_side_effects=True),
    )(*owned, small)


class Reduce:
    def __init__(self, at, place, terms, out, bufs, send, recv, near):
        self.at, self.place, self.terms, self.out = at, place, terms, out
        self.mine, self.other, self.from_x, self.from_y, self.line_in, self.last_x, self.total = bufs
        self.send, self.recv, self.near = send, recv, near
        self.deep, self.half = self.mine.shape[2], self.mine.shape[3] // 2

    def cols_of(self, x):
        return pl.ds(pl.multiple_of(x * self.half, 128), self.half)

    def sems(self, kind, block=0):
        return self.send.at[self.at, kind, block], self.recv.at[self.at, kind, block]

    def core_copy(self):
        p = self.place
        return remote(self.terms.at[:, :, 1 - p.c], self.other, *self.sems(0), p.core)

    def near_copy(self):
        return pltpu.make_async_copy(self.terms.at[:, :, self.place.c], self.mine, self.near.at[self.at])

    def x_copy(self):
        p = self.place
        return remote(self.mine.at[:, 1 - p.y, :, self.cols_of(1 - p.x)], self.from_x, *self.sems(1), p.xway)

    def y_copy(self):
        p = self.place
        return remote(self.mine.at[:, 1 - p.y, :, self.cols_of(p.x)], self.from_y, *self.sems(2), p.yway)

    def line_copy(self, way, block):
        p = self.place
        return remote(
            self.mine.at[block, p.y], self.line_in.at[way, block], *self.sems(3 + way, block), (p.up, p.down)[way]
        )

    def last_copy(self):
        p = self.place
        return remote(self.mine.at[p.z, p.y], self.last_x, *self.sems(5), p.xway)

    def out_rows(self, c):
        return self.out.at[pl.ds(pl.multiple_of(c * self.deep, 8), self.deep)]

    def out_copy(self):
        return remote(self.total, self.out_rows(self.place.c), *self.sems(6), self.place.core)

    def out_near(self):
        return pltpu.make_async_copy(self.total, self.out_rows(self.place.c), self.near.at[self.at])

    def start(self):
        self.core_copy().start()
        self.near_copy().start()

    def add_core(self):
        self.near_copy().wait()
        self.core_copy().wait_recv()
        lines = self.mine.shape[0]

        def body(at, carry):
            block, y = at // 2, at % 2
            self.mine[block, y] = self.mine[block, y] + self.other[block, y]
            return carry

        lax.fori_loop(0, 2 * lines, body, 0)
        self.x_copy().start()

    def add_x(self):
        p = self.place
        self.x_copy().wait_recv()
        cols = self.cols_of(p.x)

        def body(block, carry):
            self.mine[block, 1 - p.y, :, cols] = self.mine[block, 1 - p.y, :, cols] + self.from_x[block]
            return carry

        lax.fori_loop(0, self.mine.shape[0], body, 0)
        self.y_copy().start()

    def add_y(self):
        p = self.place
        self.y_copy().wait_recv()
        cols = self.cols_of(p.x)

        def body(block, carry):
            self.mine[block, p.y, :, cols] = self.mine[block, p.y, :, cols] + self.from_y[block]
            return carry

        lax.fori_loop(0, self.mine.shape[0], body, 0)

    def add_line(self, way, block):
        p = self.place
        self.line_copy(way, block).wait_recv()
        self.mine[block, p.y] = self.mine[block, p.y] + self.line_in[way, block]

    def line_step(self, k):
        p, line = self.place, self.place.line
        far = line - 1 - k
        for way, block, valid, more in (
            (0, far, far > p.z, p.has_down),
            (1, k, k < p.z, p.has_up),
        ):

            def body(way=way, block=block, more=more):
                pl.when(more)(lambda: self.add_line(way, block))
                self.line_copy(way, block).start()

            pl.when(valid)(body)

    def own_step(self):
        p = self.place
        pl.when(p.has_down)(lambda: self.add_line(0, p.z))
        pl.when(p.has_up)(lambda: self.add_line(1, p.z))
        self.last_copy().start()

    def finish(self):
        p = self.place
        self.last_copy().wait_recv()
        self.total[...] = self.mine[p.z, p.y].astype(jnp.float32) + self.last_x[...].astype(jnp.float32)
        self.out_copy().start()
        self.out_near().start()

    def stages(self):
        line = self.place.line
        steps = [self.start, self.add_core, self.add_x, self.add_y]
        steps += [functools.partial(self.line_step, k) for k in range(line - 1)]
        return steps + [self.own_step, self.finish]

    def drain(self):
        p = self.place
        self.core_copy().wait_send()
        self.x_copy().wait_send()
        self.y_copy().wait_send()
        for block in range(p.line):
            pl.when(block > p.z)(lambda: self.line_copy(0, block).wait_send())
            pl.when(block < p.z)(lambda: self.line_copy(1, block).wait_send())
        self.last_copy().wait_send()
        self.out_copy().wait()
        self.out_near().wait()


def reduce_kernel(line, order, *refs):
    terms, small, outs, small_out = refs[:8], refs[8], refs[9:13], refs[13]
    bufs, refs = refs[14 : 14 + 7 * 8], refs[14 + 7 * 8 :]
    small_in, small_sum, small_four, send, recv, near, small_send, small_recv = refs
    place = Place(line)
    place.greet()
    fs, dp, n = place.fs, place.dp, 2 * line
    for step in range(1, n):
        other = lax.rem(fs + step, n)
        remote(small.at[other], small_in.at[fs], small_send.at[0, other], small_recv.at[0, fs], (dp, other)).start()
    kept = pltpu.make_async_copy(small.at[fs], small_in.at[fs], small_send.at[0, fs])
    kept.start()
    units = [
        Reduce(at, place, terms[layer * 4 + which], outs[which].at[layer], bufs[7 * at : 7 * at + 7], send, recv, near)
        for at, (layer, which) in enumerate(order)
    ]
    steps = [unit.stages() for unit in units]
    deep = len(steps[0])
    for slot in range(len(units) + deep - 1):
        if slot == 2:
            kept.wait()
            for step in range(1, n):
                other = lax.rem(fs + step, n)
                remote(
                    small.at[other], small_in.at[other], small_send.at[0, other], small_recv.at[0, other], (dp, other)
                ).wait()
            small_sum[...] = jnp.sum(small_in[...], axis=0)
            small_four[dp] = small_sum[...]
            for step in range(1, 4):
                other = lax.rem(dp + step, 4)
                remote(
                    small_sum, small_four.at[dp], small_send.at[1, other], small_recv.at[1, dp], (other, fs)
                ).start()
        if slot == 4:
            for step in range(1, 4):
                other = lax.rem(dp + step, 4)
                remote(
                    small_sum, small_four.at[other], small_send.at[1, other], small_recv.at[1, other], (other, fs)
                ).wait()
            small_out[...] = jnp.sum(small_four[...], axis=0)
        for j in range(deep):
            if 0 <= slot - j < len(units):
                steps[slot - j][j]()
    for unit in units:
        unit.drain()


def reduce_all(line, terms, small):
    order = [(layer, which) for layer in range(2) for which in (3, 2, 1, 0)]
    split, bufs = [], []
    for term in terms:
        deep = term.shape[0] // (4 * line)
        split.append(term.reshape(line, 2, 2, deep, term.shape[1]))
    for layer, which in order:
        _, _, _, deep, width = split[layer * 4 + which].shape
        low = jnp.bfloat16
        bufs += [
            pltpu.VMEM((line, 2, deep, width), low),
            pltpu.VMEM((line, 2, deep, width), low),
            pltpu.VMEM((line, deep, width // 2), low),
            pltpu.VMEM((line, deep, width // 2), low),
            pltpu.VMEM((2, line, deep, width), low),
            pltpu.VMEM((deep, width), low),
            pltpu.VMEM((deep, width), jnp.float32),
        ]
    outs = [
        jax.ShapeDtypeStruct((2, split[which].shape[3] * 2, split[which].shape[4]), jnp.float32) for which in range(4)
    ]
    outs.append(jax.ShapeDtypeStruct(small.shape[1:], jnp.float32))
    anywhere = pl.BlockSpec(memory_space=pl.ANY)
    inside = pl.BlockSpec(memory_space=pltpu.VMEM)
    return pl.pallas_call(
        functools.partial(reduce_kernel, line, order),
        out_shape=outs,
        in_specs=[anywhere] * 8 + [inside],
        out_specs=[anywhere] * 4 + [inside],
        scratch_shapes=bufs
        + [
            pltpu.VMEM(small.shape, jnp.float32),
            pltpu.VMEM(small.shape[1:], jnp.float32),
            pltpu.VMEM((4, *small.shape[1:]), jnp.float32),
            pltpu.SemaphoreType.DMA((8, 7, line)),
            pltpu.SemaphoreType.DMA((8, 7, line)),
            pltpu.SemaphoreType.DMA((8,)),
            pltpu.SemaphoreType.DMA((2, 2 * line)),
            pltpu.SemaphoreType.DMA((2, 2 * line)),
        ],
        compiler_params=pltpu.CompilerParams(collective_id=1, has_side_effects=True, vmem_limit_bytes=62 * 2**20),
    )(*split, small)

def normed(values, gain, shift):
    center = values - jnp.mean(values, axis=-1, keepdims=True)
    spread = jnp.mean(center * center, axis=-1, keepdims=True)
    return center * lax.rsqrt(spread + 1e-05) * gain + shift


def gelu_exact(values):
    return jax.nn.gelu(values, approximate=False)


def segment_ids(lengths, seq_len):
    bounds = jnp.cumsum(lengths, axis=-1)
    positions = jnp.arange(seq_len, dtype=jnp.int32)
    return jnp.sum((positions[None, :, None] >= bounds[:, None, :]).astype(jnp.int32), axis=-1)


def split_heads(values):
    batch, length, width = values.shape
    return values.reshape(batch, length, width // HEAD, HEAD)


def masked_scores(queries, keys_all, segment):
    scores = jnp.einsum(
        "bqhd,bkhd->bhqk",
        split_heads(queries),
        split_heads(keys_all),
        preferred_element_type=jnp.float32,
    )
    same = (segment[:, :, None] == segment[:, None, :])[:, None]
    return (jnp.where(same, scores, -1e30), same)


def attention(queries, keys_all, values_all, segment):
    scores, same = masked_scores(queries, keys_all, segment)
    largest = jnp.max(scores, axis=-1, keepdims=True)
    raised = jnp.exp(scores - largest)
    totals = jnp.sum(raised, axis=-1, keepdims=True)
    attn_weights = raised / totals
    log_total = largest + jnp.log(totals)
    mixed = jnp.einsum(
        "bhqk,bkhd->bqhd",
        attn_weights.astype(jnp.bfloat16),
        split_heads(values_all),
        preferred_element_type=jnp.float32,
    )
    return (mixed.reshape(queries.shape).astype(jnp.bfloat16), log_total)


def attention_back(queries, keys_all, values_all, segment, log_total, grad_mixed):
    scores, same = masked_scores(queries, keys_all, segment)
    attn_weights = jnp.where(same, jnp.exp(scores - log_total), 0.0)
    grad_heads = split_heads(grad_mixed)
    grad_weights = jnp.einsum(
        "bqhd,bkhd->bhqk", grad_heads, split_heads(values_all), preferred_element_type=jnp.float32
    )
    inner = jnp.sum(attn_weights * grad_weights, axis=-1, keepdims=True)
    grad_scores = (attn_weights * (grad_weights - inner)).astype(jnp.bfloat16)
    grad_queries = jnp.einsum(
        "bhqk,bkhd->bqhd", grad_scores, split_heads(keys_all), preferred_element_type=jnp.float32
    )
    grad_keys = jnp.einsum(
        "bhqk,bqhd->bkhd", grad_scores, split_heads(queries), preferred_element_type=jnp.float32
    )
    grad_values = jnp.einsum(
        "bhqk,bqhd->bkhd",
        attn_weights.astype(jnp.bfloat16),
        grad_heads,
        preferred_element_type=jnp.float32,
    )
    shape_rows = queries.shape
    return (
        grad_queries.reshape(shape_rows),
        grad_keys.reshape(shape_rows),
        grad_values.reshape(shape_rows),
    )


def forward_layer(inputs, weights, segment):
    qkv_weight, out_weight, up_weight, down_weight, gains, biases, up_bias = weights
    width = inputs.shape[-1]
    source = inputs.astype(jnp.float32)
    normed_a = normed(source, gains[0], biases[0]).astype(jnp.bfloat16)
    project = jnp.einsum("bld,de->ble", normed_a, qkv_weight, preferred_element_type=jnp.float32)
    queries = ((project[..., :width] + biases[2]) * HEAD ** (-0.5)).astype(jnp.bfloat16)
    keys_all = project[..., width : 2 * width].astype(jnp.bfloat16)
    values_all = (project[..., 2 * width :] + biases[3]).astype(jnp.bfloat16)
    mixed, log_total = attention(queries, keys_all, values_all, segment)
    hidden = (
        source
        + jnp.einsum("bld,de->ble", mixed, out_weight, preferred_element_type=jnp.float32)
        + biases[4]
    )
    normed_c = normed(hidden, gains[1], biases[1]).astype(jnp.bfloat16)
    before = (
        jnp.einsum("bld,df->blf", normed_c, up_weight, preferred_element_type=jnp.float32) + up_bias
    )
    activated = gelu_exact(before).astype(jnp.bfloat16)
    result = (
        hidden
        + jnp.einsum("blf,fd->bld", activated, down_weight, preferred_element_type=jnp.float32)
        + biases[5]
    )
    return (
        source,
        normed_a,
        queries,
        keys_all,
        values_all,
        log_total,
        mixed,
        hidden,
        normed_c,
        before,
        activated,
        result,
    )


def backward_layer(inputs, cotangent, weights, segment):
    qkv_weight, out_weight, up_weight, down_weight, gains, biases, up_bias = weights
    width = inputs.shape[-1]
    (
        source,
        normed_a,
        queries,
        keys_all,
        values_all,
        log_total,
        mixed,
        hidden,
        normed_c,
        before,
        activated,
        result,
    ) = forward_layer(inputs, weights, segment)
    grad_result = cotangent.astype(jnp.float32)
    grad_downw = jnp.einsum("blf,bld->fd", activated, cotangent, preferred_element_type=jnp.float32)
    grad_act = jnp.einsum("bld,fd->blf", cotangent, down_weight, preferred_element_type=jnp.float32)
    grad_before = jax.vjp(gelu_exact, before)[1](grad_act)[0].astype(jnp.bfloat16)
    grad_upw = jnp.einsum("bld,blf->df", normed_c, grad_before, preferred_element_type=jnp.float32)
    grad_upb = jnp.sum(grad_before.astype(jnp.float32), axis=(0, 1))
    grad_normc = jnp.einsum(
        "blf,df->bld", grad_before, up_weight, preferred_element_type=jnp.float32
    )
    hidden_back = jax.vjp(
        normed, hidden, gains[1].astype(jnp.float32), biases[1].astype(jnp.float32)
    )[1]
    grad_hidden_ln, grad_gain_two, grad_shift_two = hidden_back(grad_normc)
    grad_hidden = grad_result + grad_hidden_ln
    grad_branch = grad_hidden.astype(jnp.bfloat16)
    grad_outw = jnp.einsum("bld,ble->de", mixed, grad_branch, preferred_element_type=jnp.float32)
    grad_mixed = jnp.einsum(
        "ble,de->bld", grad_branch, out_weight, preferred_element_type=jnp.float32
    ).astype(jnp.bfloat16)
    grad_queries, grad_keys, grad_values = attention_back(
        queries, keys_all, values_all, segment, log_total, grad_mixed
    )
    grad_project = jnp.concatenate(
        [
            grad_queries.astype(jnp.bfloat16) * HEAD ** (-0.5),
            grad_keys.astype(jnp.bfloat16),
            grad_values.astype(jnp.bfloat16),
        ],
        axis=-1,
    )
    grad_qkvw = jnp.einsum(
        "bld,ble->de", normed_a, grad_project, preferred_element_type=jnp.float32
    )
    column_sums = jnp.sum(grad_project.astype(jnp.float32), axis=(0, 1))
    grad_norma = jnp.einsum(
        "ble,de->bld", grad_project, qkv_weight, preferred_element_type=jnp.float32
    )
    source_back = jax.vjp(
        normed, source, gains[0].astype(jnp.float32), biases[0].astype(jnp.float32)
    )[1]
    grad_source_ln, grad_gain_one, grad_shift_one = source_back(grad_norma)
    grad_inputs = grad_hidden + grad_source_ln
    grad_gains = jnp.stack([grad_gain_one, grad_gain_two])
    grad_biases = jnp.stack(
        [
            grad_shift_one,
            grad_shift_two,
            column_sums[:width],
            column_sums[2 * width :],
            jnp.sum(grad_branch.astype(jnp.float32), axis=(0, 1)),
            jnp.sum(grad_result, axis=(0, 1)),
        ]
    )
    return (
        result.astype(jnp.bfloat16),
        grad_inputs,
        (grad_qkvw, grad_outw, grad_upw, grad_downw, grad_gains, grad_biases, grad_upb),
    )


def fetch_weights(layer_index, w_qkv, w_out, w_up, w_down, gains, biases, b_up):
    return (
        lax.all_gather(w_qkv[layer_index], "fsdp", axis=0, tiled=True),
        lax.all_gather(w_out[layer_index], "fsdp", axis=0, tiled=True),
        lax.all_gather(w_up[layer_index], "fsdp", axis=0, tiled=True),
        lax.all_gather(w_down[layer_index], "fsdp", axis=0, tiled=True),
        lax.all_gather(gains[layer_index], "fsdp", axis=1, tiled=True),
        lax.all_gather(biases[layer_index], "fsdp", axis=1, tiled=True),
        lax.all_gather(b_up[layer_index], "fsdp", axis=0, tiled=True),
    )


def fetch_again(layer_index, w_qkv, w_out, w_up, w_down, gains, biases, b_up):
    return (
        lax.all_gather(w_qkv[layer_index], "fsdp", axis=0, tiled=True),
        lax.all_gather(w_out[layer_index], "fsdp", axis=0, tiled=True),
        lax.all_gather(w_up[layer_index], "fsdp", axis=0, tiled=True),
        lax.all_gather(w_down[layer_index], "fsdp", axis=0, tiled=True),
        lax.all_gather(gains[layer_index], "fsdp", axis=1, tiled=True),
        lax.all_gather(biases[layer_index], "fsdp", axis=1, tiled=True),
        lax.all_gather(b_up[layer_index], "fsdp", axis=0, tiled=True),
    )


def reduce_grads(gradients):
    shares = (
        lax.psum_scatter(gradients[0], "fsdp", scatter_dimension=0, tiled=True),
        lax.psum_scatter(gradients[1], "fsdp", scatter_dimension=0, tiled=True),
        lax.psum_scatter(gradients[2], "fsdp", scatter_dimension=0, tiled=True),
        lax.psum_scatter(gradients[3], "fsdp", scatter_dimension=0, tiled=True),
        lax.psum_scatter(gradients[4], "fsdp", scatter_dimension=1, tiled=True),
        lax.psum_scatter(gradients[5], "fsdp", scatter_dimension=1, tiled=True),
        lax.psum_scatter(gradients[6], "fsdp", scatter_dimension=0, tiled=True),
    )
    quarters = (
        lax.psum_scatter(
            shares[0].astype(jnp.bfloat16), "dp", scatter_dimension=0, tiled=True
        ).astype(jnp.float32),
        lax.psum_scatter(
            shares[1].astype(jnp.bfloat16), "dp", scatter_dimension=0, tiled=True
        ).astype(jnp.float32),
        lax.psum_scatter(
            shares[2].astype(jnp.bfloat16), "dp", scatter_dimension=0, tiled=True
        ).astype(jnp.float32),
        lax.psum_scatter(
            shares[3].astype(jnp.bfloat16), "dp", scatter_dimension=0, tiled=True
        ).astype(jnp.float32),
        lax.psum_scatter(
            shares[4].astype(jnp.bfloat16), "dp", scatter_dimension=1, tiled=True
        ).astype(jnp.float32),
        lax.psum_scatter(
            shares[5].astype(jnp.bfloat16), "dp", scatter_dimension=1, tiled=True
        ).astype(jnp.float32),
        lax.psum_scatter(
            shares[6].astype(jnp.bfloat16), "dp", scatter_dimension=0, tiled=True
        ).astype(jnp.float32),
    )
    return (
        lax.all_gather(quarters[0].astype(jnp.bfloat16), "dp", axis=0, tiled=True).astype(
            jnp.float32
        ),
        lax.all_gather(quarters[1].astype(jnp.bfloat16), "dp", axis=0, tiled=True).astype(
            jnp.float32
        ),
        lax.all_gather(quarters[2].astype(jnp.bfloat16), "dp", axis=0, tiled=True).astype(
            jnp.float32
        ),
        lax.all_gather(quarters[3].astype(jnp.bfloat16), "dp", axis=0, tiled=True).astype(
            jnp.float32
        ),
        lax.all_gather(quarters[4].astype(jnp.bfloat16), "dp", axis=1, tiled=True).astype(
            jnp.float32
        ),
        lax.all_gather(quarters[5].astype(jnp.bfloat16), "dp", axis=1, tiled=True).astype(
            jnp.float32
        ),
        lax.all_gather(quarters[6].astype(jnp.bfloat16), "dp", axis=0, tiled=True).astype(
            jnp.float32
        ),
    )


def plain(
    images,
    image_cot,
    captions,
    caption_cot,
    lengths,
    w_qkv,
    w_out,
    w_up,
    w_down,
    gains,
    biases,
    b_up,
):
    owned = (w_qkv, w_out, w_up, w_down, gains, biases, b_up)
    image_seg = jnp.zeros((images.shape[0], images.shape[1]), jnp.int32)
    caption_seg = segment_ids(lengths, captions.shape[1])
    first_weights = fetch_weights(0, *owned)
    image_out = forward_layer(images, first_weights, image_seg)[-1].astype(jnp.bfloat16)
    second_weights = fetch_weights(1, *owned)
    caption_out = forward_layer(captions, second_weights, caption_seg)[-1].astype(jnp.bfloat16)
    second_back = fetch_again(1, *owned)
    _, caption_grad, caption_terms = backward_layer(captions, caption_cot, second_back, caption_seg)
    caption_shares = reduce_grads(caption_terms)
    first_back = fetch_again(0, *owned)
    _, image_grad, image_terms = backward_layer(images, image_cot, first_back, image_seg)
    image_shares = reduce_grads(image_terms)
    stacked = tuple((jnp.stack([image_shares[index], caption_shares[index]]) for index in range(7)))
    return (image_out, caption_out, image_grad, caption_grad) + stacked


def kernels_fit(mesh, w_qkv):
    return mesh.shape["dp"] == 4 and mesh.shape["fsdp"] % 2 == 0 and w_qkv.shape[1] % 32 == 0


def pack_small(gains, biases, b_up):
    rows = jnp.concatenate([gains.reshape(2, -1), biases.reshape(2, -1), b_up], axis=1).astype(jnp.float32).reshape(-1)
    return jnp.pad(rows, (0, -rows.size % 1024)).reshape(-1, 128)


def unpack_small(blocks, width, deep):
    count = blocks.shape[0]
    flat = blocks.reshape(count, -1)[:, : 2 * (8 * width + deep)].reshape(count, 2, 8 * width + deep)
    rows = flat[:, :, : 8 * width].reshape(count, 2, 8, width).transpose(1, 2, 0, 3).reshape(2, 8, count * width)
    up = flat[:, :, 8 * width :].transpose(1, 0, 2).reshape(2, count * deep)
    return rows[:, :2], rows[:, 2:], up


def spread_small(count, gains, biases, b_up):
    rows = jnp.concatenate([gains, biases], axis=1)
    width, deep = rows.shape[2] // count, b_up.shape[1] // count
    rows = rows.reshape(2, 8, count, width).transpose(2, 0, 1, 3).reshape(count, 2, 8 * width)
    up = b_up.reshape(2, count, deep).transpose(1, 0, 2)
    flat = jnp.concatenate([rows, up], axis=2).reshape(count, -1)
    return jnp.pad(flat, ((0, 0), (0, -flat.shape[1] % 1024))).reshape(count, -1, 128)


def local(mesh, images, image_cot, captions, caption_cot, lengths, w_qkv, w_out, w_up, w_down, gains, biases, b_up):
    if not kernels_fit(mesh, w_qkv):
        return plain(
            images, image_cot, captions, caption_cot, lengths, w_qkv, w_out, w_up, w_down, gains, biases, b_up
        )
    count = mesh.shape["fsdp"]
    line = count // 2
    width, deep = gains.shape[2], b_up.shape[1]
    *fulls, small = gather_all(line, (w_qkv, w_out, w_up, w_down), pack_small(gains, biases, b_up))
    gains_all, biases_all, up_all = unpack_small(small, width, deep)
    outs, grads, terms, smalls = [], [], [], []
    image_seg = jnp.zeros((images.shape[0], images.shape[1]), jnp.int32)
    caption_seg = segment_ids(lengths, captions.shape[1])
    for layer, (rows, cot, seg) in enumerate(((images, image_cot, image_seg), (captions, caption_cot, caption_seg))):
        weights = (*fulls[layer * 4 : layer * 4 + 4], gains_all[layer], biases_all[layer], up_all[layer])
        result, grad, found = backward_layer(rows, cot, weights, seg)
        outs.append(result)
        grads.append(grad)
        terms += [term.astype(jnp.bfloat16) for term in found[:4]]
        smalls.append(found[4:])
    packed = spread_small(count, *(jnp.stack([smalls[0][at], smalls[1][at]]) for at in range(3)))
    *shares, small_share = reduce_all(line, terms, packed)
    rest = unpack_small(small_share[None], width, deep)
    return (*outs, *grads, *shares, *rest)


def solution(mesh):
    placed = (
        P(("dp", "fsdp"), None, None),
        P(("dp", "fsdp"), None, None),
        P(("dp", "fsdp"), None, None),
        P(("dp", "fsdp"), None, None),
        P(("dp", "fsdp"), None),
        P(None, "fsdp", None),
        P(None, "fsdp", None),
        P(None, "fsdp", None),
        P(None, "fsdp", None),
        P(None, None, "fsdp"),
        P(None, None, "fsdp"),
        P(None, "fsdp"),
    )
    return jax.shard_map(
        functools.partial(local, mesh),
        mesh=mesh,
        in_specs=placed,
        out_specs=(
            P(("dp", "fsdp"), None, None),
            P(("dp", "fsdp"), None, None),
            P(("dp", "fsdp"), None, None),
            P(("dp", "fsdp"), None, None),
            P(None, "fsdp", None),
            P(None, "fsdp", None),
            P(None, "fsdp", None),
            P(None, "fsdp", None),
            P(None, None, "fsdp"),
            P(None, None, "fsdp"),
            P(None, "fsdp"),
        ),
        check_vma=False,
    )
```

```python
import functools

import jax
import jax.numpy as jnp
from jax import lax
from jax.experimental import pallas as pl
from jax.experimental.pallas import tpu as pltpu
from jax.sharding import PartitionSpec as P

HEAD = 64

NT = (((1,), (1,)), ((), ()))
TN = (((0,), (0,)), ((), ()))
TILE = 256
CHUNK = 64


def dot(a, b, dims=(((1,), (0,)), ((), ()))):
    return lax.dot_general(a, b, dims, preferred_element_type=jnp.float32)


def at(t, size=TILE):
    return pl.ds(pl.multiple_of(t * size, size), size)


def layer_scratch(n, width, deep):
    low, full = jnp.bfloat16, jnp.float32
    return dict(
        x=pltpu.VMEM((n, width), low),
        dy=pltpu.VMEM((n, width), low),
        a=pltpu.VMEM((n, width), low),
        a_t=pltpu.VMEM((width, n), low),
        qkv=pltpu.VMEM((n, 3 * width), low),
        bias=pltpu.VMEM((n, n), full),
        wt=pltpu.VMEM((width // HEAD, n, n), low),
        ds=pltpu.VMEM((2, n, n), low),
        o=pltpu.VMEM((n, width), low),
        o_t=pltpu.VMEM((width, n), low),
        h=pltpu.VMEM((n, width), full),
        c=pltpu.VMEM((n, width), low),
        c_t=pltpu.VMEM((width, n), low),
        g=pltpu.VMEM((n, deep), low),
        du=pltpu.VMEM((n, deep), low),
        sums=pltpu.VMEM((n, width), full),
        dh=pltpu.VMEM((n, width), full),
        rows=pltpu.VMEM((8, 3 * width), full),
        tall=pltpu.VMEM((2, width, TILE), low),
        wide=pltpu.VMEM((2, TILE, width), low),
        tall_sem=pltpu.SemaphoreType.DMA((2,)),
        wide_sem=pltpu.SemaphoreType.DMA((2,)),
    )


class Layer:
    def __init__(self, n, kept, weights, small, terms, outs):
        self.n, self.s = n, kept
        self.w_qkv, self.w_out, self.w_up, self.w_down = weights
        self.par, self.b_up = small
        self.g_qkv, self.g_out, self.g_up, self.g_down = terms
        self.y_out, self.x_grad, self.g_par, self.g_bup = outs
        self.width, self.deep = self.w_qkv.shape[0], self.w_up.shape[1]

    def chunks(self, body):
        def step(i, carry):
            body(at(i, CHUNK))
            return carry

        lax.fori_loop(0, self.n // CHUNK, step, 0)

    def tiles(self, first, last, body):
        def step(i, carry):
            body(i)
            return carry

        lax.fori_loop(first, last, step, 0)

    def row(self, ref, i):
        return ref[i : i + 1, :]

    def tall_copy(self, ref, slot, t):
        return pltpu.make_async_copy(self.s["tall"].at[slot], ref.at[:, at(t)], self.s["tall_sem"].at[slot])

    def wide_copy(self, ref, slot, t):
        return pltpu.make_async_copy(self.s["wide"].at[slot], ref.at[at(t)], self.s["wide_sem"].at[slot])

    def put(self, copy, buf, ref, t, count, value):
        slot = lax.rem(t, 2)
        pl.when(t >= 2)(lambda: copy(ref, slot, t - 2).wait())
        buf[slot] = value.astype(jnp.bfloat16)
        copy(ref, slot, t).start()

    def put_end(self, copy, ref, count):
        for t in range(max(0, count - 2), count):
            copy(ref, t % 2, t).wait()

    def load(self, x, dy, seg_col, seg_row):
        s, have = self.s, x.shape[0]
        if have < self.n:
            start = have // 16 * 16
            s["x"][start:, :] = jnp.zeros((self.n - start, self.width), jnp.bfloat16)
            s["dy"][start:, :] = jnp.zeros((self.n - start, self.width), jnp.bfloat16)
        s["x"][0:have, :] = x[...]
        s["dy"][0:have, :] = dy[...]
        s["bias"][...] = jnp.where(seg_col[...] == seg_row[...], 0.0, -1e30)
        self.g_par[...] = jnp.zeros_like(self.g_par)
        width = self.width
        s["rows"][0:1, 0:width] = self.par[4:5, :]
        s["rows"][0:1, width : 2 * width] = jnp.zeros((1, width), jnp.float32)
        s["rows"][0:1, 2 * width :] = self.par[5:6, :]

    def norm_parts(self, values):
        center = values - jnp.mean(values, axis=-1, keepdims=True)
        scale = lax.rsqrt(jnp.mean(center * center, axis=-1, keepdims=True) + 1e-05)
        return center * scale, scale

    def norm(self, src, dst, which):
        def body(rows):
            unit, _ = self.norm_parts(src[rows, :].astype(jnp.float32))
            dst[rows, :] = (unit * self.row(self.par, which) + self.row(self.par, 2 + which)).astype(jnp.bfloat16)

        self.chunks(body)

    def norm_a(self):
        self.norm(self.s["x"], self.s["a"], 0)

    def project(self):
        s = self.s
        queries = self.width // TILE

        def body(t):
            scale = jnp.where(t < queries, HEAD ** (-0.5), 1.0)
            found = dot(s["a"][...], self.w_qkv[:, at(t)]) + s["rows"][0:1, at(t)]
            s["qkv"][:, at(t)] = (found * scale).astype(jnp.bfloat16)

        self.tiles(0, 3 * queries, body)
        s["a_t"][...] = s["a"][...].T

    def pair(self, i, which):
        start = which * self.width + i * 128
        return self.s["qkv"].at[:, pl.ds(pl.multiple_of(start, 128), 128)]

    def own_lanes(self, value, head):
        lanes = lax.broadcasted_iota(jnp.int32, value.shape, 1)
        return jnp.where((lanes < HEAD) == (head == 0), value, jnp.zeros_like(value))

    def attend(self, first, last):
        s = self.s

        def body(i):
            q, k, v = (self.pair(i, which) for which in range(3))
            keys = [self.own_lanes(k[...], head) for head in range(2)]
            vals = [self.own_lanes(v[...], head) for head in range(2)]
            for part in range(self.n // TILE):
                cols = slice(part * TILE, part * TILE + TILE)
                mixed = None
                for head in range(2):
                    scores = dot(keys[head], q[cols, :], NT) + s["bias"][:, cols]
                    raised = jnp.exp(scores - jnp.max(scores, axis=0, keepdims=True))
                    share = 1.0 / jnp.sum(raised, axis=0, keepdims=True)
                    weights = (raised * share).astype(jnp.bfloat16)
                    s["wt"][2 * i + head, :, cols] = weights
                    found = dot(vals[head], weights, TN)
                    mixed = found if mixed is None else mixed + found
                s["o"][cols, at(i, 128)] = mixed.T.astype(jnp.bfloat16)

        self.tiles(first, last, body)

    def branch(self):
        s = self.s

        def body(t):
            found = dot(s["o"][...], self.w_out[:, at(t)]) + self.par[6:7, at(t)]
            s["h"][:, at(t)] = s["x"][:, at(t)].astype(jnp.float32) + found

        self.tiles(0, self.width // TILE, body)
        s["o_t"][...] = s["o"][...].T

    def norm_c(self):
        self.norm(self.s["h"], self.s["c"], 1)

    def up(self, first, last):
        s = self.s

        def body(t):
            before = dot(s["c"][...], self.w_up[:, at(t)]) + self.b_up[0:1, at(t)]
            chance = 0.5 + 0.5 * lax.erf(before * 0.7071067811865476)
            s["g"][:, at(t)] = (before * chance).astype(jnp.bfloat16)
            slope = chance + before * (jnp.exp(before * before * -0.5) * 0.3989422804014327)
            s["du"][:, at(t)] = slope.astype(jnp.bfloat16)

        self.tiles(first, last, body)

    def turn_c(self):
        self.s["c_t"][...] = self.s["c"][...].T

    def down(self):
        s = self.s

        def body(t):
            found = dot(s["g"][...], self.w_down[:, at(t)]) + self.par[7:8, at(t)]
            s["sums"][:, at(t)] = s["h"][:, at(t)] + found

        self.tiles(0, self.width // TILE, body)
        have = self.y_out.shape[0]
        self.y_out[...] = s["sums"][0:have, :].astype(jnp.bfloat16)

    def feed_back(self, first, last):
        s = self.s
        count = self.deep // TILE

        def body(t):
            grad = dot(s["dy"][...], self.w_down[at(t), :], NT)
            low = (grad * s["du"][:, at(t)].astype(jnp.float32)).astype(jnp.bfloat16)
            s["du"][:, at(t)] = low
            self.g_bup[0:1, at(t)] = jnp.sum(low.astype(jnp.float32), axis=0, keepdims=True)
            self.put(self.wide_copy, s["wide"], self.g_down, t, count, dot(s["g"][:, at(t)], s["dy"][...], TN))
            self.put(self.tall_copy, s["tall"], self.g_up, t, count, dot(s["c_t"][...], low))

        self.tiles(first, last, body)

    def feed_end(self):
        self.put_end(self.wide_copy, self.g_down, self.deep // TILE)
        self.put_end(self.tall_copy, self.g_up, self.deep // TILE)

    def up_back(self):
        s = self.s

        def body(t):
            s["sums"][:, at(t)] = dot(s["du"][...], self.w_up[at(t), :], NT)

        self.tiles(0, self.width // TILE, body)

    def norm_back(self, src, which, grad, rest, body_out):
        def body(rows):
            unit, scale = self.norm_parts(src[rows, :].astype(jnp.float32))
            came = grad[rows, :]
            gained = came * self.row(self.par, which)
            self.g_par[which : which + 1, :] += jnp.sum(came * unit, axis=0, keepdims=True)
            self.g_par[2 + which : 3 + which, :] += jnp.sum(came, axis=0, keepdims=True)
            inner = gained - jnp.mean(gained, axis=-1, keepdims=True)
            inner = inner - unit * jnp.mean(gained * unit, axis=-1, keepdims=True)
            body_out(rows, rest[rows, :].astype(jnp.float32) + inner * scale)

        self.chunks(body)

    def norm_c_back(self):
        s = self.s

        def keep(rows, grad):
            s["dh"][rows, :] = grad
            low = grad.astype(jnp.bfloat16)
            s["c"][rows, :] = low
            self.g_par[6:7, :] += jnp.sum(low.astype(jnp.float32), axis=0, keepdims=True)
            self.g_par[7:8, :] += jnp.sum(s["dy"][rows, :].astype(jnp.float32), axis=0, keepdims=True)

        self.norm_back(s["h"], 1, s["sums"], s["dy"], keep)

    def branch_back(self):
        s = self.s
        count = self.width // TILE

        def body(t):
            s["a"][:, at(t)] = dot(s["c"][...], self.w_out[at(t), :], NT).astype(jnp.bfloat16)
            self.put(self.tall_copy, s["tall"], self.g_out, t, count, dot(s["o_t"][...], s["c"][:, at(t)]))

        self.tiles(0, count, body)
        self.put_end(self.tall_copy, self.g_out, count)

    def attend_back(self, first, last):
        s, width = self.s, self.width

        def body(i):
            q, k, v = (self.pair(i, which) for which in range(3))
            came = s["a"].at[:, at(i, 128)]
            dq = dk = dv = None
            for head in range(2):
                vals = self.own_lanes(v[...], head)
                for part in range(self.n // TILE):
                    cols = slice(part * TILE, part * TILE + TILE)
                    grad = dot(vals, came[cols, :], NT)
                    weights = s["wt"][2 * i + head, :, cols].astype(jnp.float32)
                    product = weights * grad
                    inner = jnp.sum(product, axis=0, keepdims=True)
                    s["ds"][head, :, cols] = (product - weights * inner).astype(jnp.bfloat16)
                one_q = dot(self.own_lanes(k[...], head), s["ds"][head], TN)
                one_k = dot(s["ds"][head], self.own_lanes(q[...], head))
                one_v = dot(s["wt"][2 * i + head], self.own_lanes(came[...], head))
                dq, dk, dv = (one_q, one_k, one_v) if head == 0 else (dq + one_q, dk + one_k, dv + one_v)
            s["g"][:, at(i, 128)] = dq.T.astype(jnp.bfloat16) * HEAD ** (-0.5)
            s["g"][:, pl.ds(pl.multiple_of(width + i * 128, 128), 128)] = dk.astype(jnp.bfloat16)
            s["g"][:, pl.ds(pl.multiple_of(2 * width + i * 128, 128), 128)] = dv.astype(jnp.bfloat16)

        self.tiles(first, last, body)

    def project_terms(self):
        s = self.s
        count = 3 * self.width // TILE

        def body(t):
            grad = s["g"][:, at(t)]
            s["rows"][1:2, at(t)] = jnp.sum(grad.astype(jnp.float32), axis=0, keepdims=True)
            self.put(self.tall_copy, s["tall"], self.g_qkv, t, count, dot(s["a_t"][...], grad))

        self.tiles(0, count, body)
        self.put_end(self.tall_copy, self.g_qkv, count)
        self.g_par[4:5, :] = s["rows"][1:2, 0 : self.width]
        self.g_par[5:6, :] = s["rows"][1:2, 2 * self.width :]

    def project_back(self):
        s = self.s

        def body(t):
            s["sums"][:, at(t)] = dot(s["g"][:, 0 : 3 * self.width], self.w_qkv[at(t), :], NT)

        self.tiles(0, self.width // TILE, body)

    def norm_a_back(self):
        s = self.s
        have = self.x_grad.shape[0]

        def keep(rows, grad):
            s["dh"][rows, :] = grad

        self.norm_back(s["x"], 0, s["sums"], s["dh"], keep)
        self.x_grad[...] = s["dh"][0:have, :]


def layer_kernel(n, names, *refs):
    x, dy, seg_col, seg_row, par, b_up, *weights = refs[:10]
    y_out, x_grad, g_par, g_bup, *terms = refs[10:18]
    near, *held = refs[18:23]
    kept = dict(zip(names, refs[23:]))
    loads = [pltpu.make_async_copy(weights[i], held[i], near.at[i]) for i in range(4)]
    for load in loads:
        load.start()
    layer = Layer(n, kept, held, (par, b_up), terms, (y_out.at[0], x_grad.at[0], g_par, g_bup))
    heads, tiles = layer.width // 128, layer.deep // TILE
    layer.load(x.at[0], dy.at[0], seg_col, seg_row)
    layer.norm_a()
    loads[0].wait()
    layer.project()
    layer.attend(0, heads)
    loads[1].wait()
    layer.branch()
    layer.norm_c()
    loads[2].wait()
    layer.up(0, tiles)
    layer.turn_c()
    loads[3].wait()
    layer.down()
    layer.feed_back(0, tiles)
    layer.feed_end()
    layer.up_back()
    layer.norm_c_back()
    layer.branch_back()
    layer.attend_back(0, heads)
    layer.project_terms()
    layer.project_back()
    layer.norm_a_back()


def padded(rows):
    return -(-rows // TILE) * TILE


def run_layer(x, dy, segment, weights, par, b_up):
    have, width = x.shape[1:]
    n, deep = padded(have), b_up.shape[1]
    segment = jnp.pad(segment, ((0, 0), (0, n - have)), constant_values=-1)
    kept = layer_scratch(n, width, deep)
    anywhere, inside = pl.BlockSpec(memory_space=pl.ANY), pl.BlockSpec(memory_space=pltpu.VMEM)
    outs = [
        jax.ShapeDtypeStruct(x.shape, jnp.bfloat16),
        jax.ShapeDtypeStruct(x.shape, jnp.float32),
        jax.ShapeDtypeStruct(par.shape, jnp.float32),
        jax.ShapeDtypeStruct(b_up.shape, jnp.float32),
    ] + [jax.ShapeDtypeStruct(weight.shape, jnp.bfloat16) for weight in weights]
    return pl.pallas_call(
        functools.partial(layer_kernel, n, list(kept)),
        out_shape=outs,
        in_specs=[inside] * 6 + [anywhere] * 4,
        out_specs=[inside] * 4 + [anywhere] * 4,
        scratch_shapes=[pltpu.SemaphoreType.DMA((4,))]
        + [pltpu.VMEM(weight.shape, weight.dtype) for weight in weights]
        + list(kept.values()),
        compiler_params=pltpu.CompilerParams(vmem_limit_bytes=62 * 2**20),
    )(x, dy, segment.reshape(n, 1), segment, par, b_up, *weights)


MESH = pl.DeviceIdType.MESH
UP, DOWN, YWAY, XWAY, CORE, COREY, COREX = range(7)


class Place:
    def __init__(self, line):
        dp, fs = lax.axis_index("dp"), lax.axis_index("fsdp")
        self.line = line
        self.dp, self.fs = dp, fs
        self.x, self.c = dp // 2, dp % 2
        self.z, self.y = fs // 2, fs % 2
        self.up = (dp, fs + 2)
        self.down = (dp, fs - 2)
        self.yway = (dp, self.z * 2 + 1 - self.y)
        self.xway = ((1 - self.x) * 2 + self.c, fs)
        self.core = (self.x * 2 + 1 - self.c, fs)
        self.has_up = self.z + 1 < line
        self.has_down = self.z > 0

    def greet(self):
        barrier = pltpu.get_barrier_semaphore()
        total = 0
        for step in range(1, 2 * self.line):
            other = lax.rem(self.fs + step, 2 * self.line)
            pl.semaphore_signal(barrier, inc=1, device_id=(self.dp, other), device_id_type=MESH)
            total += 1
        for step in range(1, 4):
            other = lax.rem(self.dp + step, 4)
            pl.semaphore_signal(barrier, inc=1, device_id=(other, self.fs), device_id_type=MESH)
            total += 1
        pl.semaphore_wait(barrier, total)


def remote(src, dst, send, recv, device):
    return pltpu.make_async_remote_copy(
        src_ref=src, dst_ref=dst, send_sem=send, recv_sem=recv, device_id=device, device_id_type=MESH
    )


class Gather:
    def __init__(self, at, place, own, full, send, recv, near):
        self.at, self.place, self.own, self.full = at, place, own, full
        self.send, self.recv, self.near = send, recv, near
        self.rows = own.shape[0]
        self.deep = self.rows // 2
        self.half = own.shape[1] // 2

    def rows_of(self, block, y, c):
        start = (block * 2 + y) * self.rows + c * self.deep
        return pl.ds(pl.multiple_of(start, 16), self.deep)

    def cols_of(self, x):
        return pl.ds(pl.multiple_of(x * self.half, 128), self.half)

    def copy(self, kind, block):
        p, s, r = self.place, self.send.at[self.at, kind, block], None
        if kind in (UP, DOWN):
            ref = self.full.at[self.rows_of(block, p.y, p.c)]
            return remote(ref, ref, s, self.recv.at[self.at, UP, block], p.up if kind == UP else p.down)
        if kind == YWAY:
            ref = self.full.at[self.rows_of(block, p.y, p.c), self.cols_of(p.x)]
            return remote(ref, ref, s, self.recv.at[self.at, kind, block], p.yway)
        if kind == XWAY:
            ref = self.full.at[self.rows_of(block, 1 - p.y, p.c), self.cols_of(p.x)]
            return remote(ref, ref, s, self.recv.at[self.at, kind, block], p.xway)
        if kind == CORE:
            ref = self.full.at[self.rows_of(block, p.y, p.c)]
        elif kind == COREY:
            ref = self.full.at[self.rows_of(block, 1 - p.y, p.c), self.cols_of(p.x)]
        else:
            ref = self.full.at[self.rows_of(block, 1 - p.y, p.c), self.cols_of(1 - p.x)]
        return remote(ref, ref, s, self.recv.at[self.at, kind, block], p.core)

    def landed(self, kind, block):
        p, s = self.place, self.send.at[self.at, kind, block]
        r = self.recv.at[self.at, kind, block]
        if kind == UP:
            ref = self.full.at[self.rows_of(block, p.y, p.c)]
        elif kind == YWAY:
            ref = self.full.at[self.rows_of(block, 1 - p.y, p.c), self.cols_of(p.x)]
        elif kind == XWAY:
            ref = self.full.at[self.rows_of(block, 1 - p.y, p.c), self.cols_of(1 - p.x)]
        elif kind == CORE:
            ref = self.full.at[self.rows_of(block, p.y, 1 - p.c)]
        elif kind == COREY:
            ref = self.full.at[self.rows_of(block, 1 - p.y, 1 - p.c), self.cols_of(p.x)]
        else:
            ref = self.full.at[self.rows_of(block, 1 - p.y, 1 - p.c), self.cols_of(1 - p.x)]
        return remote(ref, ref, s, r, p.core)

    def own_copy(self):
        start = pl.multiple_of(self.place.fs * self.rows, 16)
        return pltpu.make_async_copy(self.own, self.full.at[pl.ds(start, self.rows)], self.near.at[self.at])

    def first(self):
        p = self.place
        self.own_copy().start()
        mine = self.own.at[pl.ds(pl.multiple_of(p.c * self.deep, 16), self.deep)]
        there = self.full.at[self.rows_of(p.z, p.y, p.c)]

        def out(kind, device):
            return remote(mine, there, self.send.at[self.at, kind, p.z], self.recv.at[self.at, UP, p.z], device)

        pl.when(p.has_up)(lambda: out(UP, p.up).start())
        pl.when(p.has_down)(lambda: out(DOWN, p.down).start())
        cols = self.cols_of(p.x)
        remote(
            mine.at[:, cols],
            there.at[:, cols],
            self.send.at[self.at, YWAY, p.z],
            self.recv.at[self.at, YWAY, p.z],
            p.yway,
        ).start()

    def line_step(self, k):
        p = self.place

        def pass_on(block, kind, more):
            self.landed(UP, block).wait_recv()
            pl.when(more)(lambda: self.copy(kind, block).start())
            self.copy(YWAY, block).start()
            self.copy(CORE, block).start()

        pl.when(p.z - k >= 0)(lambda: pass_on(p.z - k, UP, p.has_up))
        pl.when(p.z + k < p.line)(lambda: pass_on(p.z + k, DOWN, p.has_down))

    def near_blocks(self, k, body):
        p = self.place
        if k == 0:
            body(p.z)
            return
        pl.when(p.z - k >= 0)(lambda: body(p.z - k))
        pl.when(p.z + k < p.line)(lambda: body(p.z + k))

    def y_step(self, k):
        def body(block):
            self.landed(YWAY, block).wait_recv()
            self.copy(XWAY, block).start()
            self.copy(COREY, block).start()

        self.near_blocks(k, body)

    def x_step(self, k):
        def body(block):
            self.landed(XWAY, block).wait_recv()
            self.copy(COREX, block).start()

        self.near_blocks(k, body)

    def stage(self, j):
        line = self.place.line
        if j == 0:
            self.first()
        if 1 <= j < line:
            self.line_step(j)
        if 1 <= j <= line:
            self.y_step(j - 1)
        if 2 <= j <= line + 1:
            self.x_step(j - 2)

    def arrive(self):
        p = self.place
        self.own_copy().wait()

        def body(block, carry):
            pl.when(block != p.z)(lambda: self.landed(CORE, block).wait_recv())
            self.landed(COREY, block).wait_recv()
            self.landed(COREX, block).wait_recv()
            return carry

        lax.fori_loop(0, p.line, body, 0)

    def drain(self):
        p = self.place

        def body(block, carry):
            pl.when(p.has_up & (block <= p.z))(lambda: self.copy(UP, block).wait_send())
            pl.when(p.has_down & (block >= p.z))(lambda: self.copy(DOWN, block).wait_send())
            pl.when(block != p.z)(lambda: self.copy(CORE, block).wait_send())
            for kind in (YWAY, XWAY, COREY, COREX):
                self.copy(kind, block).wait_send()
            return carry

        lax.fori_loop(0, p.line, body, 0)


GATHER_STAGES = 2


def gather_kernel(line, order, *refs):
    owned, small, fulls, small_all = refs[:4], refs[4], refs[5:13], refs[13]
    send, recv, near, small_send, small_recv = refs[14:]
    place = Place(line)
    place.greet()
    smalls = []
    for step in range(1, 2 * line):
        other = lax.rem(place.fs + step, 2 * line)
        smalls.append(
            remote(small, small_all.at[place.fs], small_send.at[step], small_recv.at[place.fs], (place.dp, other))
        )
        smalls[-1].start()
    kept = pltpu.make_async_copy(small, small_all.at[place.fs], small_send.at[0])
    kept.start()
    units = [
        Gather(at, place, owned[which].at[layer], fulls[layer * 4 + which], send, recv, near)
        for at, (layer, which) in enumerate(order)
    ]
    stages = line + GATHER_STAGES
    for slot in range(len(units) + stages - 1):
        for j in range(stages):
            if 0 <= slot - j < len(units):
                units[slot - j].stage(j)
    for unit in units:
        unit.arrive()
    for unit in units:
        unit.drain()
    kept.wait()
    for step in range(1, 2 * line):
        other = lax.rem(place.fs + step, 2 * line)
        smalls[step - 1].wait_send()
        remote(
            small, small_all.at[other], small_send.at[step], small_recv.at[other], (place.dp, other)
        ).wait_recv()


def gather_all(line, owned, small):
    width = [ref.shape for ref in owned]
    outs = [
        jax.ShapeDtypeStruct((2 * line * width[which][1], width[which][2]), owned[which].dtype)
        for layer in range(2)
        for which in range(4)
    ]
    outs.append(jax.ShapeDtypeStruct((2 * line, *small.shape), small.dtype))
    order = [(layer, which) for layer in range(2) for which in range(4)]
    anywhere = pl.BlockSpec(memory_space=pl.ANY)
    return pl.pallas_call(
        functools.partial(gather_kernel, line, order),
        out_shape=outs,
        in_specs=[anywhere] * 5,
        out_specs=[anywhere] * 9,
        scratch_shapes=[
            pltpu.SemaphoreType.DMA((8, 7, line)),
            pltpu.SemaphoreType.DMA((8, 7, line)),
            pltpu.SemaphoreType.DMA((8,)),
            pltpu.SemaphoreType.DMA((2 * line,)),
            pltpu.SemaphoreType.DMA((2 * line,)),
        ],
        compiler_params=pltpu.CompilerParams(collective_id=0, has_side_effects=True),
    )(*owned, small)


class Reduce:
    def __init__(self, at, place, terms, out, bufs, send, recv, near):
        self.at, self.place, self.terms, self.out = at, place, terms, out
        self.mine, self.other, self.from_x, self.from_y, self.line_in, self.last_x, self.total = bufs
        self.send, self.recv, self.near = send, recv, near
        self.deep, self.half = self.mine.shape[2], self.mine.shape[3] // 2

    def cols_of(self, x):
        return pl.ds(pl.multiple_of(x * self.half, 128), self.half)

    def sems(self, kind, block=0):
        return self.send.at[self.at, kind, block], self.recv.at[self.at, kind, block]

    def core_copy(self):
        p = self.place
        return remote(self.terms.at[:, :, 1 - p.c], self.other, *self.sems(0), p.core)

    def near_copy(self):
        return pltpu.make_async_copy(self.terms.at[:, :, self.place.c], self.mine, self.near.at[self.at])

    def x_copy(self):
        p = self.place
        return remote(self.mine.at[:, 1 - p.y, :, self.cols_of(1 - p.x)], self.from_x, *self.sems(1), p.xway)

    def y_copy(self):
        p = self.place
        return remote(self.mine.at[:, 1 - p.y, :, self.cols_of(p.x)], self.from_y, *self.sems(2), p.yway)

    def line_copy(self, way, block):
        p = self.place
        return remote(
            self.mine.at[block, p.y], self.line_in.at[way, block], *self.sems(3 + way, block), (p.up, p.down)[way]
        )

    def last_copy(self):
        p = self.place
        return remote(self.mine.at[p.z, p.y], self.last_x, *self.sems(5), p.xway)

    def out_rows(self, c):
        return self.out.at[pl.ds(pl.multiple_of(c * self.deep, 8), self.deep)]

    def out_copy(self):
        return remote(self.total, self.out_rows(self.place.c), *self.sems(6), self.place.core)

    def out_near(self):
        return pltpu.make_async_copy(self.total, self.out_rows(self.place.c), self.near.at[self.at])

    def start(self):
        self.core_copy().start()
        self.near_copy().start()

    def add_core(self):
        self.near_copy().wait()
        self.core_copy().wait_recv()
        lines = self.mine.shape[0]

        def body(at, carry):
            block, y = at // 2, at % 2
            self.mine[block, y] = self.mine[block, y] + self.other[block, y]
            return carry

        lax.fori_loop(0, 2 * lines, body, 0)
        self.x_copy().start()

    def add_x(self):
        p = self.place
        self.x_copy().wait_recv()
        cols = self.cols_of(p.x)

        def body(block, carry):
            self.mine[block, 1 - p.y, :, cols] = self.mine[block, 1 - p.y, :, cols] + self.from_x[block]
            return carry

        lax.fori_loop(0, self.mine.shape[0], body, 0)
        self.y_copy().start()

    def add_y(self):
        p = self.place
        self.y_copy().wait_recv()
        cols = self.cols_of(p.x)

        def body(block, carry):
            self.mine[block, p.y, :, cols] = self.mine[block, p.y, :, cols] + self.from_y[block]
            return carry

        lax.fori_loop(0, self.mine.shape[0], body, 0)

    def add_line(self, way, block):
        p = self.place
        self.line_copy(way, block).wait_recv()
        self.mine[block, p.y] = self.mine[block, p.y] + self.line_in[way, block]

    def line_step(self, k):
        p, line = self.place, self.place.line
        far = line - 1 - k
        for way, block, valid, more in (
            (0, far, far > p.z, p.has_down),
            (1, k, k < p.z, p.has_up),
        ):

            def body(way=way, block=block, more=more):
                pl.when(more)(lambda: self.add_line(way, block))
                self.line_copy(way, block).start()

            pl.when(valid)(body)

    def own_step(self):
        p = self.place
        pl.when(p.has_down)(lambda: self.add_line(0, p.z))
        pl.when(p.has_up)(lambda: self.add_line(1, p.z))
        self.last_copy().start()

    def finish(self):
        p = self.place
        self.last_copy().wait_recv()
        self.total[...] = self.mine[p.z, p.y].astype(jnp.float32) + self.last_x[...].astype(jnp.float32)
        self.out_copy().start()
        self.out_near().start()

    def stages(self):
        line = self.place.line
        steps = [self.start, self.add_core, self.add_x, self.add_y]
        steps += [functools.partial(self.line_step, k) for k in range(line - 1)]
        return steps + [self.own_step, self.finish]

    def drain(self):
        p = self.place
        self.core_copy().wait_send()
        self.x_copy().wait_send()
        self.y_copy().wait_send()
        for block in range(p.line):
            pl.when(block > p.z)(lambda: self.line_copy(0, block).wait_send())
            pl.when(block < p.z)(lambda: self.line_copy(1, block).wait_send())
        self.last_copy().wait_send()
        self.out_copy().wait()
        self.out_near().wait()


def reduce_kernel(line, order, *refs):
    terms, small, outs, small_out = refs[:8], refs[8], refs[9:13], refs[13]
    bufs, refs = refs[14 : 14 + 7 * 8], refs[14 + 7 * 8 :]
    small_in, small_sum, small_four, send, recv, near, small_send, small_recv = refs
    place = Place(line)
    place.greet()
    fs, dp, n = place.fs, place.dp, 2 * line
    for step in range(1, n):
        other = lax.rem(fs + step, n)
        remote(small.at[other], small_in.at[fs], small_send.at[0, other], small_recv.at[0, fs], (dp, other)).start()
    kept = pltpu.make_async_copy(small.at[fs], small_in.at[fs], small_send.at[0, fs])
    kept.start()
    units = [
        Reduce(at, place, terms[layer * 4 + which], outs[which].at[layer], bufs[7 * at : 7 * at + 7], send, recv, near)
        for at, (layer, which) in enumerate(order)
    ]
    steps = [unit.stages() for unit in units]
    deep = len(steps[0])
    for slot in range(len(units) + deep - 1):
        if slot == 2:
            kept.wait()
            for step in range(1, n):
                other = lax.rem(fs + step, n)
                remote(
                    small.at[other], small_in.at[other], small_send.at[0, other], small_recv.at[0, other], (dp, other)
                ).wait()
            small_sum[...] = jnp.sum(small_in[...], axis=0)
            small_four[dp] = small_sum[...]
            for step in range(1, 4):
                other = lax.rem(dp + step, 4)
                remote(
                    small_sum, small_four.at[dp], small_send.at[1, other], small_recv.at[1, dp], (other, fs)
                ).start()
        if slot == 4:
            for step in range(1, 4):
                other = lax.rem(dp + step, 4)
                remote(
                    small_sum, small_four.at[other], small_send.at[1, other], small_recv.at[1, other], (other, fs)
                ).wait()
            small_out[...] = jnp.sum(small_four[...], axis=0)
        for j in range(deep):
            if 0 <= slot - j < len(units):
                steps[slot - j][j]()
    for unit in units:
        unit.drain()


def reduce_all(line, terms, small):
    order = [(layer, which) for layer in range(2) for which in (3, 2, 1, 0)]
    split, bufs = [], []
    for term in terms:
        deep = term.shape[0] // (4 * line)
        split.append(term.reshape(line, 2, 2, deep, term.shape[1]))
    for layer, which in order:
        _, _, _, deep, width = split[layer * 4 + which].shape
        low = jnp.bfloat16
        bufs += [
            pltpu.VMEM((line, 2, deep, width), low),
            pltpu.VMEM((line, 2, deep, width), low),
            pltpu.VMEM((line, deep, width // 2), low),
            pltpu.VMEM((line, deep, width // 2), low),
            pltpu.VMEM((2, line, deep, width), low),
            pltpu.VMEM((deep, width), low),
            pltpu.VMEM((deep, width), jnp.float32),
        ]
    outs = [
        jax.ShapeDtypeStruct((2, split[which].shape[3] * 2, split[which].shape[4]), jnp.float32) for which in range(4)
    ]
    outs.append(jax.ShapeDtypeStruct(small.shape[1:], jnp.float32))
    anywhere = pl.BlockSpec(memory_space=pl.ANY)
    inside = pl.BlockSpec(memory_space=pltpu.VMEM)
    return pl.pallas_call(
        functools.partial(reduce_kernel, line, order),
        out_shape=outs,
        in_specs=[anywhere] * 8 + [inside],
        out_specs=[anywhere] * 4 + [inside],
        scratch_shapes=bufs
        + [
            pltpu.VMEM(small.shape, jnp.float32),
            pltpu.VMEM(small.shape[1:], jnp.float32),
            pltpu.VMEM((4, *small.shape[1:]), jnp.float32),
            pltpu.SemaphoreType.DMA((8, 7, line)),
            pltpu.SemaphoreType.DMA((8, 7, line)),
            pltpu.SemaphoreType.DMA((8,)),
            pltpu.SemaphoreType.DMA((2, 2 * line)),
            pltpu.SemaphoreType.DMA((2, 2 * line)),
        ],
        compiler_params=pltpu.CompilerParams(collective_id=1, has_side_effects=True, vmem_limit_bytes=62 * 2**20),
    )(*split, small)

def normed(values, gain, shift):
    center = values - jnp.mean(values, axis=-1, keepdims=True)
    spread = jnp.mean(center * center, axis=-1, keepdims=True)
    return center * lax.rsqrt(spread + 1e-05) * gain + shift


def gelu_exact(values):
    return jax.nn.gelu(values, approximate=False)


def segment_ids(lengths, seq_len):
    bounds = jnp.cumsum(lengths, axis=-1)
    positions = jnp.arange(seq_len, dtype=jnp.int32)
    return jnp.sum((positions[None, :, None] >= bounds[:, None, :]).astype(jnp.int32), axis=-1)


def split_heads(values):
    batch, length, width = values.shape
    return values.reshape(batch, length, width // HEAD, HEAD)


def masked_scores(queries, keys_all, segment):
    scores = jnp.einsum(
        "bqhd,bkhd->bhqk",
        split_heads(queries),
        split_heads(keys_all),
        preferred_element_type=jnp.float32,
    )
    same = (segment[:, :, None] == segment[:, None, :])[:, None]
    return (jnp.where(same, scores, -1e30), same)


def attention(queries, keys_all, values_all, segment):
    scores, same = masked_scores(queries, keys_all, segment)
    largest = jnp.max(scores, axis=-1, keepdims=True)
    raised = jnp.exp(scores - largest)
    totals = jnp.sum(raised, axis=-1, keepdims=True)
    attn_weights = raised / totals
    log_total = largest + jnp.log(totals)
    mixed = jnp.einsum(
        "bhqk,bkhd->bqhd",
        attn_weights.astype(jnp.bfloat16),
        split_heads(values_all),
        preferred_element_type=jnp.float32,
    )
    return (mixed.reshape(queries.shape).astype(jnp.bfloat16), log_total)


def attention_back(queries, keys_all, values_all, segment, log_total, grad_mixed):
    scores, same = masked_scores(queries, keys_all, segment)
    attn_weights = jnp.where(same, jnp.exp(scores - log_total), 0.0)
    grad_heads = split_heads(grad_mixed)
    grad_weights = jnp.einsum(
        "bqhd,bkhd->bhqk", grad_heads, split_heads(values_all), preferred_element_type=jnp.float32
    )
    inner = jnp.sum(attn_weights * grad_weights, axis=-1, keepdims=True)
    grad_scores = (attn_weights * (grad_weights - inner)).astype(jnp.bfloat16)
    grad_queries = jnp.einsum(
        "bhqk,bkhd->bqhd", grad_scores, split_heads(keys_all), preferred_element_type=jnp.float32
    )
    grad_keys = jnp.einsum(
        "bhqk,bqhd->bkhd", grad_scores, split_heads(queries), preferred_element_type=jnp.float32
    )
    grad_values = jnp.einsum(
        "bhqk,bqhd->bkhd",
        attn_weights.astype(jnp.bfloat16),
        grad_heads,
        preferred_element_type=jnp.float32,
    )
    shape_rows = queries.shape
    return (
        grad_queries.reshape(shape_rows),
        grad_keys.reshape(shape_rows),
        grad_values.reshape(shape_rows),
    )


def forward_layer(inputs, weights, segment):
    qkv_weight, out_weight, up_weight, down_weight, gains, biases, up_bias = weights
    width = inputs.shape[-1]
    source = inputs.astype(jnp.float32)
    normed_a = normed(source, gains[0], biases[0]).astype(jnp.bfloat16)
    project = jnp.einsum("bld,de->ble", normed_a, qkv_weight, preferred_element_type=jnp.float32)
    queries = ((project[..., :width] + biases[2]) * HEAD ** (-0.5)).astype(jnp.bfloat16)
    keys_all = project[..., width : 2 * width].astype(jnp.bfloat16)
    values_all = (project[..., 2 * width :] + biases[3]).astype(jnp.bfloat16)
    mixed, log_total = attention(queries, keys_all, values_all, segment)
    hidden = (
        source
        + jnp.einsum("bld,de->ble", mixed, out_weight, preferred_element_type=jnp.float32)
        + biases[4]
    )
    normed_c = normed(hidden, gains[1], biases[1]).astype(jnp.bfloat16)
    before = (
        jnp.einsum("bld,df->blf", normed_c, up_weight, preferred_element_type=jnp.float32) + up_bias
    )
    activated = gelu_exact(before).astype(jnp.bfloat16)
    result = (
        hidden
        + jnp.einsum("blf,fd->bld", activated, down_weight, preferred_element_type=jnp.float32)
        + biases[5]
    )
    return (
        source,
        normed_a,
        queries,
        keys_all,
        values_all,
        log_total,
        mixed,
        hidden,
        normed_c,
        before,
        activated,
        result,
    )


def backward_layer(inputs, cotangent, weights, segment):
    qkv_weight, out_weight, up_weight, down_weight, gains, biases, up_bias = weights
    width = inputs.shape[-1]
    (
        source,
        normed_a,
        queries,
        keys_all,
        values_all,
        log_total,
        mixed,
        hidden,
        normed_c,
        before,
        activated,
        result,
    ) = forward_layer(inputs, weights, segment)
    grad_result = cotangent.astype(jnp.float32)
    grad_downw = jnp.einsum("blf,bld->fd", activated, cotangent, preferred_element_type=jnp.float32)
    grad_act = jnp.einsum("bld,fd->blf", cotangent, down_weight, preferred_element_type=jnp.float32)
    grad_before = jax.vjp(gelu_exact, before)[1](grad_act)[0].astype(jnp.bfloat16)
    grad_upw = jnp.einsum("bld,blf->df", normed_c, grad_before, preferred_element_type=jnp.float32)
    grad_upb = jnp.sum(grad_before.astype(jnp.float32), axis=(0, 1))
    grad_normc = jnp.einsum(
        "blf,df->bld", grad_before, up_weight, preferred_element_type=jnp.float32
    )
    hidden_back = jax.vjp(
        normed, hidden, gains[1].astype(jnp.float32), biases[1].astype(jnp.float32)
    )[1]
    grad_hidden_ln, grad_gain_two, grad_shift_two = hidden_back(grad_normc)
    grad_hidden = grad_result + grad_hidden_ln
    grad_branch = grad_hidden.astype(jnp.bfloat16)
    grad_outw = jnp.einsum("bld,ble->de", mixed, grad_branch, preferred_element_type=jnp.float32)
    grad_mixed = jnp.einsum(
        "ble,de->bld", grad_branch, out_weight, preferred_element_type=jnp.float32
    ).astype(jnp.bfloat16)
    grad_queries, grad_keys, grad_values = attention_back(
        queries, keys_all, values_all, segment, log_total, grad_mixed
    )
    grad_project = jnp.concatenate(
        [
            grad_queries.astype(jnp.bfloat16) * HEAD ** (-0.5),
            grad_keys.astype(jnp.bfloat16),
            grad_values.astype(jnp.bfloat16),
        ],
        axis=-1,
    )
    grad_qkvw = jnp.einsum(
        "bld,ble->de", normed_a, grad_project, preferred_element_type=jnp.float32
    )
    column_sums = jnp.sum(grad_project.astype(jnp.float32), axis=(0, 1))
    grad_norma = jnp.einsum(
        "ble,de->bld", grad_project, qkv_weight, preferred_element_type=jnp.float32
    )
    source_back = jax.vjp(
        normed, source, gains[0].astype(jnp.float32), biases[0].astype(jnp.float32)
    )[1]
    grad_source_ln, grad_gain_one, grad_shift_one = source_back(grad_norma)
    grad_inputs = grad_hidden + grad_source_ln
    grad_gains = jnp.stack([grad_gain_one, grad_gain_two])
    grad_biases = jnp.stack(
        [
            grad_shift_one,
            grad_shift_two,
            column_sums[:width],
            column_sums[2 * width :],
            jnp.sum(grad_branch.astype(jnp.float32), axis=(0, 1)),
            jnp.sum(grad_result, axis=(0, 1)),
        ]
    )
    return (
        result.astype(jnp.bfloat16),
        grad_inputs,
        (grad_qkvw, grad_outw, grad_upw, grad_downw, grad_gains, grad_biases, grad_upb),
    )


def fetch_weights(layer_index, w_qkv, w_out, w_up, w_down, gains, biases, b_up):
    return (
        lax.all_gather(w_qkv[layer_index], "fsdp", axis=0, tiled=True),
        lax.all_gather(w_out[layer_index], "fsdp", axis=0, tiled=True),
        lax.all_gather(w_up[layer_index], "fsdp", axis=0, tiled=True),
        lax.all_gather(w_down[layer_index], "fsdp", axis=0, tiled=True),
        lax.all_gather(gains[layer_index], "fsdp", axis=1, tiled=True),
        lax.all_gather(biases[layer_index], "fsdp", axis=1, tiled=True),
        lax.all_gather(b_up[layer_index], "fsdp", axis=0, tiled=True),
    )


def fetch_again(layer_index, w_qkv, w_out, w_up, w_down, gains, biases, b_up):
    return (
        lax.all_gather(w_qkv[layer_index], "fsdp", axis=0, tiled=True),
        lax.all_gather(w_out[layer_index], "fsdp", axis=0, tiled=True),
        lax.all_gather(w_up[layer_index], "fsdp", axis=0, tiled=True),
        lax.all_gather(w_down[layer_index], "fsdp", axis=0, tiled=True),
        lax.all_gather(gains[layer_index], "fsdp", axis=1, tiled=True),
        lax.all_gather(biases[layer_index], "fsdp", axis=1, tiled=True),
        lax.all_gather(b_up[layer_index], "fsdp", axis=0, tiled=True),
    )


def reduce_grads(gradients):
    shares = (
        lax.psum_scatter(gradients[0], "fsdp", scatter_dimension=0, tiled=True),
        lax.psum_scatter(gradients[1], "fsdp", scatter_dimension=0, tiled=True),
        lax.psum_scatter(gradients[2], "fsdp", scatter_dimension=0, tiled=True),
        lax.psum_scatter(gradients[3], "fsdp", scatter_dimension=0, tiled=True),
        lax.psum_scatter(gradients[4], "fsdp", scatter_dimension=1, tiled=True),
        lax.psum_scatter(gradients[5], "fsdp", scatter_dimension=1, tiled=True),
        lax.psum_scatter(gradients[6], "fsdp", scatter_dimension=0, tiled=True),
    )
    quarters = (
        lax.psum_scatter(
            shares[0].astype(jnp.bfloat16), "dp", scatter_dimension=0, tiled=True
        ).astype(jnp.float32),
        lax.psum_scatter(
            shares[1].astype(jnp.bfloat16), "dp", scatter_dimension=0, tiled=True
        ).astype(jnp.float32),
        lax.psum_scatter(
            shares[2].astype(jnp.bfloat16), "dp", scatter_dimension=0, tiled=True
        ).astype(jnp.float32),
        lax.psum_scatter(
            shares[3].astype(jnp.bfloat16), "dp", scatter_dimension=0, tiled=True
        ).astype(jnp.float32),
        lax.psum_scatter(
            shares[4].astype(jnp.bfloat16), "dp", scatter_dimension=1, tiled=True
        ).astype(jnp.float32),
        lax.psum_scatter(
            shares[5].astype(jnp.bfloat16), "dp", scatter_dimension=1, tiled=True
        ).astype(jnp.float32),
        lax.psum_scatter(
            shares[6].astype(jnp.bfloat16), "dp", scatter_dimension=0, tiled=True
        ).astype(jnp.float32),
    )
    return (
        lax.all_gather(quarters[0].astype(jnp.bfloat16), "dp", axis=0, tiled=True).astype(
            jnp.float32
        ),
        lax.all_gather(quarters[1].astype(jnp.bfloat16), "dp", axis=0, tiled=True).astype(
            jnp.float32
        ),
        lax.all_gather(quarters[2].astype(jnp.bfloat16), "dp", axis=0, tiled=True).astype(
            jnp.float32
        ),
        lax.all_gather(quarters[3].astype(jnp.bfloat16), "dp", axis=0, tiled=True).astype(
            jnp.float32
        ),
        lax.all_gather(quarters[4].astype(jnp.bfloat16), "dp", axis=1, tiled=True).astype(
            jnp.float32
        ),
        lax.all_gather(quarters[5].astype(jnp.bfloat16), "dp", axis=1, tiled=True).astype(
            jnp.float32
        ),
        lax.all_gather(quarters[6].astype(jnp.bfloat16), "dp", axis=0, tiled=True).astype(
            jnp.float32
        ),
    )


def plain(
    images,
    image_cot,
    captions,
    caption_cot,
    lengths,
    w_qkv,
    w_out,
    w_up,
    w_down,
    gains,
    biases,
    b_up,
):
    owned = (w_qkv, w_out, w_up, w_down, gains, biases, b_up)
    image_seg = jnp.zeros((images.shape[0], images.shape[1]), jnp.int32)
    caption_seg = segment_ids(lengths, captions.shape[1])
    first_weights = fetch_weights(0, *owned)
    image_out = forward_layer(images, first_weights, image_seg)[-1].astype(jnp.bfloat16)
    second_weights = fetch_weights(1, *owned)
    caption_out = forward_layer(captions, second_weights, caption_seg)[-1].astype(jnp.bfloat16)
    second_back = fetch_again(1, *owned)
    _, caption_grad, caption_terms = backward_layer(captions, caption_cot, second_back, caption_seg)
    caption_shares = reduce_grads(caption_terms)
    first_back = fetch_again(0, *owned)
    _, image_grad, image_terms = backward_layer(images, image_cot, first_back, image_seg)
    image_shares = reduce_grads(image_terms)
    stacked = tuple((jnp.stack([image_shares[index], caption_shares[index]]) for index in range(7)))
    return (image_out, caption_out, image_grad, caption_grad) + stacked


def kernels_fit(mesh, w_qkv):
    return mesh.shape["dp"] == 4 and mesh.shape["fsdp"] % 2 == 0 and w_qkv.shape[1] % 32 == 0


def pack_small(gains, biases, b_up):
    rows = jnp.concatenate([gains.reshape(2, -1), biases.reshape(2, -1), b_up], axis=1).astype(jnp.float32).reshape(-1)
    return jnp.pad(rows, (0, -rows.size % 1024)).reshape(-1, 128)


def unpack_small(blocks, width, deep):
    count = blocks.shape[0]
    flat = blocks.reshape(count, -1)[:, : 2 * (8 * width + deep)].reshape(count, 2, 8 * width + deep)
    rows = flat[:, :, : 8 * width].reshape(count, 2, 8, width).transpose(1, 2, 0, 3).reshape(2, 8, count * width)
    up = flat[:, :, 8 * width :].transpose(1, 0, 2).reshape(2, count * deep)
    return rows[:, :2], rows[:, 2:], up


def spread_small(count, gains, biases, b_up):
    rows = jnp.concatenate([gains, biases], axis=1)
    width, deep = rows.shape[2] // count, b_up.shape[1] // count
    rows = rows.reshape(2, 8, count, width).transpose(2, 0, 1, 3).reshape(count, 2, 8 * width)
    up = b_up.reshape(2, count, deep).transpose(1, 0, 2)
    flat = jnp.concatenate([rows, up], axis=2).reshape(count, -1)
    return jnp.pad(flat, ((0, 0), (0, -flat.shape[1] % 1024))).reshape(count, -1, 128)


def local(mesh, images, image_cot, captions, caption_cot, lengths, w_qkv, w_out, w_up, w_down, gains, biases, b_up):
    if not kernels_fit(mesh, w_qkv):
        return plain(
            images, image_cot, captions, caption_cot, lengths, w_qkv, w_out, w_up, w_down, gains, biases, b_up
        )
    count = mesh.shape["fsdp"]
    line = count // 2
    width, deep = gains.shape[2], b_up.shape[1]
    *fulls, small = gather_all(line, (w_qkv, w_out, w_up, w_down), pack_small(gains, biases, b_up))
    gains_all, biases_all, up_all = unpack_small(small, width, deep)
    outs, grads, terms, smalls = [], [], [], []
    image_seg = jnp.zeros((images.shape[0], images.shape[1]), jnp.int32)
    caption_seg = segment_ids(lengths, captions.shape[1])
    par = jnp.concatenate([gains_all, biases_all], axis=1)
    for layer, (rows, cot, seg) in enumerate(((images, image_cot, image_seg), (captions, caption_cot, caption_seg))):
        weights = fulls[layer * 4 : layer * 4 + 4]
        result, grad, g_par, g_bup, *found = run_layer(rows, cot, seg, weights, par[layer], up_all[layer : layer + 1])
        outs.append(result)
        grads.append(grad)
        terms += found
        smalls.append((g_par[:2], g_par[2:], g_bup[0]))
    packed = spread_small(count, *(jnp.stack([smalls[0][at], smalls[1][at]]) for at in range(3)))
    *shares, small_share = reduce_all(line, terms, packed)
    rest = unpack_small(small_share[None], width, deep)
    return (*outs, *grads, *shares, *rest)


def solution(mesh):
    placed = (
        P(("dp", "fsdp"), None, None),
        P(("dp", "fsdp"), None, None),
        P(("dp", "fsdp"), None, None),
        P(("dp", "fsdp"), None, None),
        P(("dp", "fsdp"), None),
        P(None, "fsdp", None),
        P(None, "fsdp", None),
        P(None, "fsdp", None),
        P(None, "fsdp", None),
        P(None, None, "fsdp"),
        P(None, None, "fsdp"),
        P(None, "fsdp"),
    )
    return jax.shard_map(
        functools.partial(local, mesh),
        mesh=mesh,
        in_specs=placed,
        out_specs=(
            P(("dp", "fsdp"), None, None),
            P(("dp", "fsdp"), None, None),
            P(("dp", "fsdp"), None, None),
            P(("dp", "fsdp"), None, None),
            P(None, "fsdp", None),
            P(None, "fsdp", None),
            P(None, "fsdp", None),
            P(None, "fsdp", None),
            P(None, None, "fsdp"),
            P(None, None, "fsdp"),
            P(None, "fsdp"),
        ),
        check_vma=False,
    )
```

```python
import functools

import jax
import jax.numpy as jnp
from jax import lax
from jax.experimental import pallas as pl
from jax.experimental.pallas import tpu as pltpu
from jax.sharding import PartitionSpec as P

HEAD = 64

NT = (((1,), (1,)), ((), ()))
TN = (((0,), (0,)), ((), ()))
TILE = 256
CHUNK = 64


def dot(a, b, dims=(((1,), (0,)), ((), ()))):
    return lax.dot_general(a, b, dims, preferred_element_type=jnp.float32)


def flat(value):
    return value.reshape(-1, value.shape[-1])


def at(t, size=TILE):
    return pl.ds(pl.multiple_of(t * size, size), size)


def layer_scratch(n, width, deep, split):
    low, full = jnp.bfloat16, jnp.float32
    return dict(
        x=pltpu.VMEM((n, width), low),
        dy=pltpu.VMEM((n, width), low),
        a=pltpu.VMEM((n, width), low),
        a_t=pltpu.VMEM((width, n), low),
        qkv=pltpu.VMEM((n, 3 * width), low),
        bias=pltpu.VMEM((n, n), full),
        wt=pltpu.VMEM((width // HEAD, n, n), low),
        ds=pltpu.VMEM((2, n, n), low),
        o=pltpu.VMEM((n, width), low),
        o_t=pltpu.VMEM((width, n), low),
        h=pltpu.VMEM((n, width), full),
        c=pltpu.VMEM((n, width), low),
        c_t=pltpu.VMEM((width, n), low),
        g=pltpu.VMEM((n, deep), low),
        du=pltpu.VMEM((n, deep), low),
        sums=pltpu.VMEM((n, width), full),
        dh=pltpu.VMEM((n, width), full),
        rows=pltpu.VMEM((8, 3 * width), full),
        tall=pltpu.VMEM((2, *split, width), low),
        wide=pltpu.VMEM((2, *split[1:3], deep // width, split[3], width), low),
        tall_sem=pltpu.SemaphoreType.DMA((2,)),
        wide_sem=pltpu.SemaphoreType.DMA((2,)),
    )


class Layer:
    def __init__(self, n, kept, weights, small, terms, outs):
        self.n, self.s = n, kept
        self.w_qkv, self.w_out, self.w_up, self.w_down = weights
        self.par, self.b_up = small
        self.g_qkv, self.g_out, self.g_up, self.g_down = terms
        self.y_out, self.x_grad, self.g_par, self.g_bup = outs
        self.width, self.deep = self.w_out.shape[-1], self.w_up.shape[-1]

    def chunks(self, body):
        def step(i, carry):
            body(at(i, CHUNK))
            return carry

        lax.fori_loop(0, self.n // CHUNK, step, 0)

    def tiles(self, first, last, body):
        def step(i, carry):
            body(i)
            return carry

        lax.fori_loop(first, last, step, 0)

    def row(self, ref, i):
        return ref[i : i + 1, :]

    def tall_copy(self, ref, slot, t):
        cols = at(t, self.width)
        return pltpu.make_async_copy(self.s["tall"].at[slot], ref.at[:, :, :, :, cols], self.s["tall_sem"].at[slot])

    def wide_copy(self, ref, slot, t):
        return pltpu.make_async_copy(self.s["wide"].at[slot], ref.at[t], self.s["wide_sem"].at[slot])

    def put(self, copy, buf, ref, t, count, value):
        slot = t % 2
        pl.when(t >= 2)(lambda: copy(ref, slot, t - 2).wait())
        buf[slot] = value.astype(jnp.bfloat16).reshape(buf.shape[1:])
        copy(ref, slot, t).start()

    def put_end(self, copy, ref, count):
        for t in range(max(0, count - 2), count):
            copy(ref, t % 2, t).wait()

    def load(self, x, dy, seg_col, seg_row):
        s, have = self.s, x.shape[0]
        if have < self.n:
            start = have // 16 * 16
            s["x"][start:, :] = jnp.zeros((self.n - start, self.width), jnp.bfloat16)
            s["dy"][start:, :] = jnp.zeros((self.n - start, self.width), jnp.bfloat16)
        s["x"][0:have, :] = x[...]
        s["dy"][0:have, :] = dy[...]
        s["bias"][...] = jnp.where(seg_col[...] == seg_row[...], 0.0, -1e30)
        self.g_par[...] = jnp.zeros_like(self.g_par)
        width = self.width
        s["rows"][0:1, 0:width] = self.par[4:5, :]
        s["rows"][0:1, width : 2 * width] = jnp.zeros((1, width), jnp.float32)
        s["rows"][0:1, 2 * width :] = self.par[5:6, :]

    def norm_parts(self, values):
        center = values - jnp.mean(values, axis=-1, keepdims=True)
        scale = lax.rsqrt(jnp.mean(center * center, axis=-1, keepdims=True) + 1e-05)
        return center * scale, scale

    def norm(self, src, dst, which):
        def body(rows):
            unit, _ = self.norm_parts(src[rows, :].astype(jnp.float32))
            dst[rows, :] = (unit * self.row(self.par, which) + self.row(self.par, 2 + which)).astype(jnp.bfloat16)

        self.chunks(body)

    def norm_a(self):
        self.norm(self.s["x"], self.s["a"], 0)

    def project(self):
        s = self.s
        queries = self.width // TILE

        def body(t):
            scale = jnp.where(t < queries, HEAD ** (-0.5), 1.0)
            found = dot(s["a"][...], flat(self.w_qkv[:, :, :, :, at(t)])) + s["rows"][0:1, at(t)]
            s["qkv"][:, at(t)] = (found * scale).astype(jnp.bfloat16)

        self.tiles(0, 3 * queries, body)
        s["a_t"][...] = s["a"][...].T

    def pair(self, i, which):
        start = which * self.width + i * 128
        return self.s["qkv"].at[:, pl.ds(pl.multiple_of(start, 128), 128)]

    def own_lanes(self, value, head):
        lanes = lax.broadcasted_iota(jnp.int32, value.shape, 1)
        return jnp.where((lanes < HEAD) == (head == 0), value, jnp.zeros_like(value))

    def attend(self, first, last):
        s = self.s

        def body(i):
            q, k, v = (self.pair(i, which) for which in range(3))
            keys = [self.own_lanes(k[...], head) for head in range(2)]
            vals = [self.own_lanes(v[...], head) for head in range(2)]
            for part in range(self.n // TILE):
                cols = slice(part * TILE, part * TILE + TILE)
                mixed = None
                for head in range(2):
                    scores = dot(keys[head], q[cols, :], NT) + s["bias"][:, cols]
                    raised = jnp.exp(scores - jnp.max(scores, axis=0, keepdims=True))
                    share = 1.0 / jnp.sum(raised, axis=0, keepdims=True)
                    weights = (raised * share).astype(jnp.bfloat16)
                    s["wt"][2 * i + head, :, cols] = weights
                    found = dot(vals[head], weights, TN)
                    mixed = found if mixed is None else mixed + found
                s["o"][cols, at(i, 128)] = mixed.T.astype(jnp.bfloat16)

        self.tiles(first, last, body)

    def branch(self):
        s = self.s

        def body(t):
            found = dot(s["o"][...], flat(self.w_out[:, :, :, :, at(t)])) + self.par[6:7, at(t)]
            s["h"][:, at(t)] = s["x"][:, at(t)].astype(jnp.float32) + found

        self.tiles(0, self.width // TILE, body)
        s["o_t"][...] = s["o"][...].T

    def norm_c(self):
        self.norm(self.s["h"], self.s["c"], 1)

    def up(self, first, last):
        s = self.s

        def body(t):
            before = dot(s["c"][...], flat(self.w_up[:, :, :, :, at(t)])) + self.b_up[0:1, at(t)]
            chance = 0.5 + 0.5 * lax.erf(before * 0.7071067811865476)
            s["g"][:, at(t)] = (before * chance).astype(jnp.bfloat16)
            slope = chance + before * (jnp.exp(before * before * -0.5) * 0.3989422804014327)
            s["du"][:, at(t)] = slope.astype(jnp.bfloat16)

        self.tiles(first, last, body)

    def turn_c(self):
        self.s["c_t"][...] = self.s["c"][...].T

    def down(self):
        s = self.s

        def body(t):
            found = dot(s["g"][...], flat(self.w_down[:, :, :, :, :, at(t)])) + self.par[7:8, at(t)]
            s["sums"][:, at(t)] = s["h"][:, at(t)] + found

        self.tiles(0, self.width // TILE, body)
        have = self.y_out.shape[0]
        self.y_out[...] = s["sums"][0:have, :].astype(jnp.bfloat16)

    def feed_back(self, first, last):
        s = self.s
        count, width = self.deep // self.width, self.width

        def body(t):
            cols = at(t, width)
            grad = dot(s["dy"][...], flat(self.w_down[t]), NT)
            low = (grad * s["du"][:, cols].astype(jnp.float32)).astype(jnp.bfloat16)
            s["du"][:, cols] = low
            self.g_bup[0:1, cols] = jnp.sum(low.astype(jnp.float32), axis=0, keepdims=True)
            self.put(self.wide_copy, s["wide"], self.g_down, t, count, dot(s["g"][:, cols], s["dy"][...], TN))
            self.put(self.tall_copy, s["tall"], self.g_up, t, count, dot(s["c_t"][...], low))

        self.tiles(first, last, body)

    def feed_end(self):
        self.put_end(self.wide_copy, self.g_down, self.deep // self.width)
        self.put_end(self.tall_copy, self.g_up, self.deep // self.width)

    def up_back(self):
        self.s["sums"][...] = dot(self.s["du"][...], flat(self.w_up[...]), NT)

    def norm_back(self, src, which, grad, rest, body_out):
        def body(rows):
            unit, scale = self.norm_parts(src[rows, :].astype(jnp.float32))
            came = grad[rows, :]
            gained = came * self.row(self.par, which)
            self.g_par[which : which + 1, :] += jnp.sum(came * unit, axis=0, keepdims=True)
            self.g_par[2 + which : 3 + which, :] += jnp.sum(came, axis=0, keepdims=True)
            inner = gained - jnp.mean(gained, axis=-1, keepdims=True)
            inner = inner - unit * jnp.mean(gained * unit, axis=-1, keepdims=True)
            body_out(rows, rest[rows, :].astype(jnp.float32) + inner * scale)

        self.chunks(body)

    def norm_c_back(self):
        s = self.s

        def keep(rows, grad):
            s["dh"][rows, :] = grad
            low = grad.astype(jnp.bfloat16)
            s["c"][rows, :] = low
            self.g_par[6:7, :] += jnp.sum(low.astype(jnp.float32), axis=0, keepdims=True)
            self.g_par[7:8, :] += jnp.sum(s["dy"][rows, :].astype(jnp.float32), axis=0, keepdims=True)

        self.norm_back(s["h"], 1, s["sums"], s["dy"], keep)

    def branch_back(self):
        s = self.s
        self.put(self.tall_copy, s["tall"], self.g_out, 0, 1, dot(s["o_t"][...], s["c"][...]))
        s["a"][...] = dot(s["c"][...], flat(self.w_out[...]), NT).astype(jnp.bfloat16)
        self.put_end(self.tall_copy, self.g_out, 1)

    def attend_back(self, first, last):
        s, width = self.s, self.width

        def body(i):
            q, k, v = (self.pair(i, which) for which in range(3))
            came = s["a"].at[:, at(i, 128)]
            dq = dk = dv = None
            for head in range(2):
                vals = self.own_lanes(v[...], head)
                for part in range(self.n // TILE):
                    cols = slice(part * TILE, part * TILE + TILE)
                    grad = dot(vals, came[cols, :], NT)
                    weights = s["wt"][2 * i + head, :, cols].astype(jnp.float32)
                    product = weights * grad
                    inner = jnp.sum(product, axis=0, keepdims=True)
                    s["ds"][head, :, cols] = (product - weights * inner).astype(jnp.bfloat16)
                one_q = dot(self.own_lanes(k[...], head), s["ds"][head], TN)
                one_k = dot(s["ds"][head], self.own_lanes(q[...], head))
                one_v = dot(s["wt"][2 * i + head], self.own_lanes(came[...], head))
                dq, dk, dv = (one_q, one_k, one_v) if head == 0 else (dq + one_q, dk + one_k, dv + one_v)
            s["g"][:, at(i, 128)] = dq.T.astype(jnp.bfloat16) * HEAD ** (-0.5)
            s["g"][:, pl.ds(pl.multiple_of(width + i * 128, 128), 128)] = dk.astype(jnp.bfloat16)
            s["g"][:, pl.ds(pl.multiple_of(2 * width + i * 128, 128), 128)] = dv.astype(jnp.bfloat16)

        self.tiles(first, last, body)

    def project_terms(self):
        s = self.s
        count, width = 3, self.width

        def body(t):
            grad = s["g"][:, at(t, width)]
            s["rows"][1:2, at(t, width)] = jnp.sum(grad.astype(jnp.float32), axis=0, keepdims=True)
            self.put(self.tall_copy, s["tall"], self.g_qkv, t, count, dot(s["a_t"][...], grad))

        self.tiles(0, count, body)
        self.put_end(self.tall_copy, self.g_qkv, count)
        self.g_par[4:5, :] = s["rows"][1:2, 0 : self.width]
        self.g_par[5:6, :] = s["rows"][1:2, 2 * self.width :]

    def project_back(self):
        s = self.s
        s["sums"][...] = dot(s["g"][:, 0 : 3 * self.width], flat(self.w_qkv[...]), NT)

    def norm_a_back(self):
        s = self.s
        have = self.x_grad.shape[0]

        def keep(rows, grad):
            s["dh"][rows, :] = grad

        self.norm_back(s["x"], 0, s["sums"], s["dh"], keep)
        self.x_grad[...] = s["dh"][0:have, :]


def layer_kernel(n, names, *refs):
    x, dy, seg_col, seg_row, par, b_up, *weights = refs[:10]
    y_out, x_grad, g_par, g_bup, *terms = refs[10:18]
    near, *held = refs[18:23]
    kept = dict(zip(names, refs[23:]))
    loads = [pltpu.make_async_copy(weights[i], held[i], near.at[i]) for i in range(4)]
    for load in loads:
        load.start()
    layer = Layer(n, kept, held, (par, b_up), terms, (y_out.at[0], x_grad.at[0], g_par, g_bup))
    heads, tiles, panels = layer.width // 128, layer.deep // TILE, layer.deep // layer.width
    layer.load(x.at[0], dy.at[0], seg_col, seg_row)
    layer.norm_a()
    loads[0].wait()
    layer.project()
    layer.attend(0, heads)
    loads[1].wait()
    layer.branch()
    layer.norm_c()
    loads[2].wait()
    layer.up(0, tiles)
    layer.turn_c()
    loads[3].wait()
    layer.down()
    layer.feed_back(0, panels)
    layer.feed_end()
    layer.up_back()
    layer.norm_c_back()
    layer.branch_back()
    layer.attend_back(0, heads)
    layer.project_terms()
    layer.project_back()
    layer.norm_a_back()


def padded(rows):
    return -(-rows // TILE) * TILE


def run_layer(x, dy, segment, weights, par, b_up):
    have, width = x.shape[1:]
    n, deep = padded(have), b_up.shape[1]
    segment = jnp.pad(segment, ((0, 0), (0, n - have)), constant_values=-1)
    kept = layer_scratch(n, width, deep, weights[1].shape[:4])
    anywhere, inside = pl.BlockSpec(memory_space=pl.ANY), pl.BlockSpec(memory_space=pltpu.VMEM)
    outs = [
        jax.ShapeDtypeStruct(x.shape, jnp.bfloat16),
        jax.ShapeDtypeStruct(x.shape, jnp.float32),
        jax.ShapeDtypeStruct(par.shape, jnp.float32),
        jax.ShapeDtypeStruct(b_up.shape, jnp.float32),
    ] + [jax.ShapeDtypeStruct(weight.shape, jnp.bfloat16) for weight in weights]
    return pl.pallas_call(
        functools.partial(layer_kernel, n, list(kept)),
        out_shape=outs,
        in_specs=[inside] * 6 + [anywhere] * 4,
        out_specs=[inside] * 4 + [anywhere] * 4,
        scratch_shapes=[pltpu.SemaphoreType.DMA((4,))]
        + [pltpu.VMEM(weight.shape, weight.dtype) for weight in weights]
        + list(kept.values()),
        compiler_params=pltpu.CompilerParams(vmem_limit_bytes=62 * 2**20),
    )(x, dy, segment.reshape(n, 1), segment, par, b_up, *weights)


MESH = pl.DeviceIdType.MESH
UP, DOWN, YWAY, XWAY, CORE, COREY, COREX = range(7)


class Place:
    def __init__(self, line):
        dp, fs = lax.axis_index("dp"), lax.axis_index("fsdp")
        self.line = line
        self.dp, self.fs = dp, fs
        self.x, self.c = dp // 2, dp % 2
        self.z, self.y = fs // 2, fs % 2
        self.up = (dp, fs + 2)
        self.down = (dp, fs - 2)
        self.yway = (dp, self.z * 2 + 1 - self.y)
        self.xway = ((1 - self.x) * 2 + self.c, fs)
        self.core = (self.x * 2 + 1 - self.c, fs)
        self.has_up = self.z + 1 < line
        self.has_down = self.z > 0

    def greet(self):
        barrier = pltpu.get_barrier_semaphore()
        total = 0
        for step in range(1, 2 * self.line):
            other = lax.rem(self.fs + step, 2 * self.line)
            pl.semaphore_signal(barrier, inc=1, device_id=(self.dp, other), device_id_type=MESH)
            total += 1
        for step in range(1, 4):
            other = lax.rem(self.dp + step, 4)
            pl.semaphore_signal(barrier, inc=1, device_id=(other, self.fs), device_id_type=MESH)
            total += 1
        pl.semaphore_wait(barrier, total)


def remote(src, dst, send, recv, device):
    return pltpu.make_async_remote_copy(
        src_ref=src, dst_ref=dst, send_sem=send, recv_sem=recv, device_id=device, device_id_type=MESH
    )


class Gather:
    def __init__(self, at, place, own, full, send, recv, near):
        self.at, self.place, self.own, self.full = at, place, own, full
        self.send, self.recv, self.near = send, recv, near
        self.rows = own.shape[0]
        self.deep = self.rows // 2
        self.half = own.shape[1] // 2

    def rows_of(self, block, y, c):
        start = (block * 2 + y) * self.rows + c * self.deep
        return pl.ds(pl.multiple_of(start, 16), self.deep)

    def cols_of(self, x):
        return pl.ds(pl.multiple_of(x * self.half, 128), self.half)

    def copy(self, kind, block):
        p, s, r = self.place, self.send.at[self.at, kind, block], None
        if kind in (UP, DOWN):
            ref = self.full.at[self.rows_of(block, p.y, p.c)]
            return remote(ref, ref, s, self.recv.at[self.at, UP, block], p.up if kind == UP else p.down)
        if kind == YWAY:
            ref = self.full.at[self.rows_of(block, p.y, p.c), self.cols_of(p.x)]
            return remote(ref, ref, s, self.recv.at[self.at, kind, block], p.yway)
        if kind == XWAY:
            ref = self.full.at[self.rows_of(block, 1 - p.y, p.c), self.cols_of(p.x)]
            return remote(ref, ref, s, self.recv.at[self.at, kind, block], p.xway)
        if kind == CORE:
            ref = self.full.at[self.rows_of(block, p.y, p.c)]
        elif kind == COREY:
            ref = self.full.at[self.rows_of(block, 1 - p.y, p.c), self.cols_of(p.x)]
        else:
            ref = self.full.at[self.rows_of(block, 1 - p.y, p.c), self.cols_of(1 - p.x)]
        return remote(ref, ref, s, self.recv.at[self.at, kind, block], p.core)

    def landed(self, kind, block):
        p, s = self.place, self.send.at[self.at, kind, block]
        r = self.recv.at[self.at, kind, block]
        if kind == UP:
            ref = self.full.at[self.rows_of(block, p.y, p.c)]
        elif kind == YWAY:
            ref = self.full.at[self.rows_of(block, 1 - p.y, p.c), self.cols_of(p.x)]
        elif kind == XWAY:
            ref = self.full.at[self.rows_of(block, 1 - p.y, p.c), self.cols_of(1 - p.x)]
        elif kind == CORE:
            ref = self.full.at[self.rows_of(block, p.y, 1 - p.c)]
        elif kind == COREY:
            ref = self.full.at[self.rows_of(block, 1 - p.y, 1 - p.c), self.cols_of(p.x)]
        else:
            ref = self.full.at[self.rows_of(block, 1 - p.y, 1 - p.c), self.cols_of(1 - p.x)]
        return remote(ref, ref, s, r, p.core)

    def own_copy(self):
        start = pl.multiple_of(self.place.fs * self.rows, 16)
        return pltpu.make_async_copy(self.own, self.full.at[pl.ds(start, self.rows)], self.near.at[self.at])

    def first(self):
        p = self.place
        self.own_copy().start()
        mine = self.own.at[pl.ds(pl.multiple_of(p.c * self.deep, 16), self.deep)]
        there = self.full.at[self.rows_of(p.z, p.y, p.c)]

        def out(kind, device):
            return remote(mine, there, self.send.at[self.at, kind, p.z], self.recv.at[self.at, UP, p.z], device)

        pl.when(p.has_up)(lambda: out(UP, p.up).start())
        pl.when(p.has_down)(lambda: out(DOWN, p.down).start())
        cols = self.cols_of(p.x)
        remote(
            mine.at[:, cols],
            there.at[:, cols],
            self.send.at[self.at, YWAY, p.z],
            self.recv.at[self.at, YWAY, p.z],
            p.yway,
        ).start()

    def line_step(self, k):
        p = self.place

        def pass_on(block, kind, more):
            self.landed(UP, block).wait_recv()
            pl.when(more)(lambda: self.copy(kind, block).start())
            self.copy(YWAY, block).start()
            self.copy(CORE, block).start()

        pl.when(p.z - k >= 0)(lambda: pass_on(p.z - k, UP, p.has_up))
        pl.when(p.z + k < p.line)(lambda: pass_on(p.z + k, DOWN, p.has_down))

    def near_blocks(self, k, body):
        p = self.place
        if k == 0:
            body(p.z)
            return
        pl.when(p.z - k >= 0)(lambda: body(p.z - k))
        pl.when(p.z + k < p.line)(lambda: body(p.z + k))

    def y_step(self, k):
        def body(block):
            self.landed(YWAY, block).wait_recv()
            self.copy(XWAY, block).start()
            self.copy(COREY, block).start()

        self.near_blocks(k, body)

    def x_step(self, k):
        def body(block):
            self.landed(XWAY, block).wait_recv()
            self.copy(COREX, block).start()

        self.near_blocks(k, body)

    def stage(self, j):
        line = self.place.line
        if j == 0:
            self.first()
        if 1 <= j < line:
            self.line_step(j)
        if 1 <= j <= line:
            self.y_step(j - 1)
        if 2 <= j <= line + 1:
            self.x_step(j - 2)

    def arrive(self):
        p = self.place
        self.own_copy().wait()

        def body(block, carry):
            pl.when(block != p.z)(lambda: self.landed(CORE, block).wait_recv())
            self.landed(COREY, block).wait_recv()
            self.landed(COREX, block).wait_recv()
            return carry

        lax.fori_loop(0, p.line, body, 0)

    def drain(self):
        p = self.place

        def body(block, carry):
            pl.when(p.has_up & (block <= p.z))(lambda: self.copy(UP, block).wait_send())
            pl.when(p.has_down & (block >= p.z))(lambda: self.copy(DOWN, block).wait_send())
            pl.when(block != p.z)(lambda: self.copy(CORE, block).wait_send())
            for kind in (YWAY, XWAY, COREY, COREX):
                self.copy(kind, block).wait_send()
            return carry

        lax.fori_loop(0, p.line, body, 0)


GATHER_STAGES = 2


def gather_kernel(line, order, *refs):
    owned, small, fulls, small_all = refs[:4], refs[4], refs[5:13], refs[13]
    send, recv, near, small_send, small_recv = refs[14:]
    place = Place(line)
    place.greet()
    smalls = []
    for step in range(1, 2 * line):
        other = lax.rem(place.fs + step, 2 * line)
        smalls.append(
            remote(small, small_all.at[place.fs], small_send.at[step], small_recv.at[place.fs], (place.dp, other))
        )
        smalls[-1].start()
    kept = pltpu.make_async_copy(small, small_all.at[place.fs], small_send.at[0])
    kept.start()
    units = [
        Gather(at, place, owned[which].at[layer], fulls[layer * 4 + which], send, recv, near)
        for at, (layer, which) in enumerate(order)
    ]
    stages = line + GATHER_STAGES
    for slot in range(len(units) + stages - 1):
        for j in range(stages):
            if 0 <= slot - j < len(units):
                units[slot - j].stage(j)
    for unit in units:
        unit.arrive()
    for unit in units:
        unit.drain()
    kept.wait()
    for step in range(1, 2 * line):
        other = lax.rem(place.fs + step, 2 * line)
        smalls[step - 1].wait_send()
        remote(
            small, small_all.at[other], small_send.at[step], small_recv.at[other], (place.dp, other)
        ).wait_recv()


def gather_all(line, owned, small):
    width = [ref.shape for ref in owned]
    outs = [
        jax.ShapeDtypeStruct((2 * line * width[which][1], width[which][2]), owned[which].dtype)
        for layer in range(2)
        for which in range(4)
    ]
    outs.append(jax.ShapeDtypeStruct((2 * line, *small.shape), small.dtype))
    order = [(layer, which) for layer in range(2) for which in range(4)]
    anywhere = pl.BlockSpec(memory_space=pl.ANY)
    return pl.pallas_call(
        functools.partial(gather_kernel, line, order),
        out_shape=outs,
        in_specs=[anywhere] * 5,
        out_specs=[anywhere] * 9,
        scratch_shapes=[
            pltpu.SemaphoreType.DMA((8, 7, line)),
            pltpu.SemaphoreType.DMA((8, 7, line)),
            pltpu.SemaphoreType.DMA((8,)),
            pltpu.SemaphoreType.DMA((2 * line,)),
            pltpu.SemaphoreType.DMA((2 * line,)),
        ],
        compiler_params=pltpu.CompilerParams(collective_id=0, has_side_effects=True),
    )(*owned, small)


class Reduce:
    def __init__(self, at, place, terms, out, bufs, send, recv, near):
        self.at, self.place, self.terms, self.out = at, place, terms, out
        self.mine, self.other, self.from_x, self.from_y, self.line_in, self.last_x, self.total = bufs
        self.send, self.recv, self.near = send, recv, near
        self.deep, self.half = self.mine.shape[2], self.mine.shape[3] // 2

    def cols_of(self, x):
        return pl.ds(pl.multiple_of(x * self.half, 128), self.half)

    def sems(self, kind, block=0):
        return self.send.at[self.at, kind, block], self.recv.at[self.at, kind, block]

    def core_copy(self):
        p = self.place
        return remote(self.terms.at[:, :, 1 - p.c], self.other, *self.sems(0), p.core)

    def near_copy(self):
        return pltpu.make_async_copy(self.terms.at[:, :, self.place.c], self.mine, self.near.at[self.at])

    def x_copy(self):
        p = self.place
        return remote(self.mine.at[:, 1 - p.y, :, self.cols_of(1 - p.x)], self.from_x, *self.sems(1), p.xway)

    def y_copy(self):
        p = self.place
        return remote(self.mine.at[:, 1 - p.y, :, self.cols_of(p.x)], self.from_y, *self.sems(2), p.yway)

    def line_copy(self, way, block):
        p = self.place
        return remote(
            self.mine.at[block, p.y], self.line_in.at[way, block], *self.sems(3 + way, block), (p.up, p.down)[way]
        )

    def last_copy(self):
        p = self.place
        return remote(self.mine.at[p.z, p.y], self.last_x, *self.sems(5), p.xway)

    def out_rows(self, c):
        return self.out.at[pl.ds(pl.multiple_of(c * self.deep, 8), self.deep)]

    def out_copy(self):
        return remote(self.total, self.out_rows(self.place.c), *self.sems(6), self.place.core)

    def out_near(self):
        return pltpu.make_async_copy(self.total, self.out_rows(self.place.c), self.near.at[self.at])

    def start(self):
        self.core_copy().start()
        self.near_copy().start()

    def add_core(self):
        self.near_copy().wait()
        self.core_copy().wait_recv()
        lines = self.mine.shape[0]

        def body(at, carry):
            block, y = at // 2, at % 2
            self.mine[block, y] = self.mine[block, y] + self.other[block, y]
            return carry

        lax.fori_loop(0, 2 * lines, body, 0)
        self.x_copy().start()

    def add_x(self):
        p = self.place
        self.x_copy().wait_recv()
        cols = self.cols_of(p.x)

        def body(block, carry):
            self.mine[block, 1 - p.y, :, cols] = self.mine[block, 1 - p.y, :, cols] + self.from_x[block]
            return carry

        lax.fori_loop(0, self.mine.shape[0], body, 0)
        self.y_copy().start()

    def add_y(self):
        p = self.place
        self.y_copy().wait_recv()
        cols = self.cols_of(p.x)

        def body(block, carry):
            self.mine[block, p.y, :, cols] = self.mine[block, p.y, :, cols] + self.from_y[block]
            return carry

        lax.fori_loop(0, self.mine.shape[0], body, 0)

    def add_line(self, way, block):
        p = self.place
        self.line_copy(way, block).wait_recv()
        self.mine[block, p.y] = self.mine[block, p.y] + self.line_in[way, block]

    def line_step(self, k):
        p, line = self.place, self.place.line
        far = line - 1 - k
        for way, block, valid, more in (
            (0, far, far > p.z, p.has_down),
            (1, k, k < p.z, p.has_up),
        ):

            def body(way=way, block=block, more=more):
                pl.when(more)(lambda: self.add_line(way, block))
                self.line_copy(way, block).start()

            pl.when(valid)(body)

    def own_step(self):
        p = self.place
        pl.when(p.has_down)(lambda: self.add_line(0, p.z))
        pl.when(p.has_up)(lambda: self.add_line(1, p.z))
        self.last_copy().start()

    def finish(self):
        p = self.place
        self.last_copy().wait_recv()
        self.total[...] = self.mine[p.z, p.y].astype(jnp.float32) + self.last_x[...].astype(jnp.float32)
        self.out_copy().start()
        self.out_near().start()

    def stages(self):
        line = self.place.line
        steps = [self.start, self.add_core, self.add_x, self.add_y]
        steps += [functools.partial(self.line_step, k) for k in range(line - 1)]
        return steps + [self.own_step, self.finish]

    def drain(self):
        p = self.place
        self.core_copy().wait_send()
        self.x_copy().wait_send()
        self.y_copy().wait_send()
        for block in range(p.line):
            pl.when(block > p.z)(lambda: self.line_copy(0, block).wait_send())
            pl.when(block < p.z)(lambda: self.line_copy(1, block).wait_send())
        self.last_copy().wait_send()
        self.out_copy().wait()
        self.out_near().wait()


def reduce_kernel(line, order, *refs):
    terms, small, outs, small_out = refs[:8], refs[8], refs[9:13], refs[13]
    bufs, refs = refs[14 : 14 + 7 * 8], refs[14 + 7 * 8 :]
    small_in, small_sum, small_four, send, recv, near, small_send, small_recv = refs
    place = Place(line)
    place.greet()
    fs, dp, n = place.fs, place.dp, 2 * line
    for step in range(1, n):
        other = lax.rem(fs + step, n)
        remote(small.at[other], small_in.at[fs], small_send.at[0, other], small_recv.at[0, fs], (dp, other)).start()
    kept = pltpu.make_async_copy(small.at[fs], small_in.at[fs], small_send.at[0, fs])
    kept.start()
    units = [
        Reduce(at, place, terms[layer * 4 + which], outs[which].at[layer], bufs[7 * at : 7 * at + 7], send, recv, near)
        for at, (layer, which) in enumerate(order)
    ]
    steps = [unit.stages() for unit in units]
    deep = len(steps[0])
    for slot in range(len(units) + deep - 1):
        if slot == 2:
            kept.wait()
            for step in range(1, n):
                other = lax.rem(fs + step, n)
                remote(
                    small.at[other], small_in.at[other], small_send.at[0, other], small_recv.at[0, other], (dp, other)
                ).wait()
            small_sum[...] = jnp.sum(small_in[...], axis=0)
            small_four[dp] = small_sum[...]
            for step in range(1, 4):
                other = lax.rem(dp + step, 4)
                remote(
                    small_sum, small_four.at[dp], small_send.at[1, other], small_recv.at[1, dp], (other, fs)
                ).start()
        if slot == 4:
            for step in range(1, 4):
                other = lax.rem(dp + step, 4)
                remote(
                    small_sum, small_four.at[other], small_send.at[1, other], small_recv.at[1, other], (other, fs)
                ).wait()
            small_out[...] = jnp.sum(small_four[...], axis=0)
        for j in range(deep):
            if 0 <= slot - j < len(units):
                steps[slot - j][j]()
    for unit in units:
        unit.drain()


def reduce_all(line, terms, small):
    order = [(layer, which) for layer in range(2) for which in (3, 2, 1, 0)]
    split, bufs = [], []
    for term in terms:
        deep = term.shape[0] // (4 * line)
        split.append(term.reshape(line, 2, 2, deep, term.shape[1]))
    for layer, which in order:
        _, _, _, deep, width = split[layer * 4 + which].shape
        low = jnp.bfloat16
        bufs += [
            pltpu.VMEM((line, 2, deep, width), low),
            pltpu.VMEM((line, 2, deep, width), low),
            pltpu.VMEM((line, deep, width // 2), low),
            pltpu.VMEM((line, deep, width // 2), low),
            pltpu.VMEM((2, line, deep, width), low),
            pltpu.VMEM((deep, width), low),
            pltpu.VMEM((deep, width), jnp.float32),
        ]
    outs = [
        jax.ShapeDtypeStruct((2, split[which].shape[3] * 2, split[which].shape[4]), jnp.float32) for which in range(4)
    ]
    outs.append(jax.ShapeDtypeStruct(small.shape[1:], jnp.float32))
    anywhere = pl.BlockSpec(memory_space=pl.ANY)
    inside = pl.BlockSpec(memory_space=pltpu.VMEM)
    return pl.pallas_call(
        functools.partial(reduce_kernel, line, order),
        out_shape=outs,
        in_specs=[anywhere] * 8 + [inside],
        out_specs=[anywhere] * 4 + [inside],
        scratch_shapes=bufs
        + [
            pltpu.VMEM(small.shape, jnp.float32),
            pltpu.VMEM(small.shape[1:], jnp.float32),
            pltpu.VMEM((4, *small.shape[1:]), jnp.float32),
            pltpu.SemaphoreType.DMA((8, 7, line)),
            pltpu.SemaphoreType.DMA((8, 7, line)),
            pltpu.SemaphoreType.DMA((8,)),
            pltpu.SemaphoreType.DMA((2, 2 * line)),
            pltpu.SemaphoreType.DMA((2, 2 * line)),
        ],
        compiler_params=pltpu.CompilerParams(collective_id=1, has_side_effects=True, vmem_limit_bytes=62 * 2**20),
    )(*split, small)

def normed(values, gain, shift):
    center = values - jnp.mean(values, axis=-1, keepdims=True)
    spread = jnp.mean(center * center, axis=-1, keepdims=True)
    return center * lax.rsqrt(spread + 1e-05) * gain + shift


def gelu_exact(values):
    return jax.nn.gelu(values, approximate=False)


def segment_ids(lengths, seq_len):
    bounds = jnp.cumsum(lengths, axis=-1)
    positions = jnp.arange(seq_len, dtype=jnp.int32)
    return jnp.sum((positions[None, :, None] >= bounds[:, None, :]).astype(jnp.int32), axis=-1)


def split_heads(values):
    batch, length, width = values.shape
    return values.reshape(batch, length, width // HEAD, HEAD)


def masked_scores(queries, keys_all, segment):
    scores = jnp.einsum(
        "bqhd,bkhd->bhqk",
        split_heads(queries),
        split_heads(keys_all),
        preferred_element_type=jnp.float32,
    )
    same = (segment[:, :, None] == segment[:, None, :])[:, None]
    return (jnp.where(same, scores, -1e30), same)


def attention(queries, keys_all, values_all, segment):
    scores, same = masked_scores(queries, keys_all, segment)
    largest = jnp.max(scores, axis=-1, keepdims=True)
    raised = jnp.exp(scores - largest)
    totals = jnp.sum(raised, axis=-1, keepdims=True)
    attn_weights = raised / totals
    log_total = largest + jnp.log(totals)
    mixed = jnp.einsum(
        "bhqk,bkhd->bqhd",
        attn_weights.astype(jnp.bfloat16),
        split_heads(values_all),
        preferred_element_type=jnp.float32,
    )
    return (mixed.reshape(queries.shape).astype(jnp.bfloat16), log_total)


def attention_back(queries, keys_all, values_all, segment, log_total, grad_mixed):
    scores, same = masked_scores(queries, keys_all, segment)
    attn_weights = jnp.where(same, jnp.exp(scores - log_total), 0.0)
    grad_heads = split_heads(grad_mixed)
    grad_weights = jnp.einsum(
        "bqhd,bkhd->bhqk", grad_heads, split_heads(values_all), preferred_element_type=jnp.float32
    )
    inner = jnp.sum(attn_weights * grad_weights, axis=-1, keepdims=True)
    grad_scores = (attn_weights * (grad_weights - inner)).astype(jnp.bfloat16)
    grad_queries = jnp.einsum(
        "bhqk,bkhd->bqhd", grad_scores, split_heads(keys_all), preferred_element_type=jnp.float32
    )
    grad_keys = jnp.einsum(
        "bhqk,bqhd->bkhd", grad_scores, split_heads(queries), preferred_element_type=jnp.float32
    )
    grad_values = jnp.einsum(
        "bhqk,bqhd->bkhd",
        attn_weights.astype(jnp.bfloat16),
        grad_heads,
        preferred_element_type=jnp.float32,
    )
    shape_rows = queries.shape
    return (
        grad_queries.reshape(shape_rows),
        grad_keys.reshape(shape_rows),
        grad_values.reshape(shape_rows),
    )


def forward_layer(inputs, weights, segment):
    qkv_weight, out_weight, up_weight, down_weight, gains, biases, up_bias = weights
    width = inputs.shape[-1]
    source = inputs.astype(jnp.float32)
    normed_a = normed(source, gains[0], biases[0]).astype(jnp.bfloat16)
    project = jnp.einsum("bld,de->ble", normed_a, qkv_weight, preferred_element_type=jnp.float32)
    queries = ((project[..., :width] + biases[2]) * HEAD ** (-0.5)).astype(jnp.bfloat16)
    keys_all = project[..., width : 2 * width].astype(jnp.bfloat16)
    values_all = (project[..., 2 * width :] + biases[3]).astype(jnp.bfloat16)
    mixed, log_total = attention(queries, keys_all, values_all, segment)
    hidden = (
        source
        + jnp.einsum("bld,de->ble", mixed, out_weight, preferred_element_type=jnp.float32)
        + biases[4]
    )
    normed_c = normed(hidden, gains[1], biases[1]).astype(jnp.bfloat16)
    before = (
        jnp.einsum("bld,df->blf", normed_c, up_weight, preferred_element_type=jnp.float32) + up_bias
    )
    activated = gelu_exact(before).astype(jnp.bfloat16)
    result = (
        hidden
        + jnp.einsum("blf,fd->bld", activated, down_weight, preferred_element_type=jnp.float32)
        + biases[5]
    )
    return (
        source,
        normed_a,
        queries,
        keys_all,
        values_all,
        log_total,
        mixed,
        hidden,
        normed_c,
        before,
        activated,
        result,
    )


def backward_layer(inputs, cotangent, weights, segment):
    qkv_weight, out_weight, up_weight, down_weight, gains, biases, up_bias = weights
    width = inputs.shape[-1]
    (
        source,
        normed_a,
        queries,
        keys_all,
        values_all,
        log_total,
        mixed,
        hidden,
        normed_c,
        before,
        activated,
        result,
    ) = forward_layer(inputs, weights, segment)
    grad_result = cotangent.astype(jnp.float32)
    grad_downw = jnp.einsum("blf,bld->fd", activated, cotangent, preferred_element_type=jnp.float32)
    grad_act = jnp.einsum("bld,fd->blf", cotangent, down_weight, preferred_element_type=jnp.float32)
    grad_before = jax.vjp(gelu_exact, before)[1](grad_act)[0].astype(jnp.bfloat16)
    grad_upw = jnp.einsum("bld,blf->df", normed_c, grad_before, preferred_element_type=jnp.float32)
    grad_upb = jnp.sum(grad_before.astype(jnp.float32), axis=(0, 1))
    grad_normc = jnp.einsum(
        "blf,df->bld", grad_before, up_weight, preferred_element_type=jnp.float32
    )
    hidden_back = jax.vjp(
        normed, hidden, gains[1].astype(jnp.float32), biases[1].astype(jnp.float32)
    )[1]
    grad_hidden_ln, grad_gain_two, grad_shift_two = hidden_back(grad_normc)
    grad_hidden = grad_result + grad_hidden_ln
    grad_branch = grad_hidden.astype(jnp.bfloat16)
    grad_outw = jnp.einsum("bld,ble->de", mixed, grad_branch, preferred_element_type=jnp.float32)
    grad_mixed = jnp.einsum(
        "ble,de->bld", grad_branch, out_weight, preferred_element_type=jnp.float32
    ).astype(jnp.bfloat16)
    grad_queries, grad_keys, grad_values = attention_back(
        queries, keys_all, values_all, segment, log_total, grad_mixed
    )
    grad_project = jnp.concatenate(
        [
            grad_queries.astype(jnp.bfloat16) * HEAD ** (-0.5),
            grad_keys.astype(jnp.bfloat16),
            grad_values.astype(jnp.bfloat16),
        ],
        axis=-1,
    )
    grad_qkvw = jnp.einsum(
        "bld,ble->de", normed_a, grad_project, preferred_element_type=jnp.float32
    )
    column_sums = jnp.sum(grad_project.astype(jnp.float32), axis=(0, 1))
    grad_norma = jnp.einsum(
        "ble,de->bld", grad_project, qkv_weight, preferred_element_type=jnp.float32
    )
    source_back = jax.vjp(
        normed, source, gains[0].astype(jnp.float32), biases[0].astype(jnp.float32)
    )[1]
    grad_source_ln, grad_gain_one, grad_shift_one = source_back(grad_norma)
    grad_inputs = grad_hidden + grad_source_ln
    grad_gains = jnp.stack([grad_gain_one, grad_gain_two])
    grad_biases = jnp.stack(
        [
            grad_shift_one,
            grad_shift_two,
            column_sums[:width],
            column_sums[2 * width :],
            jnp.sum(grad_branch.astype(jnp.float32), axis=(0, 1)),
            jnp.sum(grad_result, axis=(0, 1)),
        ]
    )
    return (
        result.astype(jnp.bfloat16),
        grad_inputs,
        (grad_qkvw, grad_outw, grad_upw, grad_downw, grad_gains, grad_biases, grad_upb),
    )


def fetch_weights(layer_index, w_qkv, w_out, w_up, w_down, gains, biases, b_up):
    return (
        lax.all_gather(w_qkv[layer_index], "fsdp", axis=0, tiled=True),
        lax.all_gather(w_out[layer_index], "fsdp", axis=0, tiled=True),
        lax.all_gather(w_up[layer_index], "fsdp", axis=0, tiled=True),
        lax.all_gather(w_down[layer_index], "fsdp", axis=0, tiled=True),
        lax.all_gather(gains[layer_index], "fsdp", axis=1, tiled=True),
        lax.all_gather(biases[layer_index], "fsdp", axis=1, tiled=True),
        lax.all_gather(b_up[layer_index], "fsdp", axis=0, tiled=True),
    )


def fetch_again(layer_index, w_qkv, w_out, w_up, w_down, gains, biases, b_up):
    return (
        lax.all_gather(w_qkv[layer_index], "fsdp", axis=0, tiled=True),
        lax.all_gather(w_out[layer_index], "fsdp", axis=0, tiled=True),
        lax.all_gather(w_up[layer_index], "fsdp", axis=0, tiled=True),
        lax.all_gather(w_down[layer_index], "fsdp", axis=0, tiled=True),
        lax.all_gather(gains[layer_index], "fsdp", axis=1, tiled=True),
        lax.all_gather(biases[layer_index], "fsdp", axis=1, tiled=True),
        lax.all_gather(b_up[layer_index], "fsdp", axis=0, tiled=True),
    )


def reduce_grads(gradients):
    shares = (
        lax.psum_scatter(gradients[0], "fsdp", scatter_dimension=0, tiled=True),
        lax.psum_scatter(gradients[1], "fsdp", scatter_dimension=0, tiled=True),
        lax.psum_scatter(gradients[2], "fsdp", scatter_dimension=0, tiled=True),
        lax.psum_scatter(gradients[3], "fsdp", scatter_dimension=0, tiled=True),
        lax.psum_scatter(gradients[4], "fsdp", scatter_dimension=1, tiled=True),
        lax.psum_scatter(gradients[5], "fsdp", scatter_dimension=1, tiled=True),
        lax.psum_scatter(gradients[6], "fsdp", scatter_dimension=0, tiled=True),
    )
    quarters = (
        lax.psum_scatter(
            shares[0].astype(jnp.bfloat16), "dp", scatter_dimension=0, tiled=True
        ).astype(jnp.float32),
        lax.psum_scatter(
            shares[1].astype(jnp.bfloat16), "dp", scatter_dimension=0, tiled=True
        ).astype(jnp.float32),
        lax.psum_scatter(
            shares[2].astype(jnp.bfloat16), "dp", scatter_dimension=0, tiled=True
        ).astype(jnp.float32),
        lax.psum_scatter(
            shares[3].astype(jnp.bfloat16), "dp", scatter_dimension=0, tiled=True
        ).astype(jnp.float32),
        lax.psum_scatter(
            shares[4].astype(jnp.bfloat16), "dp", scatter_dimension=1, tiled=True
        ).astype(jnp.float32),
        lax.psum_scatter(
            shares[5].astype(jnp.bfloat16), "dp", scatter_dimension=1, tiled=True
        ).astype(jnp.float32),
        lax.psum_scatter(
            shares[6].astype(jnp.bfloat16), "dp", scatter_dimension=0, tiled=True
        ).astype(jnp.float32),
    )
    return (
        lax.all_gather(quarters[0].astype(jnp.bfloat16), "dp", axis=0, tiled=True).astype(
            jnp.float32
        ),
        lax.all_gather(quarters[1].astype(jnp.bfloat16), "dp", axis=0, tiled=True).astype(
            jnp.float32
        ),
        lax.all_gather(quarters[2].astype(jnp.bfloat16), "dp", axis=0, tiled=True).astype(
            jnp.float32
        ),
        lax.all_gather(quarters[3].astype(jnp.bfloat16), "dp", axis=0, tiled=True).astype(
            jnp.float32
        ),
        lax.all_gather(quarters[4].astype(jnp.bfloat16), "dp", axis=1, tiled=True).astype(
            jnp.float32
        ),
        lax.all_gather(quarters[5].astype(jnp.bfloat16), "dp", axis=1, tiled=True).astype(
            jnp.float32
        ),
        lax.all_gather(quarters[6].astype(jnp.bfloat16), "dp", axis=0, tiled=True).astype(
            jnp.float32
        ),
    )


def plain(
    images,
    image_cot,
    captions,
    caption_cot,
    lengths,
    w_qkv,
    w_out,
    w_up,
    w_down,
    gains,
    biases,
    b_up,
):
    owned = (w_qkv, w_out, w_up, w_down, gains, biases, b_up)
    image_seg = jnp.zeros((images.shape[0], images.shape[1]), jnp.int32)
    caption_seg = segment_ids(lengths, captions.shape[1])
    first_weights = fetch_weights(0, *owned)
    image_out = forward_layer(images, first_weights, image_seg)[-1].astype(jnp.bfloat16)
    second_weights = fetch_weights(1, *owned)
    caption_out = forward_layer(captions, second_weights, caption_seg)[-1].astype(jnp.bfloat16)
    second_back = fetch_again(1, *owned)
    _, caption_grad, caption_terms = backward_layer(captions, caption_cot, second_back, caption_seg)
    caption_shares = reduce_grads(caption_terms)
    first_back = fetch_again(0, *owned)
    _, image_grad, image_terms = backward_layer(images, image_cot, first_back, image_seg)
    image_shares = reduce_grads(image_terms)
    stacked = tuple((jnp.stack([image_shares[index], caption_shares[index]]) for index in range(7)))
    return (image_out, caption_out, image_grad, caption_grad) + stacked


def kernels_fit(mesh, w_qkv):
    return mesh.shape["dp"] == 4 and mesh.shape["fsdp"] % 2 == 0 and w_qkv.shape[1] % 32 == 0


def pack_small(gains, biases, b_up):
    rows = jnp.concatenate([gains.reshape(2, -1), biases.reshape(2, -1), b_up], axis=1).astype(jnp.float32).reshape(-1)
    return jnp.pad(rows, (0, -rows.size % 1024)).reshape(-1, 128)


def unpack_small(blocks, width, deep):
    count = blocks.shape[0]
    flat = blocks.reshape(count, -1)[:, : 2 * (8 * width + deep)].reshape(count, 2, 8 * width + deep)
    rows = flat[:, :, : 8 * width].reshape(count, 2, 8, width).transpose(1, 2, 0, 3).reshape(2, 8, count * width)
    up = flat[:, :, 8 * width :].transpose(1, 0, 2).reshape(2, count * deep)
    return rows[:, :2], rows[:, 2:], up


def spread_small(count, gains, biases, b_up):
    rows = jnp.concatenate([gains, biases], axis=1)
    width, deep = rows.shape[2] // count, b_up.shape[1] // count
    rows = rows.reshape(2, 8, count, width).transpose(2, 0, 1, 3).reshape(count, 2, 8 * width)
    up = b_up.reshape(2, count, deep).transpose(1, 0, 2)
    flat = jnp.concatenate([rows, up], axis=2).reshape(count, -1)
    return jnp.pad(flat, ((0, 0), (0, -flat.shape[1] % 1024))).reshape(count, -1, 128)


def local(mesh, images, image_cot, captions, caption_cot, lengths, w_qkv, w_out, w_up, w_down, gains, biases, b_up):
    if not kernels_fit(mesh, w_qkv):
        return plain(
            images, image_cot, captions, caption_cot, lengths, w_qkv, w_out, w_up, w_down, gains, biases, b_up
        )
    count = mesh.shape["fsdp"]
    line = count // 2
    width, deep = gains.shape[2], b_up.shape[1]
    image_seg = jnp.zeros((images.shape[0], images.shape[1]), jnp.int32)
    caption_seg = segment_ids(lengths, captions.shape[1])
    own = tuple(w.reshape(2, 2, -1, w.shape[2]) for w in (w_qkv, w_out, w_up)) + (w_down.reshape(2, 2, 4, -1, w_down.shape[2]),)
    n = padded(images.shape[1])
    kept = layer_scratch(n, 768, 3072, (line, 2, 2, 48))
    order = [(layer, which) for layer in range(2) for which in range(4)]
    anywhere, inside = pl.BlockSpec(memory_space=pl.ANY), pl.BlockSpec(memory_space=pltpu.VMEM)
    wshape = [(line, 2, 2, 48, 2304), (line, 2, 2, 48, 768), (line, 2, 2, 48, 3072), (line, 2, 2, 4, 48, 768)]
    flatshape = [(768, 2304), (768, 768), (768, 3072), (3072, 768)]
    outs = [jax.ShapeDtypeStruct(flatshape[which], jnp.bfloat16) for layer in range(2) for which in range(4)]
    packed_small = pack_small(gains, biases, b_up)
    outs.append(jax.ShapeDtypeStruct((2 * line, *packed_small.shape), jnp.float32))
    outs += [
        jax.ShapeDtypeStruct(images.shape, jnp.bfloat16),
        jax.ShapeDtypeStruct(images.shape, jnp.float32),
        jax.ShapeDtypeStruct((8, 768), jnp.float32),
        jax.ShapeDtypeStruct((1, 3072), jnp.float32),
    ] + [jax.ShapeDtypeStruct(shape, jnp.bfloat16) for shape in wshape]
    sems = [
            pltpu.SemaphoreType.DMA((8, 7, line)),
            pltpu.SemaphoreType.DMA((8, 7, line)),
            pltpu.SemaphoreType.DMA((8,)),
            pltpu.SemaphoreType.DMA((2 * line,)),
            pltpu.SemaphoreType.DMA((2 * line,)),
    ]
    ln = [pltpu.SemaphoreType.DMA((4,))] + [pltpu.VMEM(shape, jnp.bfloat16) for shape in wshape]
    def merged(*refs):
        owned, small = refs[:4], refs[4]
        x, dy, seg_col, seg_row, par, b_upr = refs[5:11]
        fulls, small_all = refs[11:19], refs[19]
        y_out, x_grad, g_par, g_bup, *terms = refs[20:28]
        scr = refs[28:]
        gather_kernel(line, order, *owned, small, *fulls, small_all, *scr[:5])
        weights=[fulls[0].reshape(*wshape[0]),fulls[1].reshape(*wshape[1]),fulls[2].reshape(*wshape[2]),fulls[3].reshape(*wshape[3])]
        layer_kernel(n, list(kept), x, dy, seg_col, seg_row, par, b_upr, *weights, y_out, x_grad, g_par, g_bup, *terms, *scr[5:])
    segment = jnp.pad(image_seg, ((0, 0), (0, n - 197)), constant_values=-1)
    gains_all, biases_all, up_all = (
        lax.all_gather(part.astype(jnp.float32), "fsdp", axis=part.ndim - 1, tiled=True) for part in (gains, biases, b_up)
    )
    par = jnp.concatenate([gains_all, biases_all], axis=1)
    res = pl.pallas_call(merged, out_shape=outs, in_specs=[anywhere] * 5 + [inside] * 6,
        out_specs=[anywhere] * 9 + [inside] * 4 + [anywhere] * 4,
        scratch_shapes=sems + ln + list(kept.values()),
        compiler_params=pltpu.CompilerParams(collective_id=0, has_side_effects=True, vmem_limit_bytes=62 * 2**20))(
        w_qkv, w_out, w_up, w_down, packed_small, images, image_cot, segment.reshape(n, 1), segment, par[0], up_all[:1])
    fulls, small = res[:8], res[8]
    outs, grads, terms, smalls = [res[9]], [res[10]], [t.reshape(-1, t.shape[-1]) for t in res[13:]], [(res[11][:2], res[11][2:], res[12][0])]
    rows, cot, seg, layer = captions, caption_cot, caption_seg, 1
    weights = fulls[layer * 4 : layer * 4 + 4]
    weights = [w.reshape(line, 2, 2, -1, w.shape[1]) for w in weights[:3]] + [weights[3].reshape(line, 2, 2, 4, -1, weights[3].shape[1])]
    result, grad, g_par, g_bup, *found = run_layer(rows, cot, seg, weights, par[layer], up_all[layer : layer + 1])
    outs.append(result)
    grads.append(grad)
    terms += [t.reshape(-1, t.shape[-1]) for t in found]
    smalls.append((g_par[:2], g_par[2:], g_bup[0]))
    packed = spread_small(count, *(jnp.stack([smalls[0][at], smalls[1][at]]) for at in range(3)))
    *shares, small_share = reduce_all(line, terms, packed)
    rest = unpack_small(small_share[None], width, deep)
    return (*outs, *grads, *shares, *rest)


def solution(mesh):
    placed = (
        P(("dp", "fsdp"), None, None),
        P(("dp", "fsdp"), None, None),
        P(("dp", "fsdp"), None, None),
        P(("dp", "fsdp"), None, None),
        P(("dp", "fsdp"), None),
        P(None, "fsdp", None),
        P(None, "fsdp", None),
        P(None, "fsdp", None),
        P(None, "fsdp", None),
        P(None, None, "fsdp"),
        P(None, None, "fsdp"),
        P(None, "fsdp"),
    )
    return jax.shard_map(
        functools.partial(local, mesh),
        mesh=mesh,
        in_specs=placed,
        out_specs=(
            P(("dp", "fsdp"), None, None),
            P(("dp", "fsdp"), None, None),
            P(("dp", "fsdp"), None, None),
            P(("dp", "fsdp"), None, None),
            P(None, "fsdp", None),
            P(None, "fsdp", None),
            P(None, "fsdp", None),
            P(None, "fsdp", None),
            P(None, None, "fsdp"),
            P(None, None, "fsdp"),
            P(None, "fsdp"),
        ),
        check_vma=False,
    )
```

```python
import functools

import jax
import jax.numpy as jnp
from jax import lax
from jax.experimental import pallas as pl
from jax.experimental.pallas import tpu as pltpu
from jax.sharding import PartitionSpec as P

HEAD = 64

MESH = pl.DeviceIdType.MESH
NT = (((1,), (1,)), ((), ()))
TN = (((0,), (0,)), ((), ()))
TILE = 256
CHUNK = 64
ALL = slice(None)


def dot(a, b, dims=(((1,), (0,)), ((), ()))):
    return lax.dot_general(a, b, dims, preferred_element_type=jnp.float32)


def flat(value):
    return value.reshape(-1, value.shape[-1])


def at(t, size=TILE):
    return pl.ds(pl.multiple_of(t * size, size), size)


def remote(src, dst, send, recv, device):
    return pltpu.make_async_remote_copy(
        src_ref=src, dst_ref=dst, send_sem=send, recv_sem=recv, device_id=device, device_id_type=MESH
    )


class Place:
    def __init__(self, line):
        dp, fs = lax.axis_index("dp"), lax.axis_index("fsdp")
        self.line, self.dp, self.fs = line, dp, fs
        self.x, self.c = dp // 2, dp % 2
        self.z, self.y = fs // 2, fs % 2
        self.up, self.down = (dp, fs + 2), (dp, fs - 2)
        self.yway = (dp, self.z * 2 + 1 - self.y)
        self.xway = ((1 - self.x) * 2 + self.c, fs)
        self.core = (self.x * 2 + 1 - self.c, fs)
        self.has_up, self.has_down = self.z + 1 < line, self.z > 0

    def others(self):
        return [lax.rem(self.fs + step, 2 * self.line) for step in range(1, 2 * self.line)]

    def greet(self):
        barrier = pltpu.get_barrier_semaphore()
        known = [(self.dp, other) for other in self.others()] + [self.xway, self.core]
        for device in known:
            pl.semaphore_signal(barrier, inc=1, device_id=device, device_id_type=MESH)
        pl.semaphore_wait(barrier, len(known))


class Panel:
    def __init__(self, which, part, width):
        self.which, self.part, self.width = which, part, width

    def cols(self, x):
        base = 0 if self.which == 3 else self.part * self.width
        if x is None:
            return pl.ds(base, self.width)
        half = self.width // 2
        return pl.ds(pl.multiple_of(base + x * half, 128), half)

    def of(self, ref, *lead, x=None):
        if self.which == 3:
            return ref.at[(*lead, self.part, ALL, self.cols(x))]
        return ref.at[(*lead, ALL, self.cols(x))]


def panels_of(layer_shapes, width, order):
    made = []
    for which in order:
        count = layer_shapes[which]
        made += [Panel(which, part, width) for part in range(count)]
    return made


class Gather:
    def __init__(self, at, place, own, panel, full, split, send, recv, near):
        self.at, self.place, self.own, self.panel, self.full = at, place, own, panel, full
        self.send, self.recv, self.near = send, recv, near
        self.split = split
        self.lane = place.x if split else None

    def view(self, block, y, c, x=None):
        return self.panel.of(self.full, block, y, c, x=x)

    def sent(self, slot):
        return self.send.at[self.at, slot]

    def got(self, slot):
        return self.recv.at[self.at, slot]

    def line_copy(self, way, block):
        p = self.place
        ref = self.view(block, p.y, p.c, self.lane)
        return remote(ref, ref, self.sent(way * p.line + block), self.got(block), (p.up, p.down)[way])

    def near_copy(self):
        p = self.place
        mine = self.panel.of(self.own, p.c, x=self.lane)
        return pltpu.make_async_copy(mine, self.view(p.z, p.y, p.c, self.lane), self.near.at[self.at])

    def far_copy(self, kind):
        p, line = self.place, self.place.line
        ref, device = {
            "y": (lambda: (self.view(ALL, p.y, p.c, p.x), p.yway)),
            "x": (lambda: (self.view(ALL, 1 - p.y, p.c, p.x), p.xway)),
            "x_own": (lambda: (self.view(ALL, p.y, p.c, p.x), p.xway)),
            "core_own": (lambda: (self.view(ALL, p.y, p.c), p.core)),
            "core": (lambda: (self.view(ALL, 1 - p.y, p.c), p.core)),
        }[kind]()
        slot = ("y", "x", "x_own", "core_own", "core").index(kind)
        return remote(ref, ref, self.sent(2 * line + slot), self.got(line + slot), device)

    def landed(self, kind):
        p, line = self.place, self.place.line
        ref = {
            "y": lambda: self.view(ALL, 1 - p.y, p.c, p.x),
            "x": lambda: self.view(ALL, 1 - p.y, p.c, 1 - p.x),
            "x_own": lambda: self.view(ALL, p.y, p.c, 1 - p.x),
            "core_own": lambda: self.view(ALL, p.y, 1 - p.c),
            "core": lambda: self.view(ALL, 1 - p.y, 1 - p.c),
        }[kind]()
        slot = ("y", "x", "x_own", "core_own", "core").index(kind)
        return remote(ref, ref, self.sent(2 * line + slot), self.got(line + slot), p.core)

    def kinds(self):
        return ("y", "x", "x_own", "core_own", "core") if self.split else ("y", "x", "core_own", "core")

    def first(self):
        p = self.place
        self.near_copy().start()
        mine = self.panel.of(self.own, p.c, x=self.lane)
        there = self.view(p.z, p.y, p.c, self.lane)
        for way, able, device in ((0, p.has_up, p.up), (1, p.has_down, p.down)):
            copy = functools.partial(remote, mine, there, self.sent(way * p.line + p.z), self.got(p.z), device)
            pl.when(able)(lambda copy=copy: copy().start())

    def hop(self, k):
        p = self.place

        def pass_on(way, block, more):
            self.line_copy(way, block).wait_recv()
            pl.when(more)(lambda: self.line_copy(way, block).start())

        pl.when(p.z - k >= 0)(lambda: pass_on(0, p.z - k, p.has_up))
        pl.when(p.z + k < p.line)(lambda: pass_on(1, p.z + k, p.has_down))
        if k == p.line - 1:
            self.near_copy().wait()
            self.far_copy("y").start()
            self.far_copy("x_own" if self.split else "core_own").start()

    def cross(self):
        self.landed("y").wait_recv()
        self.far_copy("x").start()
        if self.split:
            self.landed("x_own").wait_recv()
            self.far_copy("core_own").start()

    def share(self):
        self.landed("x").wait_recv()
        self.far_copy("core").start()

    def stages(self):
        hops = [functools.partial(self.hop, k) for k in range(1, self.place.line)]
        return [self.first, *hops, self.cross, self.share]

    def arrive(self):
        self.landed("core_own").wait_recv()
        self.landed("core").wait_recv()

    def drain(self):
        p = self.place

        def body(block, carry):
            pl.when(p.has_up & (block <= p.z))(lambda: self.line_copy(0, block).wait_send())
            pl.when(p.has_down & (block >= p.z))(lambda: self.line_copy(1, block).wait_send())
            return carry

        lax.fori_loop(0, p.line, body, 0)
        for kind in self.kinds():
            self.far_copy(kind).wait_send()


RINGS = dict(own=10, away=5, other=3, from_x=3, from_y=3, line_in=4, last=3, total=3)
CREDITS = ("other", "from_x", "from_y", "line_up", "line_down", "last")


class Reduce:
    def __init__(self, at, count, place, panel, terms, out, bufs, credit, send, recv, near):
        self.at, self.count, self.place, self.panel, self.terms, self.out = at, count, place, panel, terms, out
        self.credit, self.send, self.recv, self.near = credit, send, recv, near
        self.b = {name: ref.at[at % RINGS[name]] for name, ref in bufs.items()}
        self.half = panel.width // 2

    def cols_of(self, x):
        return pl.ds(pl.multiple_of(x * self.half, 128), self.half)

    def spend(self, name, ring):
        if self.at >= RINGS[ring]:
            pl.semaphore_wait(self.credit.at[CREDITS.index(name)], 1)

    def grant(self, name, ring, device):
        if self.at + RINGS[ring] < self.count:
            pl.semaphore_signal(
                self.credit.at[CREDITS.index(name)], inc=1, device_id=device, device_id_type=MESH
            )

    def sems(self, slot):
        return self.send.at[self.at, slot], self.recv.at[self.at, slot]

    def core_copy(self):
        p = self.place
        return remote(self.panel.of(self.terms, ALL, ALL, 1 - p.c), self.b["other"], *self.sems(0), p.core)

    def near_copy(self, away):
        p = self.place
        src = self.panel.of(self.terms, ALL, (1 - p.y) if away else p.y, p.c)
        return pltpu.make_async_copy(src, self.b["away" if away else "own"], self.near.at[self.at, int(away)])

    def x_copy(self):
        p = self.place
        return remote(self.b["away"].at[:, :, self.cols_of(1 - p.x)], self.b["from_x"], *self.sems(1), p.xway)

    def y_copy(self):
        p = self.place
        return remote(self.b["away"].at[:, :, self.cols_of(p.x)], self.b["from_y"], *self.sems(2), p.yway)

    def came(self, way, block):
        return self.b["line_in"].at[block - 1 if way == 0 else self.place.line - 1 + block]

    def line_copy(self, way, block):
        p = self.place
        slot = 5 + way * p.line + block
        return remote(self.b["own"].at[block], self.came(way, block), *self.sems(slot), (p.up, p.down)[way])

    def last_copy(self):
        p = self.place
        return remote(self.b["own"].at[p.z], self.b["last"], *self.sems(3), p.xway)

    def out_copy(self):
        ref = self.panel.of(self.out, self.place.c)
        return remote(self.b["total"], ref, *self.sems(4), self.place.core)

    def out_landed(self):
        ref = self.panel.of(self.out, 1 - self.place.c)
        return remote(self.b["total"], ref, *self.sems(4), self.place.core)

    def out_near(self):
        return pltpu.make_async_copy(self.b["total"], self.panel.of(self.out, self.place.c), self.near.at[self.at, 2])

    def each(self, body):
        def step(block, carry):
            body(block)
            return carry

        lax.fori_loop(0, self.place.line, step, 0)

    def start(self):
        self.spend("other", "other")
        self.core_copy().start()
        self.near_copy(False).start()
        self.near_copy(True).start()

    def add_core(self):
        p, b = self.place, self.b
        self.near_copy(False).wait()
        self.near_copy(True).wait()
        self.core_copy().wait_recv()

        def body(block):
            b["away"][block] = b["away"][block] + b["other"][block, 1 - p.y]

        self.each(body)
        self.spend("from_x", "from_x")
        self.x_copy().start()

        def rest(block):
            b["own"][block] = b["own"][block] + b["other"][block, p.y]

        self.each(rest)
        self.grant("other", "other", p.core)

    def add_x(self):
        p, b = self.place, self.b
        self.x_copy().wait_recv()
        cols = self.cols_of(p.x)

        def body(block):
            b["away"][block, :, cols] = b["away"][block, :, cols] + b["from_x"][block]

        self.each(body)
        self.spend("from_y", "from_y")
        self.y_copy().start()
        self.grant("from_x", "from_x", p.xway)

    def add_y(self):
        p, b = self.place, self.b
        self.y_copy().wait_recv()
        cols = self.cols_of(p.x)

        def body(block):
            b["own"][block, :, cols] = b["own"][block, :, cols] + b["from_y"][block]

        self.each(body)
        self.grant("from_y", "from_y", p.yway)

    def add_line(self, way, block):
        self.line_copy(way, block).wait_recv()
        self.b["own"][block] = self.b["own"][block] + self.came(way, block)[...]

    def line_step(self, k):
        p, line = self.place, self.place.line
        if k == 0:
            pl.when(p.has_up)(lambda: self.spend("line_up", "line_in"))
            pl.when(p.has_down)(lambda: self.spend("line_down", "line_in"))
        far = line - 1 - k
        for way, block, valid, more in ((0, far, far > p.z, p.has_down), (1, k, k < p.z, p.has_up)):

            def body(way=way, block=block, more=more):
                pl.when(more)(lambda: self.add_line(way, block))
                self.line_copy(way, block).start()

            pl.when(valid)(body)

    def own_step(self):
        p = self.place
        pl.when(p.has_down)(lambda: self.add_line(0, p.z))
        pl.when(p.has_up)(lambda: self.add_line(1, p.z))
        self.spend("last", "last")
        self.last_copy().start()
        pl.when(p.has_down)(lambda: self.grant("line_up", "line_in", p.down))
        pl.when(p.has_up)(lambda: self.grant("line_down", "line_in", p.up))

    def finish(self):
        p, b = self.place, self.b
        self.last_copy().wait_recv()
        b["total"][...] = b["own"][p.z].astype(jnp.float32) + b["last"][...].astype(jnp.float32)
        self.grant("last", "last", p.xway)
        self.out_copy().start()
        self.out_near().start()

    def stages(self):
        steps = [self.start, self.add_core, self.add_x, self.add_y]
        steps += [functools.partial(self.line_step, k) for k in range(self.place.line - 1)]
        return steps + [self.own_step, self.finish]

    def free_away(self):
        self.core_copy().wait_send()
        self.x_copy().wait_send()
        self.y_copy().wait_send()

    def free_own(self):
        p = self.place
        for block in range(p.line):
            pl.when(block > p.z)(lambda block=block: self.line_copy(0, block).wait_send())
            pl.when(block < p.z)(lambda block=block: self.line_copy(1, block).wait_send())
        self.last_copy().wait_send()

    def free_total(self):
        self.out_copy().wait_send()
        self.out_near().wait()


class Pump:
    def __init__(self, units, before=None):
        self.units, self.steps, self.slot = units, [unit.stages() for unit in units], 0
        self.deep, self.before = len(self.steps[0]), before
        self.ready = len(units)

    def total(self):
        return len(self.units) + self.deep - 1

    def left(self):
        return self.total() - self.slot

    def pump(self, count=1):
        for _ in range(count):
            if self.slot >= self.total():
                return
            if self.slot < len(self.units) and self.slot >= self.ready:
                return
            for j in [0, *range(self.deep - 1, 0, -1)]:
                unit = self.slot - j
                if 0 <= unit < len(self.units):
                    if self.before is not None:
                        self.before(unit, j)
                    self.steps[unit][j]()
            self.slot += 1

    def pump_to(self, slot):
        self.pump(max(0, slot - self.slot))

    def done_with(self, unit):
        self.pump_to(unit + self.deep)


class Layer:
    def __init__(self, n, kept, weights, par, b_up, terms, g_par, g_bup):
        self.n, self.s = n, kept
        self.w_qkv, self.w_out, self.w_up, self.w_down = weights
        self.par, self.b_up = par, b_up
        self.g_qkv, self.g_out, self.g_up, self.g_down = terms
        self.g_par, self.g_bup = g_par, g_bup
        self.width, self.deep = self.w_out.shape[-1], self.w_up.shape[-1]
        self.pending = [None, None]

    def chunks(self, body):
        def step(i, carry):
            body(at(i, CHUNK))
            return carry

        lax.fori_loop(0, self.n // CHUNK, step, 0)

    def tiles(self, first, last, body):
        def step(i, carry):
            body(i)
            return carry

        lax.fori_loop(first, last, step, 0)

    def row(self, ref, i):
        return ref[i : i + 1, :]

    def tall_copy(self, ref, slot, t):
        stage = self.s["stage"].at[slot].reshape(*ref.shape[:4], self.width)
        cols = at(t, self.width)
        return pltpu.make_async_copy(stage, ref.at[:, :, :, :, cols], self.s["stage_sem"].at[slot])

    def wide_copy(self, ref, slot, t):
        stage = self.s["stage"].at[slot].reshape(*ref.shape[1:])
        return pltpu.make_async_copy(stage, ref.at[t], self.s["stage_sem"].at[slot])

    def put(self, make, slot, t, first, value):
        held = self.pending[slot]
        pl.when(t > first)(lambda: make(slot, t - 1).wait())
        if held is not None:
            pl.when(t == first)(lambda: held.wait())
        self.s["stage"][slot] = value.astype(jnp.bfloat16)
        make(slot, t).start()

    def put_all(self):
        for slot in range(2):
            if self.pending[slot] is not None:
                self.pending[slot].wait()
            self.pending[slot] = None

    def prepare(self, seg_col, seg_row):
        s, width = self.s, self.width
        s["bias"][...] = jnp.where(seg_col[...] == seg_row[...], 0.0, -1e30)
        s["rows"][0:1, 0:width] = self.par[4:5, :]
        s["rows"][0:1, width : 2 * width] = jnp.zeros((1, width), jnp.float32)
        s["rows"][0:1, 2 * width :] = self.par[5:6, :]

    def norm_parts(self, values):
        center = values - jnp.mean(values, axis=-1, keepdims=True)
        scale = lax.rsqrt(jnp.mean(center * center, axis=-1, keepdims=True) + 1e-05)
        return center * scale, scale

    def norm(self, src, dst, which):
        def body(rows):
            unit, _ = self.norm_parts(src[rows, :].astype(jnp.float32))
            dst[rows, :] = (unit * self.row(self.par, which) + self.row(self.par, 2 + which)).astype(jnp.bfloat16)

        self.chunks(body)

    def norm_a(self):
        self.norm(self.s["x"], self.s["a"], 0)

    def project(self):
        s = self.s
        queries = self.width // TILE

        def body(t):
            scale = jnp.where(t < queries, HEAD ** (-0.5), 1.0)
            found = dot(s["a"][...], flat(self.w_qkv[:, :, :, :, at(t)])) + s["rows"][0:1, at(t)]
            s["qkv"][:, at(t)] = (found * scale).astype(jnp.bfloat16)

        self.tiles(0, 3 * queries, body)
        s["a_t"][...] = s["a"][...].T

    def pair(self, i, which):
        start = which * self.width + i * 128
        return self.s["qkv"].at[:, pl.ds(pl.multiple_of(start, 128), 128)]

    def own_lanes(self, value, head):
        lanes = lax.broadcasted_iota(jnp.int32, value.shape, 1)
        return jnp.where((lanes < HEAD) == (head == 0), value, jnp.zeros_like(value))

    def attend(self, first, last):
        s = self.s

        def body(i):
            q, k, v = (self.pair(i, which) for which in range(3))
            keys = [self.own_lanes(k[...], head) for head in range(2)]
            vals = [self.own_lanes(v[...], head) for head in range(2)]
            for part in range(self.n // TILE):
                cols = slice(part * TILE, part * TILE + TILE)
                mixed = None
                for head in range(2):
                    scores = dot(keys[head], q[cols, :], NT) + s["bias"][:, cols]
                    raised = jnp.exp(scores - jnp.max(scores, axis=0, keepdims=True))
                    share = 1.0 / jnp.sum(raised, axis=0, keepdims=True)
                    weights = (raised * share).astype(jnp.bfloat16)
                    s["wt"][2 * i + head, :, cols] = weights
                    found = dot(vals[head], weights, TN)
                    mixed = found if mixed is None else mixed + found
                s["o"][cols, at(i, 128)] = mixed.T.astype(jnp.bfloat16)

        self.tiles(first, last, body)

    def branch(self):
        s = self.s

        def body(t):
            found = dot(s["o"][...], flat(self.w_out[:, :, :, :, at(t)])) + self.par[6:7, at(t)]
            s["h"][:, at(t)] = s["x"][:, at(t)].astype(jnp.float32) + found

        self.tiles(0, self.width // TILE, body)
        s["o_t"][...] = s["o"][...].T

    def norm_c(self):
        self.norm(self.s["h"], self.s["c"], 1)

    def up(self, first, last):
        s = self.s

        def body(t):
            before = dot(s["c"][...], flat(self.w_up[:, :, :, :, at(t)])) + self.b_up[0:1, at(t)]
            chance = 0.5 + 0.5 * lax.erf(before * 0.7071067811865476)
            s["g"][:, at(t)] = (before * chance).astype(jnp.bfloat16)
            slope = chance + before * (jnp.exp(before * before * -0.5) * 0.3989422804014327)
            s["du"][:, at(t)] = slope.astype(jnp.bfloat16)

        self.tiles(first, last, body)

    def turn_c(self):
        self.s["c_t"][...] = self.s["c"][...].T

    def down(self):
        s = self.s

        def body(t):
            found = dot(s["g"][...], flat(self.w_down[:, :, :, :, :, at(t)])) + self.par[7:8, at(t)]
            s["a"][:, at(t)] = (s["h"][:, at(t)] + found).astype(jnp.bfloat16)

        self.tiles(0, self.width // TILE, body)

    def feed_back(self, first, last):
        s, width = self.s, self.width
        wide, tall = functools.partial(self.wide_copy, self.g_down), functools.partial(self.tall_copy, self.g_up)

        def body(t):
            cols = at(t, width)
            grad = dot(s["dy"][...], flat(self.w_down[t]), NT)
            low = (grad * s["du"][:, cols].astype(jnp.float32)).astype(jnp.bfloat16)
            s["du"][:, cols] = low
            self.g_bup[0:1, cols] = jnp.sum(low.astype(jnp.float32), axis=0, keepdims=True)
            self.put(wide, 0, t, first, dot(s["g"][:, cols], s["dy"][...], TN))
            self.put(tall, 1, t, first, dot(s["c_t"][...], low))

        self.tiles(first, last, body)
        self.pending = [wide(0, last - 1), tall(1, last - 1)]

    def up_back(self):
        self.s["sums"][...] = dot(self.s["du"][...], flat(self.w_up[...]), NT)

    def norm_back(self, src, which, grad, rest, body_out):
        def body(rows):
            unit, scale = self.norm_parts(src[rows, :].astype(jnp.float32))
            came = grad[rows, :]
            gained = came * self.row(self.par, which)
            self.g_par[which : which + 1, :] += jnp.sum(came * unit, axis=0, keepdims=True)
            self.g_par[2 + which : 3 + which, :] += jnp.sum(came, axis=0, keepdims=True)
            inner = gained - jnp.mean(gained, axis=-1, keepdims=True)
            inner = inner - unit * jnp.mean(gained * unit, axis=-1, keepdims=True)
            body_out(rows, rest[rows, :].astype(jnp.float32) + inner * scale)

        self.chunks(body)

    def norm_c_back(self):
        s = self.s

        def keep(rows, grad):
            s["dh"][rows, :] = grad
            low = grad.astype(jnp.bfloat16)
            s["c"][rows, :] = low
            self.g_par[6:7, :] += jnp.sum(low.astype(jnp.float32), axis=0, keepdims=True)
            self.g_par[7:8, :] += jnp.sum(s["dy"][rows, :].astype(jnp.float32), axis=0, keepdims=True)

        self.norm_back(s["h"], 1, s["sums"], s["dy"], keep)

    def branch_back(self):
        s = self.s
        tall = functools.partial(self.tall_copy, self.g_out)
        self.put(tall, 0, 0, 0, dot(s["o_t"][...], s["c"][...]))
        self.pending[0] = tall(0, 0)
        s["a"][...] = dot(s["c"][...], flat(self.w_out[...]), NT).astype(jnp.bfloat16)

    def attend_back(self, first, last):
        s, width = self.s, self.width

        def body(i):
            q, k, v = (self.pair(i, which) for which in range(3))
            came = s["a"].at[:, at(i, 128)]
            dq = dk = dv = None
            for head in range(2):
                vals = self.own_lanes(v[...], head)
                for part in range(self.n // TILE):
                    cols = slice(part * TILE, part * TILE + TILE)
                    grad = dot(vals, came[cols, :], NT)
                    weights = s["wt"][2 * i + head, :, cols].astype(jnp.float32)
                    product = weights * grad
                    inner = jnp.sum(product, axis=0, keepdims=True)
                    s["ds"][head, :, cols] = (product - weights * inner).astype(jnp.bfloat16)
                one_q = dot(self.own_lanes(k[...], head), s["ds"][head], TN)
                one_k = dot(s["ds"][head], self.own_lanes(q[...], head))
                one_v = dot(s["wt"][2 * i + head], self.own_lanes(came[...], head))
                dq, dk, dv = (one_q, one_k, one_v) if head == 0 else (dq + one_q, dk + one_k, dv + one_v)
            s["g"][:, at(i, 128)] = dq.T.astype(jnp.bfloat16) * HEAD ** (-0.5)
            s["g"][:, pl.ds(pl.multiple_of(width + i * 128, 128), 128)] = dk.astype(jnp.bfloat16)
            s["g"][:, pl.ds(pl.multiple_of(2 * width + i * 128, 128), 128)] = dv.astype(jnp.bfloat16)

        self.tiles(first, last, body)

    def project_terms(self, first, last):
        s, width = self.s, self.width
        tall = functools.partial(self.tall_copy, self.g_qkv)
        for t in range(first, last):
            grad = s["g"][:, t * width : (t + 1) * width]
            if t != 1:
                row = 4 + t // 2
                self.g_par[row : row + 1, :] = jnp.sum(grad.astype(jnp.float32), axis=0, keepdims=True)
            slot = (t + 1) % 2
            self.put(tall, slot, t, t, dot(s["a_t"][...], grad))
            self.pending[slot] = tall(slot, t)

    def project_back(self):
        s = self.s
        s["sums"][...] = dot(s["g"][:, 0 : 3 * self.width], flat(self.w_qkv[...]), NT)

    def norm_a_back(self):
        s = self.s

        def keep(rows, grad):
            s["dh"][rows, :] = grad

        self.norm_back(s["x"], 0, s["sums"], s["dh"], keep)


def layer_scratch(n, width, deep):
    low, full = jnp.bfloat16, jnp.float32
    return dict(
        a=pltpu.VMEM((n, width), low),
        a_t=pltpu.VMEM((width, n), low),
        qkv=pltpu.VMEM((n, 3 * width), low),
        bias=pltpu.VMEM((n, n), full),
        wt=pltpu.VMEM((width // HEAD, n, n), low),
        ds=pltpu.VMEM((2, n, n), low),
        o=pltpu.VMEM((n, width), low),
        o_t=pltpu.VMEM((width, n), low),
        h=pltpu.VMEM((n, width), full),
        c=pltpu.VMEM((n, width), low),
        c_t=pltpu.VMEM((width, n), low),
        g=pltpu.VMEM((n, deep), low),
        du=pltpu.VMEM((n, deep), low),
        sums=pltpu.VMEM((n, width), full),
        dh=pltpu.VMEM((n, width), full),
        rows=pltpu.VMEM((8, 3 * width), full),
        stage=pltpu.VMEM((2, width, width), low),
        stage_sem=pltpu.SemaphoreType.DMA((2,)),
    )


def cut(kept, n):
    cuts = dict(kept)
    for name in ("a", "qkv", "o", "h", "c", "g", "du", "sums", "dh"):
        cuts[name] = kept[name].at[0:n]
    for name in ("a_t", "o_t", "c_t"):
        cuts[name] = kept[name].at[:, 0:n]
    cuts["bias"] = kept["bias"].at[0:n, 0:n]
    for name in ("wt", "ds"):
        cuts[name] = kept[name].at[:, 0:n, 0:n]
    return cuts


ORDER = (0, 1, 2, 3)
BACK = (3, 2, 1, 0)


class SmallSum:
    def __init__(self, place, parts, land, line_land, out, send, recv):
        self.place, self.parts, self.land, self.line_land, self.out = place, parts, land, line_land, out
        self.send, self.recv = send, recv

    def near(self, step):
        p = self.place
        device = (p.core, p.xway, p.yway)[step]
        return remote(self.parts.at[step], self.land.at[step], self.send.at[step], self.recv.at[step], device)

    def far(self, step):
        p = self.place
        other = lax.rem(p.z + step, p.line)
        device = (p.dp, other * 2 + p.y)
        src = self.parts.at[3]
        return remote(src, self.line_land.at[p.z], self.send.at[3 + other], self.recv.at[3 + p.z], device)

    def from_far(self, step):
        p = self.place
        other = lax.rem(p.z + step, p.line)
        device = (p.dp, other * 2 + p.y)
        src = self.parts.at[3]
        return remote(src, self.line_land.at[other], self.send.at[3 + other], self.recv.at[3 + other], device)

    def stage(self, step):
        p = self.place
        if step:
            if step <= 3:
                self.near(step - 1).wait_recv()
                self.parts[step] = self.parts[step - 1] + self.land[step - 1]
        if step < 3:
            self.near(step).start()
        if step == 3:
            for other in range(1, p.line):
                self.far(other).start()
            self.line_land[p.z] = self.parts[3]
        if step == 4:
            for other in range(1, p.line):
                self.from_far(other).wait_recv()
            total = self.line_land[0]
            for block in range(1, p.line):
                total = total + self.line_land[block]
            self.out[...] = total
            for near in range(3):
                self.near(near).wait_send()
            for other in range(1, p.line):
                self.far(other).wait_send()


def whole_kernel(line, sizes, names, ring_names, splits, *refs):
    take = list(refs)

    def some(count):
        found = take[:count]
        del take[:count]
        return found

    owned, (small,) = some(4), some(1)
    x_t, dy_t, col_t, row_t, x_i, dy_i, col_i, row_i = some(8)
    y_i, y_t, gx_i, gx_t = some(4)
    shares, (small_out,) = some(4), some(1)
    far_weights, terms_t, terms_i = some(4), some(4), some(4)
    weights = some(4)
    kept = dict(zip(names, some(len(names))))
    bufs = dict(zip(ring_names, some(len(ring_names))))
    pad_x, pad_dy, small_all, par, b_up, g_parts, g_land, g_line = some(8)
    ag_send, ag_recv, ag_near, rs_send, rs_recv, rs_near, credit = some(7)
    s_send, s_recv, g_send, g_recv, load_sem, io_sem = some(6)
    n_t, n_i, counts = sizes
    width = weights[1].shape[-1]
    place = Place(line)
    place.greet()

    first = panels_of(counts, width, ORDER)
    units = [
        Gather(u, place, owned[p.which].at[1], p, weights[p.which], u in splits, ag_send, ag_recv, ag_near)
        for u, p in enumerate(first)
    ]
    base = len(first)
    units += [
        Gather(base + u, place, owned[p.which].at[0], p, far_weights[p.which], base + u in splits, ag_send, ag_recv, ag_near)
        for u, p in enumerate(first)
    ]
    ag = Pump(units)
    back = panels_of(counts, width, BACK)
    sums = []
    for u, p in enumerate(back + back):
        layer = 1 if u < len(back) else 0
        terms = (terms_i, terms_t)[layer]
        sums.append(
            Reduce(u, 2 * len(back), place, p, terms[p.which], shares[p.which].at[layer], bufs, credit, rs_send, rs_recv, rs_near)
        )

    def before(unit, stage):
        last = len(sums[0].stages()) - 1
        if stage == 0:
            if unit >= RINGS["away"]:
                sums[unit - RINGS["away"]].free_away()
            if unit >= RINGS["own"]:
                sums[unit - RINGS["own"]].free_own()
        if stage == last and unit >= RINGS["total"]:
            sums[unit - RINGS["total"]].free_total()

    rs = Pump(sums, before)
    rs.ready = 0

    def both(count=1, more=1):
        for _ in range(max(count, more)):
            if count > 0:
                ag.pump(1)
            if more > 0:
                rs.pump(1)
            count, more = count - 1, more - 1

    smalls = []
    for step, other in enumerate(place.others()):
        smalls.append(
            remote(small, small_all.at[place.fs], s_send.at[step], s_recv.at[place.fs], (place.dp, other))
        )
        smalls[-1].start()
    ag.pump(1)
    small_all[place.fs] = small[...]
    g_parts[0] = jnp.zeros(g_parts.shape[1:], jnp.float32)
    ag.pump(1)
    for step, other in enumerate(place.others()):
        remote(small, small_all.at[other], s_send.at[step], s_recv.at[other], (place.dp, other)).wait_recv()
    piece, deep = width // (2 * line), b_up.shape[-1] // (2 * line)
    for layer in range(2):
        for block in range(2 * line):
            par[layer, :, block * piece : (block + 1) * piece] = small_all[block, layer, 0:8, 0:piece]
            for j in range(deep // 128):
                start = block * deep + j * 128
                b_up[layer, 0:1, start : start + 128] = small_all[block, layer, 8 + j : 9 + j, :]
    for copy in smalls:
        copy.wait_send()

    def layer_of(layer, n, view, terms):
        return Layer(n, view, weights, par.at[layer], b_up.at[layer], terms, g_parts.at[0, layer, 0:8], g_bup.at[layer])

    g_bup = b_up.at[2:4]
    starts = [sum(counts[:which]) for which in range(5)]

    text = layer_of(1, n_t, {**kept, "x": x_t.at[0], "dy": dy_t.at[0]}, terms_t)
    text.prepare(col_t, row_t)
    text.norm_a()

    def need(unit):
        ag.done_with(unit)
        units[unit].arrive()

    for unit in range(starts[0], starts[1]):
        need(unit)
    text.project()
    heads = width // 128
    for i in range(0, heads, 2):
        text.attend(i, i + 2)
        ag.pump(1)
    need(starts[1])
    text.branch()
    ag.pump(1)
    text.norm_c()
    tiles = width // TILE
    for part in range(counts[2]):
        need(starts[2] + part)
        text.up(part * tiles, (part + 1) * tiles)
    text.turn_c()
    for part in range(counts[3]):
        need(starts[3] + part)
    text.down()
    y_copy = pltpu.make_async_copy(kept["a"], y_t.at[0], io_sem.at[0])
    y_copy.start()
    ag.pump(1)
    panels = counts[3]
    text.feed_back(0, panels // 2)
    ag.pump(2)
    text.feed_back(panels // 2, panels)
    text.put_all()
    rs.ready = counts[3] + counts[2]
    both()
    text.up_back()
    both()
    text.norm_c_back()
    both()
    y_copy.wait()
    text.branch_back()
    text.put_all()
    rs.ready += 1
    both()
    for i in range(0, heads, 2):
        text.attend_back(i, i + 2)
        both()
    text.project_terms(0, 3)
    text.put_all()
    rs.ready += 3
    both()
    text.project_back()
    both()
    text.norm_a_back()
    grad_copy = pltpu.make_async_copy(kept["dh"], gx_t.at[0], io_sem.at[1])
    grad_copy.start()

    for src, dst in ((x_i, pad_x), (dy_i, pad_dy)):
        have = src.shape[1]
        if have < n_i:
            cut_at = have // 16 * 16
            dst[cut_at:, :] = jnp.zeros((n_i - cut_at, width), jnp.bfloat16)
        dst[0:have, :] = src[0]
    view = {**cut(kept, n_i), "x": pad_x, "dy": pad_dy}
    image = layer_of(0, n_i, view, terms_i)
    image.prepare(col_i, row_i)
    image.norm_a()
    loads = [pltpu.make_async_copy(far_weights[i], weights[i], load_sem.at[i]) for i in range(4)]
    for which in range(4):
        for unit in range(starts[which], starts[which + 1]):
            need(base + unit)
            units[unit].drain()
        loads[which].start()
    loads[0].wait()
    image.project()
    rs.pump(1)
    image.attend(0, heads)
    rs.pump(1)
    loads[1].wait()
    image.branch()
    image.norm_c()
    rs.pump(1)
    loads[2].wait()
    image.up(0, counts[2] * tiles)
    rs.pump(1)
    image.turn_c()
    loads[3].wait()
    image.down()
    y_i[0] = view["a"][0 : y_i.shape[1], :]
    rs.pump(1)
    image.feed_back(0, panels)
    image.put_all()
    rs.ready += counts[3] + counts[2]
    rs.pump(1)
    image.up_back()
    rs.pump(1)
    grad_copy.wait()
    image.norm_c_back()
    rs.pump(1)
    image.branch_back()
    image.put_all()
    rs.ready += 1
    rs.pump(1)
    image.attend_back(0, heads)
    rs.pump(1)
    image.project_terms(0, 3)
    image.put_all()
    rs.ready += 3
    rs.pump(1)
    image.project_back()
    rs.pump(1)
    image.norm_a_back()
    gx_i[0] = view["dh"][0 : gx_i.shape[1], :]
    for layer in range(2):
        for j in range(b_up.shape[-1] // width):
            g_parts[0, layer, 8 + j : 9 + j, :] = g_bup[layer, 0:1, j * width : (j + 1) * width]
    small_sum = SmallSum(place, g_parts, g_land, g_line, small_out, g_send, g_recv)
    for step in range(5):
        small_sum.stage(step)
        rs.pump(1)
    rs.pump(rs.left())
    total = len(sums)
    for unit in sums[total - RINGS["away"] :]:
        unit.free_away()
    for unit in sums[total - RINGS["own"] :]:
        unit.free_own()
    for unit in sums[total - RINGS["total"] :]:
        unit.free_total()
    for unit in sums:
        unit.out_landed().wait_recv()
    for unit in units[base:]:
        unit.drain()


def padded(rows):
    return -(-rows // TILE) * TILE


def whole(line, x_i, dy_i, x_t, dy_t, seg_i, seg_t, owned, small):
    width, deep = owned[1].shape[2], owned[2].shape[2]
    rows = owned[1].shape[1] // 2
    counts = (3, 1, deep // width, deep // width)
    own = [w.reshape(2, 2, rows, w.shape[2]) for w in owned[:3]] + [owned[3].reshape(2, 2, counts[3], rows, width)]
    n_t, n_i = padded(x_t.shape[1]), padded(x_i.shape[1])
    low, full = jnp.bfloat16, jnp.float32
    kept = layer_scratch(n_t, width, deep)
    pads = lambda seg, n: jnp.pad(seg, ((0, 0), (0, n - seg.shape[1])), constant_values=-1)
    seg_t, seg_i = pads(seg_t, n_t), pads(seg_i, n_i)
    fulls = [(line, 2, *w.shape[1:]) for w in own]
    rings = dict(
        own=pltpu.VMEM((RINGS["own"], line, rows, width), low),
        away=pltpu.VMEM((RINGS["away"], line, rows, width), low),
        other=pltpu.VMEM((RINGS["other"], line, 2, rows, width), low),
        from_x=pltpu.VMEM((RINGS["from_x"], line, rows, width // 2), low),
        from_y=pltpu.VMEM((RINGS["from_y"], line, rows, width // 2), low),
        line_in=pltpu.VMEM((RINGS["line_in"], 2 * line - 2, rows, width), low),
        last=pltpu.VMEM((RINGS["last"], rows, width), low),
        total=pltpu.VMEM((RINGS["total"], rows, width), full),
    )
    panels = 2 * sum(counts)
    splits = ()
    small_rows = 8 + deep // width
    small_rows += -small_rows % 8
    anywhere, inside = pl.BlockSpec(memory_space=pl.ANY), pl.BlockSpec(memory_space=pltpu.VMEM)
    dma = pltpu.SemaphoreType.DMA
    outs = [
        jax.ShapeDtypeStruct(x_i.shape, low),
        jax.ShapeDtypeStruct(x_t.shape, low),
        jax.ShapeDtypeStruct(x_i.shape, full),
        jax.ShapeDtypeStruct(x_t.shape, full),
        *[jax.ShapeDtypeStruct(w.shape, full) for w in own],
        jax.ShapeDtypeStruct((2, small_rows, width), full),
        *[jax.ShapeDtypeStruct(shape, low) for shape in fulls * 3],
    ]
    scratch = [
        *[pltpu.VMEM(shape, low) for shape in fulls],
        *kept.values(),
        *rings.values(),
        pltpu.VMEM((n_i, width), low),
        pltpu.VMEM((n_i, width), low),
        pltpu.VMEM((2 * line, *small.shape), full),
        pltpu.VMEM((2, 8, width), full),
        pltpu.VMEM((4, 1, deep), full),
        pltpu.VMEM((4, 2, small_rows, width), full),
        pltpu.VMEM((3, 2, small_rows, width), full),
        pltpu.VMEM((line, 2, small_rows, width), full),
        dma((panels, 2 * line + 5)),
        dma((panels, line + 5)),
        dma((panels,)),
        dma((panels, 5 + 2 * line)),
        dma((panels, 5 + 2 * line)),
        dma((panels, 3)),
        pltpu.SemaphoreType.REGULAR((len(CREDITS),)),
        dma((2 * line,)),
        dma((2 * line,)),
        dma((3 + line,)),
        dma((3 + line,)),
        dma((4,)),
        dma((2,)),
    ]
    found = pl.pallas_call(
        functools.partial(whole_kernel, line, (n_t, n_i, counts), list(kept), list(rings), splits),
        out_shape=outs,
        in_specs=[anywhere] * 4 + [inside] * 9,
        out_specs=[inside, anywhere, inside, anywhere] + [anywhere] * 4 + [inside] + [anywhere] * 12,
        scratch_shapes=scratch,
        compiler_params=pltpu.CompilerParams(collective_id=0, has_side_effects=True, vmem_limit_bytes=63 * 2**20),
    )(*own, small, x_t, dy_t, seg_t.reshape(n_t, 1), seg_t, x_i, dy_i, seg_i.reshape(n_i, 1), seg_i)
    shares = [share.reshape(w.shape) for share, w in zip(found[4:8], owned)]
    return found[:4], shares, found[8]


def normed(values, gain, shift):
    center = values - jnp.mean(values, axis=-1, keepdims=True)
    spread = jnp.mean(center * center, axis=-1, keepdims=True)
    return center * lax.rsqrt(spread + 1e-05) * gain + shift


def gelu_exact(values):
    return jax.nn.gelu(values, approximate=False)


def segment_ids(lengths, seq_len):
    bounds = jnp.cumsum(lengths, axis=-1)
    positions = jnp.arange(seq_len, dtype=jnp.int32)
    return jnp.sum((positions[None, :, None] >= bounds[:, None, :]).astype(jnp.int32), axis=-1)


def split_heads(values):
    batch, length, width = values.shape
    return values.reshape(batch, length, width // HEAD, HEAD)


def masked_scores(queries, keys_all, segment):
    scores = jnp.einsum(
        "bqhd,bkhd->bhqk",
        split_heads(queries),
        split_heads(keys_all),
        preferred_element_type=jnp.float32,
    )
    same = (segment[:, :, None] == segment[:, None, :])[:, None]
    return (jnp.where(same, scores, -1e30), same)


def attention(queries, keys_all, values_all, segment):
    scores, same = masked_scores(queries, keys_all, segment)
    largest = jnp.max(scores, axis=-1, keepdims=True)
    raised = jnp.exp(scores - largest)
    totals = jnp.sum(raised, axis=-1, keepdims=True)
    attn_weights = raised / totals
    log_total = largest + jnp.log(totals)
    mixed = jnp.einsum(
        "bhqk,bkhd->bqhd",
        attn_weights.astype(jnp.bfloat16),
        split_heads(values_all),
        preferred_element_type=jnp.float32,
    )
    return (mixed.reshape(queries.shape).astype(jnp.bfloat16), log_total)


def attention_back(queries, keys_all, values_all, segment, log_total, grad_mixed):
    scores, same = masked_scores(queries, keys_all, segment)
    attn_weights = jnp.where(same, jnp.exp(scores - log_total), 0.0)
    grad_heads = split_heads(grad_mixed)
    grad_weights = jnp.einsum(
        "bqhd,bkhd->bhqk", grad_heads, split_heads(values_all), preferred_element_type=jnp.float32
    )
    inner = jnp.sum(attn_weights * grad_weights, axis=-1, keepdims=True)
    grad_scores = (attn_weights * (grad_weights - inner)).astype(jnp.bfloat16)
    grad_queries = jnp.einsum(
        "bhqk,bkhd->bqhd", grad_scores, split_heads(keys_all), preferred_element_type=jnp.float32
    )
    grad_keys = jnp.einsum(
        "bhqk,bqhd->bkhd", grad_scores, split_heads(queries), preferred_element_type=jnp.float32
    )
    grad_values = jnp.einsum(
        "bhqk,bqhd->bkhd",
        attn_weights.astype(jnp.bfloat16),
        grad_heads,
        preferred_element_type=jnp.float32,
    )
    shape_rows = queries.shape
    return (
        grad_queries.reshape(shape_rows),
        grad_keys.reshape(shape_rows),
        grad_values.reshape(shape_rows),
    )


def forward_layer(inputs, weights, segment):
    qkv_weight, out_weight, up_weight, down_weight, gains, biases, up_bias = weights
    width = inputs.shape[-1]
    source = inputs.astype(jnp.float32)
    normed_a = normed(source, gains[0], biases[0]).astype(jnp.bfloat16)
    project = jnp.einsum("bld,de->ble", normed_a, qkv_weight, preferred_element_type=jnp.float32)
    queries = ((project[..., :width] + biases[2]) * HEAD ** (-0.5)).astype(jnp.bfloat16)
    keys_all = project[..., width : 2 * width].astype(jnp.bfloat16)
    values_all = (project[..., 2 * width :] + biases[3]).astype(jnp.bfloat16)
    mixed, log_total = attention(queries, keys_all, values_all, segment)
    hidden = (
        source
        + jnp.einsum("bld,de->ble", mixed, out_weight, preferred_element_type=jnp.float32)
        + biases[4]
    )
    normed_c = normed(hidden, gains[1], biases[1]).astype(jnp.bfloat16)
    before = (
        jnp.einsum("bld,df->blf", normed_c, up_weight, preferred_element_type=jnp.float32) + up_bias
    )
    activated = gelu_exact(before).astype(jnp.bfloat16)
    result = (
        hidden
        + jnp.einsum("blf,fd->bld", activated, down_weight, preferred_element_type=jnp.float32)
        + biases[5]
    )
    return (
        source,
        normed_a,
        queries,
        keys_all,
        values_all,
        log_total,
        mixed,
        hidden,
        normed_c,
        before,
        activated,
        result,
    )


def backward_layer(inputs, cotangent, weights, segment):
    qkv_weight, out_weight, up_weight, down_weight, gains, biases, up_bias = weights
    width = inputs.shape[-1]
    (
        source,
        normed_a,
        queries,
        keys_all,
        values_all,
        log_total,
        mixed,
        hidden,
        normed_c,
        before,
        activated,
        result,
    ) = forward_layer(inputs, weights, segment)
    grad_result = cotangent.astype(jnp.float32)
    grad_downw = jnp.einsum("blf,bld->fd", activated, cotangent, preferred_element_type=jnp.float32)
    grad_act = jnp.einsum("bld,fd->blf", cotangent, down_weight, preferred_element_type=jnp.float32)
    grad_before = jax.vjp(gelu_exact, before)[1](grad_act)[0].astype(jnp.bfloat16)
    grad_upw = jnp.einsum("bld,blf->df", normed_c, grad_before, preferred_element_type=jnp.float32)
    grad_upb = jnp.sum(grad_before.astype(jnp.float32), axis=(0, 1))
    grad_normc = jnp.einsum(
        "blf,df->bld", grad_before, up_weight, preferred_element_type=jnp.float32
    )
    hidden_back = jax.vjp(
        normed, hidden, gains[1].astype(jnp.float32), biases[1].astype(jnp.float32)
    )[1]
    grad_hidden_ln, grad_gain_two, grad_shift_two = hidden_back(grad_normc)
    grad_hidden = grad_result + grad_hidden_ln
    grad_branch = grad_hidden.astype(jnp.bfloat16)
    grad_outw = jnp.einsum("bld,ble->de", mixed, grad_branch, preferred_element_type=jnp.float32)
    grad_mixed = jnp.einsum(
        "ble,de->bld", grad_branch, out_weight, preferred_element_type=jnp.float32
    ).astype(jnp.bfloat16)
    grad_queries, grad_keys, grad_values = attention_back(
        queries, keys_all, values_all, segment, log_total, grad_mixed
    )
    grad_project = jnp.concatenate(
        [
            grad_queries.astype(jnp.bfloat16) * HEAD ** (-0.5),
            grad_keys.astype(jnp.bfloat16),
            grad_values.astype(jnp.bfloat16),
        ],
        axis=-1,
    )
    grad_qkvw = jnp.einsum(
        "bld,ble->de", normed_a, grad_project, preferred_element_type=jnp.float32
    )
    column_sums = jnp.sum(grad_project.astype(jnp.float32), axis=(0, 1))
    grad_norma = jnp.einsum(
        "ble,de->bld", grad_project, qkv_weight, preferred_element_type=jnp.float32
    )
    source_back = jax.vjp(
        normed, source, gains[0].astype(jnp.float32), biases[0].astype(jnp.float32)
    )[1]
    grad_source_ln, grad_gain_one, grad_shift_one = source_back(grad_norma)
    grad_inputs = grad_hidden + grad_source_ln
    grad_gains = jnp.stack([grad_gain_one, grad_gain_two])
    grad_biases = jnp.stack(
        [
            grad_shift_one,
            grad_shift_two,
            column_sums[:width],
            column_sums[2 * width :],
            jnp.sum(grad_branch.astype(jnp.float32), axis=(0, 1)),
            jnp.sum(grad_result, axis=(0, 1)),
        ]
    )
    return (
        result.astype(jnp.bfloat16),
        grad_inputs,
        (grad_qkvw, grad_outw, grad_upw, grad_downw, grad_gains, grad_biases, grad_upb),
    )


def fetch_weights(layer_index, w_qkv, w_out, w_up, w_down, gains, biases, b_up):
    return (
        lax.all_gather(w_qkv[layer_index], "fsdp", axis=0, tiled=True),
        lax.all_gather(w_out[layer_index], "fsdp", axis=0, tiled=True),
        lax.all_gather(w_up[layer_index], "fsdp", axis=0, tiled=True),
        lax.all_gather(w_down[layer_index], "fsdp", axis=0, tiled=True),
        lax.all_gather(gains[layer_index], "fsdp", axis=1, tiled=True),
        lax.all_gather(biases[layer_index], "fsdp", axis=1, tiled=True),
        lax.all_gather(b_up[layer_index], "fsdp", axis=0, tiled=True),
    )


def fetch_again(layer_index, w_qkv, w_out, w_up, w_down, gains, biases, b_up):
    return (
        lax.all_gather(w_qkv[layer_index], "fsdp", axis=0, tiled=True),
        lax.all_gather(w_out[layer_index], "fsdp", axis=0, tiled=True),
        lax.all_gather(w_up[layer_index], "fsdp", axis=0, tiled=True),
        lax.all_gather(w_down[layer_index], "fsdp", axis=0, tiled=True),
        lax.all_gather(gains[layer_index], "fsdp", axis=1, tiled=True),
        lax.all_gather(biases[layer_index], "fsdp", axis=1, tiled=True),
        lax.all_gather(b_up[layer_index], "fsdp", axis=0, tiled=True),
    )


def reduce_grads(gradients):
    shares = (
        lax.psum_scatter(gradients[0], "fsdp", scatter_dimension=0, tiled=True),
        lax.psum_scatter(gradients[1], "fsdp", scatter_dimension=0, tiled=True),
        lax.psum_scatter(gradients[2], "fsdp", scatter_dimension=0, tiled=True),
        lax.psum_scatter(gradients[3], "fsdp", scatter_dimension=0, tiled=True),
        lax.psum_scatter(gradients[4], "fsdp", scatter_dimension=1, tiled=True),
        lax.psum_scatter(gradients[5], "fsdp", scatter_dimension=1, tiled=True),
        lax.psum_scatter(gradients[6], "fsdp", scatter_dimension=0, tiled=True),
    )
    quarters = (
        lax.psum_scatter(
            shares[0].astype(jnp.bfloat16), "dp", scatter_dimension=0, tiled=True
        ).astype(jnp.float32),
        lax.psum_scatter(
            shares[1].astype(jnp.bfloat16), "dp", scatter_dimension=0, tiled=True
        ).astype(jnp.float32),
        lax.psum_scatter(
            shares[2].astype(jnp.bfloat16), "dp", scatter_dimension=0, tiled=True
        ).astype(jnp.float32),
        lax.psum_scatter(
            shares[3].astype(jnp.bfloat16), "dp", scatter_dimension=0, tiled=True
        ).astype(jnp.float32),
        lax.psum_scatter(
            shares[4].astype(jnp.bfloat16), "dp", scatter_dimension=1, tiled=True
        ).astype(jnp.float32),
        lax.psum_scatter(
            shares[5].astype(jnp.bfloat16), "dp", scatter_dimension=1, tiled=True
        ).astype(jnp.float32),
        lax.psum_scatter(
            shares[6].astype(jnp.bfloat16), "dp", scatter_dimension=0, tiled=True
        ).astype(jnp.float32),
    )
    return (
        lax.all_gather(quarters[0].astype(jnp.bfloat16), "dp", axis=0, tiled=True).astype(
            jnp.float32
        ),
        lax.all_gather(quarters[1].astype(jnp.bfloat16), "dp", axis=0, tiled=True).astype(
            jnp.float32
        ),
        lax.all_gather(quarters[2].astype(jnp.bfloat16), "dp", axis=0, tiled=True).astype(
            jnp.float32
        ),
        lax.all_gather(quarters[3].astype(jnp.bfloat16), "dp", axis=0, tiled=True).astype(
            jnp.float32
        ),
        lax.all_gather(quarters[4].astype(jnp.bfloat16), "dp", axis=1, tiled=True).astype(
            jnp.float32
        ),
        lax.all_gather(quarters[5].astype(jnp.bfloat16), "dp", axis=1, tiled=True).astype(
            jnp.float32
        ),
        lax.all_gather(quarters[6].astype(jnp.bfloat16), "dp", axis=0, tiled=True).astype(
            jnp.float32
        ),
    )


def plain(
    images,
    image_cot,
    captions,
    caption_cot,
    lengths,
    w_qkv,
    w_out,
    w_up,
    w_down,
    gains,
    biases,
    b_up,
):
    owned = (w_qkv, w_out, w_up, w_down, gains, biases, b_up)
    image_seg = jnp.zeros((images.shape[0], images.shape[1]), jnp.int32)
    caption_seg = segment_ids(lengths, captions.shape[1])
    first_weights = fetch_weights(0, *owned)
    image_out = forward_layer(images, first_weights, image_seg)[-1].astype(jnp.bfloat16)
    second_weights = fetch_weights(1, *owned)
    caption_out = forward_layer(captions, second_weights, caption_seg)[-1].astype(jnp.bfloat16)
    second_back = fetch_again(1, *owned)
    _, caption_grad, caption_terms = backward_layer(captions, caption_cot, second_back, caption_seg)
    caption_shares = reduce_grads(caption_terms)
    first_back = fetch_again(0, *owned)
    _, image_grad, image_terms = backward_layer(images, image_cot, first_back, image_seg)
    image_shares = reduce_grads(image_terms)
    stacked = tuple((jnp.stack([image_shares[index], caption_shares[index]]) for index in range(7)))
    return (image_out, caption_out, image_grad, caption_grad) + stacked


def kernels_fit(mesh, w_qkv):
    return mesh.shape["dp"] == 4 and mesh.shape["fsdp"] % 2 == 0 and w_qkv.shape[1] % 32 == 0


def local(mesh, images, image_cot, captions, caption_cot, lengths, w_qkv, w_out, w_up, w_down, gains, biases, b_up):
    if not kernels_fit(mesh, w_qkv):
        return plain(
            images, image_cot, captions, caption_cot, lengths, w_qkv, w_out, w_up, w_down, gains, biases, b_up
        )
    line, width = mesh.shape["fsdp"] // 2, gains.shape[2]
    deep = b_up.shape[1]
    par = jnp.concatenate([gains, biases], axis=1)
    par = jnp.pad(par, ((0, 0), (0, 0), (0, -width % 128)))
    small = jnp.concatenate([par, b_up.reshape(2, deep // 128, 128)], axis=1).astype(jnp.float32)
    small = jnp.pad(small, ((0, 0), (0, -small.shape[1] % 8), (0, 0)))
    image_seg = jnp.zeros((images.shape[0], images.shape[1]), jnp.int32)
    caption_seg = segment_ids(lengths, captions.shape[1])
    outs, shares, sums = whole(
        line, images, image_cot, captions, caption_cot, image_seg, caption_seg, (w_qkv, w_out, w_up, w_down), small
    )
    place = lax.axis_index("fsdp")
    mine = lax.dynamic_slice_in_dim(sums[:, :8], place * width, width, 2)
    up = sums[:, 8 : 8 + deep * 2 * line // w_out.shape[2]].reshape(2, -1)
    up = lax.dynamic_slice_in_dim(up, place * deep, deep, 1)
    return (*outs, *shares, mine[:, :2], mine[:, 2:], up)


def solution(mesh):
    placed = (
        P(("dp", "fsdp"), None, None),
        P(("dp", "fsdp"), None, None),
        P(("dp", "fsdp"), None, None),
        P(("dp", "fsdp"), None, None),
        P(("dp", "fsdp"), None),
        P(None, "fsdp", None),
        P(None, "fsdp", None),
        P(None, "fsdp", None),
        P(None, "fsdp", None),
        P(None, None, "fsdp"),
        P(None, None, "fsdp"),
        P(None, "fsdp"),
    )
    return jax.shard_map(
        functools.partial(local, mesh),
        mesh=mesh,
        in_specs=placed,
        out_specs=(
            P(("dp", "fsdp"), None, None),
            P(("dp", "fsdp"), None, None),
            P(("dp", "fsdp"), None, None),
            P(("dp", "fsdp"), None, None),
            P(None, "fsdp", None),
            P(None, "fsdp", None),
            P(None, "fsdp", None),
            P(None, "fsdp", None),
            P(None, None, "fsdp"),
            P(None, None, "fsdp"),
            P(None, "fsdp"),
        ),
        check_vma=False,
    )
```

```python
import functools

import jax
import jax.numpy as jnp
from jax import lax
from jax.experimental import pallas as pl
from jax.experimental.pallas import tpu as pltpu
from jax.sharding import PartitionSpec as P

HEAD = 64

MESH = pl.DeviceIdType.MESH
NT = (((1,), (1,)), ((), ()))
TN = (((0,), (0,)), ((), ()))
TILE = 256
CHUNK = 64
ALL = slice(None)


def dot(a, b, dims=(((1,), (0,)), ((), ()))):
    return lax.dot_general(a, b, dims, preferred_element_type=jnp.float32)


def flat(value):
    return value.reshape(-1, value.shape[-1])


def at(t, size=TILE):
    return pl.ds(pl.multiple_of(t * size, size), size)


def remote(src, dst, send, recv, device):
    return pltpu.make_async_remote_copy(
        src_ref=src, dst_ref=dst, send_sem=send, recv_sem=recv, device_id=device, device_id_type=MESH
    )


class Place:
    def __init__(self, line):
        dp, fs = lax.axis_index("dp"), lax.axis_index("fsdp")
        self.line, self.dp, self.fs = line, dp, fs
        self.x, self.c = dp // 2, dp % 2
        self.z, self.y = fs // 2, fs % 2
        self.up, self.down = (dp, fs + 2), (dp, fs - 2)
        self.yway = (dp, self.z * 2 + 1 - self.y)
        self.xway = ((1 - self.x) * 2 + self.c, fs)
        self.core = (self.x * 2 + 1 - self.c, fs)
        self.has_up, self.has_down = self.z + 1 < line, self.z > 0

    def others(self):
        return [lax.rem(self.fs + step, 2 * self.line) for step in range(1, 2 * self.line)]

    def greet(self):
        barrier = pltpu.get_barrier_semaphore()
        known = [(self.dp, other) for other in self.others()] + [self.xway, self.core]
        for device in known:
            pl.semaphore_signal(barrier, inc=1, device_id=device, device_id_type=MESH)
        pl.semaphore_wait(barrier, len(known))


class Panel:
    def __init__(self, which, part, width):
        self.which, self.part, self.width = which, part, width

    def cols(self, cut):
        base = 0 if self.which == 3 else self.part * self.width
        if cut is None:
            return pl.ds(base, self.width)
        return pl.ds(pl.multiple_of(base + cut[0], 128), cut[1])

    def of(self, ref, *lead, cut=None):
        if self.which == 3:
            return ref.at[(*lead, self.part, ALL, self.cols(cut))]
        return ref.at[(*lead, ALL, self.cols(cut))]


class Cuts:
    def __init__(self, width, x, thirds):
        third = width // 3
        self.half = (x * (width // 2), width // 2)
        self.other_half = ((1 - x) * (width // 2), width // 2)
        self.wide, self.outer, self.other_outer = self.half, self.half, self.other_half
        if thirds:
            self.wide = (x * third, 2 * third)
            self.outer = (x * 2 * third, third)
            self.other_outer = ((1 - x) * 2 * third, third)


def ds(cut):
    return pl.ds(pl.multiple_of(cut[0], 128), cut[1])


def panels_of(layer_shapes, width, order):
    made = []
    for which in order:
        count = layer_shapes[which]
        made += [Panel(which, part, width) for part in range(count)]
    return made


class Gather:
    def __init__(self, at, place, own, panel, full, way, send, recv, near):
        self.at, self.place, self.own, self.panel, self.full = at, place, own, panel, full
        self.send, self.recv, self.near = send, recv, near
        self.split, self.older = way == SPLIT, None
        split = self.split
        cuts = Cuts(panel.width, place.x, way == THIRDS)
        self.lane, self.other_lane = (cuts.half, cuts.other_half) if split else (None, None)
        self.over_y = cuts.half if split else cuts.wide
        self.over_x, self.from_x = (cuts.half, cuts.other_half) if split else (cuts.outer, cuts.other_outer)

    def view(self, block, y, c, cut=None):
        return self.panel.of(self.full, block, y, c, cut=cut)

    def sent(self, slot):
        return self.send.at[self.at % AG_RING, slot]

    def got(self, slot):
        return self.recv.at[self.at, slot]

    def line_copy(self, way, block):
        p = self.place
        ref = self.view(block, p.y, p.c, self.lane)
        return remote(ref, ref, self.sent(block + way), self.got(block), (p.up, p.down)[way])

    def near_copy(self):
        p = self.place
        mine = self.panel.of(self.own, p.c, cut=self.lane)
        return pltpu.make_async_copy(mine, self.view(p.z, p.y, p.c, self.lane), self.near.at[self.at % AG_RING])

    def far_copy(self, kind):
        p, line = self.place, self.place.line
        ref, device = {
            "y": (lambda: (self.view(ALL, p.y, p.c, self.over_y), p.yway)),
            "x": (lambda: (self.view(ALL, 1 - p.y, p.c, self.over_x), p.xway)),
            "x_own": (lambda: (self.view(ALL, p.y, p.c, self.lane), p.xway)),
            "core_own": (lambda: (self.view(ALL, p.y, p.c), p.core)),
            "core": (lambda: (self.view(ALL, 1 - p.y, p.c), p.core)),
        }[kind]()
        slot = ("y", "x", "x_own", "core_own", "core").index(kind)
        return remote(ref, ref, self.sent(line + 1 + slot), self.got(line + slot), device)

    def landed(self, kind):
        p, line = self.place, self.place.line
        ref = {
            "y": lambda: self.view(ALL, 1 - p.y, p.c, self.over_y),
            "x": lambda: self.view(ALL, 1 - p.y, p.c, self.from_x),
            "x_own": lambda: self.view(ALL, p.y, p.c, self.other_lane),
            "core_own": lambda: self.view(ALL, p.y, 1 - p.c),
            "core": lambda: self.view(ALL, 1 - p.y, 1 - p.c),
        }[kind]()
        slot = ("y", "x", "x_own", "core_own", "core").index(kind)
        return remote(ref, ref, self.sent(line + 1 + slot), self.got(line + slot), p.core)

    def kinds(self):
        return ("y", "x", "x_own", "core_own", "core") if self.split else ("y", "x", "core_own", "core")

    def first(self):
        p = self.place
        if self.older is not None:
            self.older.drain()
        self.near_copy().start()
        mine = self.panel.of(self.own, p.c, cut=self.lane)
        there = self.view(p.z, p.y, p.c, self.lane)
        for way, able, device in ((0, p.has_up, p.up), (1, p.has_down, p.down)):
            copy = functools.partial(remote, mine, there, self.sent(p.z + way), self.got(p.z), device)
            pl.when(able)(lambda copy=copy: copy().start())

    def hop(self, k):
        p = self.place

        def pass_on(way, block, more):
            self.line_copy(way, block).wait_recv()
            pl.when(more)(lambda: self.line_copy(way, block).start())

        pl.when(p.z - k >= 0)(lambda: pass_on(0, p.z - k, p.has_up))
        pl.when(p.z + k < p.line)(lambda: pass_on(1, p.z + k, p.has_down))
        if k == p.line - 1:
            self.near_copy().wait()
            self.far_copy("y").start()
            self.far_copy("x_own" if self.split else "core_own").start()

    def cross(self):
        self.landed("y").wait_recv()
        self.far_copy("x").start()
        if self.split:
            self.landed("x_own").wait_recv()
            self.far_copy("core_own").start()

    def share(self):
        self.landed("x").wait_recv()
        self.far_copy("core").start()

    def stages(self):
        hops = [functools.partial(self.hop, k) for k in range(1, self.place.line)]
        return [self.first, *hops, self.cross, self.share]

    def arrive(self):
        self.landed("core_own").wait_recv()
        self.landed("core").wait_recv()

    def drain(self):
        p = self.place

        def body(block, carry):
            pl.when(p.has_up & (block <= p.z))(lambda: self.line_copy(0, block).wait_send())
            pl.when(p.has_down & (block >= p.z))(lambda: self.line_copy(1, block).wait_send())
            return carry

        lax.fori_loop(0, p.line, body, 0)
        for kind in self.kinds():
            self.far_copy(kind).wait_send()


HALVES, THIRDS, SPLIT = range(3)
AG_RING = 12
RINGS = dict(own=11, away=5, other=2, from_x=3, from_y=3, line_in=4, last=3, total=3)
SUM_SEMS = dict(
    core=(RINGS["away"], 1, RINGS["other"], 1),
    x=(RINGS["away"], 1, RINGS["from_x"], 1),
    y=(RINGS["away"], 1, RINGS["from_y"], 1),
    line=(RINGS["own"], 4, RINGS["line_in"], 5),
    last=(RINGS["own"], 1, RINGS["last"], 1),
    out=(RINGS["total"], 1, 24, 1),
)


def starts_of(kinds):
    found, out_at, in_at = {}, 0, 0
    for name, (out_ring, out_each, in_ring, in_each) in kinds.items():
        found[name] = (out_at, in_at)
        out_at, in_at = out_at + out_ring * out_each, in_at + in_ring * in_each
    return found, out_at, in_at


SUM_STARTS, SUM_SENDS, SUM_ARRIVALS = starts_of(SUM_SEMS)
CREDITS = ("other", "from_x", "from_y", "line_up", "line_down", "last")


class Reduce:
    def __init__(self, at, count, place, panel, way, terms, out, bufs, credit, send, recv, near):
        self.at, self.count, self.place, self.panel, self.terms, self.out = at, count, place, panel, terms, out
        self.credit, self.send, self.recv, self.near = credit, send, recv, near
        self.older, self.flush = {}, None
        self.b = {name: ref.at[at % RINGS[name]] for name, ref in bufs.items()}
        cuts = Cuts(panel.width, place.x, way == THIRDS)
        self.wide, self.outer, self.other_outer = ds(cuts.wide), ds(cuts.outer), ds(cuts.other_outer)
        self.b["from_x"] = self.b["from_x"].at[:, :, 0 : cuts.outer[1]]
        self.b["from_y"] = self.b["from_y"].at[:, :, 0 : cuts.wide[1]]

    def spend(self, name, ring):
        if self.at >= RINGS[ring]:
            pl.semaphore_wait(self.credit.at[CREDITS.index(name)], 1)

    def grant(self, name, ring, device):
        if self.at + RINGS[ring] < self.count:
            pl.semaphore_signal(
                self.credit.at[CREDITS.index(name)], inc=1, device_id=device, device_id_type=MESH
            )

    def sems(self, name, slot=(0, 0)):
        out_ring, out_each, in_ring, in_each = SUM_SEMS[name]
        out_at, in_at = SUM_STARTS[name]
        out_at += self.at % out_ring * out_each + slot[0]
        in_at += self.at % in_ring * in_each + slot[1]
        return self.send.at[out_at], self.recv.at[in_at]

    def core_copy(self):
        p = self.place
        return remote(self.panel.of(self.terms, ALL, ALL, 1 - p.c), self.b["other"], *self.sems("core"), p.core)

    def near_copy(self, away):
        p = self.place
        src = self.panel.of(self.terms, ALL, (1 - p.y) if away else p.y, p.c)
        return pltpu.make_async_copy(src, self.b["away" if away else "own"], self.near.at[self.at % 2 * 2 + int(away)])

    def x_copy(self):
        p = self.place
        return remote(self.b["away"].at[:, :, self.other_outer], self.b["from_x"], *self.sems("x"), p.xway)

    def y_copy(self):
        p = self.place
        return remote(self.b["away"].at[:, :, self.wide], self.b["from_y"], *self.sems("y"), p.yway)

    def came(self, way, block):
        return self.b["line_in"].at[block - 1 if way == 0 else self.place.line - 1 + block]

    def line_copy(self, way, block):
        p = self.place
        sems = self.sems("line", (block, block + 1 - way))
        return remote(self.b["own"].at[block], self.came(way, block), *sems, (p.up, p.down)[way])

    def last_copy(self):
        p = self.place
        return remote(self.b["own"].at[p.z], self.b["last"], *self.sems("last"), p.xway)

    def out_copy(self):
        ref = self.panel.of(self.out, self.place.c)
        return remote(self.b["total"], ref, *self.sems("out"), self.place.core)

    def out_landed(self):
        ref = self.panel.of(self.out, 1 - self.place.c)
        return remote(self.b["total"], ref, *self.sems("out"), self.place.core)

    def out_near(self):
        return pltpu.make_async_copy(self.b["total"], self.panel.of(self.out, self.place.c), self.near.at[4 + self.at % RINGS["total"]])

    def each(self, body):
        def step(block, carry):
            body(block)
            return carry

        lax.fori_loop(0, self.place.line, step, 0)

    def start(self):
        if self.flush is not None:
            self.flush()
        if "away" in self.older:
            self.older["away"].free_away()
        if "own" in self.older:
            self.older["own"].free_own()
        self.spend("other", "other")
        self.core_copy().start()
        self.near_copy(False).start()
        self.near_copy(True).start()

    def add_core(self):
        p, b = self.place, self.b
        self.near_copy(False).wait()
        self.near_copy(True).wait()
        self.core_copy().wait_recv()

        def body(block):
            b["away"][block] = b["away"][block] + b["other"][block, 1 - p.y]

        self.each(body)
        self.spend("from_x", "from_x")
        self.x_copy().start()

        def rest(block):
            b["own"][block] = b["own"][block] + b["other"][block, p.y]

        self.each(rest)
        self.grant("other", "other", p.core)

    def add_x(self):
        p, b = self.place, self.b
        self.x_copy().wait_recv()
        cols = self.outer

        def body(block):
            b["away"][block, :, cols] = b["away"][block, :, cols] + b["from_x"][block]

        self.each(body)
        self.spend("from_y", "from_y")
        self.y_copy().start()
        self.grant("from_x", "from_x", p.xway)

    def add_y(self):
        p, b = self.place, self.b
        self.y_copy().wait_recv()
        cols = self.wide

        def body(block):
            b["own"][block, :, cols] = b["own"][block, :, cols] + b["from_y"][block]

        self.each(body)
        self.grant("from_y", "from_y", p.yway)

    def add_line(self, way, block):
        self.line_copy(way, block).wait_recv()
        self.b["own"][block] = self.b["own"][block] + self.came(way, block)[...]

    def line_step(self, k):
        p, line = self.place, self.place.line
        if k == 0:
            pl.when(p.has_up)(lambda: self.spend("line_up", "line_in"))
            pl.when(p.has_down)(lambda: self.spend("line_down", "line_in"))
        for way, steps_in, block, more in (
            (0, p.z, line - 1 - k + p.z, p.has_down),
            (1, line - 1 - p.z, k - (line - 1 - p.z), p.has_up),
        ):

            def body(way=way, block=block, more=more):
                pl.when(more)(lambda: self.add_line(way, block))
                self.line_copy(way, block).start()

            pl.when(steps_in <= k)(body)

    def own_step(self):
        p = self.place
        pl.when(p.has_down)(lambda: self.add_line(0, p.z))
        pl.when(p.has_up)(lambda: self.add_line(1, p.z))
        self.spend("last", "last")
        self.last_copy().start()
        pl.when(p.has_down)(lambda: self.grant("line_up", "line_in", p.down))
        pl.when(p.has_up)(lambda: self.grant("line_down", "line_in", p.up))

    def finish(self):
        p, b = self.place, self.b
        if "total" in self.older:
            self.older["total"].free_total()
        self.last_copy().wait_recv()
        b["total"][...] = b["own"][p.z].astype(jnp.float32) + b["last"][...].astype(jnp.float32)
        self.grant("last", "last", p.xway)
        self.out_copy().start()
        self.out_near().start()

    def stages(self):
        def add_y_and_pass():
            self.add_y()
            self.line_step(0)

        steps = [self.start, self.add_core, self.add_x, add_y_and_pass]
        steps += [functools.partial(self.line_step, k) for k in range(1, self.place.line - 1)]
        return steps + [self.own_step, self.finish]

    def free_away(self):
        self.core_copy().wait_send()
        self.x_copy().wait_send()
        self.y_copy().wait_send()

    def free_own(self):
        p = self.place
        for block in range(p.line):
            pl.when(block > p.z)(lambda block=block: self.line_copy(0, block).wait_send())
            pl.when(block < p.z)(lambda block=block: self.line_copy(1, block).wait_send())
        self.last_copy().wait_send()

    def free_total(self):
        self.out_copy().wait_send()
        self.out_near().wait()


class Layer:
    def __init__(self, n, kept, weights, par, b_up, terms, g_par, g_bup):
        self.n, self.s = n, kept
        self.w_qkv, self.w_out, self.w_up, self.w_down = weights
        self.par, self.b_up = par, b_up
        self.g_qkv, self.g_out, self.g_up, self.g_down = terms
        self.g_par, self.g_bup = g_par, g_bup
        self.width, self.deep = self.w_out.shape[-1], self.w_up.shape[-1]
        self.pending = [None, None]

    def chunks(self, body):
        def step(i, carry):
            body(at(i, CHUNK))
            return carry

        lax.fori_loop(0, self.n // CHUNK, step, 0)

    def tiles(self, first, last, body):
        def step(i, carry):
            body(i)
            return carry

        lax.fori_loop(first, last, step, 0)

    def row(self, ref, i):
        return ref[i : i + 1, :]

    def tall_copy(self, ref, slot, t):
        stage = self.s["stage"].at[slot].reshape(*ref.shape[:4], self.width)
        cols = at(t, self.width)
        return pltpu.make_async_copy(stage, ref.at[:, :, :, :, cols], self.s["stage_sem"].at[slot])

    def wide_copy(self, ref, slot, t):
        stage = self.s["stage"].at[slot].reshape(*ref.shape[1:])
        return pltpu.make_async_copy(stage, ref.at[t], self.s["stage_sem"].at[slot])

    def put(self, make, slot, t, first, value):
        held = self.pending[slot]
        pl.when(t > first)(lambda: make(slot, t - 1).wait())
        if held is not None:
            pl.when(t == first)(lambda: held.wait())
        self.s["stage"][slot] = value.astype(jnp.bfloat16)
        make(slot, t).start()

    def put_all(self):
        for slot in range(2):
            if self.pending[slot] is not None:
                self.pending[slot].wait()
            self.pending[slot] = None

    def prepare(self, seg_col, seg_row):
        s, width = self.s, self.width
        s["bias"][...] = jnp.where(seg_col[...] == seg_row[...], 0.0, -1e30)
        s["rows"][0:1, 0:width] = self.par[4:5, :]
        s["rows"][0:1, width : 2 * width] = jnp.zeros((1, width), jnp.float32)
        s["rows"][0:1, 2 * width :] = self.par[5:6, :]

    def norm_parts(self, values):
        center = values - jnp.mean(values, axis=-1, keepdims=True)
        scale = lax.rsqrt(jnp.mean(center * center, axis=-1, keepdims=True) + 1e-05)
        return center * scale, scale

    def norm(self, src, dst, which):
        def body(rows):
            unit, _ = self.norm_parts(src[rows, :].astype(jnp.float32))
            dst[rows, :] = (unit * self.row(self.par, which) + self.row(self.par, 2 + which)).astype(jnp.bfloat16)

        self.chunks(body)

    def norm_a(self):
        self.norm(self.s["x"], self.s["a"], 0)

    def project(self, first, last):
        s = self.s
        queries = self.width // TILE

        def body(t):
            scale = jnp.where(t < queries, HEAD ** (-0.5), 1.0)
            found = dot(s["a"][...], flat(self.w_qkv[:, :, :, :, at(t)])) + s["rows"][0:1, at(t)]
            s["qkv"][:, at(t)] = (found * scale).astype(jnp.bfloat16)

        self.tiles(first, last, body)

    def turn_a(self):
        self.s["a_t"][...] = self.s["a"][...].T

    def pair(self, i, which):
        start = which * self.width + i * 128
        return self.s["qkv"].at[:, pl.ds(pl.multiple_of(start, 128), 128)]

    def own_lanes(self, value, head):
        lanes = lax.broadcasted_iota(jnp.int32, value.shape, 1)
        return jnp.where((lanes < HEAD) == (head == 0), value, jnp.zeros_like(value))

    def attend(self, first, last):
        s = self.s

        def body(i):
            q, k, v = (self.pair(i, which) for which in range(3))
            keys = [self.own_lanes(k[...], head) for head in range(2)]
            vals = [self.own_lanes(v[...], head) for head in range(2)]
            for part in range(self.n // TILE):
                cols = slice(part * TILE, part * TILE + TILE)
                mixed = None
                for head in range(2):
                    scores = dot(keys[head], q[cols, :], NT) + s["bias"][:, cols]
                    raised = jnp.exp(scores - jnp.max(scores, axis=0, keepdims=True))
                    share = 1.0 / jnp.sum(raised, axis=0, keepdims=True)
                    weights = (raised * share).astype(jnp.bfloat16)
                    s["wt"][2 * i + head, :, cols] = weights
                    found = dot(vals[head], weights, TN)
                    mixed = found if mixed is None else mixed + found
                s["o"][cols, at(i, 128)] = mixed.T.astype(jnp.bfloat16)

        self.tiles(first, last, body)

    def branch(self):
        s = self.s

        def body(t):
            found = dot(s["o"][...], flat(self.w_out[:, :, :, :, at(t)])) + self.par[6:7, at(t)]
            s["h"][:, at(t)] = s["x"][:, at(t)].astype(jnp.float32) + found

        self.tiles(0, self.width // TILE, body)
        s["o_t"][...] = s["o"][...].T

    def norm_c(self):
        self.norm(self.s["h"], self.s["c"], 1)

    def up(self, first, last):
        s = self.s

        def body(t):
            before = dot(s["c"][...], flat(self.w_up[:, :, :, :, at(t)])) + self.b_up[0:1, at(t)]
            chance = 0.5 + 0.5 * lax.erf(before * 0.7071067811865476)
            s["g"][:, at(t)] = (before * chance).astype(jnp.bfloat16)
            slope = chance + before * (jnp.exp(before * before * -0.5) * 0.3989422804014327)
            s["du"][:, at(t)] = slope.astype(jnp.bfloat16)

        self.tiles(first, last, body)

    def turn_c(self):
        self.s["c_t"][...] = self.s["c"][...].T

    def down(self):
        s = self.s

        def body(t):
            found = dot(s["g"][...], flat(self.w_down[:, :, :, :, :, at(t)])) + self.par[7:8, at(t)]
            s["a"][:, at(t)] = (s["h"][:, at(t)] + found).astype(jnp.bfloat16)

        self.tiles(0, self.width // TILE, body)

    def feed_back(self, first, last):
        s, width = self.s, self.width
        wide, tall = functools.partial(self.wide_copy, self.g_down), functools.partial(self.tall_copy, self.g_up)

        def body(t):
            cols = at(t, width)
            grad = dot(s["dy"][...], flat(self.w_down[t]), NT)
            low = (grad * s["du"][:, cols].astype(jnp.float32)).astype(jnp.bfloat16)
            s["du"][:, cols] = low
            self.g_bup[0:1, cols] = jnp.sum(low.astype(jnp.float32), axis=0, keepdims=True)
            self.put(wide, 0, t, first, dot(s["g"][:, cols], s["dy"][...], TN))
            self.put(tall, 1, t, first, dot(s["c_t"][...], low))

        self.tiles(first, last, body)
        self.pending = [wide(0, last - 1), tall(1, last - 1)]

    def up_back(self):
        self.s["sums"][...] = dot(self.s["du"][...], flat(self.w_up[...]), NT)

    def norm_back(self, src, which, grad, rest, body_out):
        def body(rows):
            unit, scale = self.norm_parts(src[rows, :].astype(jnp.float32))
            came = grad[rows, :]
            gained = came * self.row(self.par, which)
            self.g_par[which : which + 1, :] += jnp.sum(came * unit, axis=0, keepdims=True)
            self.g_par[2 + which : 3 + which, :] += jnp.sum(came, axis=0, keepdims=True)
            inner = gained - jnp.mean(gained, axis=-1, keepdims=True)
            inner = inner - unit * jnp.mean(gained * unit, axis=-1, keepdims=True)
            body_out(rows, rest[rows, :].astype(jnp.float32) + inner * scale)

        self.chunks(body)

    def norm_c_back(self):
        s = self.s

        def keep(rows, grad):
            s["h"][rows, :] = grad
            low = grad.astype(jnp.bfloat16)
            s["c"][rows, :] = low
            self.g_par[6:7, :] += jnp.sum(low.astype(jnp.float32), axis=0, keepdims=True)
            self.g_par[7:8, :] += jnp.sum(s["dy"][rows, :].astype(jnp.float32), axis=0, keepdims=True)

        self.norm_back(s["h"], 1, s["sums"], s["dy"], keep)

    def branch_back(self):
        s = self.s
        tall = functools.partial(self.tall_copy, self.g_out)
        self.put(tall, 0, 0, 0, dot(s["o_t"][...], s["c"][...]))
        self.pending[0] = tall(0, 0)
        s["a"][...] = dot(s["c"][...], flat(self.w_out[...]), NT).astype(jnp.bfloat16)

    def attend_back(self, first, last):
        s, width = self.s, self.width

        def body(i):
            q, k, v = (self.pair(i, which) for which in range(3))
            came = s["a"].at[:, at(i, 128)]
            dq = dk = dv = None
            for head in range(2):
                vals = self.own_lanes(v[...], head)
                for part in range(self.n // TILE):
                    cols = slice(part * TILE, part * TILE + TILE)
                    grad = dot(vals, came[cols, :], NT)
                    weights = s["wt"][2 * i + head, :, cols].astype(jnp.float32)
                    product = weights * grad
                    inner = jnp.sum(product, axis=0, keepdims=True)
                    s["ds"][:, cols] = (product - weights * inner).astype(jnp.bfloat16)
                one_q = dot(self.own_lanes(k[...], head), s["ds"][...], TN)
                one_k = dot(s["ds"][...], self.own_lanes(q[...], head))
                one_v = dot(s["wt"][2 * i + head], self.own_lanes(came[...], head))
                dq, dk, dv = (one_q, one_k, one_v) if head == 0 else (dq + one_q, dk + one_k, dv + one_v)
            s["g"][:, at(i, 128)] = dq.T.astype(jnp.bfloat16) * HEAD ** (-0.5)
            s["g"][:, pl.ds(pl.multiple_of(width + i * 128, 128), 128)] = dk.astype(jnp.bfloat16)
            s["g"][:, pl.ds(pl.multiple_of(2 * width + i * 128, 128), 128)] = dv.astype(jnp.bfloat16)

        self.tiles(first, last, body)

    def project_terms(self, first, last):
        s, width = self.s, self.width
        tall = functools.partial(self.tall_copy, self.g_qkv)
        for t in range(first, last):
            grad = s["g"][:, t * width : (t + 1) * width]
            if t != 1:
                row = 4 + t // 2
                self.g_par[row : row + 1, :] = jnp.sum(grad.astype(jnp.float32), axis=0, keepdims=True)
            slot = (t + 1) % 2
            self.put(tall, slot, t, t, dot(s["a_t"][...], grad))
            self.pending[slot] = tall(slot, t)

    def project_back(self):
        s = self.s
        s["sums"][...] = dot(s["g"][:, 0 : 3 * self.width], flat(self.w_qkv[...]), NT)

    def norm_a_back(self):
        s = self.s

        def keep(rows, grad):
            s["h"][rows, :] = grad

        self.norm_back(s["x"], 0, s["sums"], s["h"], keep)


def layer_scratch(n, width, deep):
    low, full = jnp.bfloat16, jnp.float32
    return dict(
        a=pltpu.VMEM((n, width), low),
        a_t=pltpu.VMEM((width, n), low),
        qkv=pltpu.VMEM((n, 3 * width), low),
        bias=pltpu.VMEM((n, n), full),
        wt=pltpu.VMEM((width // HEAD, n, n), low),
        ds=pltpu.VMEM((n, n), low),
        o=pltpu.VMEM((n, width), low),
        o_t=pltpu.VMEM((width, n), low),
        h=pltpu.VMEM((n, width), full),
        c=pltpu.VMEM((n, width), low),
        c_t=pltpu.VMEM((width, n), low),
        g=pltpu.VMEM((n, deep), low),
        du=pltpu.VMEM((n, deep), low),
        sums=pltpu.VMEM((n, width), full),
        rows=pltpu.VMEM((8, 3 * width), full),
        stage=pltpu.VMEM((2, width, width), low),
        stage_sem=pltpu.SemaphoreType.DMA((2,)),
    )


def cut(kept, n):
    cuts = dict(kept)
    for name in ("a", "qkv", "o", "h", "c", "g", "du", "sums"):
        cuts[name] = kept[name].at[0:n]
    for name in ("a_t", "o_t", "c_t"):
        cuts[name] = kept[name].at[:, 0:n]
    for name in ("bias", "ds"):
        cuts[name] = kept[name].at[0:n, 0:n]
    cuts["wt"] = kept["wt"].at[:, 0:n, 0:n]
    return cuts


ORDER = (0, 1, 2, 3)
BACK = (2, 3, 1, 0)


class SmallSum:
    def __init__(self, place, parts, land, line_land, out, send, recv):
        self.place, self.parts, self.land, self.line_land, self.out = place, parts, land, line_land, out
        self.send, self.recv = send, recv

    def near(self, step):
        p = self.place
        device = (p.core, p.xway, p.yway)[step]
        return remote(self.parts.at[step], self.land.at[step], self.send.at[step], self.recv.at[step], device)

    def far(self, step):
        p = self.place
        other = lax.rem(p.z + step, p.line)
        device = (p.dp, other * 2 + p.y)
        src = self.parts.at[3]
        return remote(src, self.line_land.at[p.z], self.send.at[3 + other], self.recv.at[3 + p.z], device)

    def from_far(self, step):
        p = self.place
        other = lax.rem(p.z + step, p.line)
        device = (p.dp, other * 2 + p.y)
        src = self.parts.at[3]
        return remote(src, self.line_land.at[other], self.send.at[3 + other], self.recv.at[3 + other], device)

    def stage(self, step):
        p = self.place
        if step:
            if step <= 3:
                self.near(step - 1).wait_recv()
                self.parts[step] = self.parts[step - 1] + self.land[step - 1]
        if step < 3:
            self.near(step).start()
        if step == 3:
            for other in range(1, p.line):
                self.far(other).start()
            self.line_land[p.z] = self.parts[3]
        if step == 4:
            for other in range(1, p.line):
                self.from_far(other).wait_recv()
            total = self.line_land[0]
            for block in range(1, p.line):
                total = total + self.line_land[block]
            self.out[...] = total
            for near in range(3):
                self.near(near).wait_send()
            for other in range(1, p.line):
                self.far(other).wait_send()


def whole_kernel(line, sizes, names, ring_names, *refs):
    take = list(refs)

    def some(count):
        found = take[:count]
        del take[:count]
        return found

    owned, (small,) = some(4), some(1)
    x_t, dy_t, col_t, row_t, x_i, dy_i, col_i, row_i = some(8)
    y_i, y_t, gx_i, gx_t = some(4)
    shares, (small_out,) = some(4), some(1)
    far_weights, terms_t, terms_i = some(4), some(4), some(4)
    weights = some(4)
    kept = dict(zip(names, some(len(names))))
    bufs = dict(zip(ring_names, some(len(ring_names))))
    pad_x, pad_dy, small_all, par, b_up, g_parts, g_land, g_line = some(8)
    ag_send, ag_recv, ag_near, rs_send, rs_recv, rs_near, credit = some(7)
    s_send, s_recv, g_send, g_recv, load_sem, io_sem = some(6)
    n_t, n_i, counts = sizes
    width = weights[1].shape[-1]
    place = Place(line)
    place.greet()

    smalls = []
    for step, other in enumerate(place.others()):
        copy = remote(small, small_all.at[place.fs], s_send.at[step], s_recv.at[place.fs], (place.dp, other))
        copy.start()
        smalls.append(copy)

    ahead, back = panels_of(counts, width, ORDER), panels_of(counts, width, BACK)
    base = len(ahead)
    units, sums = [], []
    for u in range(2 * base):
        panel, layer, into = ahead[u % base], u // base, (weights, far_weights)[u // base]
        own, full = owned[panel.which].at[layer], into[panel.which]
        units.append(Gather(u, place, own, panel, full, GATHER_WAYS[u], ag_send, ag_recv, ag_near))
        units[u].older = units[u - AG_RING] if u >= AG_RING else None
    for u in range(2 * base):
        panel, layer, terms = back[u % base], u // base, (terms_i, terms_t)[u // base]
        share, term = shares[panel.which].at[layer], terms[panel.which]
        sems = credit, rs_send, rs_recv, rs_near
        sums.append(Reduce(u, 2 * base, place, panel, SUM_WAYS[u], term, share, bufs, *sems))
        sums[u].older = {name: sums[u - RINGS[name]] for name in ("away", "own", "total") if u >= RINGS[name]}

    def layer_of(layer, n, view, terms):
        grads = g_parts.at[0, layer, 0:8], b_up.at[2 + layer]
        return Layer(n, view, weights, par.at[layer], b_up.at[layer], terms, *grads)

    text = layer_of(1, n_t, {**kept, "x": x_t.at[0], "dy": dy_t.at[0]}, terms_t)
    view = {**cut(kept, n_i), "x": pad_x, "dy": pad_dy}
    image = layer_of(0, n_i, view, terms_i)
    for u, unit in enumerate(sums):
        unit.flush = image.put_all if u < base else text.put_all
    starts = [sum(counts[:which]) for which in range(5)]
    heads, tiles, panels = width // 128, width // TILE, counts[3]
    y_copy = pltpu.make_async_copy(kept["a"], y_t.at[0], io_sem.at[0])
    grad_copy = pltpu.make_async_copy(kept["h"], gx_t.at[0], io_sem.at[1])
    loads = [pltpu.make_async_copy(far_weights[i], weights[i], load_sem.at[i]) for i in range(4)]

    steps = []

    def add(body, *args, needs=()):
        def step():
            for unit in needs:
                units[unit].arrive()
            body(*args)

        step.needs = tuple(needs)
        steps.append(step)

    def first():
        small_all[place.fs] = small[...]
        g_parts[0] = jnp.zeros(g_parts.shape[1:], jnp.float32)
        for step, other in enumerate(place.others()):
            remote(small, small_all.at[other], s_send.at[step], s_recv.at[other], (place.dp, other)).wait_recv()
        piece, deep = width // (2 * line), b_up.shape[-1] // (2 * line)
        for layer in range(2):
            for block in range(2 * line):
                par[layer, :, block * piece : (block + 1) * piece] = small_all[block, layer, 0:8, 0:piece]
                for j in range(deep // 128):
                    start = block * deep + j * 128
                    b_up[layer, 0:1, start : start + 128] = small_all[block, layer, 8 + j : 9 + j, :]
        for src, dst in ((x_i, pad_x), (dy_i, pad_dy)):
            have = src.shape[1]
            if have < n_i:
                cut_at = have // 16 * 16
                dst[cut_at:, :] = jnp.zeros((n_i - cut_at, width), jnp.bfloat16)
            dst[0:have, :] = src[0]
        image.prepare(col_i, row_i)
        image.norm_a()

    def image_out():
        image.down()
        y_i[0] = view["a"][0 : y_i.shape[1], :]

    def image_last():
        image.norm_a_back()
        gx_i[0] = view["h"][0 : gx_i.shape[1], :]

    def text_first():
        text.prepare(col_t, row_t)
        text.norm_a()

    def waiting(load, body):
        def step(*args):
            load.wait()
            body(*args)

        return step

    def text_out():
        loads[3].wait()
        text.down()
        y_copy.start()

    def text_branch_back():
        y_copy.wait()
        text.branch_back()

    def text_last():
        text.norm_a_back()
        grad_copy.start()
        for layer in range(2):
            for j in range(b_up.shape[-1] // width):
                g_parts[0, layer, 8 + j : 9 + j, :] = b_up[2 + layer, 0:1, j * width : (j + 1) * width]

    def load(which):
        add(loads[which].start, needs=range(base + starts[which], base + starts[which + 1]))

    add(first)
    for part in range(3):
        add(image.project, part * tiles, (part + 1) * tiles, needs=(part,))
    add(image.turn_a)
    for i in range(0, heads, 2):
        add(image.attend, i, i + 2)
    add(image.branch, needs=(starts[1],))
    add(image.norm_c)
    for part in range(panels):
        add(image.up, part * tiles, (part + 1) * tiles, needs=(starts[2] + part,))
    add(image.turn_c)
    add(image_out, needs=range(starts[3], starts[4]))
    for part in range(panels):
        add(image.feed_back, part, part + 1)
    add(image.up_back)
    add(image.norm_c_back)
    add(image.branch_back)
    for i in range(0, heads, 2):
        add(image.attend_back, i, i + 2)
    for part in range(3):
        add(image.project_terms, part, part + 1)
    add(image.project_back)
    add(image_last)
    load(0)
    add(text_first)
    for part in range(3):
        body = waiting(loads[0], text.project) if part == 0 else text.project
        add(body, part * tiles, (part + 1) * tiles)
    add(text.turn_a)
    load(1)
    for i in range(heads):
        add(text.attend, i, i + 1)
    add(waiting(loads[1], text.branch))
    load(2)
    add(text.norm_c)
    for part in range(panels):
        add(waiting(loads[2], text.up) if part == 0 else text.up, part * tiles, (part + 1) * tiles)
    load(3)
    add(text.turn_c)
    add(text_out)
    for part in range(panels):
        add(text.feed_back, part, part + 1)
    add(text.up_back)
    add(text.norm_c_back)
    add(text_branch_back)
    for i in range(heads):
        add(text.attend_back, i, i + 1)
    for part in range(3):
        add(text.project_terms, part, part + 1)
    add(text.project_back)
    add(text_last)
    small_sum = SmallSum(place, g_parts, g_land, g_line, small_out, g_send, g_recv)
    for stage in range(5):
        add(small_sum.stage, stage)

    drive(steps, [unit.stages() for unit in units], [unit.stages() for unit in sums])

    for unit in sums[-RINGS["away"] :]:
        unit.free_away()
    for unit in sums[-RINGS["own"] :]:
        unit.free_own()
    for unit in sums[-RINGS["total"] :]:
        unit.free_total()
    for unit in sums:
        unit.out_landed().wait_recv()
    for unit in units[-AG_RING:]:
        unit.drain()
    for copy in smalls:
        copy.wait_send()
    grad_copy.wait()


GATHER_WAYS = (
    0, 2, 0, 0, 2, 0, 0, 2, 0, 0, 2, 0, 0, 0, 0, 0, 0, 0, 0, 0, 0, 0, 0, 0,
)
SUM_WAYS = (
    0, 0, 1, 0, 0, 1, 0, 0, 1, 0, 0, 1, 0, 0, 1, 0, 0, 1, 0, 0, 1, 0, 0, 1,
)
PLAN = (
    0, 10, 20, 30, 40, 50, -1, 1, 11, 21, 31, 41, 2, 12, 22, 32, 42, 3, 13, 23, 33, 43, 51, 52, 4, 53, 14, 24,
    5, 60, -1, 34, 15, 70, -1, 61, 44, 25, 80, -1, 54, 62, 71, 63, 35, 90, -1, -1, 72, 81, -1, 45, 73, 100, 64,
    -1, 55, 82, 91, 110, 120, 83, -1, -1, 101, 92, 74, -1, -1, 84, 111, 102, 65, 130, 121, -1, 93, 112, 75, 140,
    103, -1, 131, 85, 150, 122, -1, 94, 113, 141, 104, 132, 151, 95, 160, 114, 123, 105, 170, 142, 133, 152,
    124, 115, 180, -1, 134, 161, 171, -1, 125, 143, 190, 153, -1, 1000, 135, 181, 200, -1, 1001, 144, 162, 172,
    -1, 1010, 191, 154, -1, 1002, 1011, 1020, 182, 201, 1030, 163, -1, 1021, 145, 173, 210, 1040, 1031, 1003,
    192, 1050, 155, 220, 183, -1, 202, 164, 1012, -1, 1022, 1041, 174, 193, 211, 1051, 1004, -1, 1032, 184, 203,
    221, -1, 1060, 212, 1013, 165, 222, 230, -1, 1061, 1005, 213, -1, 1042, 223, -1, 1023, -1, 175, 1014, 194,
    231, -1, 1052, 1006, -1, -1, 232, 1024, 1033, 233, 185, -1, 1015, 204, -1, 1062, -1, 214, 1025, -1, -1, -1,
    1034, 195, -1, 1007, 1016, 1043, 1070, -1, 1026, -1, 1035, 1071, 205, 224, -1, 1044, -1, 215, -1, 1017,
    1036, 1053, 1080, 1045, -1, 1027, 1090, -1, 1081, 234, -1, 1046, 1054, 1063, 1072, 1091, -1, 225, -1, 1037,
    1100, 1055, 1073, 1064, -1, 1082, 1101, 1056, 1074, 1065, 1075, 235, -1, 1047, 1110, -1, 1083, -1, 1066,
    1076, 1084, 1092, 1102, 1111, -1, 1057, 1067, 1085, 1077, 1093, 1120, 1094, -1, 1095, 1103, 1112, 1121,
    1130, 1086, -1, 1104, 1131, 1140, 1122, 1113, 1096, 1114, 1087, 1105, 1141, -1, 1115, 1123, 1132, 1150,
    1097, 1160, 1124, -1, 1106, 1125, 1133, 1142, 1151, 1161, 1134, 1116, -1, 1107, 1170, -1, 1135, 1171, 1143,
    1144, 1152, 1126, -1, -1, 1145, 1162, 1153, 1117, 1154, 1180, 1136, -1, 1172, 1181, 1155, 1127, 1163, 1190,
    -1, 1137, 1146, 1164, 1200, 1191, -1, 1173, 1174, 1182, 1165, 1201, -1, 1147, 1156, 1175, -1, 1210, -1,
    1183, 1192, 1184, 1211, -1, 1166, 1202, -1, 1157, 1176, 1185, 1193, 1194, 1220, 1212, -1, 1167, 1221, 1230,
    1203, 1204, 1177, -1, -1, 1195, 1231, 1213, 1205, -1, 1186, 1214, 1222, -1, 1187, 1196, 1215, 1232, -1,
    1197, 1206, 1223, 1216, 1233, 1224, 1234, 1225, 1235, 1207, 1217, 1226, 1236, 1227, 1237,
)


def drive(steps, gathers, sums):
    at_step = 0
    for code in PLAN:
        if code < 0:
            steps[at_step]()
            at_step += 1
        elif code < 1000:
            gathers[code // 10][code % 10]()
        else:
            sums[code // 10 - 100][code % 10]()


def padded(rows):
    return -(-rows // TILE) * TILE


def whole(line, x_i, dy_i, x_t, dy_t, seg_i, seg_t, owned, small):
    width, deep = owned[1].shape[2], owned[2].shape[2]
    rows = owned[1].shape[1] // 2
    counts = (3, 1, deep // width, deep // width)
    own = [w.reshape(2, 2, rows, w.shape[2]) for w in owned[:3]] + [owned[3].reshape(2, 2, counts[3], rows, width)]
    n_t, n_i = padded(x_t.shape[1]), padded(x_i.shape[1])
    low, full = jnp.bfloat16, jnp.float32
    kept = layer_scratch(n_t, width, deep)
    pads = lambda seg, n: jnp.pad(seg, ((0, 0), (0, n - seg.shape[1])), constant_values=-1)
    seg_t, seg_i = pads(seg_t, n_t), pads(seg_i, n_i)
    fulls = [(line, 2, *w.shape[1:]) for w in own]
    rings = dict(
        own=pltpu.VMEM((RINGS["own"], line, rows, width), low),
        away=pltpu.VMEM((RINGS["away"], line, rows, width), low),
        other=pltpu.VMEM((RINGS["other"], line, 2, rows, width), low),
        from_x=pltpu.VMEM((RINGS["from_x"], line, rows, width // 2), low),
        from_y=pltpu.VMEM((RINGS["from_y"], line, rows, 2 * width // 3), low),
        line_in=pltpu.VMEM((RINGS["line_in"], 2 * line - 2, rows, width), low),
        last=pltpu.VMEM((RINGS["last"], rows, width), low),
        total=pltpu.VMEM((RINGS["total"], rows, width), full),
    )
    panels = 2 * sum(counts)
    small_rows = 8 + deep // width
    small_rows += -small_rows % 8
    anywhere, inside = pl.BlockSpec(memory_space=pl.ANY), pl.BlockSpec(memory_space=pltpu.VMEM)
    dma = pltpu.SemaphoreType.DMA
    outs = [
        jax.ShapeDtypeStruct(x_i.shape, low),
        jax.ShapeDtypeStruct(x_t.shape, low),
        jax.ShapeDtypeStruct(x_i.shape, full),
        jax.ShapeDtypeStruct(x_t.shape, full),
        *[jax.ShapeDtypeStruct(w.shape, full) for w in own],
        jax.ShapeDtypeStruct((2, small_rows, width), full),
        *[jax.ShapeDtypeStruct(shape, low) for shape in fulls * 3],
    ]
    scratch = [
        *[pltpu.VMEM(shape, low) for shape in fulls],
        *kept.values(),
        *rings.values(),
        pltpu.VMEM((n_i, width), low),
        pltpu.VMEM((n_i, width), low),
        pltpu.VMEM((2 * line, *small.shape), full),
        pltpu.VMEM((2, 8, width), full),
        pltpu.VMEM((4, 1, deep), full),
        pltpu.VMEM((4, 2, small_rows, width), full),
        pltpu.VMEM((3, 2, small_rows, width), full),
        pltpu.VMEM((line, 2, small_rows, width), full),
        dma((AG_RING, line + 6)),
        dma((panels, line + 5)),
        dma((AG_RING,)),
        dma((SUM_SENDS,)),
        dma((SUM_ARRIVALS,)),
        dma((4 + RINGS["total"],)),
        pltpu.SemaphoreType.REGULAR((len(CREDITS),)),
        dma((2 * line,)),
        dma((2 * line,)),
        dma((3 + line,)),
        dma((3 + line,)),
        dma((4,)),
        dma((2,)),
    ]
    found = pl.pallas_call(
        functools.partial(whole_kernel, line, (n_t, n_i, counts), list(kept), list(rings)),
        out_shape=outs,
        in_specs=[anywhere] * 4 + [inside] * 9,
        out_specs=[inside, anywhere, inside, anywhere] + [anywhere] * 4 + [inside] + [anywhere] * 12,
        scratch_shapes=scratch,
        compiler_params=pltpu.CompilerParams(collective_id=0, has_side_effects=True, vmem_limit_bytes=63 * 2**20),
    )(*own, small, x_t, dy_t, seg_t.reshape(n_t, 1), seg_t, x_i, dy_i, seg_i.reshape(n_i, 1), seg_i)
    shares = [share.reshape(w.shape) for share, w in zip(found[4:8], owned)]
    return found[:4], shares, found[8]


def normed(values, gain, shift):
    center = values - jnp.mean(values, axis=-1, keepdims=True)
    spread = jnp.mean(center * center, axis=-1, keepdims=True)
    return center * lax.rsqrt(spread + 1e-05) * gain + shift


def gelu_exact(values):
    return jax.nn.gelu(values, approximate=False)


def segment_ids(lengths, seq_len):
    bounds = jnp.cumsum(lengths, axis=-1)
    positions = jnp.arange(seq_len, dtype=jnp.int32)
    return jnp.sum((positions[None, :, None] >= bounds[:, None, :]).astype(jnp.int32), axis=-1)


def split_heads(values):
    batch, length, width = values.shape
    return values.reshape(batch, length, width // HEAD, HEAD)


def masked_scores(queries, keys_all, segment):
    scores = jnp.einsum(
        "bqhd,bkhd->bhqk",
        split_heads(queries),
        split_heads(keys_all),
        preferred_element_type=jnp.float32,
    )
    same = (segment[:, :, None] == segment[:, None, :])[:, None]
    return (jnp.where(same, scores, -1e30), same)


def attention(queries, keys_all, values_all, segment):
    scores, same = masked_scores(queries, keys_all, segment)
    largest = jnp.max(scores, axis=-1, keepdims=True)
    raised = jnp.exp(scores - largest)
    totals = jnp.sum(raised, axis=-1, keepdims=True)
    attn_weights = raised / totals
    log_total = largest + jnp.log(totals)
    mixed = jnp.einsum(
        "bhqk,bkhd->bqhd",
        attn_weights.astype(jnp.bfloat16),
        split_heads(values_all),
        preferred_element_type=jnp.float32,
    )
    return (mixed.reshape(queries.shape).astype(jnp.bfloat16), log_total)


def attention_back(queries, keys_all, values_all, segment, log_total, grad_mixed):
    scores, same = masked_scores(queries, keys_all, segment)
    attn_weights = jnp.where(same, jnp.exp(scores - log_total), 0.0)
    grad_heads = split_heads(grad_mixed)
    grad_weights = jnp.einsum(
        "bqhd,bkhd->bhqk", grad_heads, split_heads(values_all), preferred_element_type=jnp.float32
    )
    inner = jnp.sum(attn_weights * grad_weights, axis=-1, keepdims=True)
    grad_scores = (attn_weights * (grad_weights - inner)).astype(jnp.bfloat16)
    grad_queries = jnp.einsum(
        "bhqk,bkhd->bqhd", grad_scores, split_heads(keys_all), preferred_element_type=jnp.float32
    )
    grad_keys = jnp.einsum(
        "bhqk,bqhd->bkhd", grad_scores, split_heads(queries), preferred_element_type=jnp.float32
    )
    grad_values = jnp.einsum(
        "bhqk,bqhd->bkhd",
        attn_weights.astype(jnp.bfloat16),
        grad_heads,
        preferred_element_type=jnp.float32,
    )
    shape_rows = queries.shape
    return (
        grad_queries.reshape(shape_rows),
        grad_keys.reshape(shape_rows),
        grad_values.reshape(shape_rows),
    )


def forward_layer(inputs, weights, segment):
    qkv_weight, out_weight, up_weight, down_weight, gains, biases, up_bias = weights
    width = inputs.shape[-1]
    source = inputs.astype(jnp.float32)
    normed_a = normed(source, gains[0], biases[0]).astype(jnp.bfloat16)
    project = jnp.einsum("bld,de->ble", normed_a, qkv_weight, preferred_element_type=jnp.float32)
    queries = ((project[..., :width] + biases[2]) * HEAD ** (-0.5)).astype(jnp.bfloat16)
    keys_all = project[..., width : 2 * width].astype(jnp.bfloat16)
    values_all = (project[..., 2 * width :] + biases[3]).astype(jnp.bfloat16)
    mixed, log_total = attention(queries, keys_all, values_all, segment)
    hidden = (
        source
        + jnp.einsum("bld,de->ble", mixed, out_weight, preferred_element_type=jnp.float32)
        + biases[4]
    )
    normed_c = normed(hidden, gains[1], biases[1]).astype(jnp.bfloat16)
    before = (
        jnp.einsum("bld,df->blf", normed_c, up_weight, preferred_element_type=jnp.float32) + up_bias
    )
    activated = gelu_exact(before).astype(jnp.bfloat16)
    result = (
        hidden
        + jnp.einsum("blf,fd->bld", activated, down_weight, preferred_element_type=jnp.float32)
        + biases[5]
    )
    return (
        source,
        normed_a,
        queries,
        keys_all,
        values_all,
        log_total,
        mixed,
        hidden,
        normed_c,
        before,
        activated,
        result,
    )


def backward_layer(inputs, cotangent, weights, segment):
    qkv_weight, out_weight, up_weight, down_weight, gains, biases, up_bias = weights
    width = inputs.shape[-1]
    (
        source,
        normed_a,
        queries,
        keys_all,
        values_all,
        log_total,
        mixed,
        hidden,
        normed_c,
        before,
        activated,
        result,
    ) = forward_layer(inputs, weights, segment)
    grad_result = cotangent.astype(jnp.float32)
    grad_downw = jnp.einsum("blf,bld->fd", activated, cotangent, preferred_element_type=jnp.float32)
    grad_act = jnp.einsum("bld,fd->blf", cotangent, down_weight, preferred_element_type=jnp.float32)
    grad_before = jax.vjp(gelu_exact, before)[1](grad_act)[0].astype(jnp.bfloat16)
    grad_upw = jnp.einsum("bld,blf->df", normed_c, grad_before, preferred_element_type=jnp.float32)
    grad_upb = jnp.sum(grad_before.astype(jnp.float32), axis=(0, 1))
    grad_normc = jnp.einsum(
        "blf,df->bld", grad_before, up_weight, preferred_element_type=jnp.float32
    )
    hidden_back = jax.vjp(
        normed, hidden, gains[1].astype(jnp.float32), biases[1].astype(jnp.float32)
    )[1]
    grad_hidden_ln, grad_gain_two, grad_shift_two = hidden_back(grad_normc)
    grad_hidden = grad_result + grad_hidden_ln
    grad_branch = grad_hidden.astype(jnp.bfloat16)
    grad_outw = jnp.einsum("bld,ble->de", mixed, grad_branch, preferred_element_type=jnp.float32)
    grad_mixed = jnp.einsum(
        "ble,de->bld", grad_branch, out_weight, preferred_element_type=jnp.float32
    ).astype(jnp.bfloat16)
    grad_queries, grad_keys, grad_values = attention_back(
        queries, keys_all, values_all, segment, log_total, grad_mixed
    )
    grad_project = jnp.concatenate(
        [
            grad_queries.astype(jnp.bfloat16) * HEAD ** (-0.5),
            grad_keys.astype(jnp.bfloat16),
            grad_values.astype(jnp.bfloat16),
        ],
        axis=-1,
    )
    grad_qkvw = jnp.einsum(
        "bld,ble->de", normed_a, grad_project, preferred_element_type=jnp.float32
    )
    column_sums = jnp.sum(grad_project.astype(jnp.float32), axis=(0, 1))
    grad_norma = jnp.einsum(
        "ble,de->bld", grad_project, qkv_weight, preferred_element_type=jnp.float32
    )
    source_back = jax.vjp(
        normed, source, gains[0].astype(jnp.float32), biases[0].astype(jnp.float32)
    )[1]
    grad_source_ln, grad_gain_one, grad_shift_one = source_back(grad_norma)
    grad_inputs = grad_hidden + grad_source_ln
    grad_gains = jnp.stack([grad_gain_one, grad_gain_two])
    grad_biases = jnp.stack(
        [
            grad_shift_one,
            grad_shift_two,
            column_sums[:width],
            column_sums[2 * width :],
            jnp.sum(grad_branch.astype(jnp.float32), axis=(0, 1)),
            jnp.sum(grad_result, axis=(0, 1)),
        ]
    )
    return (
        result.astype(jnp.bfloat16),
        grad_inputs,
        (grad_qkvw, grad_outw, grad_upw, grad_downw, grad_gains, grad_biases, grad_upb),
    )


def fetch_weights(layer_index, w_qkv, w_out, w_up, w_down, gains, biases, b_up):
    return (
        lax.all_gather(w_qkv[layer_index], "fsdp", axis=0, tiled=True),
        lax.all_gather(w_out[layer_index], "fsdp", axis=0, tiled=True),
        lax.all_gather(w_up[layer_index], "fsdp", axis=0, tiled=True),
        lax.all_gather(w_down[layer_index], "fsdp", axis=0, tiled=True),
        lax.all_gather(gains[layer_index], "fsdp", axis=1, tiled=True),
        lax.all_gather(biases[layer_index], "fsdp", axis=1, tiled=True),
        lax.all_gather(b_up[layer_index], "fsdp", axis=0, tiled=True),
    )


def fetch_again(layer_index, w_qkv, w_out, w_up, w_down, gains, biases, b_up):
    return (
        lax.all_gather(w_qkv[layer_index], "fsdp", axis=0, tiled=True),
        lax.all_gather(w_out[layer_index], "fsdp", axis=0, tiled=True),
        lax.all_gather(w_up[layer_index], "fsdp", axis=0, tiled=True),
        lax.all_gather(w_down[layer_index], "fsdp", axis=0, tiled=True),
        lax.all_gather(gains[layer_index], "fsdp", axis=1, tiled=True),
        lax.all_gather(biases[layer_index], "fsdp", axis=1, tiled=True),
        lax.all_gather(b_up[layer_index], "fsdp", axis=0, tiled=True),
    )


def reduce_grads(gradients):
    shares = (
        lax.psum_scatter(gradients[0], "fsdp", scatter_dimension=0, tiled=True),
        lax.psum_scatter(gradients[1], "fsdp", scatter_dimension=0, tiled=True),
        lax.psum_scatter(gradients[2], "fsdp", scatter_dimension=0, tiled=True),
        lax.psum_scatter(gradients[3], "fsdp", scatter_dimension=0, tiled=True),
        lax.psum_scatter(gradients[4], "fsdp", scatter_dimension=1, tiled=True),
        lax.psum_scatter(gradients[5], "fsdp", scatter_dimension=1, tiled=True),
        lax.psum_scatter(gradients[6], "fsdp", scatter_dimension=0, tiled=True),
    )
    quarters = (
        lax.psum_scatter(
            shares[0].astype(jnp.bfloat16), "dp", scatter_dimension=0, tiled=True
        ).astype(jnp.float32),
        lax.psum_scatter(
            shares[1].astype(jnp.bfloat16), "dp", scatter_dimension=0, tiled=True
        ).astype(jnp.float32),
        lax.psum_scatter(
            shares[2].astype(jnp.bfloat16), "dp", scatter_dimension=0, tiled=True
        ).astype(jnp.float32),
        lax.psum_scatter(
            shares[3].astype(jnp.bfloat16), "dp", scatter_dimension=0, tiled=True
        ).astype(jnp.float32),
        lax.psum_scatter(
            shares[4].astype(jnp.bfloat16), "dp", scatter_dimension=1, tiled=True
        ).astype(jnp.float32),
        lax.psum_scatter(
            shares[5].astype(jnp.bfloat16), "dp", scatter_dimension=1, tiled=True
        ).astype(jnp.float32),
        lax.psum_scatter(
            shares[6].astype(jnp.bfloat16), "dp", scatter_dimension=0, tiled=True
        ).astype(jnp.float32),
    )
    return (
        lax.all_gather(quarters[0].astype(jnp.bfloat16), "dp", axis=0, tiled=True).astype(
            jnp.float32
        ),
        lax.all_gather(quarters[1].astype(jnp.bfloat16), "dp", axis=0, tiled=True).astype(
            jnp.float32
        ),
        lax.all_gather(quarters[2].astype(jnp.bfloat16), "dp", axis=0, tiled=True).astype(
            jnp.float32
        ),
        lax.all_gather(quarters[3].astype(jnp.bfloat16), "dp", axis=0, tiled=True).astype(
            jnp.float32
        ),
        lax.all_gather(quarters[4].astype(jnp.bfloat16), "dp", axis=1, tiled=True).astype(
            jnp.float32
        ),
        lax.all_gather(quarters[5].astype(jnp.bfloat16), "dp", axis=1, tiled=True).astype(
            jnp.float32
        ),
        lax.all_gather(quarters[6].astype(jnp.bfloat16), "dp", axis=0, tiled=True).astype(
            jnp.float32
        ),
    )


def plain(
    images,
    image_cot,
    captions,
    caption_cot,
    lengths,
    w_qkv,
    w_out,
    w_up,
    w_down,
    gains,
    biases,
    b_up,
):
    owned = (w_qkv, w_out, w_up, w_down, gains, biases, b_up)
    image_seg = jnp.zeros((images.shape[0], images.shape[1]), jnp.int32)
    caption_seg = segment_ids(lengths, captions.shape[1])
    first_weights = fetch_weights(0, *owned)
    image_out = forward_layer(images, first_weights, image_seg)[-1].astype(jnp.bfloat16)
    second_weights = fetch_weights(1, *owned)
    caption_out = forward_layer(captions, second_weights, caption_seg)[-1].astype(jnp.bfloat16)
    second_back = fetch_again(1, *owned)
    _, caption_grad, caption_terms = backward_layer(captions, caption_cot, second_back, caption_seg)
    caption_shares = reduce_grads(caption_terms)
    first_back = fetch_again(0, *owned)
    _, image_grad, image_terms = backward_layer(images, image_cot, first_back, image_seg)
    image_shares = reduce_grads(image_terms)
    stacked = tuple((jnp.stack([image_shares[index], caption_shares[index]]) for index in range(7)))
    return (image_out, caption_out, image_grad, caption_grad) + stacked


def kernels_fit(mesh, w_qkv):
    return mesh.shape["dp"] == 4 and mesh.shape["fsdp"] % 2 == 0 and w_qkv.shape[1] % 32 == 0


def local(mesh, images, image_cot, captions, caption_cot, lengths, w_qkv, w_out, w_up, w_down, gains, biases, b_up):
    if not kernels_fit(mesh, w_qkv):
        return plain(
            images, image_cot, captions, caption_cot, lengths, w_qkv, w_out, w_up, w_down, gains, biases, b_up
        )
    line, width = mesh.shape["fsdp"] // 2, gains.shape[2]
    deep = b_up.shape[1]
    par = jnp.concatenate([gains, biases], axis=1)
    par = jnp.pad(par, ((0, 0), (0, 0), (0, -width % 128)))
    small = jnp.concatenate([par, b_up.reshape(2, deep // 128, 128)], axis=1).astype(jnp.float32)
    small = jnp.pad(small, ((0, 0), (0, -small.shape[1] % 8), (0, 0)))
    image_seg = jnp.zeros((images.shape[0], images.shape[1]), jnp.int32)
    caption_seg = segment_ids(lengths, captions.shape[1])
    outs, shares, sums = whole(
        line, images, image_cot, captions, caption_cot, image_seg, caption_seg, (w_qkv, w_out, w_up, w_down), small
    )
    place = lax.axis_index("fsdp")
    mine = lax.dynamic_slice_in_dim(sums[:, :8], place * width, width, 2)
    up = sums[:, 8 : 8 + deep * 2 * line // w_out.shape[2]].reshape(2, -1)
    up = lax.dynamic_slice_in_dim(up, place * deep, deep, 1)
    return (*outs, *shares, mine[:, :2], mine[:, 2:], up)


def solution(mesh):
    placed = (
        P(("dp", "fsdp"), None, None),
        P(("dp", "fsdp"), None, None),
        P(("dp", "fsdp"), None, None),
        P(("dp", "fsdp"), None, None),
        P(("dp", "fsdp"), None),
        P(None, "fsdp", None),
        P(None, "fsdp", None),
        P(None, "fsdp", None),
        P(None, "fsdp", None),
        P(None, None, "fsdp"),
        P(None, None, "fsdp"),
        P(None, "fsdp"),
    )
    return jax.shard_map(
        functools.partial(local, mesh),
        mesh=mesh,
        in_specs=placed,
        out_specs=(
            P(("dp", "fsdp"), None, None),
            P(("dp", "fsdp"), None, None),
            P(("dp", "fsdp"), None, None),
            P(("dp", "fsdp"), None, None),
            P(None, "fsdp", None),
            P(None, "fsdp", None),
            P(None, "fsdp", None),
            P(None, "fsdp", None),
            P(None, None, "fsdp"),
            P(None, None, "fsdp"),
            P(None, "fsdp"),
        ),
        check_vma=False,
    )
```

```python
import functools

import jax
import jax.numpy as jnp
from jax import lax
from jax.experimental import pallas as pl
from jax.experimental.pallas import tpu as pltpu
from jax.sharding import PartitionSpec as P

HEAD = 64

MESH = pl.DeviceIdType.MESH
NT = (((1,), (1,)), ((), ()))
TN = (((0,), (0,)), ((), ()))
TILE = 256
CHUNK = 64
ALL = slice(None)


def dot(a, b, dims=(((1,), (0,)), ((), ()))):
    return lax.dot_general(a, b, dims, preferred_element_type=jnp.float32)


def flat(value):
    return value.reshape(-1, value.shape[-1])


def at(t, size=TILE):
    return pl.ds(pl.multiple_of(t * size, size), size)


def remote(src, dst, send, recv, device):
    return pltpu.make_async_remote_copy(
        src_ref=src, dst_ref=dst, send_sem=send, recv_sem=recv, device_id=device, device_id_type=MESH
    )


class Place:
    def __init__(self, line):
        dp, fs = lax.axis_index("dp"), lax.axis_index("fsdp")
        self.line, self.dp, self.fs = line, dp, fs
        self.x, self.c = dp // 2, dp % 2
        self.z, self.y = fs // 2, fs % 2
        self.up, self.down = (dp, fs + 2), (dp, fs - 2)
        self.yway = (dp, self.z * 2 + 1 - self.y)
        self.xway = ((1 - self.x) * 2 + self.c, fs)
        self.core = (self.x * 2 + 1 - self.c, fs)
        self.has_up, self.has_down = self.z + 1 < line, self.z > 0

    def others(self):
        return [lax.rem(self.fs + step, 2 * self.line) for step in range(1, 2 * self.line)]

    def greet(self):
        barrier = pltpu.get_barrier_semaphore()
        known = [(self.dp, other) for other in self.others()] + [self.xway, self.core]
        for device in known:
            pl.semaphore_signal(barrier, inc=1, device_id=device, device_id_type=MESH)
        pl.semaphore_wait(barrier, len(known))


class Panel:
    def __init__(self, which, part, width):
        self.which, self.part, self.width = which, part, width

    def cols(self, cut):
        base = 0 if self.which == 3 else self.part * self.width
        if cut is None:
            return pl.ds(base, self.width)
        return pl.ds(pl.multiple_of(base + cut[0], 128), cut[1])

    def of(self, ref, *lead, cut=None):
        if self.which == 3:
            return ref.at[(*lead, self.part, ALL, self.cols(cut))]
        return ref.at[(*lead, ALL, self.cols(cut))]


class Cuts:
    def __init__(self, width, x, thirds):
        third = width // 3
        self.half = (x * (width // 2), width // 2)
        self.other_half = ((1 - x) * (width // 2), width // 2)
        self.wide, self.outer, self.other_outer = self.half, self.half, self.other_half
        if thirds:
            self.wide = (x * third, 2 * third)
            self.outer = (x * 2 * third, third)
            self.other_outer = ((1 - x) * 2 * third, third)


def ds(cut):
    return pl.ds(pl.multiple_of(cut[0], 128), cut[1])


def panels_of(layer_shapes, width, order):
    made = []
    for which in order:
        count = layer_shapes[which]
        made += [Panel(which, part, width) for part in range(count)]
    return made


class Gather:
    def __init__(self, at, place, own, panel, full, way, send, recv, near):
        self.at, self.place, self.own, self.panel, self.full = at, place, own, panel, full
        self.send, self.recv, self.near = send, recv, near
        self.split, self.older = way == SPLIT, None
        split = self.split
        cuts = Cuts(panel.width, place.x, way == THIRDS)
        self.lane, self.other_lane = (cuts.half, cuts.other_half) if split else (None, None)
        self.over_y = cuts.half if split else cuts.wide
        self.over_x, self.from_x = (cuts.half, cuts.other_half) if split else (cuts.outer, cuts.other_outer)

    def view(self, block, y, c, cut=None):
        return self.panel.of(self.full, block, y, c, cut=cut)

    def sent(self, slot):
        return self.send.at[self.at % AG_RING, slot]

    def got(self, slot):
        return self.recv.at[self.at, slot]

    def line_copy(self, way, block):
        p = self.place
        ref = self.view(block, p.y, p.c, self.lane)
        return remote(ref, ref, self.sent(block + way), self.got(block), (p.up, p.down)[way])

    def near_copy(self):
        p = self.place
        mine = self.panel.of(self.own, p.c, cut=self.lane)
        return pltpu.make_async_copy(mine, self.view(p.z, p.y, p.c, self.lane), self.near.at[self.at % AG_RING])

    def far_copy(self, kind):
        p, line = self.place, self.place.line
        ref, device = {
            "y": (lambda: (self.view(ALL, p.y, p.c, self.over_y), p.yway)),
            "x": (lambda: (self.view(ALL, 1 - p.y, p.c, self.over_x), p.xway)),
            "x_own": (lambda: (self.view(ALL, p.y, p.c, self.lane), p.xway)),
            "core_own": (lambda: (self.view(ALL, p.y, p.c), p.core)),
            "core": (lambda: (self.view(ALL, 1 - p.y, p.c), p.core)),
        }[kind]()
        slot = ("y", "x", "x_own", "core_own", "core").index(kind)
        return remote(ref, ref, self.sent(line + 1 + slot), self.got(line + slot), device)

    def landed(self, kind):
        p, line = self.place, self.place.line
        ref = {
            "y": lambda: self.view(ALL, 1 - p.y, p.c, self.over_y),
            "x": lambda: self.view(ALL, 1 - p.y, p.c, self.from_x),
            "x_own": lambda: self.view(ALL, p.y, p.c, self.other_lane),
            "core_own": lambda: self.view(ALL, p.y, 1 - p.c),
            "core": lambda: self.view(ALL, 1 - p.y, 1 - p.c),
        }[kind]()
        slot = ("y", "x", "x_own", "core_own", "core").index(kind)
        return remote(ref, ref, self.sent(line + 1 + slot), self.got(line + slot), p.core)

    def kinds(self):
        return ("y", "x", "x_own", "core_own", "core") if self.split else ("y", "x", "core_own", "core")

    def first(self):
        p = self.place
        if self.older is not None:
            self.older.drain()
        self.near_copy().start()
        mine = self.panel.of(self.own, p.c, cut=self.lane)
        there = self.view(p.z, p.y, p.c, self.lane)
        for way, able, device in ((0, p.has_up, p.up), (1, p.has_down, p.down)):
            copy = functools.partial(remote, mine, there, self.sent(p.z + way), self.got(p.z), device)
            pl.when(able)(lambda copy=copy: copy().start())

    def hop(self, k):
        p = self.place

        def pass_on(way, block, more):
            self.line_copy(way, block).wait_recv()
            pl.when(more)(lambda: self.line_copy(way, block).start())

        pl.when(p.z - k >= 0)(lambda: pass_on(0, p.z - k, p.has_up))
        pl.when(p.z + k < p.line)(lambda: pass_on(1, p.z + k, p.has_down))
        if k == p.line - 1:
            self.near_copy().wait()
            self.far_copy("y").start()
            self.far_copy("x_own" if self.split else "core_own").start()

    def cross(self):
        self.landed("y").wait_recv()
        self.far_copy("x").start()
        if self.split:
            self.landed("x_own").wait_recv()
            self.far_copy("core_own").start()

    def share(self):
        self.landed("x").wait_recv()
        self.far_copy("core").start()

    def stages(self):
        hops = [functools.partial(self.hop, k) for k in range(1, self.place.line)]
        return [self.first, *hops, self.cross, self.share]

    def arrive(self):
        self.landed("core_own").wait_recv()
        self.landed("core").wait_recv()

    def drain(self):
        p = self.place

        def body(block, carry):
            pl.when(p.has_up & (block <= p.z))(lambda: self.line_copy(0, block).wait_send())
            pl.when(p.has_down & (block >= p.z))(lambda: self.line_copy(1, block).wait_send())
            return carry

        lax.fori_loop(0, p.line, body, 0)
        for kind in self.kinds():
            self.far_copy(kind).wait_send()


HALVES, THIRDS, SPLIT = range(3)
AG_RING = 12
RINGS = dict(own=11, away=5, other=2, from_x=4, from_y=4, line_in=4, last=3, total=3)
SUM_SEMS = dict(
    core=(RINGS["away"], 1, RINGS["other"], 1),
    x=(RINGS["away"], 1, RINGS["from_x"], 1),
    y=(RINGS["away"], 1, RINGS["from_y"], 1),
    line=(RINGS["own"], 4, RINGS["line_in"], 5),
    last=(RINGS["own"], 1, RINGS["last"], 1),
    out=(RINGS["total"], 1, 24, 1),
)


def starts_of(kinds):
    found, out_at, in_at = {}, 0, 0
    for name, (out_ring, out_each, in_ring, in_each) in kinds.items():
        found[name] = (out_at, in_at)
        out_at, in_at = out_at + out_ring * out_each, in_at + in_ring * in_each
    return found, out_at, in_at


SUM_STARTS, SUM_SENDS, SUM_ARRIVALS = starts_of(SUM_SEMS)
CREDITS, CREDIT_COUNT = {}, 0
for _name in ("other", "from_x", "from_y", "line_up", "line_down", "last"):
    CREDITS[_name] = CREDIT_COUNT
    CREDIT_COUNT += RINGS["line_in" if _name[:4] == "line" else _name]


class Reduce:
    def __init__(self, at, count, place, panel, way, terms, out, bufs, credit, send, recv, near):
        self.at, self.count, self.place, self.panel, self.terms, self.out = at, count, place, panel, terms, out
        self.credit, self.send, self.recv, self.near = credit, send, recv, near
        self.older, self.flush = {}, None
        self.b = {name: ref.at[at % RINGS[name]] for name, ref in bufs.items()}
        cuts = Cuts(panel.width, place.x, way == THIRDS)
        self.split = way == SPLIT
        self.wide, self.outer, self.other_outer = ds(cuts.wide), ds(cuts.outer), ds(cuts.other_outer)
        self.lane = self.outer if self.split else pl.ds(0, panel.width)
        if self.split:
            self.wide = pl.ds(0, panel.width)
        self.lanes, over_y = (panel.width // 2, panel.width) if self.split else (panel.width, cuts.wide[1])
        self.b["from_x"] = self.b["from_x"].at[:, :, 0 : cuts.outer[1]]
        self.b["from_y"] = self.b["from_y"].at[:, :, 0:over_y]
        self.b["last"] = self.b["last"].at[:, 0 : self.lanes]

    def spend(self, name, ring):
        if self.at >= RINGS[ring]:
            pl.semaphore_wait(self.credit.at[CREDITS[name] + self.at % RINGS[ring]], 1)

    def grant(self, name, ring, device):
        if self.at + RINGS[ring] < self.count:
            credit = self.credit.at[CREDITS[name] + self.at % RINGS[ring]]
            pl.semaphore_signal(credit, inc=1, device_id=device, device_id_type=MESH)

    def sems(self, name, slot=(0, 0)):
        out_ring, out_each, in_ring, in_each = SUM_SEMS[name]
        out_at, in_at = SUM_STARTS[name]
        out_at += self.at % out_ring * out_each + slot[0]
        in_at += self.at % in_ring * in_each + slot[1]
        return self.send.at[out_at], self.recv.at[in_at]

    def core_copy(self):
        p = self.place
        return remote(self.panel.of(self.terms, ALL, ALL, 1 - p.c), self.b["other"], *self.sems("core"), p.core)

    def near_copy(self, away):
        p = self.place
        src = self.panel.of(self.terms, ALL, (1 - p.y) if away else p.y, p.c)
        return pltpu.make_async_copy(src, self.b["away" if away else "own"], self.near.at[self.at % 2 * 2 + int(away)])

    def x_copy(self):
        p = self.place
        src = self.b["own" if self.split else "away"].at[:, :, self.other_outer]
        return remote(src, self.b["from_x"], *self.sems("x"), p.xway)

    def y_copy(self):
        p = self.place
        return remote(self.b["away"].at[:, :, self.wide], self.b["from_y"], *self.sems("y"), p.yway)

    def came(self, way, block):
        slot = block - 1 if way == 0 else self.place.line - 1 + block
        return self.b["line_in"].at[slot, :, 0 : self.lanes]

    def line_copy(self, way, block):
        p = self.place
        sems = self.sems("line", (block, block + 1 - way))
        src = self.b["own"].at[block, :, self.lane]
        return remote(src, self.came(way, block), *sems, (p.up, p.down)[way])

    def last_copy(self):
        p = self.place
        return remote(self.b["own"].at[p.z, :, self.lane], self.b["last"], *self.sems("last"), p.xway)

    def out_copy(self):
        ref = self.panel.of(self.out, self.place.c)
        return remote(self.b["total"], ref, *self.sems("out"), self.place.core)

    def out_landed(self):
        ref = self.panel.of(self.out, 1 - self.place.c)
        return remote(self.b["total"], ref, *self.sems("out"), self.place.core)

    def out_near(self):
        return pltpu.make_async_copy(self.b["total"], self.panel.of(self.out, self.place.c), self.near.at[4 + self.at % RINGS["total"]])

    def each(self, body):
        def step(block, carry):
            body(block)
            return carry

        lax.fori_loop(0, self.place.line, step, 0)

    def start(self):
        if self.flush is not None:
            self.flush()
        if "away" in self.older:
            self.older["away"].free_away()
        if "own" in self.older:
            self.older["own"].free_own()
        self.spend("other", "other")
        self.core_copy().start()
        self.near_copy(False).start()
        self.near_copy(True).start()

    def add_core(self):
        p, b = self.place, self.b
        self.near_copy(False).wait()
        self.near_copy(True).wait()
        self.core_copy().wait_recv()

        def body(block):
            b["away"][block] = b["away"][block] + b["other"][block, 1 - p.y]

        self.each(body)
        if self.split:
            self.spend("from_y", "from_y")
            self.y_copy().start()
        else:
            self.spend("from_x", "from_x")
            self.x_copy().start()

        def rest(block):
            b["own"][block] = b["own"][block] + b["other"][block, p.y]

        self.each(rest)
        self.grant("other", "other", p.core)

    def add_x(self):
        p, b = self.place, self.b
        self.x_copy().wait_recv()
        cols = self.outer

        def body(block):
            b["away"][block, :, cols] = b["away"][block, :, cols] + b["from_x"][block]

        self.each(body)
        self.spend("from_y", "from_y")
        self.y_copy().start()
        self.grant("from_x", "from_x", p.xway)

    def add_x_after(self):
        p, b = self.place, self.b
        self.x_copy().wait_recv()
        cols = self.outer

        def body(block):
            b["own"][block, :, cols] = b["own"][block, :, cols] + b["from_x"][block]

        self.each(body)
        self.grant("from_x", "from_x", p.xway)
        self.line_step(0)

    def add_y(self):
        p, b = self.place, self.b
        self.y_copy().wait_recv()
        cols = self.wide

        def body(block):
            b["own"][block, :, cols] = b["own"][block, :, cols] + b["from_y"][block]

        self.each(body)
        self.grant("from_y", "from_y", p.yway)
        if self.split:
            self.spend("from_x", "from_x")
            self.x_copy().start()
        else:
            self.line_step(0)

    def add_line(self, way, block):
        self.line_copy(way, block).wait_recv()
        own, lane = self.b["own"], self.lane
        own[block, :, lane] = own[block, :, lane] + self.came(way, block)[...]

    def line_step(self, k):
        p, line = self.place, self.place.line
        if k == 0:
            pl.when(p.has_up)(lambda: self.spend("line_up", "line_in"))
            pl.when(p.has_down)(lambda: self.spend("line_down", "line_in"))
        for way, steps_in, block, more in (
            (0, p.z, line - 1 - k + p.z, p.has_down),
            (1, line - 1 - p.z, k - (line - 1 - p.z), p.has_up),
        ):

            def body(way=way, block=block, more=more):
                pl.when(more)(lambda: self.add_line(way, block))
                self.line_copy(way, block).start()

            pl.when(steps_in <= k)(body)

    def own_step(self):
        p = self.place
        pl.when(p.has_down)(lambda: self.add_line(0, p.z))
        pl.when(p.has_up)(lambda: self.add_line(1, p.z))
        self.spend("last", "last")
        self.last_copy().start()
        pl.when(p.has_down)(lambda: self.grant("line_up", "line_in", p.down))
        pl.when(p.has_up)(lambda: self.grant("line_down", "line_in", p.up))

    def finish(self):
        p, b = self.place, self.b
        if "total" in self.older:
            self.older["total"].free_total()
        self.last_copy().wait_recv()
        if self.split:
            b["total"][:, self.outer] = b["own"][p.z, :, self.outer].astype(jnp.float32)
            b["total"][:, self.other_outer] = b["last"][...].astype(jnp.float32)
        else:
            b["total"][...] = b["own"][p.z].astype(jnp.float32) + b["last"][...].astype(jnp.float32)
        self.grant("last", "last", p.xway)
        self.out_copy().start()
        self.out_near().start()

    def stages(self):
        steps = [self.start, self.add_core]
        steps += [self.add_y, self.add_x_after] if self.split else [self.add_x, self.add_y]
        steps += [functools.partial(self.line_step, k) for k in range(1, self.place.line - 1)]
        return steps + [self.own_step, self.finish]

    def free_away(self):
        self.core_copy().wait_send()
        self.x_copy().wait_send()
        self.y_copy().wait_send()

    def free_own(self):
        p = self.place
        for block in range(p.line):
            pl.when(block > p.z)(lambda block=block: self.line_copy(0, block).wait_send())
            pl.when(block < p.z)(lambda block=block: self.line_copy(1, block).wait_send())
        self.last_copy().wait_send()

    def free_total(self):
        self.out_copy().wait_send()
        self.out_near().wait()


class Layer:
    def __init__(self, n, kept, weights, par, b_up, terms, g_par, g_bup):
        self.n, self.s = n, kept
        self.w_qkv, self.w_out, self.w_up, self.w_down = weights
        self.par, self.b_up = par, b_up
        self.g_qkv, self.g_out, self.g_up, self.g_down = terms
        self.g_par, self.g_bup = g_par, g_bup
        self.width, self.deep = self.w_out.shape[-1], self.w_up.shape[-1]
        self.pending = [None, None]

    def chunks(self, body):
        def step(i, carry):
            body(at(i, CHUNK))
            return carry

        lax.fori_loop(0, self.n // CHUNK, step, 0)

    def tiles(self, first, last, body):
        def step(i, carry):
            body(i)
            return carry

        lax.fori_loop(first, last, step, 0)

    def row(self, ref, i):
        return ref[i : i + 1, :]

    def tall_copy(self, ref, slot, t):
        stage = self.s["stage"].at[slot].reshape(*ref.shape[:4], self.width)
        cols = at(t, self.width)
        return pltpu.make_async_copy(stage, ref.at[:, :, :, :, cols], self.s["stage_sem"].at[slot])

    def wide_copy(self, ref, slot, t):
        stage = self.s["stage"].at[slot].reshape(*ref.shape[1:])
        return pltpu.make_async_copy(stage, ref.at[t], self.s["stage_sem"].at[slot])

    def put(self, make, slot, t, first, value):
        held = self.pending[slot]
        pl.when(t > first)(lambda: make(slot, t - 1).wait())
        if held is not None:
            pl.when(t == first)(lambda: held.wait())
        self.s["stage"][slot] = value.astype(jnp.bfloat16)
        make(slot, t).start()

    def put_all(self):
        for slot in range(2):
            if self.pending[slot] is not None:
                self.pending[slot].wait()
            self.pending[slot] = None

    def prepare(self, ends):
        s, width = self.s, self.width

        def mask(rows):
            shape = (CHUNK, self.n)
            at_row = lax.broadcasted_iota(jnp.int32, shape, 0) + rows.start
            at_col = lax.broadcasted_iota(jnp.int32, shape, 1)
            one, other = jnp.zeros(shape, jnp.int32), jnp.zeros(shape, jnp.int32)
            for end in ends:
                one = one + (at_row >= end).astype(jnp.int32)
                other = other + (at_col >= end).astype(jnp.int32)
            s["bias"][rows, :] = jnp.where(one == other, 0.0, -1e30)

        self.chunks(mask)
        s["rows"][0:1, 0:width] = self.par[4:5, :]
        s["rows"][0:1, width : 2 * width] = jnp.zeros((1, width), jnp.float32)
        s["rows"][0:1, 2 * width :] = self.par[5:6, :]

    def norm_parts(self, values):
        center = values - jnp.mean(values, axis=-1, keepdims=True)
        scale = lax.rsqrt(jnp.mean(center * center, axis=-1, keepdims=True) + 1e-05)
        return center * scale, scale

    def norm(self, src, dst, which):
        def body(rows):
            unit, _ = self.norm_parts(src[rows, :].astype(jnp.float32))
            dst[rows, :] = (unit * self.row(self.par, which) + self.row(self.par, 2 + which)).astype(jnp.bfloat16)

        self.chunks(body)

    def norm_a(self):
        self.norm(self.s["x"], self.s["a"], 0)

    def project(self, first, last):
        s = self.s
        queries = self.width // TILE

        def body(t):
            scale = jnp.where(t < queries, HEAD ** (-0.5), 1.0)
            found = dot(s["a"][...], flat(self.w_qkv[:, :, :, :, at(t)])) + s["rows"][0:1, at(t)]
            s["qkv"][:, at(t)] = (found * scale).astype(jnp.bfloat16)

        self.tiles(first, last, body)

    def turn_a(self):
        self.s["a_t"][...] = self.s["a"][...].T

    def pair(self, i, which):
        start = which * self.width + i * 128
        return self.s["qkv"].at[:, pl.ds(pl.multiple_of(start, 128), 128)]

    def own_lanes(self, value, head):
        lanes = lax.broadcasted_iota(jnp.int32, value.shape, 1)
        return jnp.where((lanes < HEAD) == (head == 0), value, jnp.zeros_like(value))

    def attend(self, first, last):
        s = self.s

        def body(i):
            q, k, v = (self.pair(i, which) for which in range(3))
            keys = [self.own_lanes(k[...], head) for head in range(2)]
            vals = [self.own_lanes(v[...], head) for head in range(2)]
            for part in range(self.n // TILE):
                cols = slice(part * TILE, part * TILE + TILE)
                mixed = None
                for head in range(2):
                    scores = dot(keys[head], q[cols, :], NT) + s["bias"][:, cols]
                    raised = jnp.exp(scores - jnp.max(scores, axis=0, keepdims=True))
                    share = 1.0 / jnp.sum(raised, axis=0, keepdims=True)
                    weights = (raised * share).astype(jnp.bfloat16)
                    s["wt"][2 * i + head, :, cols] = weights
                    found = dot(vals[head], weights, TN)
                    mixed = found if mixed is None else mixed + found
                s["o"][cols, at(i, 128)] = mixed.T.astype(jnp.bfloat16)

        self.tiles(first, last, body)

    def branch(self):
        s = self.s

        def body(t):
            found = dot(s["o"][...], flat(self.w_out[:, :, :, :, at(t)])) + self.par[6:7, at(t)]
            s["h"][:, at(t)] = s["x"][:, at(t)].astype(jnp.float32) + found

        self.tiles(0, self.width // TILE, body)
        s["o_t"][...] = s["o"][...].T

    def norm_c(self):
        self.norm(self.s["h"], self.s["c"], 1)

    def up(self, first, last):
        s = self.s

        def body(t):
            before = dot(s["c"][...], flat(self.w_up[:, :, :, :, at(t)])) + self.b_up[0:1, at(t)]
            chance = 0.5 + 0.5 * lax.erf(before * 0.7071067811865476)
            s["g"][:, at(t)] = (before * chance).astype(jnp.bfloat16)
            slope = chance + before * (jnp.exp(before * before * -0.5) * 0.3989422804014327)
            s["du"][:, at(t)] = slope.astype(jnp.bfloat16)

        self.tiles(first, last, body)

    def turn_c(self):
        self.s["c_t"][...] = self.s["c"][...].T

    def down(self):
        s = self.s

        def body(t):
            found = dot(s["g"][...], flat(self.w_down[:, :, :, :, :, at(t)])) + self.par[7:8, at(t)]
            s["a"][:, at(t)] = (s["h"][:, at(t)] + found).astype(jnp.bfloat16)

        self.tiles(0, self.width // TILE, body)

    def feed_back(self, first, last):
        s, width = self.s, self.width
        tall = functools.partial(self.tall_copy, self.g_up)

        def body(t):
            cols = at(t, width)
            grad = dot(s["dy"][...], flat(self.w_down[t]), NT)
            low = (grad * s["du"][:, cols].astype(jnp.float32)).astype(jnp.bfloat16)
            s["du"][:, cols] = low
            self.g_bup[0:1, cols] = jnp.sum(low.astype(jnp.float32), axis=0, keepdims=True)
            self.put(tall, 1, t, first, dot(s["c_t"][...], low))

        self.tiles(first, last, body)
        self.pending[1] = tall(1, last - 1)

    def down_terms(self, first, last):
        s, width = self.s, self.width
        wide = functools.partial(self.wide_copy, self.g_down)

        def body(t):
            self.put(wide, 0, t, first, dot(s["g"][:, at(t, width)], s["dy"][...], TN))

        self.tiles(first, last, body)
        self.pending[0] = wide(0, last - 1)

    def up_back(self):
        self.s["sums"][...] = dot(self.s["du"][...], flat(self.w_up[...]), NT)

    def norm_back(self, src, which, grad, rest, body_out):
        def body(rows):
            unit, scale = self.norm_parts(src[rows, :].astype(jnp.float32))
            came = grad[rows, :]
            gained = came * self.row(self.par, which)
            self.g_par[which : which + 1, :] += jnp.sum(came * unit, axis=0, keepdims=True)
            self.g_par[2 + which : 3 + which, :] += jnp.sum(came, axis=0, keepdims=True)
            inner = gained - jnp.mean(gained, axis=-1, keepdims=True)
            inner = inner - unit * jnp.mean(gained * unit, axis=-1, keepdims=True)
            body_out(rows, rest[rows, :].astype(jnp.float32) + inner * scale)

        self.chunks(body)

    def norm_c_back(self):
        s = self.s

        def keep(rows, grad):
            s["h"][rows, :] = grad
            low = grad.astype(jnp.bfloat16)
            s["c"][rows, :] = low
            self.g_par[6:7, :] += jnp.sum(low.astype(jnp.float32), axis=0, keepdims=True)
            self.g_par[7:8, :] += jnp.sum(s["dy"][rows, :].astype(jnp.float32), axis=0, keepdims=True)

        self.norm_back(s["h"], 1, s["sums"], s["dy"], keep)

    def branch_back(self):
        s = self.s
        tall = functools.partial(self.tall_copy, self.g_out)
        self.put(tall, 0, 0, 0, dot(s["o_t"][...], s["c"][...]))
        self.pending[0] = tall(0, 0)
        s["a"][...] = dot(s["c"][...], flat(self.w_out[...]), NT).astype(jnp.bfloat16)

    def attend_back(self, first, last):
        s, width = self.s, self.width

        def body(i):
            q, k, v = (self.pair(i, which) for which in range(3))
            came = s["a"].at[:, at(i, 128)]
            dq = dk = dv = None
            for head in range(2):
                vals = self.own_lanes(v[...], head)
                for part in range(self.n // TILE):
                    cols = slice(part * TILE, part * TILE + TILE)
                    grad = dot(vals, came[cols, :], NT)
                    weights = s["wt"][2 * i + head, :, cols].astype(jnp.float32)
                    product = weights * grad
                    inner = jnp.sum(product, axis=0, keepdims=True)
                    s["ds"][:, cols] = (product - weights * inner).astype(jnp.bfloat16)
                one_q = dot(self.own_lanes(k[...], head), s["ds"][...], TN)
                one_k = dot(s["ds"][...], self.own_lanes(q[...], head))
                one_v = dot(s["wt"][2 * i + head], self.own_lanes(came[...], head))
                dq, dk, dv = (one_q, one_k, one_v) if head == 0 else (dq + one_q, dk + one_k, dv + one_v)
            s["g"][:, at(i, 128)] = dq.T.astype(jnp.bfloat16) * HEAD ** (-0.5)
            s["g"][:, pl.ds(pl.multiple_of(width + i * 128, 128), 128)] = dk.astype(jnp.bfloat16)
            s["g"][:, pl.ds(pl.multiple_of(2 * width + i * 128, 128), 128)] = dv.astype(jnp.bfloat16)

        self.tiles(first, last, body)

    def project_terms(self, first, last):
        s, width = self.s, self.width
        tall = functools.partial(self.tall_copy, self.g_qkv)
        for t in range(first, last):
            grad = s["g"][:, t * width : (t + 1) * width]
            if t != 1:
                row = 4 + t // 2
                self.g_par[row : row + 1, :] = jnp.sum(grad.astype(jnp.float32), axis=0, keepdims=True)
            slot = (t + 1) % 2
            self.put(tall, slot, t, t, dot(s["a_t"][...], grad))
            self.pending[slot] = tall(slot, t)

    def project_back(self):
        s = self.s
        s["sums"][...] = dot(s["g"][:, 0 : 3 * self.width], flat(self.w_qkv[...]), NT)

    def norm_a_back(self):
        s = self.s

        def keep(rows, grad):
            s["h"][rows, :] = grad

        self.norm_back(s["x"], 0, s["sums"], s["h"], keep)


def layer_scratch(n, width, deep):
    low, full = jnp.bfloat16, jnp.float32
    return dict(
        a=pltpu.VMEM((n, width), low),
        a_t=pltpu.VMEM((width, n), low),
        qkv=pltpu.VMEM((n, 3 * width), low),
        bias=pltpu.VMEM((n, n), full),
        wt=pltpu.VMEM((width // HEAD, n, n), low),
        ds=pltpu.VMEM((n, n), low),
        o=pltpu.VMEM((n, width), low),
        o_t=pltpu.VMEM((width, n), low),
        h=pltpu.VMEM((n, width), full),
        c=pltpu.VMEM((n, width), low),
        c_t=pltpu.VMEM((width, n), low),
        g=pltpu.VMEM((n, deep), low),
        du=pltpu.VMEM((n, deep), low),
        sums=pltpu.VMEM((n, width), full),
        rows=pltpu.VMEM((8, 3 * width), full),
        stage=pltpu.VMEM((2, width, width), low),
        stage_sem=pltpu.SemaphoreType.DMA((2,)),
    )


def cut(kept, n):
    cuts = dict(kept)
    for name in ("a", "qkv", "o", "h", "c", "g", "du", "sums"):
        cuts[name] = kept[name].at[0:n]
    for name in ("a_t", "o_t", "c_t"):
        cuts[name] = kept[name].at[:, 0:n]
    for name in ("bias", "ds"):
        cuts[name] = kept[name].at[0:n, 0:n]
    cuts["wt"] = kept["wt"].at[:, 0:n, 0:n]
    return cuts


ORDER = (0, 1, 2, 3)
BACK = (3, 2, 1, 0)


class SmallSum:
    def __init__(self, place, parts, land, line_land, out, send, recv):
        self.place, self.parts, self.land, self.line_land, self.out = place, parts, land, line_land, out
        self.send, self.recv = send, recv

    def near(self, step):
        p = self.place
        device = (p.core, p.xway, p.yway)[step]
        return remote(self.parts.at[step], self.land.at[step], self.send.at[step], self.recv.at[step], device)

    def far(self, step):
        p = self.place
        other = lax.rem(p.z + step, p.line)
        device = (p.dp, other * 2 + p.y)
        src = self.parts.at[3]
        return remote(src, self.line_land.at[p.z], self.send.at[3 + other], self.recv.at[3 + p.z], device)

    def from_far(self, step):
        p = self.place
        other = lax.rem(p.z + step, p.line)
        device = (p.dp, other * 2 + p.y)
        src = self.parts.at[3]
        return remote(src, self.line_land.at[other], self.send.at[3 + other], self.recv.at[3 + other], device)

    def stage(self, step):
        p = self.place
        if step:
            if step <= 3:
                self.near(step - 1).wait_recv()
                self.parts[step] = self.parts[step - 1] + self.land[step - 1]
        if step < 3:
            self.near(step).start()
        if step == 3:
            for other in range(1, p.line):
                self.far(other).start()
            self.line_land[p.z] = self.parts[3]
        if step == 4:
            for other in range(1, p.line):
                self.from_far(other).wait_recv()
            gains, biases, b_up = self.out
            piece, deep = gains.shape[-1], b_up.shape[-1]
            wide = self.line_land.shape[-1] // deep

            def mine(block):
                for block_at in range(p.line):
                    part = self.line_land[block_at, :, 0:8, block * piece : (block + 1) * piece]
                    row, start = 8 + block // wide, block % wide * deep
                    up = self.line_land[block_at, :, row, start : start + deep]
                    if block_at == 0:
                        total, total_up = part, up
                    else:
                        total, total_up = total + part, total_up + up
                gains[...] = total[:, 0:2]
                biases[...] = total[:, 2:8]
                b_up[...] = total_up

            for block in range(2 * p.line):
                pl.when(p.fs == block)(functools.partial(mine, block))
            for near in range(3):
                self.near(near).wait_send()
            for other in range(1, p.line):
                self.far(other).wait_send()


def whole_kernel(line, sizes, names, ring_names, *refs):
    take = list(refs)

    def some(count):
        found = take[:count]
        del take[:count]
        return found

    owned = some(4)
    gains, biases, own_up, lengths, x_t, dy_t, x_i, dy_i = some(8)
    y_i, y_t, gx_i, gx_t = some(4)
    shares, small_out = some(4), some(3)
    far_weights, terms_t, terms_i = some(4), some(4), some(4)
    weights = some(4)
    kept = dict(zip(names, some(len(names))))
    bufs = dict(zip(ring_names, some(len(ring_names))))
    pad_x, pad_dy, small, small_all, par, b_up, g_parts, g_land, g_line = some(9)
    ag_send, ag_recv, ag_near, rs_send, rs_recv, rs_near, credit = some(7)
    s_send, s_recv, g_send, g_recv, load_sem, io_sem = some(6)
    n_t, n_i, counts = sizes
    width = weights[1].shape[-1]
    place = Place(line)
    small[...] = jnp.zeros_like(small)
    small[:, 0:2, 0 : gains.shape[2]] = gains[...].astype(jnp.float32)
    small[:, 2:8, 0 : biases.shape[2]] = biases[...].astype(jnp.float32)
    for j in range(own_up.shape[1] // 128):
        small[:, 8 + j, :] = own_up[:, j * 128 : (j + 1) * 128].astype(jnp.float32)
    place.greet()

    smalls = []
    for step, other in enumerate(place.others()):
        copy = remote(small, small_all.at[place.fs], s_send.at[step], s_recv.at[place.fs], (place.dp, other))
        copy.start()
        smalls.append(copy)

    ahead, back = panels_of(counts, width, ORDER), panels_of(counts, width, BACK)
    base = len(ahead)
    units, sums = [], []
    for u in range(2 * base):
        panel, layer, into = ahead[u % base], u // base, (weights, far_weights)[u // base]
        own, full = owned[panel.which].at[layer], into[panel.which]
        units.append(Gather(u, place, own, panel, full, GATHER_WAYS[u], ag_send, ag_recv, ag_near))
        units[u].older = units[u - AG_RING] if u >= AG_RING else None
    for u in range(2 * base):
        panel, layer, terms = back[u % base], u // base, (terms_i, terms_t)[u // base]
        share, term = shares[panel.which].at[layer], terms[panel.which]
        sems = credit, rs_send, rs_recv, rs_near
        sums.append(Reduce(u, 2 * base, place, panel, SUM_WAYS[u], term, share, bufs, *sems))
        sums[u].older = {name: sums[u - RINGS[name]] for name in ("away", "own", "total") if u >= RINGS[name]}

    def layer_of(layer, n, view, terms):
        grads = g_parts.at[0, layer, 0:8], b_up.at[2 + layer]
        return Layer(n, view, weights, par.at[layer], b_up.at[layer], terms, *grads)

    text = layer_of(1, n_t, {**kept, "x": x_t.at[0], "dy": dy_t.at[0]}, terms_t)
    view = {**cut(kept, n_i), "x": pad_x, "dy": pad_dy}
    image = layer_of(0, n_i, view, terms_i)
    for u, unit in enumerate(sums):
        unit.flush = image.put_all if u < base else text.put_all
    starts = [sum(counts[:which]) for which in range(5)]
    heads, tiles, panels = width // 128, width // TILE, counts[3]
    y_copy = pltpu.make_async_copy(kept["a"], y_t.at[0], io_sem.at[0])
    grad_copy = pltpu.make_async_copy(kept["h"], gx_t.at[0], io_sem.at[1])
    loads = [pltpu.make_async_copy(far_weights[i], weights[i], load_sem.at[i]) for i in range(4)]

    steps = []

    def add(body, *args, needs=()):
        def step():
            for unit in needs:
                units[unit].arrive()
            body(*args)

        step.needs = tuple(needs)
        steps.append(step)

    def first():
        small_all[place.fs] = small[...]
        g_parts[0] = jnp.zeros(g_parts.shape[1:], jnp.float32)
        for step, other in enumerate(place.others()):
            remote(small, small_all.at[other], s_send.at[step], s_recv.at[other], (place.dp, other)).wait_recv()
        piece, deep = width // (2 * line), b_up.shape[-1] // (2 * line)
        for layer in range(2):
            for block in range(2 * line):
                par[layer, :, block * piece : (block + 1) * piece] = small_all[block, layer, 0:8, 0:piece]
                for j in range(deep // 128):
                    start = block * deep + j * 128
                    b_up[layer, 0:1, start : start + 128] = small_all[block, layer, 8 + j : 9 + j, :]
        for src, dst in ((x_i, pad_x), (dy_i, pad_dy)):
            have = src.shape[1]
            if have < n_i:
                cut_at = have // 16 * 16
                dst[cut_at:, :] = jnp.zeros((n_i - cut_at, width), jnp.bfloat16)
            dst[0:have, :] = src[0]
        image.prepare([x_i.shape[1]])
        image.norm_a()

    def image_out():
        image.down()
        y_i[0] = view["a"][0 : y_i.shape[1], :]

    def image_last():
        image.norm_a_back()
        gx_i[0] = view["h"][0 : gx_i.shape[1], :]

    def text_first():
        ends = [lengths[0, 0]]
        for j in range(1, lengths.shape[1]):
            ends.append(ends[-1] + lengths[0, j])
        text.prepare(ends)
        text.norm_a()

    def waiting(load, body):
        def step(*args):
            load.wait()
            body(*args)

        return step

    def text_out():
        loads[3].wait()
        text.down()
        y_copy.start()

    def text_branch_back():
        y_copy.wait()
        text.branch_back()

    def text_last():
        text.norm_a_back()
        grad_copy.start()
        for layer in range(2):
            for j in range(b_up.shape[-1] // width):
                g_parts[0, layer, 8 + j : 9 + j, :] = b_up[2 + layer, 0:1, j * width : (j + 1) * width]

    def load(which):
        add(loads[which].start, needs=range(base + starts[which], base + starts[which + 1]))

    add(first)
    for part in range(3):
        add(image.project, part * tiles, (part + 1) * tiles, needs=(part,))
    add(image.turn_a)
    for i in range(0, heads, 2):
        add(image.attend, i, i + 2)
    add(image.branch, needs=(starts[1],))
    add(image.norm_c)
    for part in range(panels):
        add(image.up, part * tiles, (part + 1) * tiles, needs=(starts[2] + part,))
        add(image.down_terms, part, part + 1)
    add(image.turn_c)
    add(image_out, needs=range(starts[3], starts[4]))
    for part in range(panels):
        add(image.feed_back, part, part + 1)
    add(image.up_back)
    add(image.norm_c_back)
    add(image.branch_back)
    for i in range(0, heads, 2):
        add(image.attend_back, i, i + 2)
    for part in range(3):
        add(image.project_terms, part, part + 1)
    add(image.project_back)
    add(image_last)
    load(0)
    add(text_first)
    for part in range(3):
        body = waiting(loads[0], text.project) if part == 0 else text.project
        add(body, part * tiles, (part + 1) * tiles)
    add(text.turn_a)
    load(1)
    for i in range(heads):
        add(text.attend, i, i + 1)
    add(waiting(loads[1], text.branch))
    load(2)
    add(text.norm_c)
    for part in range(panels):
        add(waiting(loads[2], text.up) if part == 0 else text.up, part * tiles, (part + 1) * tiles)
        add(text.down_terms, part, part + 1)
    load(3)
    add(text.turn_c)
    add(text_out)
    for part in range(panels):
        add(text.feed_back, part, part + 1)
    add(text.up_back)
    add(text.norm_c_back)
    add(text_branch_back)
    for i in range(heads):
        add(text.attend_back, i, i + 1)
    for part in range(3):
        add(text.project_terms, part, part + 1)
    add(text.project_back)
    add(text_last)
    small_sum = SmallSum(place, g_parts, g_land, g_line, small_out, g_send, g_recv)
    for stage in range(5):
        add(small_sum.stage, stage)

    drive(steps, [unit.stages() for unit in units], [unit.stages() for unit in sums])

    for unit in sums[-RINGS["away"] :]:
        unit.free_away()
    for unit in sums[-RINGS["own"] :]:
        unit.free_own()
    for unit in sums[-RINGS["total"] :]:
        unit.free_total()
    for unit in sums:
        unit.out_landed().wait_recv()
    for unit in units[-AG_RING:]:
        unit.drain()
    for copy in smalls:
        copy.wait_send()
    grad_copy.wait()


GATHER_WAYS = (
    1, 2, 1, 1, 2, 1, 2, 1, 1, 2, 1, 2, 1, 0, 1, 0, 1, 0, 1, 0, 1, 0, 1, 0,
)
SUM_WAYS = (
    0, 0, 0, 0, 0, 0, 0, 0, 0, 0, 0, 0, 1, 2, 0, 1, 2, 0, 1, 2, 0, 1, 2, 0,
)
PLAN = (
    0, 10, 20, 30, 40, 50, 60, 70, -1, 1, 11, 21, 31, 41, 51, 61, 71, 2, 12, 22, 32, 42, 52, 62, 72, 3, 13, 23,
    33, 43, 53, 63, 73, 4, 14, 24, 5, 80, -1, 15, 90, -1, 25, 34, 100, 81, -1, 44, 91, -1, -1, 35, 82, 110, 83,
    92, -1, 54, 93, 101, 45, -1, 64, 111, 102, -1, 55, 103, 112, 120, 130, 113, -1, -1, 74, -1, -1, -1, 121, 84,
    65, 131, 140, -1, 122, -1, 94, 132, 141, 123, 75, 150, -1, 85, 104, 133, 142, 160, -1, -1, 151, 1000, 95,
    114, 170, 1010, 143, 105, 180, 161, 1001, 1020, 152, 124, 1011, 171, 115, 190, -1, 134, 153, 162, 181, 1002,
    1021, 1030, 125, 200, -1, 144, 172, -1, 1031, 1012, 1040, 191, -1, 154, 163, -1, 135, 182, 210, -1, 173,
    201, 1003, 1041, 1050, 1022, -1, 192, 1060, 1013, -1, 145, 183, 1051, 220, -1, 211, 1004, 1032, 164, 202,
    1014, -1, 193, -1, 155, 174, 221, 1005, 230, 212, 1070, 1015, -1, 1042, 203, 1023, 1061, -1, -1, 222, -1,
    184, 1006, 1052, -1, 165, 231, -1, -1, 213, 1024, 1033, 1071, 1080, 1016, 175, -1, 223, -1, 194, 232, 1062,
    -1, 233, 1025, 1090, 185, -1, 1043, 1034, 1081, -1, -1, 1007, -1, -1, 204, 1026, 1072, -1, 1017, 1044, -1,
    1035, 1053, 1091, 1100, -1, 195, -1, 214, 1045, -1, -1, 1036, 1082, -1, 205, 224, 1027, 1046, 1054, -1,
    1110, 1063, 1101, -1, 1092, -1, 234, 1055, -1, 215, 1064, -1, 1073, 1037, 1111, -1, 1056, 225, -1, 1065,
    1083, 1047, 1120, 1074, 1130, 1093, 1102, 1121, 1084, 1066, 1140, 1131, 1075, 235, 1150, -1, 1094, 1103,
    1141, -1, -1, 1057, 1067, 1076, 1085, 1095, 1104, 1112, 1122, 1132, -1, -1, 1077, 1086, 1113, 1142, 1151,
    1096, 1160, -1, 1105, -1, 1087, 1114, 1123, 1133, 1170, -1, 1097, 1106, 1115, 1152, 1161, 1171, 1124, -1,
    1134, 1143, 1180, 1190, 1116, 1107, -1, 1125, 1135, 1181, -1, 1144, 1153, 1200, -1, 1117, 1126, 1136, 1191,
    -1, 1145, -1, 1127, 1137, 1154, 1162, 1172, 1182, -1, 1146, -1, 1155, -1, 1163, -1, 1147, 1192, 1164, 1201,
    1210, 1156, -1, 1173, 1165, 1211, -1, 1166, 1174, 1220, 1230, 1183, 1193, -1, 1202, -1, -1, 1157, 1175,
    1184, 1194, -1, 1167, 1176, 1203, 1212, 1185, -1, 1177, 1195, 1204, 1186, 1221, 1231, -1, 1187, 1213, 1196,
    1205, 1214, 1197, 1222, 1232, 1206, 1215, 1223, 1233, 1224, 1207, 1234, 1225, 1216, 1235, 1217, 1226, 1227,
    1236, 1237,
)


def drive(steps, gathers, sums):
    at_step = 0
    for code in PLAN:
        if code < 0:
            steps[at_step]()
            at_step += 1
        elif code < 1000:
            gathers[code // 10][code % 10]()
        else:
            sums[code // 10 - 100][code % 10]()


def padded(rows):
    return -(-rows // TILE) * TILE


def whole(line, x_i, dy_i, x_t, dy_t, lengths, owned, gains, biases, b_up):
    width, deep = owned[1].shape[2], owned[2].shape[2]
    rows = owned[1].shape[1] // 2
    counts = (3, 1, deep // width, deep // width)
    own = [w.reshape(2, 2, rows, w.shape[2]) for w in owned[:3]] + [owned[3].reshape(2, 2, counts[3], rows, width)]
    n_t, n_i = padded(x_t.shape[1]), padded(x_i.shape[1])
    low, full = jnp.bfloat16, jnp.float32
    kept = layer_scratch(n_t, width, deep)
    fulls = [(line, 2, *w.shape[1:]) for w in own]
    rings = dict(
        own=pltpu.VMEM((RINGS["own"], line, rows, width), low),
        away=pltpu.VMEM((RINGS["away"], line, rows, width), low),
        other=pltpu.VMEM((RINGS["other"], line, 2, rows, width), low),
        from_x=pltpu.VMEM((RINGS["from_x"], line, rows, width // 2), low),
        from_y=pltpu.VMEM((RINGS["from_y"], line, rows, width), low),
        line_in=pltpu.VMEM((RINGS["line_in"], 2 * line - 2, rows, width), low),
        last=pltpu.VMEM((RINGS["last"], rows, width), low),
        total=pltpu.VMEM((RINGS["total"], rows, width), full),
    )
    panels = 2 * sum(counts)
    small_rows = 8 + deep // width
    small_rows += -small_rows % 8
    own_rows = 8 + b_up.shape[1] // 128
    own_rows += -own_rows % 8
    anywhere, inside = pl.BlockSpec(memory_space=pl.ANY), pl.BlockSpec(memory_space=pltpu.VMEM)
    dma = pltpu.SemaphoreType.DMA
    outs = [
        jax.ShapeDtypeStruct(x_i.shape, low),
        jax.ShapeDtypeStruct(x_t.shape, low),
        jax.ShapeDtypeStruct(x_i.shape, full),
        jax.ShapeDtypeStruct(x_t.shape, full),
        *[jax.ShapeDtypeStruct(w.shape, full) for w in own],
        *[jax.ShapeDtypeStruct(v.shape, full) for v in (gains, biases, b_up)],
        *[jax.ShapeDtypeStruct(shape, low) for shape in fulls * 3],
    ]
    scratch = [
        *[pltpu.VMEM(shape, low) for shape in fulls],
        *kept.values(),
        *rings.values(),
        pltpu.VMEM((n_i, width), low),
        pltpu.VMEM((n_i, width), low),
        pltpu.VMEM((2, own_rows, 128), full),
        pltpu.VMEM((2 * line, 2, own_rows, 128), full),
        pltpu.VMEM((2, 8, width), full),
        pltpu.VMEM((4, 1, deep), full),
        pltpu.VMEM((4, 2, small_rows, width), full),
        pltpu.VMEM((3, 2, small_rows, width), full),
        pltpu.VMEM((line, 2, small_rows, width), full),
        dma((AG_RING, line + 6)),
        dma((panels, line + 5)),
        dma((AG_RING,)),
        dma((SUM_SENDS,)),
        dma((SUM_ARRIVALS,)),
        dma((4 + RINGS["total"],)),
        pltpu.SemaphoreType.REGULAR((CREDIT_COUNT,)),
        dma((2 * line,)),
        dma((2 * line,)),
        dma((3 + line,)),
        dma((3 + line,)),
        dma((4,)),
        dma((2,)),
    ]
    found = pl.pallas_call(
        functools.partial(whole_kernel, line, (n_t, n_i, counts), list(kept), list(rings)),
        out_shape=outs,
        in_specs=[anywhere] * 4 + [inside] * 3 + [pl.BlockSpec(memory_space=pltpu.SMEM)] + [inside] * 4,
        out_specs=[inside, anywhere, inside, anywhere] + [anywhere] * 4 + [inside] * 3 + [anywhere] * 12,
        scratch_shapes=scratch,
        compiler_params=pltpu.CompilerParams(collective_id=0, has_side_effects=True, vmem_limit_bytes=63 * 2**20),
    )(*own, gains, biases, b_up, lengths, x_t, dy_t, x_i, dy_i)
    found = hand_over(found[:11])
    shares = [share.reshape(w.shape) for share, w in zip(found[4:8], owned)]
    return (*found[:4], *shares, *found[8:])


def hand_over(found):
    def kernel(*refs):
        count = len(found)
        held, (there, back) = refs[2 * count : -2], refs[-2:]
        copies = [pltpu.make_async_copy(refs[i], held[i], there.at[i]) for i in range(count)]
        for copy in copies:
            copy.start()
        outs = [pltpu.make_async_copy(held[i], refs[count + i], back.at[i]) for i in range(count)]
        for copy, out in zip(copies, outs):
            copy.wait()
            out.start()
        for out in outs:
            out.wait()

    anywhere = pl.BlockSpec(memory_space=pl.ANY)
    sems = pltpu.SemaphoreType.DMA((len(found),))
    return pl.pallas_call(
        kernel,
        out_shape=[jax.ShapeDtypeStruct(v.shape, v.dtype) for v in found],
        in_specs=[anywhere] * len(found),
        out_specs=[anywhere] * len(found),
        scratch_shapes=[pltpu.VMEM(v.shape, v.dtype) for v in found] + [sems, sems],
        compiler_params=pltpu.CompilerParams(vmem_limit_bytes=63 * 2**20),
    )(*found)


def normed(values, gain, shift):
    center = values - jnp.mean(values, axis=-1, keepdims=True)
    spread = jnp.mean(center * center, axis=-1, keepdims=True)
    return center * lax.rsqrt(spread + 1e-05) * gain + shift


def gelu_exact(values):
    return jax.nn.gelu(values, approximate=False)


def segment_ids(lengths, seq_len):
    bounds = jnp.cumsum(lengths, axis=-1)
    positions = jnp.arange(seq_len, dtype=jnp.int32)
    return jnp.sum((positions[None, :, None] >= bounds[:, None, :]).astype(jnp.int32), axis=-1)


def split_heads(values):
    batch, length, width = values.shape
    return values.reshape(batch, length, width // HEAD, HEAD)


def masked_scores(queries, keys_all, segment):
    scores = jnp.einsum(
        "bqhd,bkhd->bhqk",
        split_heads(queries),
        split_heads(keys_all),
        preferred_element_type=jnp.float32,
    )
    same = (segment[:, :, None] == segment[:, None, :])[:, None]
    return (jnp.where(same, scores, -1e30), same)


def attention(queries, keys_all, values_all, segment):
    scores, same = masked_scores(queries, keys_all, segment)
    largest = jnp.max(scores, axis=-1, keepdims=True)
    raised = jnp.exp(scores - largest)
    totals = jnp.sum(raised, axis=-1, keepdims=True)
    attn_weights = raised / totals
    log_total = largest + jnp.log(totals)
    mixed = jnp.einsum(
        "bhqk,bkhd->bqhd",
        attn_weights.astype(jnp.bfloat16),
        split_heads(values_all),
        preferred_element_type=jnp.float32,
    )
    return (mixed.reshape(queries.shape).astype(jnp.bfloat16), log_total)


def attention_back(queries, keys_all, values_all, segment, log_total, grad_mixed):
    scores, same = masked_scores(queries, keys_all, segment)
    attn_weights = jnp.where(same, jnp.exp(scores - log_total), 0.0)
    grad_heads = split_heads(grad_mixed)
    grad_weights = jnp.einsum(
        "bqhd,bkhd->bhqk", grad_heads, split_heads(values_all), preferred_element_type=jnp.float32
    )
    inner = jnp.sum(attn_weights * grad_weights, axis=-1, keepdims=True)
    grad_scores = (attn_weights * (grad_weights - inner)).astype(jnp.bfloat16)
    grad_queries = jnp.einsum(
        "bhqk,bkhd->bqhd", grad_scores, split_heads(keys_all), preferred_element_type=jnp.float32
    )
    grad_keys = jnp.einsum(
        "bhqk,bqhd->bkhd", grad_scores, split_heads(queries), preferred_element_type=jnp.float32
    )
    grad_values = jnp.einsum(
        "bhqk,bqhd->bkhd",
        attn_weights.astype(jnp.bfloat16),
        grad_heads,
        preferred_element_type=jnp.float32,
    )
    shape_rows = queries.shape
    return (
        grad_queries.reshape(shape_rows),
        grad_keys.reshape(shape_rows),
        grad_values.reshape(shape_rows),
    )


def forward_layer(inputs, weights, segment):
    qkv_weight, out_weight, up_weight, down_weight, gains, biases, up_bias = weights
    width = inputs.shape[-1]
    source = inputs.astype(jnp.float32)
    normed_a = normed(source, gains[0], biases[0]).astype(jnp.bfloat16)
    project = jnp.einsum("bld,de->ble", normed_a, qkv_weight, preferred_element_type=jnp.float32)
    queries = ((project[..., :width] + biases[2]) * HEAD ** (-0.5)).astype(jnp.bfloat16)
    keys_all = project[..., width : 2 * width].astype(jnp.bfloat16)
    values_all = (project[..., 2 * width :] + biases[3]).astype(jnp.bfloat16)
    mixed, log_total = attention(queries, keys_all, values_all, segment)
    hidden = (
        source
        + jnp.einsum("bld,de->ble", mixed, out_weight, preferred_element_type=jnp.float32)
        + biases[4]
    )
    normed_c = normed(hidden, gains[1], biases[1]).astype(jnp.bfloat16)
    before = (
        jnp.einsum("bld,df->blf", normed_c, up_weight, preferred_element_type=jnp.float32) + up_bias
    )
    activated = gelu_exact(before).astype(jnp.bfloat16)
    result = (
        hidden
        + jnp.einsum("blf,fd->bld", activated, down_weight, preferred_element_type=jnp.float32)
        + biases[5]
    )
    return (
        source,
        normed_a,
        queries,
        keys_all,
        values_all,
        log_total,
        mixed,
        hidden,
        normed_c,
        before,
        activated,
        result,
    )


def backward_layer(inputs, cotangent, weights, segment):
    qkv_weight, out_weight, up_weight, down_weight, gains, biases, up_bias = weights
    width = inputs.shape[-1]
    (
        source,
        normed_a,
        queries,
        keys_all,
        values_all,
        log_total,
        mixed,
        hidden,
        normed_c,
        before,
        activated,
        result,
    ) = forward_layer(inputs, weights, segment)
    grad_result = cotangent.astype(jnp.float32)
    grad_downw = jnp.einsum("blf,bld->fd", activated, cotangent, preferred_element_type=jnp.float32)
    grad_act = jnp.einsum("bld,fd->blf", cotangent, down_weight, preferred_element_type=jnp.float32)
    grad_before = jax.vjp(gelu_exact, before)[1](grad_act)[0].astype(jnp.bfloat16)
    grad_upw = jnp.einsum("bld,blf->df", normed_c, grad_before, preferred_element_type=jnp.float32)
    grad_upb = jnp.sum(grad_before.astype(jnp.float32), axis=(0, 1))
    grad_normc = jnp.einsum(
        "blf,df->bld", grad_before, up_weight, preferred_element_type=jnp.float32
    )
    hidden_back = jax.vjp(
        normed, hidden, gains[1].astype(jnp.float32), biases[1].astype(jnp.float32)
    )[1]
    grad_hidden_ln, grad_gain_two, grad_shift_two = hidden_back(grad_normc)
    grad_hidden = grad_result + grad_hidden_ln
    grad_branch = grad_hidden.astype(jnp.bfloat16)
    grad_outw = jnp.einsum("bld,ble->de", mixed, grad_branch, preferred_element_type=jnp.float32)
    grad_mixed = jnp.einsum(
        "ble,de->bld", grad_branch, out_weight, preferred_element_type=jnp.float32
    ).astype(jnp.bfloat16)
    grad_queries, grad_keys, grad_values = attention_back(
        queries, keys_all, values_all, segment, log_total, grad_mixed
    )
    grad_project = jnp.concatenate(
        [
            grad_queries.astype(jnp.bfloat16) * HEAD ** (-0.5),
            grad_keys.astype(jnp.bfloat16),
            grad_values.astype(jnp.bfloat16),
        ],
        axis=-1,
    )
    grad_qkvw = jnp.einsum(
        "bld,ble->de", normed_a, grad_project, preferred_element_type=jnp.float32
    )
    column_sums = jnp.sum(grad_project.astype(jnp.float32), axis=(0, 1))
    grad_norma = jnp.einsum(
        "ble,de->bld", grad_project, qkv_weight, preferred_element_type=jnp.float32
    )
    source_back = jax.vjp(
        normed, source, gains[0].astype(jnp.float32), biases[0].astype(jnp.float32)
    )[1]
    grad_source_ln, grad_gain_one, grad_shift_one = source_back(grad_norma)
    grad_inputs = grad_hidden + grad_source_ln
    grad_gains = jnp.stack([grad_gain_one, grad_gain_two])
    grad_biases = jnp.stack(
        [
            grad_shift_one,
            grad_shift_two,
            column_sums[:width],
            column_sums[2 * width :],
            jnp.sum(grad_branch.astype(jnp.float32), axis=(0, 1)),
            jnp.sum(grad_result, axis=(0, 1)),
        ]
    )
    return (
        result.astype(jnp.bfloat16),
        grad_inputs,
        (grad_qkvw, grad_outw, grad_upw, grad_downw, grad_gains, grad_biases, grad_upb),
    )


def fetch_weights(layer_index, w_qkv, w_out, w_up, w_down, gains, biases, b_up):
    return (
        lax.all_gather(w_qkv[layer_index], "fsdp", axis=0, tiled=True),
        lax.all_gather(w_out[layer_index], "fsdp", axis=0, tiled=True),
        lax.all_gather(w_up[layer_index], "fsdp", axis=0, tiled=True),
        lax.all_gather(w_down[layer_index], "fsdp", axis=0, tiled=True),
        lax.all_gather(gains[layer_index], "fsdp", axis=1, tiled=True),
        lax.all_gather(biases[layer_index], "fsdp", axis=1, tiled=True),
        lax.all_gather(b_up[layer_index], "fsdp", axis=0, tiled=True),
    )


def fetch_again(layer_index, w_qkv, w_out, w_up, w_down, gains, biases, b_up):
    return (
        lax.all_gather(w_qkv[layer_index], "fsdp", axis=0, tiled=True),
        lax.all_gather(w_out[layer_index], "fsdp", axis=0, tiled=True),
        lax.all_gather(w_up[layer_index], "fsdp", axis=0, tiled=True),
        lax.all_gather(w_down[layer_index], "fsdp", axis=0, tiled=True),
        lax.all_gather(gains[layer_index], "fsdp", axis=1, tiled=True),
        lax.all_gather(biases[layer_index], "fsdp", axis=1, tiled=True),
        lax.all_gather(b_up[layer_index], "fsdp", axis=0, tiled=True),
    )


def reduce_grads(gradients):
    shares = (
        lax.psum_scatter(gradients[0], "fsdp", scatter_dimension=0, tiled=True),
        lax.psum_scatter(gradients[1], "fsdp", scatter_dimension=0, tiled=True),
        lax.psum_scatter(gradients[2], "fsdp", scatter_dimension=0, tiled=True),
        lax.psum_scatter(gradients[3], "fsdp", scatter_dimension=0, tiled=True),
        lax.psum_scatter(gradients[4], "fsdp", scatter_dimension=1, tiled=True),
        lax.psum_scatter(gradients[5], "fsdp", scatter_dimension=1, tiled=True),
        lax.psum_scatter(gradients[6], "fsdp", scatter_dimension=0, tiled=True),
    )
    quarters = (
        lax.psum_scatter(
            shares[0].astype(jnp.bfloat16), "dp", scatter_dimension=0, tiled=True
        ).astype(jnp.float32),
        lax.psum_scatter(
            shares[1].astype(jnp.bfloat16), "dp", scatter_dimension=0, tiled=True
        ).astype(jnp.float32),
        lax.psum_scatter(
            shares[2].astype(jnp.bfloat16), "dp", scatter_dimension=0, tiled=True
        ).astype(jnp.float32),
        lax.psum_scatter(
            shares[3].astype(jnp.bfloat16), "dp", scatter_dimension=0, tiled=True
        ).astype(jnp.float32),
        lax.psum_scatter(
            shares[4].astype(jnp.bfloat16), "dp", scatter_dimension=1, tiled=True
        ).astype(jnp.float32),
        lax.psum_scatter(
            shares[5].astype(jnp.bfloat16), "dp", scatter_dimension=1, tiled=True
        ).astype(jnp.float32),
        lax.psum_scatter(
            shares[6].astype(jnp.bfloat16), "dp", scatter_dimension=0, tiled=True
        ).astype(jnp.float32),
    )
    return (
        lax.all_gather(quarters[0].astype(jnp.bfloat16), "dp", axis=0, tiled=True).astype(
            jnp.float32
        ),
        lax.all_gather(quarters[1].astype(jnp.bfloat16), "dp", axis=0, tiled=True).astype(
            jnp.float32
        ),
        lax.all_gather(quarters[2].astype(jnp.bfloat16), "dp", axis=0, tiled=True).astype(
            jnp.float32
        ),
        lax.all_gather(quarters[3].astype(jnp.bfloat16), "dp", axis=0, tiled=True).astype(
            jnp.float32
        ),
        lax.all_gather(quarters[4].astype(jnp.bfloat16), "dp", axis=1, tiled=True).astype(
            jnp.float32
        ),
        lax.all_gather(quarters[5].astype(jnp.bfloat16), "dp", axis=1, tiled=True).astype(
            jnp.float32
        ),
        lax.all_gather(quarters[6].astype(jnp.bfloat16), "dp", axis=0, tiled=True).astype(
            jnp.float32
        ),
    )


def plain(
    images,
    image_cot,
    captions,
    caption_cot,
    lengths,
    w_qkv,
    w_out,
    w_up,
    w_down,
    gains,
    biases,
    b_up,
):
    owned = (w_qkv, w_out, w_up, w_down, gains, biases, b_up)
    image_seg = jnp.zeros((images.shape[0], images.shape[1]), jnp.int32)
    caption_seg = segment_ids(lengths, captions.shape[1])
    first_weights = fetch_weights(0, *owned)
    image_out = forward_layer(images, first_weights, image_seg)[-1].astype(jnp.bfloat16)
    second_weights = fetch_weights(1, *owned)
    caption_out = forward_layer(captions, second_weights, caption_seg)[-1].astype(jnp.bfloat16)
    second_back = fetch_again(1, *owned)
    _, caption_grad, caption_terms = backward_layer(captions, caption_cot, second_back, caption_seg)
    caption_shares = reduce_grads(caption_terms)
    first_back = fetch_again(0, *owned)
    _, image_grad, image_terms = backward_layer(images, image_cot, first_back, image_seg)
    image_shares = reduce_grads(image_terms)
    stacked = tuple((jnp.stack([image_shares[index], caption_shares[index]]) for index in range(7)))
    return (image_out, caption_out, image_grad, caption_grad) + stacked


def kernels_fit(mesh, w_qkv):
    return mesh.shape["dp"] == 4 and mesh.shape["fsdp"] % 2 == 0 and w_qkv.shape[1] % 32 == 0


def local(mesh, images, image_cot, captions, caption_cot, lengths, w_qkv, w_out, w_up, w_down, gains, biases, b_up):
    if not kernels_fit(mesh, w_qkv):
        return plain(
            images, image_cot, captions, caption_cot, lengths, w_qkv, w_out, w_up, w_down, gains, biases, b_up
        )
    return whole(
        mesh.shape["fsdp"] // 2, images, image_cot, captions, caption_cot, lengths,
        (w_qkv, w_out, w_up, w_down), gains, biases, b_up
    )


def solution(mesh):
    placed = (
        P(("dp", "fsdp"), None, None),
        P(("dp", "fsdp"), None, None),
        P(("dp", "fsdp"), None, None),
        P(("dp", "fsdp"), None, None),
        P(("dp", "fsdp"), None),
        P(None, "fsdp", None),
        P(None, "fsdp", None),
        P(None, "fsdp", None),
        P(None, "fsdp", None),
        P(None, None, "fsdp"),
        P(None, None, "fsdp"),
        P(None, "fsdp"),
    )
    return jax.shard_map(
        functools.partial(local, mesh),
        mesh=mesh,
        in_specs=placed,
        out_specs=(
            P(("dp", "fsdp"), None, None),
            P(("dp", "fsdp"), None, None),
            P(("dp", "fsdp"), None, None),
            P(("dp", "fsdp"), None, None),
            P(None, "fsdp", None),
            P(None, "fsdp", None),
            P(None, "fsdp", None),
            P(None, "fsdp", None),
            P(None, None, "fsdp"),
            P(None, None, "fsdp"),
            P(None, "fsdp"),
        ),
        check_vma=False,
    )
```

```python
import functools

import jax
import jax.numpy as jnp
from jax import lax
from jax.experimental import pallas as pl
from jax.experimental.pallas import tpu as pltpu
from jax.sharding import PartitionSpec as P

HEAD = 64

MESH = pl.DeviceIdType.MESH
NT = (((1,), (1,)), ((), ()))
TN = (((0,), (0,)), ((), ()))
TILE = 256
CHUNK = 64
ALL = slice(None)


def dot(a, b, dims=(((1,), (0,)), ((), ()))):
    return lax.dot_general(a, b, dims, preferred_element_type=jnp.float32)


def flat(value):
    return value.reshape(-1, value.shape[-1])


def at(t, size=TILE):
    return pl.ds(pl.multiple_of(t * size, size), size)


def remote(src, dst, send, recv, device):
    return pltpu.make_async_remote_copy(
        src_ref=src, dst_ref=dst, send_sem=send, recv_sem=recv, device_id=device, device_id_type=MESH
    )


class Place:
    def __init__(self, line):
        dp, fs = lax.axis_index("dp"), lax.axis_index("fsdp")
        self.line, self.dp, self.fs = line, dp, fs
        self.x, self.c = dp // 2, dp % 2
        self.z, self.y = fs // 2, fs % 2
        self.up, self.down = (dp, fs + 2), (dp, fs - 2)
        self.yway = (dp, self.z * 2 + 1 - self.y)
        self.xway = ((1 - self.x) * 2 + self.c, fs)
        self.core = (self.x * 2 + 1 - self.c, fs)
        self.has_up, self.has_down = self.z + 1 < line, self.z > 0

    def others(self):
        return [lax.rem(self.fs + step, 2 * self.line) for step in range(1, 2 * self.line)]

    def greet(self, meanwhile):
        barrier = pltpu.get_barrier_semaphore()
        known = [(self.dp, other) for other in self.others()] + [self.xway, self.core]
        for device in known:
            pl.semaphore_signal(barrier, inc=1, device_id=device, device_id_type=MESH)
        meanwhile()
        pl.semaphore_wait(barrier, len(known))


class Panel:
    def __init__(self, which, part, width):
        self.which, self.part, self.width = which, part, width

    def cols(self, cut):
        base = 0 if self.which == 3 else self.part * self.width
        if cut is None:
            return pl.ds(base, self.width)
        return pl.ds(pl.multiple_of(base + cut[0], 128), cut[1])

    def of(self, ref, *lead, cut=None):
        if self.which == 3:
            return ref.at[(*lead, self.part, ALL, self.cols(cut))]
        return ref.at[(*lead, ALL, self.cols(cut))]


class Cuts:
    def __init__(self, width, x, thirds):
        third = width // 3
        self.half = (x * (width // 2), width // 2)
        self.other_half = ((1 - x) * (width // 2), width // 2)
        self.wide, self.outer, self.other_outer = self.half, self.half, self.other_half
        if thirds:
            self.wide = (x * third, 2 * third)
            self.outer = (x * 2 * third, third)
            self.other_outer = ((1 - x) * 2 * third, third)


def ds(cut):
    return pl.ds(pl.multiple_of(cut[0], 128), cut[1])


def panels_of(layer_shapes, width, order):
    made = []
    for which in order:
        count = layer_shapes[which]
        made += [Panel(which, part, width) for part in range(count)]
    return made


class Gather:
    def __init__(self, at, place, own, panel, full, way, send, recv, near):
        self.at, self.place, self.own, self.panel, self.full = at, place, own, panel, full
        self.send, self.recv, self.near = send, recv, near
        self.split, self.older = way == SPLIT, None
        split = self.split
        cuts = Cuts(panel.width, place.x, way == THIRDS)
        self.lane, self.other_lane = (cuts.half, cuts.other_half) if split else (None, None)
        self.over_y = cuts.half if split else cuts.wide
        self.over_x, self.from_x = (cuts.half, cuts.other_half) if split else (cuts.outer, cuts.other_outer)

    def view(self, block, y, c, cut=None):
        return self.panel.of(self.full, block, y, c, cut=cut)

    def sent(self, slot):
        return self.send.at[self.at % AG_RING, slot]

    def got(self, slot):
        return self.recv.at[self.at, slot]

    def line_copy(self, way, block):
        p = self.place
        ref = self.view(block, p.y, p.c, self.lane)
        return remote(ref, ref, self.sent(block + way), self.got(block), (p.up, p.down)[way])

    def near_copy(self):
        p = self.place
        mine = self.panel.of(self.own, p.c)
        return pltpu.make_async_copy(mine, self.view(p.z, p.y, p.c), self.near.at[self.at % AG_RING])

    def far_copy(self, kind):
        p, line = self.place, self.place.line
        ref, device = {
            "y": (lambda: (self.view(ALL, p.y, p.c, self.over_y), p.yway)),
            "x": (lambda: (self.view(ALL, 1 - p.y, p.c, self.over_x), p.xway)),
            "core_own": (lambda: (self.view(ALL, p.y, p.c), p.core)),
            "core": (lambda: (self.view(ALL, 1 - p.y, p.c), p.core)),
        }[kind]()
        slot = FAR.index(kind)
        return remote(ref, ref, self.sent(line + 1 + slot), self.got(line + slot), device)

    def trade_copy(self, block, lane):
        p, line = self.place, self.place.line
        ref = self.view(block, p.y, p.c, lane)
        return remote(ref, ref, self.sent(line + 5 + block), self.got(line + 4 + block), p.xway)

    def landed(self, kind):
        p, line = self.place, self.place.line
        ref = {
            "y": lambda: self.view(ALL, 1 - p.y, p.c, self.over_y),
            "x": lambda: self.view(ALL, 1 - p.y, p.c, self.from_x),
            "core_own": lambda: self.view(ALL, p.y, 1 - p.c),
            "core": lambda: self.view(ALL, 1 - p.y, 1 - p.c),
        }[kind]()
        slot = FAR.index(kind)
        return remote(ref, ref, self.sent(line + 1 + slot), self.got(line + slot), p.core)

    def kinds(self):
        return FAR

    def first(self):
        p = self.place
        if self.older is not None:
            self.older.drain()
        self.near_copy().start()
        mine = self.panel.of(self.own, p.c, cut=self.lane)
        there = self.view(p.z, p.y, p.c, self.lane)
        for way, able, device in ((0, p.has_up, p.up), (1, p.has_down, p.down)):
            copy = functools.partial(remote, mine, there, self.sent(p.z + way), self.got(p.z), device)
            pl.when(able)(lambda copy=copy: copy().start())

    def hop(self, k):
        p = self.place

        def pass_on(way, block, more):
            self.line_copy(way, block).wait_recv()
            pl.when(more)(lambda: self.line_copy(way, block).start())
            if self.split:
                self.trade_copy(block, self.lane).start()

        pl.when(p.z - k >= 0)(lambda: pass_on(0, p.z - k, p.has_up))
        pl.when(p.z + k < p.line)(lambda: pass_on(1, p.z + k, p.has_down))
        if k == p.line - 1:
            self.near_copy().wait()
            self.far_copy("y").start()
            if not self.split:
                self.far_copy("core_own").start()

    def cross(self):
        self.landed("y").wait_recv()
        self.far_copy("x").start()
        if self.split:
            self.trades(lambda block: self.trade_copy(block, self.other_lane).wait_recv())
            self.far_copy("core_own").start()

    def trades(self, body):
        for block in range(self.place.line):
            pl.when(block != self.place.z)(functools.partial(body, block))

    def share(self):
        self.landed("x").wait_recv()
        self.far_copy("core").start()

    def stages(self):
        hops = [functools.partial(self.hop, k) for k in range(1, self.place.line)]
        return [self.first, *hops, self.cross, self.share]

    def arrive(self):
        self.landed("core_own").wait_recv()
        self.landed("core").wait_recv()

    def drain(self):
        p = self.place

        def body(block, carry):
            pl.when(p.has_up & (block <= p.z))(lambda: self.line_copy(0, block).wait_send())
            pl.when(p.has_down & (block >= p.z))(lambda: self.line_copy(1, block).wait_send())
            return carry

        lax.fori_loop(0, p.line, body, 0)
        for kind in self.kinds():
            self.far_copy(kind).wait_send()
        if self.split:
            self.trades(lambda block: self.trade_copy(block, self.lane).wait_send())


FAR = ("y", "x", "core_own", "core")
HALVES, THIRDS, SPLIT, LINE_FIRST = range(4)
AG_RING = 12
GATHER_WAYS = (
    1, 2, 1, 1, 2, 1, 2, 1, 1, 2, 1, 2, 1, 0, 0, 1, 0, 0, 1, 0, 0, 1, 0, 0,
)
SUM_WAYS = (
    0, 1, 0, 1, 0, 1, 0, 1, 0, 1, 0, 1, 0, 2, 0, 0, 2, 0, 1, 2, 0, 0, 2, 1,
)
RINGS = dict(own=12, away=6, other=3, from_x=4, from_y=4, line_in=5, last=3, total=3, line_away=1)
LINE_FIRSTS = min(1, SUM_WAYS.count(LINE_FIRST))
SUM_SEMS = dict(
    core=(RINGS["away"], 1, RINGS["other"], 1),
    x=(RINGS["away"], 1, RINGS["from_x"], 1),
    y=(RINGS["away"], 1, RINGS["from_y"], 1),
    line=(RINGS["own"], 4, RINGS["line_in"], 5),
    line_away=(LINE_FIRSTS and RINGS["own"], 4, LINE_FIRSTS and RINGS["line_away"], 5),
    last=(RINGS["own"], 1, RINGS["last"], 1),
    out=(RINGS["total"], 1, 24, 1),
)


def starts_of(kinds):
    found, out_at, in_at = {}, 0, 0
    for name, (out_ring, out_each, in_ring, in_each) in kinds.items():
        found[name] = (out_at, in_at)
        out_at, in_at = out_at + out_ring * out_each, in_at + in_ring * in_each
    return found, out_at, in_at


SUM_STARTS, SUM_SENDS, SUM_ARRIVALS = starts_of(SUM_SEMS)
CREDITS, CREDIT_COUNT = {}, 0
for _name, _ring in (
    ("other", "other"),
    ("from_x", "from_x"),
    ("from_y", "from_y"),
    ("line_up", "line_in"),
    ("line_down", "line_in"),
    ("away_up", "line_away"),
    ("away_down", "line_away"),
    ("last", "last"),
):
    CREDITS[_name] = CREDIT_COUNT
    CREDIT_COUNT += RINGS[_ring]


class Reduce:
    def __init__(self, at, count, turn, place, panel, way, terms, out, bufs, credit, send, recv, near):
        self.at, self.count, self.place, self.panel, self.terms, self.out = at, count, place, panel, terms, out
        self.credit, self.send, self.recv, self.near = credit, send, recv, near
        self.older, self.flush = {}, None
        self.turn = turn
        self.b = {name: ref.at[self.slot(name)] for name, ref in bufs.items()}
        cuts = Cuts(panel.width, place.x, way == THIRDS)
        self.split, self.line_first = way == SPLIT, way == LINE_FIRST
        self.wide, self.outer, self.other_outer = ds(cuts.wide), ds(cuts.outer), ds(cuts.other_outer)
        self.lane = self.outer if self.split else pl.ds(0, panel.width)
        if self.split:
            self.wide = pl.ds(0, panel.width)
        self.lanes = panel.width // 2 if self.split else panel.width
        over_y = panel.width if self.split or self.line_first else cuts.wide[1]
        self.b["from_x"] = self.b["from_x"].at[:, :, 0 : cuts.outer[1]]
        self.b["from_y"] = self.b["from_y"].at[:, :, 0:over_y]
        self.b["last"] = self.b["last"].at[:, 0 : self.lanes]

    def turn_of(self, ring):
        return self.turn if ring == "line_away" else (self.at, self.count)

    def slot(self, ring):
        return self.turn_of(ring)[0] % RINGS[ring]

    def spend(self, name, ring):
        if self.turn_of(ring)[0] >= RINGS[ring]:
            pl.semaphore_wait(self.credit.at[CREDITS[name] + self.slot(ring)], 1)

    def grant(self, name, ring, device):
        turn, count = self.turn_of(ring)
        if turn + RINGS[ring] < count:
            credit = self.credit.at[CREDITS[name] + self.slot(ring)]
            pl.semaphore_signal(credit, inc=1, device_id=device, device_id_type=MESH)

    def sems(self, name, slot=(0, 0)):
        out_ring, out_each, in_ring, in_each = SUM_SEMS[name]
        out_at, in_at = SUM_STARTS[name]
        out_at += self.at % out_ring * out_each + slot[0]
        in_at += (self.slot(name) if name == "line_away" else self.at % in_ring) * in_each + slot[1]
        return self.send.at[out_at], self.recv.at[in_at]

    def core_copy(self):
        p = self.place
        return remote(self.panel.of(self.terms, ALL, ALL, 1 - p.c), self.b["other"], *self.sems("core"), p.core)

    def near_copy(self, away):
        p = self.place
        src = self.panel.of(self.terms, ALL, (1 - p.y) if away else p.y, p.c)
        return pltpu.make_async_copy(src, self.b["away" if away else "own"], self.near.at[self.at % 2 * 2 + int(away)])

    def x_copy(self):
        p = self.place
        src = self.b["own" if self.split else "away"].at[:, :, self.other_outer]
        return remote(src, self.b["from_x"], *self.sems("x"), p.xway)

    def y_copy(self):
        p = self.place
        if self.line_first:
            return remote(self.b["away"].at[p.z], self.b["from_y"].at[0], *self.sems("y"), p.yway)
        return remote(self.b["away"].at[:, :, self.wide], self.b["from_y"], *self.sems("y"), p.yway)

    def came(self, way, block, away=False):
        return self.b["line_away" if away else "line_in"].at[block + 1 - way, :, 0 : self.lanes]

    def line_copy(self, way, block, away=False):
        p = self.place
        sems = self.sems("line_away" if away else "line", (block, block + 1 - way))
        src = self.b["away" if away else "own"].at[block, :, self.lane]
        return remote(src, self.came(way, block, away), *sems, (p.up, p.down)[way])

    def columns(self):
        return (False, True) if self.line_first else (False,)

    def last_copy(self):
        p = self.place
        return remote(self.b["own"].at[p.z, :, self.lane], self.b["last"], *self.sems("last"), p.xway)

    def out_copy(self):
        ref = self.panel.of(self.out, self.place.c)
        return remote(self.b["total"], ref, *self.sems("out"), self.place.core)

    def out_landed(self):
        ref = self.panel.of(self.out, 1 - self.place.c)
        return remote(self.b["total"], ref, *self.sems("out"), self.place.core)

    def out_near(self):
        return pltpu.make_async_copy(self.b["total"], self.panel.of(self.out, self.place.c), self.near.at[4 + self.at % RINGS["total"]])

    def each(self, body):
        def step(block, carry):
            body(block)
            return carry

        lax.fori_loop(0, self.place.line, step, 0)

    def start(self):
        if self.flush is not None:
            self.flush()
        if "away" in self.older:
            self.older["away"].free_away()
        if "own" in self.older:
            self.older["own"].free_own()
        self.spend("other", "other")
        self.core_copy().start()
        self.near_copy(False).start()
        self.near_copy(True).start()

    def add_core(self):
        p, b = self.place, self.b
        self.near_copy(False).wait()
        self.near_copy(True).wait()
        self.core_copy().wait_recv()

        def body(block):
            b["away"][block] = b["away"][block] + b["other"][block, 1 - p.y]

        self.each(body)
        if self.split:
            self.spend("from_y", "from_y")
            self.y_copy().start()
        else:
            self.spend("from_x", "from_x")
            if self.line_first:
                self.grant("from_x", "from_x", p.xway)
            else:
                self.x_copy().start()

        def rest(block):
            b["own"][block] = b["own"][block] + b["other"][block, p.y]

        self.each(rest)
        self.grant("other", "other", p.core)

    def add_x(self):
        p, b = self.place, self.b
        self.x_copy().wait_recv()
        cols = self.outer

        def body(block):
            b["away"][block, :, cols] = b["away"][block, :, cols] + b["from_x"][block]

        self.each(body)
        self.spend("from_y", "from_y")
        self.y_copy().start()
        self.grant("from_x", "from_x", p.xway)

    def add_x_after(self):
        p, b = self.place, self.b
        self.x_copy().wait_recv()
        cols = self.outer

        def body(block):
            b["own"][block, :, cols] = b["own"][block, :, cols] + b["from_x"][block]

        self.each(body)
        self.grant("from_x", "from_x", p.xway)
        self.line_step(0)

    def add_y(self):
        p, b = self.place, self.b
        self.y_copy().wait_recv()
        cols = self.wide

        def body(block):
            b["own"][block, :, cols] = b["own"][block, :, cols] + b["from_y"][block]

        self.each(body)
        self.grant("from_y", "from_y", p.yway)
        if self.split:
            self.spend("from_x", "from_x")
            self.x_copy().start()
        else:
            self.line_step(0)

    def add_line(self, way, block):
        for away in self.columns():
            self.line_copy(way, block, away).wait_recv()
            sums, lane = self.b["away" if away else "own"], self.lane
            sums[block, :, lane] = sums[block, :, lane] + self.came(way, block, away)[...]

    def line_step(self, k):
        p, line = self.place, self.place.line
        if k == 0:
            pl.when(p.has_up)(lambda: self.spend("line_up", "line_in"))
            pl.when(p.has_down)(lambda: self.spend("line_down", "line_in"))
            if self.line_first:
                pl.when(p.has_up)(lambda: self.spend("away_up", "line_away"))
                pl.when(p.has_down)(lambda: self.spend("away_down", "line_away"))
        for way, steps_in, block, more in (
            (0, p.z, line - 1 - k + p.z, p.has_down),
            (1, line - 1 - p.z, k - (line - 1 - p.z), p.has_up),
        ):

            def body(way=way, block=block, more=more):
                pl.when(more)(lambda: self.add_line(way, block))
                for away in self.columns():
                    self.line_copy(way, block, away).start()

            pl.when(steps_in <= k)(body)

    def own_step(self):
        p = self.place
        pl.when(p.has_down)(lambda: self.add_line(0, p.z))
        pl.when(p.has_up)(lambda: self.add_line(1, p.z))
        if self.line_first:
            self.spend("from_y", "from_y")
            self.y_copy().start()
            pl.when(p.has_down)(lambda: self.grant("away_up", "line_away", p.down))
            pl.when(p.has_up)(lambda: self.grant("away_down", "line_away", p.up))
        else:
            self.spend("last", "last")
            self.last_copy().start()
        pl.when(p.has_down)(lambda: self.grant("line_up", "line_in", p.down))
        pl.when(p.has_up)(lambda: self.grant("line_down", "line_in", p.up))

    def add_y_last(self):
        p, b = self.place, self.b
        self.y_copy().wait_recv()
        b["own"][p.z] = b["own"][p.z] + b["from_y"][0]
        self.grant("from_y", "from_y", p.yway)
        self.spend("last", "last")
        self.last_copy().start()

    def finish(self):
        p, b = self.place, self.b
        if "total" in self.older:
            self.older["total"].free_total()
        self.last_copy().wait_recv()
        if self.split:
            b["total"][:, self.outer] = b["own"][p.z, :, self.outer].astype(jnp.float32)
            b["total"][:, self.other_outer] = b["last"][...].astype(jnp.float32)
        else:
            b["total"][...] = b["own"][p.z].astype(jnp.float32) + b["last"][...].astype(jnp.float32)
        self.grant("last", "last", p.xway)
        self.out_copy().start()
        self.out_near().start()

    def stages(self):
        if self.line_first:
            steps = [functools.partial(self.line_step, k) for k in range(self.place.line - 1)]
            return [self.start, self.add_core, *steps, self.own_step, self.add_y_last, self.finish]
        steps = [self.start, self.add_core]
        steps += [self.add_y, self.add_x_after] if self.split else [self.add_x, self.add_y]
        steps += [functools.partial(self.line_step, k) for k in range(1, self.place.line - 1)]
        return steps + [self.own_step, self.finish]

    def uses(self):
        if self.line_first:
            return dict(from_x=(1, 1), from_y=(5, 6), line_in=(2, 5), line_away=(2, 5), last=(6, 7))
        if self.split:
            return dict(from_y=(1, 2), from_x=(2, 3), line_in=(3, 6), last=(6, 7))
        return dict(from_x=(1, 2), from_y=(2, 3), line_in=(3, 6), last=(6, 7))

    def free_away(self):
        self.core_copy().wait_send()
        if not self.line_first:
            self.x_copy().wait_send()
        self.y_copy().wait_send()
        if self.line_first:
            self.free_line(True)

    def free_line(self, away):
        p = self.place
        for block in range(p.line):
            pl.when(block > p.z)(lambda block=block: self.line_copy(0, block, away).wait_send())
            pl.when(block < p.z)(lambda block=block: self.line_copy(1, block, away).wait_send())

    def free_own(self):
        self.free_line(False)
        self.last_copy().wait_send()

    def free_total(self):
        self.out_copy().wait_send()
        self.out_near().wait()


class Layer:
    def __init__(self, n, kept, weights, par, b_up, terms, g_par, g_bup):
        self.n, self.s = n, kept
        self.w_qkv, self.w_out, self.w_up, self.w_down = weights
        self.par, self.b_up = par, b_up
        self.g_qkv, self.g_out, self.g_up, self.g_down = terms
        self.g_par, self.g_bup = g_par, g_bup
        self.width, self.deep = self.w_out.shape[-1], self.w_up.shape[-1]
        self.pending = [None, None]

    def chunks(self, body):
        def step(i, carry):
            body(at(i, CHUNK))
            return carry

        lax.fori_loop(0, self.n // CHUNK, step, 0)

    def tiles(self, first, last, body):
        def step(i, carry):
            body(i)
            return carry

        lax.fori_loop(first, last, step, 0)

    def row(self, ref, i):
        return ref[i : i + 1, :]

    def tall_copy(self, ref, slot, t):
        stage = self.s["stage"].at[slot].reshape(*ref.shape[:4], self.width)
        cols = at(t, self.width)
        return pltpu.make_async_copy(stage, ref.at[:, :, :, :, cols], self.s["stage_sem"].at[slot])

    def wide_copy(self, ref, slot, t):
        stage = self.s["stage"].at[slot].reshape(*ref.shape[1:])
        return pltpu.make_async_copy(stage, ref.at[t], self.s["stage_sem"].at[slot])

    def put(self, make, slot, t, first, value):
        held = self.pending[slot]
        pl.when(t > first)(lambda: make(slot, t - 1).wait())
        if held is not None:
            pl.when(t == first)(lambda: held.wait())
        self.s["stage"][slot] = value.astype(jnp.bfloat16)
        make(slot, t).start()

    def put_all(self):
        for slot in range(2):
            if self.pending[slot] is not None:
                self.pending[slot].wait()
            self.pending[slot] = None

    def mask(self, ends):
        s = self.s

        def mask(rows):
            shape = (CHUNK, self.n)
            at_row = lax.broadcasted_iota(jnp.int32, shape, 0) + rows.start
            at_col = lax.broadcasted_iota(jnp.int32, shape, 1)
            one, other = jnp.zeros(shape, jnp.int32), jnp.zeros(shape, jnp.int32)
            for end in ends:
                one = one + (at_row >= end).astype(jnp.int32)
                other = other + (at_col >= end).astype(jnp.int32)
            s["bias"][rows, :] = jnp.where(one == other, 0.0, -1e30)

        self.chunks(mask)

    def prepare(self):
        s, width = self.s, self.width
        s["rows"][0:1, 0:width] = self.par[4:5, :]
        s["rows"][0:1, width : 2 * width] = jnp.zeros((1, width), jnp.float32)
        s["rows"][0:1, 2 * width :] = self.par[5:6, :]

    def norm_parts(self, values):
        center = values - jnp.mean(values, axis=-1, keepdims=True)
        scale = lax.rsqrt(jnp.mean(center * center, axis=-1, keepdims=True) + 1e-05)
        return center * scale, scale

    def norm(self, src, dst, which):
        def body(rows):
            unit, _ = self.norm_parts(src[rows, :].astype(jnp.float32))
            dst[rows, :] = (unit * self.row(self.par, which) + self.row(self.par, 2 + which)).astype(jnp.bfloat16)

        self.chunks(body)

    def norm_a(self):
        self.norm(self.s["x"], self.s["a"], 0)

    def project(self, first, last):
        s = self.s
        queries = self.width // TILE

        def body(t):
            scale = jnp.where(t < queries, HEAD ** (-0.5), 1.0)
            found = dot(s["a"][...], flat(self.w_qkv[:, :, :, :, at(t)])) + s["rows"][0:1, at(t)]
            s["qkv"][:, at(t)] = (found * scale).astype(jnp.bfloat16)

        self.tiles(first, last, body)

    def turn_a(self):
        self.s["a_t"][...] = self.s["a"][...].T

    def pair(self, i, which):
        start = which * self.width + i * 128
        return self.s["qkv"].at[:, pl.ds(pl.multiple_of(start, 128), 128)]

    def own_lanes(self, value, head):
        lanes = lax.broadcasted_iota(jnp.int32, value.shape, 1)
        return jnp.where((lanes < HEAD) == (head == 0), value, jnp.zeros_like(value))

    def attend(self, first, last):
        s = self.s

        def body(i):
            q, k, v = (self.pair(i, which) for which in range(3))
            keys = [self.own_lanes(k[...], head) for head in range(2)]
            vals = [self.own_lanes(v[...], head) for head in range(2)]
            for part in range(self.n // TILE):
                cols = slice(part * TILE, part * TILE + TILE)
                mixed = None
                for head in range(2):
                    scores = dot(keys[head], q[cols, :], NT) + s["bias"][:, cols]
                    raised = jnp.exp(scores - jnp.max(scores, axis=0, keepdims=True))
                    share = 1.0 / jnp.sum(raised, axis=0, keepdims=True)
                    weights = (raised * share).astype(jnp.bfloat16)
                    s["wt"][2 * i + head, :, cols] = weights
                    found = dot(vals[head], weights, TN)
                    mixed = found if mixed is None else mixed + found
                s["o"][cols, at(i, 128)] = mixed.T.astype(jnp.bfloat16)

        self.tiles(first, last, body)

    def branch(self):
        s = self.s

        def body(t):
            found = dot(s["o"][...], flat(self.w_out[:, :, :, :, at(t)])) + self.par[6:7, at(t)]
            s["h"][:, at(t)] = s["x"][:, at(t)].astype(jnp.float32) + found

        self.tiles(0, self.width // TILE, body)
        s["o_t"][...] = s["o"][...].T

    def norm_c(self):
        self.norm(self.s["h"], self.s["c"], 1)

    def up(self, first, last):
        s = self.s

        def body(t):
            before = dot(s["c"][...], flat(self.w_up[:, :, :, :, at(t)])) + self.b_up[0:1, at(t)]
            chance = 0.5 + 0.5 * lax.erf(before * 0.7071067811865476)
            s["g"][:, at(t)] = (before * chance).astype(jnp.bfloat16)
            slope = chance + before * (jnp.exp(before * before * -0.5) * 0.3989422804014327)
            s["du"][:, at(t)] = slope.astype(jnp.bfloat16)

        self.tiles(first, last, body)

    def turn_c(self):
        self.s["c_t"][...] = self.s["c"][...].T

    def down(self):
        s = self.s

        def body(t):
            found = dot(s["g"][...], flat(self.w_down[:, :, :, :, :, at(t)])) + self.par[7:8, at(t)]
            s["a"][:, at(t)] = (s["h"][:, at(t)] + found).astype(jnp.bfloat16)

        self.tiles(0, self.width // TILE, body)

    def feed_back(self, first, last):
        s, width = self.s, self.width
        tall = functools.partial(self.tall_copy, self.g_up)

        def body(t):
            cols = at(t, width)
            grad = dot(s["dy"][...], flat(self.w_down[t]), NT)
            low = (grad * s["du"][:, cols].astype(jnp.float32)).astype(jnp.bfloat16)
            s["du"][:, cols] = low
            self.g_bup[0:1, cols] = jnp.sum(low.astype(jnp.float32), axis=0, keepdims=True)
            self.put(tall, 1, t, first, dot(s["c_t"][...], low))

        self.tiles(first, last, body)
        self.pending[1] = tall(1, last - 1)

    def down_terms(self, first, last):
        s, width = self.s, self.width
        wide = functools.partial(self.wide_copy, self.g_down)

        def body(t):
            self.put(wide, 0, t, first, dot(s["g"][:, at(t, width)], s["dy"][...], TN))

        self.tiles(first, last, body)
        self.pending[0] = wide(0, last - 1)

    def up_back(self):
        self.s["sums"][...] = dot(self.s["du"][...], flat(self.w_up[...]), NT)

    def norm_back(self, src, which, grad, rest, body_out):
        def body(rows):
            unit, scale = self.norm_parts(src[rows, :].astype(jnp.float32))
            came = grad[rows, :]
            gained = came * self.row(self.par, which)
            self.g_par[which : which + 1, :] += jnp.sum(came * unit, axis=0, keepdims=True)
            self.g_par[2 + which : 3 + which, :] += jnp.sum(came, axis=0, keepdims=True)
            inner = gained - jnp.mean(gained, axis=-1, keepdims=True)
            inner = inner - unit * jnp.mean(gained * unit, axis=-1, keepdims=True)
            body_out(rows, rest[rows, :].astype(jnp.float32) + inner * scale)

        self.chunks(body)

    def norm_c_back(self):
        s = self.s

        def keep(rows, grad):
            s["h"][rows, :] = grad
            low = grad.astype(jnp.bfloat16)
            s["c"][rows, :] = low
            self.g_par[6:7, :] += jnp.sum(low.astype(jnp.float32), axis=0, keepdims=True)
            self.g_par[7:8, :] += jnp.sum(s["dy"][rows, :].astype(jnp.float32), axis=0, keepdims=True)

        self.norm_back(s["h"], 1, s["sums"], s["dy"], keep)

    def branch_back(self):
        s = self.s
        tall = functools.partial(self.tall_copy, self.g_out)
        self.put(tall, 0, 0, 0, dot(s["o_t"][...], s["c"][...]))
        self.pending[0] = tall(0, 0)
        s["a"][...] = dot(s["c"][...], flat(self.w_out[...]), NT).astype(jnp.bfloat16)

    def attend_back(self, first, last):
        s, width = self.s, self.width

        def body(i):
            q, k, v = (self.pair(i, which) for which in range(3))
            came = s["a"].at[:, at(i, 128)]
            dq = dk = dv = None
            for head in range(2):
                vals = self.own_lanes(v[...], head)
                for part in range(self.n // TILE):
                    cols = slice(part * TILE, part * TILE + TILE)
                    grad = dot(vals, came[cols, :], NT)
                    weights = s["wt"][2 * i + head, :, cols].astype(jnp.float32)
                    product = weights * grad
                    inner = jnp.sum(product, axis=0, keepdims=True)
                    s["ds"][:, cols] = (product - weights * inner).astype(jnp.bfloat16)
                one_q = dot(self.own_lanes(k[...], head), s["ds"][...], TN)
                one_k = dot(s["ds"][...], self.own_lanes(q[...], head))
                one_v = dot(s["wt"][2 * i + head], self.own_lanes(came[...], head))
                dq, dk, dv = (one_q, one_k, one_v) if head == 0 else (dq + one_q, dk + one_k, dv + one_v)
            s["g"][:, at(i, 128)] = dq.T.astype(jnp.bfloat16) * HEAD ** (-0.5)
            s["g"][:, pl.ds(pl.multiple_of(width + i * 128, 128), 128)] = dk.astype(jnp.bfloat16)
            s["g"][:, pl.ds(pl.multiple_of(2 * width + i * 128, 128), 128)] = dv.astype(jnp.bfloat16)

        self.tiles(first, last, body)

    def project_terms(self, first, last):
        s, width = self.s, self.width
        tall = functools.partial(self.tall_copy, self.g_qkv)
        for t in range(first, last):
            grad = s["g"][:, t * width : (t + 1) * width]
            if t != 1:
                row = 4 + t // 2
                self.g_par[row : row + 1, :] = jnp.sum(grad.astype(jnp.float32), axis=0, keepdims=True)
            slot = (t + 1) % 2
            self.put(tall, slot, t, t, dot(s["a_t"][...], grad))
            self.pending[slot] = tall(slot, t)

    def project_back(self):
        s = self.s
        s["sums"][...] = dot(s["g"][:, 0 : 3 * self.width], flat(self.w_qkv[...]), NT)

    def norm_a_back(self):
        s = self.s

        def keep(rows, grad):
            s["h"][rows, :] = grad

        self.norm_back(s["x"], 0, s["sums"], s["h"], keep)


def layer_scratch(n, width, deep):
    low, full = jnp.bfloat16, jnp.float32
    return dict(
        a=pltpu.VMEM((n, width), low),
        a_t=pltpu.VMEM((width, n), low),
        qkv=pltpu.VMEM((n, 3 * width), low),
        bias=pltpu.VMEM((n, n), full),
        wt=pltpu.VMEM((width // HEAD, n, n), low),
        ds=pltpu.VMEM((n, n), low),
        o=pltpu.VMEM((n, width), low),
        o_t=pltpu.VMEM((width, n), low),
        h=pltpu.VMEM((n, width), full),
        c=pltpu.VMEM((n, width), low),
        c_t=pltpu.VMEM((width, n), low),
        g=pltpu.VMEM((n, deep), low),
        du=pltpu.VMEM((n, deep), low),
        sums=pltpu.VMEM((n, width), full),
        rows=pltpu.VMEM((8, 3 * width), full),
        stage=pltpu.VMEM((2, width, width), low),
        stage_sem=pltpu.SemaphoreType.DMA((2,)),
    )


def cut(kept, n):
    cuts = dict(kept)
    for name in ("a", "qkv", "o", "h", "c", "g", "du", "sums"):
        cuts[name] = kept[name].at[0:n]
    for name in ("a_t", "o_t", "c_t"):
        cuts[name] = kept[name].at[:, 0:n]
    for name in ("bias", "ds"):
        cuts[name] = kept[name].at[0:n, 0:n]
    cuts["wt"] = kept["wt"].at[:, 0:n, 0:n]
    return cuts


ORDER = (0, 1, 2, 3)
BACK = (3, 2, 1, 0)


class SmallSum:
    def __init__(self, place, parts, land, line_land, out, send, recv):
        self.place, self.parts, self.land, self.line_land, self.out = place, parts, land, line_land, out
        self.send, self.recv = send, recv

    def near(self, step):
        p = self.place
        device = (p.core, p.xway, p.yway)[step]
        return remote(self.parts.at[step], self.land.at[step], self.send.at[step], self.recv.at[step], device)

    def far(self, step):
        p = self.place
        other = lax.rem(p.z + step, p.line)
        device = (p.dp, other * 2 + p.y)
        src = self.parts.at[3]
        return remote(src, self.line_land.at[p.z], self.send.at[3 + other], self.recv.at[3 + p.z], device)

    def from_far(self, step):
        p = self.place
        other = lax.rem(p.z + step, p.line)
        device = (p.dp, other * 2 + p.y)
        src = self.parts.at[3]
        return remote(src, self.line_land.at[other], self.send.at[3 + other], self.recv.at[3 + other], device)

    def stage(self, step):
        p = self.place
        if step:
            if step <= 3:
                self.near(step - 1).wait_recv()
                self.parts[step] = self.parts[step - 1] + self.land[step - 1]
        if step < 3:
            self.near(step).start()
        if step == 3:
            for other in range(1, p.line):
                self.far(other).start()
            self.line_land[p.z] = self.parts[3]
        if step == 4:
            for other in range(1, p.line):
                self.from_far(other).wait_recv()
            gains, biases, b_up = self.out
            piece, deep = gains.shape[-1], b_up.shape[-1]
            wide = self.line_land.shape[-1] // deep

            def mine(block):
                for block_at in range(p.line):
                    part = self.line_land[block_at, :, 0:8, block * piece : (block + 1) * piece]
                    row, start = 8 + block // wide, block % wide * deep
                    up = self.line_land[block_at, :, row, start : start + deep]
                    if block_at == 0:
                        total, total_up = part, up
                    else:
                        total, total_up = total + part, total_up + up
                gains[...] = total[:, 0:2]
                for row in range(biases.shape[0]):
                    biases[row] = total[:, 2 + row]
                b_up[...] = total_up

            for block in range(2 * p.line):
                pl.when(p.fs == block)(functools.partial(mine, block))
            for near in range(3):
                self.near(near).wait_send()
            for other in range(1, p.line):
                self.far(other).wait_send()


def whole_kernel(line, sizes, names, ring_names, *refs):
    take = list(refs)

    def some(count):
        found = take[:count]
        del take[:count]
        return found

    owned = some(4)
    gains, biases, own_up, lengths, x_t, dy_t, x_i, dy_i = some(8)
    y_i, y_t, gx_i, gx_t = some(4)
    shares, small_out = some(4), some(3)
    far_weights, terms_t, terms_i = some(4), some(4), some(4)
    weights = some(4)
    kept = dict(zip(names, some(len(names))))
    bufs = dict(zip(ring_names, some(len(ring_names))))
    pad_x, pad_dy, small, small_all, par, b_up, g_parts, g_land, g_line = some(9)
    ag_send, ag_recv, ag_near, rs_send, rs_recv, rs_near, credit = some(7)
    s_send, s_recv, g_send, g_recv, load_sem, io_sem = some(6)
    n_t, n_i, counts = sizes
    width = weights[1].shape[-1]
    place = Place(line)
    ahead, back = panels_of(counts, width, ORDER), panels_of(counts, width, BACK)
    base = len(ahead)
    units, sums = [], []
    for u in range(2 * base):
        panel, layer, into = ahead[u % base], u // base, (weights, far_weights)[u // base]
        own, full = owned[panel.which].at[layer], into[panel.which]
        units.append(Gather(u, place, own, panel, full, GATHER_WAYS[u], ag_send, ag_recv, ag_near))
        units[u].older = units[u - AG_RING] if u >= AG_RING else None
    for u in range(2 * base):
        panel, layer, terms = back[u % base], u // base, (terms_i, terms_t)[u // base]
        share, term = shares[panel.which].at[layer], terms[panel.which]
        sems = credit, rs_send, rs_recv, rs_near
        turn = SUM_WAYS[:u].count(LINE_FIRST), SUM_WAYS.count(LINE_FIRST)
        sums.append(Reduce(u, 2 * base, turn, place, panel, SUM_WAYS[u], term, share, bufs, *sems))
        sums[u].older = {name: sums[u - RINGS[name]] for name in ("away", "own", "total") if u >= RINGS[name]}

    def layer_of(layer, n, view, terms):
        grads = g_parts.at[0, layer, 0:8], b_up.at[2 + layer]
        return Layer(n, view, weights, par.at[layer], b_up.at[layer], terms, *grads)

    text = layer_of(1, n_t, {**kept, "x": x_t.at[0], "dy": dy_t.at[0]}, terms_t)
    view = {**cut(kept, n_i), "x": pad_x, "dy": pad_dy}
    image = layer_of(0, n_i, view, terms_i)

    def prepare():
        small[...] = jnp.zeros_like(small)
        small[:, 0:2, 0 : gains.shape[2]] = gains[...].astype(jnp.float32)
        for row in range(biases.shape[0]):
            small[:, 2 + row, 0 : biases.shape[2]] = biases[row].astype(jnp.float32)
        for j in range(own_up.shape[1] // 128):
            small[:, 8 + j, :] = own_up[:, j * 128 : (j + 1) * 128].astype(jnp.float32)
        g_parts[0] = jnp.zeros(g_parts.shape[1:], jnp.float32)
        for src, dst in ((x_i, pad_x), (dy_i, pad_dy)):
            have = src.shape[1]
            if have < n_i:
                cut_at = have // 16 * 16
                dst[cut_at:, :] = jnp.zeros((n_i - cut_at, width), jnp.bfloat16)
            dst[0:have, :] = src[0]
        image.mask([x_i.shape[1]])

    place.greet(prepare)

    smalls = []
    for step, other in enumerate(place.others()):
        copy = remote(small, small_all.at[place.fs], s_send.at[step], s_recv.at[place.fs], (place.dp, other))
        copy.start()
        smalls.append(copy)
    for u, unit in enumerate(sums):
        unit.flush = image.put_all if u < base else text.put_all
    starts = [sum(counts[:which]) for which in range(5)]
    heads, tiles, panels = width // 128, width // TILE, counts[3]
    y_copy = pltpu.make_async_copy(kept["a"], y_t.at[0], io_sem.at[0])
    grad_copy = pltpu.make_async_copy(kept["h"], gx_t.at[0], io_sem.at[1])
    loads = [pltpu.make_async_copy(far_weights[i], weights[i], load_sem.at[i]) for i in range(4)]

    steps = []

    def add(body, *args, needs=()):
        def step():
            for unit in needs:
                units[unit].arrive()
            body(*args)

        step.needs = tuple(needs)
        steps.append(step)

    def first():
        small_all[place.fs] = small[...]
        for step, other in enumerate(place.others()):
            remote(small, small_all.at[other], s_send.at[step], s_recv.at[other], (place.dp, other)).wait_recv()
        piece, deep = width // (2 * line), b_up.shape[-1] // (2 * line)
        for layer in range(2):
            for block in range(2 * line):
                par[layer, :, block * piece : (block + 1) * piece] = small_all[block, layer, 0:8, 0:piece]
                for j in range(deep // 128):
                    start = block * deep + j * 128
                    b_up[layer, 0:1, start : start + 128] = small_all[block, layer, 8 + j : 9 + j, :]
        image.prepare()
        image.norm_a()

    def image_out():
        image.down()
        y_i[0] = view["a"][0 : y_i.shape[1], :]

    def image_last():
        image.norm_a_back()
        gx_i[0] = view["h"][0 : gx_i.shape[1], :]

    def text_first():
        ends = [lengths[0, 0]]
        for j in range(1, lengths.shape[1]):
            ends.append(ends[-1] + lengths[0, j])
        text.mask(ends)
        text.prepare()
        text.norm_a()

    def waiting(load, body):
        def step(*args):
            load.wait()
            body(*args)

        return step

    def text_out():
        loads[3].wait()
        text.down()
        y_copy.start()

    def text_branch_back():
        y_copy.wait()
        text.branch_back()

    def text_last():
        text.norm_a_back()
        grad_copy.start()
        for layer in range(2):
            for j in range(b_up.shape[-1] // width):
                g_parts[0, layer, 8 + j : 9 + j, :] = b_up[2 + layer, 0:1, j * width : (j + 1) * width]

    def load(which):
        add(loads[which].start, needs=range(base + starts[which], base + starts[which + 1]))

    add(first)
    for part in range(3):
        add(image.project, part * tiles, (part + 1) * tiles, needs=(part,))
    add(image.turn_a)
    for i in range(0, heads, 2):
        add(image.attend, i, i + 2)
    add(image.branch, needs=(starts[1],))
    add(image.norm_c)
    for part in range(panels):
        add(image.up, part * tiles, (part + 1) * tiles, needs=(starts[2] + part,))
        add(image.down_terms, part, part + 1)
    add(image.turn_c)
    add(image_out, needs=range(starts[3], starts[4]))
    for part in range(panels):
        add(image.feed_back, part, part + 1)
    add(image.up_back)
    add(image.norm_c_back)
    add(image.branch_back)
    for i in range(0, heads, 2):
        add(image.attend_back, i, i + 2)
    for part in range(3):
        add(image.project_terms, part, part + 1)
    add(image.project_back)
    add(image_last)
    load(0)
    add(text_first)
    for part in range(3):
        body = waiting(loads[0], text.project) if part == 0 else text.project
        add(body, part * tiles, (part + 1) * tiles)
    add(text.turn_a)
    load(1)
    for i in range(heads):
        add(text.attend, i, i + 1)
    add(waiting(loads[1], text.branch))
    load(2)
    add(text.norm_c)
    for part in range(panels):
        add(waiting(loads[2], text.up) if part == 0 else text.up, part * tiles, (part + 1) * tiles)
        add(text.down_terms, part, part + 1)
    load(3)
    add(text.turn_c)
    add(text_out)
    for part in range(panels):
        add(text.feed_back, part, part + 1)
    add(text.up_back)
    add(text.norm_c_back)
    add(text_branch_back)
    for i in range(heads):
        add(text.attend_back, i, i + 1)
    for part in range(3):
        add(text.project_terms, part, part + 1)
    add(text.project_back)
    add(text_last)
    small_sum = SmallSum(place, g_parts, g_land, g_line, small_out, g_send, g_recv)
    for stage in range(5):
        add(small_sum.stage, stage)

    drive(steps, [unit.stages() for unit in units], [unit.stages() for unit in sums])

    for unit in sums[-RINGS["away"] :]:
        unit.free_away()
    for unit in sums[-RINGS["own"] :]:
        unit.free_own()
    for unit in sums[-RINGS["total"] :]:
        unit.free_total()
    for unit in sums:
        unit.out_landed().wait_recv()
    for unit in units[-AG_RING:]:
        unit.drain()
    for copy in smalls:
        copy.wait_send()
    grad_copy.wait()


PLAN = (
    0, -1, 10, 1, 2, 11, 20, 30, 3, 12, 21, 40, 31, 13, 22, 41, 4, 32, 23, 42, 14, 5, 50, -1, 33, 43, 15, 60,
    24, -1, 51, 34, 61, 52, 25, 70, -1, 53, 44, 62, 35, 63, 80, -1, -1, -1, 71, -1, 45, 90, 54, 81, -1, 72, -1,
    -1, 73, 64, 82, -1, 55, 100, 83, 91, -1, -1, 65, 110, 120, 92, -1, 74, 93, 101, -1, 111, 102, 121, 112, 84,
    75, 130, 103, -1, 122, 113, -1, -1, 131, 1000, 85, 140, 123, 94, 104, 114, 132, 133, 141, 1001, 95, 150,
    1010, 142, 105, 160, 124, 1011, 143, 115, 170, 151, -1, 161, 1002, 134, 1020, 144, -1, -1, 1021, 125, 152,
    180, 162, -1, 153, 1012, 1003, 171, -1, -1, 181, 135, 190, 163, 1030, 172, -1, 1004, 154, 145, 200, -1,
    1031, 182, -1, 173, 191, 1013, -1, 155, 1005, 183, -1, 164, 192, -1, 1014, 201, 1022, 1032, 210, 1040, -1,
    174, -1, 193, 1006, 1041, -1, 165, 202, 220, 1015, -1, 184, -1, -1, 1050, 175, 230, 203, 211, -1, 221, 1007,
    1023, 1051, 1016, -1, 1042, -1, 212, 231, 1033, -1, -1, -1, 1024, 185, 222, 1060, -1, 194, 1052, -1, 1034,
    232, 1017, 1061, 1070, -1, 204, 1025, 1080, 213, 223, -1, 233, 195, 1071, -1, 1081, 1035, -1, 1026, 1043,
    1062, 1090, 1100, -1, -1, 1036, 1053, 1091, 205, -1, 1101, 1044, 1110, 1054, 214, 1072, -1, -1, 1082, 1111,
    224, -1, 1027, 1045, -1, 1055, 234, 1037, -1, 1092, -1, -1, 1046, 1063, 1120, 1102, 1130, 1056, 215, 1121,
    1073, 1112, 1064, 1140, 1083, 225, 1074, 1065, 1084, 1075, 235, 1093, -1, 1047, 1066, 1131, 1141, -1, 1150,
    1085, 1057, -1, 1076, 1086, 1094, 1103, 1122, 1151, 1067, -1, 1113, -1, 1077, 1095, 1104, 1160, 1114, -1,
    1087, 1132, 1142, -1, 1096, 1105, 1123, 1152, 1170, -1, 1133, 1115, 1124, 1161, 1106, 1097, -1, 1180, 1134,
    1171, 1143, -1, 1107, 1116, 1181, 1125, -1, 1135, 1190, 1200, 1144, 1153, -1, 1162, 1172, 1191, 1126, -1,
    1136, 1145, 1182, 1117, -1, -1, 1163, 1173, -1, 1127, 1137, 1146, 1201, 1154, 1164, -1, 1174, -1, 1147,
    1192, 1155, -1, 1165, 1210, -1, 1202, 1156, 1183, 1211, 1220, 1166, 1175, -1, 1184, 1230, -1, 1193, 1157,
    1221, -1, 1203, 1231, 1194, 1185, -1, 1167, 1195, 1204, 1212, -1, 1222, 1232, 1205, 1176, 1186, 1196, -1,
    1213, 1223, 1177, 1233, 1214, 1187, 1197, 1224, 1206, 1234, 1207, 1215, 1225, 1235, 1216, 1226, 1236, 1217,
    1227, 1237,
)


def drive(steps, gathers, sums):
    at_step = 0
    for code in PLAN:
        if code < 0:
            steps[at_step]()
            at_step += 1
        elif code < 1000:
            gathers[code // 10][code % 10]()
        else:
            sums[code // 10 - 100][code % 10]()


def padded(rows):
    return -(-rows // TILE) * TILE


def whole(line, x_i, dy_i, x_t, dy_t, lengths, owned, gains, biases, b_up):
    width, deep = owned[1].shape[2], owned[2].shape[2]
    rows = owned[1].shape[1] // 2
    counts = (3, 1, deep // width, deep // width)
    own = [w.reshape(2, 2, rows, w.shape[2]) for w in owned[:3]] + [owned[3].reshape(2, 2, counts[3], rows, width)]
    n_t, n_i = padded(x_t.shape[1]), padded(x_i.shape[1])
    low, full = jnp.bfloat16, jnp.float32
    turned = biases.transpose(1, 0, 2)
    kept = layer_scratch(n_t, width, deep)
    fulls = [(line, 2, *w.shape[1:]) for w in own]
    rings = dict(
        own=pltpu.VMEM((RINGS["own"], line, rows, width), low),
        away=pltpu.VMEM((RINGS["away"], line, rows, width), low),
        other=pltpu.VMEM((RINGS["other"], line, 2, rows, width), low),
        from_x=pltpu.VMEM((RINGS["from_x"], line, rows, width // 2), low),
        from_y=pltpu.VMEM((RINGS["from_y"], line, rows, width), low),
        line_in=pltpu.VMEM((RINGS["line_in"], line + 1, rows, width), low),
        last=pltpu.VMEM((RINGS["last"], rows, width), low),
        total=pltpu.VMEM((RINGS["total"], rows, width), full),
        line_away=pltpu.VMEM((RINGS["line_away"], line + 1, rows, width), low),
    )
    panels = 2 * sum(counts)
    small_rows = 8 + deep // width
    small_rows += -small_rows % 8
    own_rows = 8 + b_up.shape[1] // 128
    own_rows += -own_rows % 8
    anywhere, inside = pl.BlockSpec(memory_space=pl.ANY), pl.BlockSpec(memory_space=pltpu.VMEM)
    dma = pltpu.SemaphoreType.DMA
    outs = [
        jax.ShapeDtypeStruct(x_i.shape, low),
        jax.ShapeDtypeStruct(x_t.shape, low),
        jax.ShapeDtypeStruct(x_i.shape, full),
        jax.ShapeDtypeStruct(x_t.shape, full),
        *[jax.ShapeDtypeStruct(w.shape, full) for w in own],
        *[jax.ShapeDtypeStruct(v.shape, full) for v in (gains, turned, b_up)],
        *[jax.ShapeDtypeStruct(shape, low) for shape in fulls * 3],
    ]
    scratch = [
        *[pltpu.VMEM(shape, low) for shape in fulls],
        *kept.values(),
        *rings.values(),
        pltpu.VMEM((n_i, width), low),
        pltpu.VMEM((n_i, width), low),
        pltpu.VMEM((2, own_rows, 128), full),
        pltpu.VMEM((2 * line, 2, own_rows, 128), full),
        pltpu.VMEM((2, 8, width), full),
        pltpu.VMEM((4, 1, deep), full),
        pltpu.VMEM((4, 2, small_rows, width), full),
        pltpu.VMEM((3, 2, small_rows, width), full),
        pltpu.VMEM((line, 2, small_rows, width), full),
        dma((AG_RING, 2 * line + 5)),
        dma((panels, 2 * line + 4)),
        dma((AG_RING,)),
        dma((SUM_SENDS,)),
        dma((SUM_ARRIVALS,)),
        dma((4 + RINGS["total"],)),
        pltpu.SemaphoreType.REGULAR((CREDIT_COUNT,)),
        dma((2 * line,)),
        dma((2 * line,)),
        dma((3 + line,)),
        dma((3 + line,)),
        dma((4,)),
        dma((2,)),
    ]
    found = pl.pallas_call(
        functools.partial(whole_kernel, line, (n_t, n_i, counts), list(kept), list(rings)),
        out_shape=outs,
        in_specs=[anywhere] * 4 + [inside] * 3 + [pl.BlockSpec(memory_space=pltpu.SMEM)] + [inside] * 4,
        out_specs=[inside, anywhere, inside, anywhere] + [anywhere] * 4 + [inside] * 3 + [anywhere] * 12,
        scratch_shapes=scratch,
        compiler_params=pltpu.CompilerParams(collective_id=0, has_side_effects=True, vmem_limit_bytes=63 * 2**20),
    )(*own, gains, turned, b_up, lengths, x_t, dy_t, x_i, dy_i)
    found = hand_over(found[:11])
    shares = [share.reshape(w.shape) for share, w in zip(found[4:8], owned)]
    image_grad = found[2].transpose(1, 0, 2)
    return (*found[:2], image_grad, found[3], *shares, found[8], found[9].transpose(1, 0, 2), found[10])


def hand_over(found):
    def kernel(*refs):
        count = len(found)
        held, (turned, there, back) = refs[2 * count : -3], refs[-3:]
        copies = [pltpu.make_async_copy(refs[i], held[i], there.at[i]) for i in range(count)]
        for copy in copies:
            copy.start()
        left = [turned if i == 2 else held[i] for i in range(count)]
        outs = [pltpu.make_async_copy(left[i], refs[count + i], back.at[i]) for i in range(count)]
        for i in range(count):
            copies[i].wait()
            if i == 2:
                turned[...] = held[i][...].reshape(turned.shape)
            outs[i].start()
        for out in outs:
            out.wait()

    anywhere = pl.BlockSpec(memory_space=pl.ANY)
    sems = pltpu.SemaphoreType.DMA((len(found),))
    kept = [jax.ShapeDtypeStruct(v.shape, v.dtype) for v in found]
    kept[2] = jax.ShapeDtypeStruct((found[2].shape[1], 1, found[2].shape[2]), found[2].dtype)
    return pl.pallas_call(
        kernel,
        out_shape=kept,
        in_specs=[anywhere] * len(found),
        out_specs=[anywhere] * len(found),
        scratch_shapes=[pltpu.VMEM(v.shape, v.dtype) for v in [*found, kept[2]]] + [sems, sems],
        compiler_params=pltpu.CompilerParams(vmem_limit_bytes=63 * 2**20),
    )(*found)


def normed(values, gain, shift):
    center = values - jnp.mean(values, axis=-1, keepdims=True)
    spread = jnp.mean(center * center, axis=-1, keepdims=True)
    return center * lax.rsqrt(spread + 1e-05) * gain + shift


def gelu_exact(values):
    return jax.nn.gelu(values, approximate=False)


def segment_ids(lengths, seq_len):
    bounds = jnp.cumsum(lengths, axis=-1)
    positions = jnp.arange(seq_len, dtype=jnp.int32)
    return jnp.sum((positions[None, :, None] >= bounds[:, None, :]).astype(jnp.int32), axis=-1)


def split_heads(values):
    batch, length, width = values.shape
    return values.reshape(batch, length, width // HEAD, HEAD)


def masked_scores(queries, keys_all, segment):
    scores = jnp.einsum(
        "bqhd,bkhd->bhqk",
        split_heads(queries),
        split_heads(keys_all),
        preferred_element_type=jnp.float32,
    )
    same = (segment[:, :, None] == segment[:, None, :])[:, None]
    return (jnp.where(same, scores, -1e30), same)


def attention(queries, keys_all, values_all, segment):
    scores, same = masked_scores(queries, keys_all, segment)
    largest = jnp.max(scores, axis=-1, keepdims=True)
    raised = jnp.exp(scores - largest)
    totals = jnp.sum(raised, axis=-1, keepdims=True)
    attn_weights = raised / totals
    log_total = largest + jnp.log(totals)
    mixed = jnp.einsum(
        "bhqk,bkhd->bqhd",
        attn_weights.astype(jnp.bfloat16),
        split_heads(values_all),
        preferred_element_type=jnp.float32,
    )
    return (mixed.reshape(queries.shape).astype(jnp.bfloat16), log_total)


def attention_back(queries, keys_all, values_all, segment, log_total, grad_mixed):
    scores, same = masked_scores(queries, keys_all, segment)
    attn_weights = jnp.where(same, jnp.exp(scores - log_total), 0.0)
    grad_heads = split_heads(grad_mixed)
    grad_weights = jnp.einsum(
        "bqhd,bkhd->bhqk", grad_heads, split_heads(values_all), preferred_element_type=jnp.float32
    )
    inner = jnp.sum(attn_weights * grad_weights, axis=-1, keepdims=True)
    grad_scores = (attn_weights * (grad_weights - inner)).astype(jnp.bfloat16)
    grad_queries = jnp.einsum(
        "bhqk,bkhd->bqhd", grad_scores, split_heads(keys_all), preferred_element_type=jnp.float32
    )
    grad_keys = jnp.einsum(
        "bhqk,bqhd->bkhd", grad_scores, split_heads(queries), preferred_element_type=jnp.float32
    )
    grad_values = jnp.einsum(
        "bhqk,bqhd->bkhd",
        attn_weights.astype(jnp.bfloat16),
        grad_heads,
        preferred_element_type=jnp.float32,
    )
    shape_rows = queries.shape
    return (
        grad_queries.reshape(shape_rows),
        grad_keys.reshape(shape_rows),
        grad_values.reshape(shape_rows),
    )


def forward_layer(inputs, weights, segment):
    qkv_weight, out_weight, up_weight, down_weight, gains, biases, up_bias = weights
    width = inputs.shape[-1]
    source = inputs.astype(jnp.float32)
    normed_a = normed(source, gains[0], biases[0]).astype(jnp.bfloat16)
    project = jnp.einsum("bld,de->ble", normed_a, qkv_weight, preferred_element_type=jnp.float32)
    queries = ((project[..., :width] + biases[2]) * HEAD ** (-0.5)).astype(jnp.bfloat16)
    keys_all = project[..., width : 2 * width].astype(jnp.bfloat16)
    values_all = (project[..., 2 * width :] + biases[3]).astype(jnp.bfloat16)
    mixed, log_total = attention(queries, keys_all, values_all, segment)
    hidden = (
        source
        + jnp.einsum("bld,de->ble", mixed, out_weight, preferred_element_type=jnp.float32)
        + biases[4]
    )
    normed_c = normed(hidden, gains[1], biases[1]).astype(jnp.bfloat16)
    before = (
        jnp.einsum("bld,df->blf", normed_c, up_weight, preferred_element_type=jnp.float32) + up_bias
    )
    activated = gelu_exact(before).astype(jnp.bfloat16)
    result = (
        hidden
        + jnp.einsum("blf,fd->bld", activated, down_weight, preferred_element_type=jnp.float32)
        + biases[5]
    )
    return (
        source,
        normed_a,
        queries,
        keys_all,
        values_all,
        log_total,
        mixed,
        hidden,
        normed_c,
        before,
        activated,
        result,
    )


def backward_layer(inputs, cotangent, weights, segment):
    qkv_weight, out_weight, up_weight, down_weight, gains, biases, up_bias = weights
    width = inputs.shape[-1]
    (
        source,
        normed_a,
        queries,
        keys_all,
        values_all,
        log_total,
        mixed,
        hidden,
        normed_c,
        before,
        activated,
        result,
    ) = forward_layer(inputs, weights, segment)
    grad_result = cotangent.astype(jnp.float32)
    grad_downw = jnp.einsum("blf,bld->fd", activated, cotangent, preferred_element_type=jnp.float32)
    grad_act = jnp.einsum("bld,fd->blf", cotangent, down_weight, preferred_element_type=jnp.float32)
    grad_before = jax.vjp(gelu_exact, before)[1](grad_act)[0].astype(jnp.bfloat16)
    grad_upw = jnp.einsum("bld,blf->df", normed_c, grad_before, preferred_element_type=jnp.float32)
    grad_upb = jnp.sum(grad_before.astype(jnp.float32), axis=(0, 1))
    grad_normc = jnp.einsum(
        "blf,df->bld", grad_before, up_weight, preferred_element_type=jnp.float32
    )
    hidden_back = jax.vjp(
        normed, hidden, gains[1].astype(jnp.float32), biases[1].astype(jnp.float32)
    )[1]
    grad_hidden_ln, grad_gain_two, grad_shift_two = hidden_back(grad_normc)
    grad_hidden = grad_result + grad_hidden_ln
    grad_branch = grad_hidden.astype(jnp.bfloat16)
    grad_outw = jnp.einsum("bld,ble->de", mixed, grad_branch, preferred_element_type=jnp.float32)
    grad_mixed = jnp.einsum(
        "ble,de->bld", grad_branch, out_weight, preferred_element_type=jnp.float32
    ).astype(jnp.bfloat16)
    grad_queries, grad_keys, grad_values = attention_back(
        queries, keys_all, values_all, segment, log_total, grad_mixed
    )
    grad_project = jnp.concatenate(
        [
            grad_queries.astype(jnp.bfloat16) * HEAD ** (-0.5),
            grad_keys.astype(jnp.bfloat16),
            grad_values.astype(jnp.bfloat16),
        ],
        axis=-1,
    )
    grad_qkvw = jnp.einsum(
        "bld,ble->de", normed_a, grad_project, preferred_element_type=jnp.float32
    )
    column_sums = jnp.sum(grad_project.astype(jnp.float32), axis=(0, 1))
    grad_norma = jnp.einsum(
        "ble,de->bld", grad_project, qkv_weight, preferred_element_type=jnp.float32
    )
    source_back = jax.vjp(
        normed, source, gains[0].astype(jnp.float32), biases[0].astype(jnp.float32)
    )[1]
    grad_source_ln, grad_gain_one, grad_shift_one = source_back(grad_norma)
    grad_inputs = grad_hidden + grad_source_ln
    grad_gains = jnp.stack([grad_gain_one, grad_gain_two])
    grad_biases = jnp.stack(
        [
            grad_shift_one,
            grad_shift_two,
            column_sums[:width],
            column_sums[2 * width :],
            jnp.sum(grad_branch.astype(jnp.float32), axis=(0, 1)),
            jnp.sum(grad_result, axis=(0, 1)),
        ]
    )
    return (
        result.astype(jnp.bfloat16),
        grad_inputs,
        (grad_qkvw, grad_outw, grad_upw, grad_downw, grad_gains, grad_biases, grad_upb),
    )


def fetch_weights(layer_index, w_qkv, w_out, w_up, w_down, gains, biases, b_up):
    return (
        lax.all_gather(w_qkv[layer_index], "fsdp", axis=0, tiled=True),
        lax.all_gather(w_out[layer_index], "fsdp", axis=0, tiled=True),
        lax.all_gather(w_up[layer_index], "fsdp", axis=0, tiled=True),
        lax.all_gather(w_down[layer_index], "fsdp", axis=0, tiled=True),
        lax.all_gather(gains[layer_index], "fsdp", axis=1, tiled=True),
        lax.all_gather(biases[layer_index], "fsdp", axis=1, tiled=True),
        lax.all_gather(b_up[layer_index], "fsdp", axis=0, tiled=True),
    )


def fetch_again(layer_index, w_qkv, w_out, w_up, w_down, gains, biases, b_up):
    return (
        lax.all_gather(w_qkv[layer_index], "fsdp", axis=0, tiled=True),
        lax.all_gather(w_out[layer_index], "fsdp", axis=0, tiled=True),
        lax.all_gather(w_up[layer_index], "fsdp", axis=0, tiled=True),
        lax.all_gather(w_down[layer_index], "fsdp", axis=0, tiled=True),
        lax.all_gather(gains[layer_index], "fsdp", axis=1, tiled=True),
        lax.all_gather(biases[layer_index], "fsdp", axis=1, tiled=True),
        lax.all_gather(b_up[layer_index], "fsdp", axis=0, tiled=True),
    )


def reduce_grads(gradients):
    shares = (
        lax.psum_scatter(gradients[0], "fsdp", scatter_dimension=0, tiled=True),
        lax.psum_scatter(gradients[1], "fsdp", scatter_dimension=0, tiled=True),
        lax.psum_scatter(gradients[2], "fsdp", scatter_dimension=0, tiled=True),
        lax.psum_scatter(gradients[3], "fsdp", scatter_dimension=0, tiled=True),
        lax.psum_scatter(gradients[4], "fsdp", scatter_dimension=1, tiled=True),
        lax.psum_scatter(gradients[5], "fsdp", scatter_dimension=1, tiled=True),
        lax.psum_scatter(gradients[6], "fsdp", scatter_dimension=0, tiled=True),
    )
    quarters = (
        lax.psum_scatter(
            shares[0].astype(jnp.bfloat16), "dp", scatter_dimension=0, tiled=True
        ).astype(jnp.float32),
        lax.psum_scatter(
            shares[1].astype(jnp.bfloat16), "dp", scatter_dimension=0, tiled=True
        ).astype(jnp.float32),
        lax.psum_scatter(
            shares[2].astype(jnp.bfloat16), "dp", scatter_dimension=0, tiled=True
        ).astype(jnp.float32),
        lax.psum_scatter(
            shares[3].astype(jnp.bfloat16), "dp", scatter_dimension=0, tiled=True
        ).astype(jnp.float32),
        lax.psum_scatter(
            shares[4].astype(jnp.bfloat16), "dp", scatter_dimension=1, tiled=True
        ).astype(jnp.float32),
        lax.psum_scatter(
            shares[5].astype(jnp.bfloat16), "dp", scatter_dimension=1, tiled=True
        ).astype(jnp.float32),
        lax.psum_scatter(
            shares[6].astype(jnp.bfloat16), "dp", scatter_dimension=0, tiled=True
        ).astype(jnp.float32),
    )
    return (
        lax.all_gather(quarters[0].astype(jnp.bfloat16), "dp", axis=0, tiled=True).astype(
            jnp.float32
        ),
        lax.all_gather(quarters[1].astype(jnp.bfloat16), "dp", axis=0, tiled=True).astype(
            jnp.float32
        ),
        lax.all_gather(quarters[2].astype(jnp.bfloat16), "dp", axis=0, tiled=True).astype(
            jnp.float32
        ),
        lax.all_gather(quarters[3].astype(jnp.bfloat16), "dp", axis=0, tiled=True).astype(
            jnp.float32
        ),
        lax.all_gather(quarters[4].astype(jnp.bfloat16), "dp", axis=1, tiled=True).astype(
            jnp.float32
        ),
        lax.all_gather(quarters[5].astype(jnp.bfloat16), "dp", axis=1, tiled=True).astype(
            jnp.float32
        ),
        lax.all_gather(quarters[6].astype(jnp.bfloat16), "dp", axis=0, tiled=True).astype(
            jnp.float32
        ),
    )


def plain(
    images,
    image_cot,
    captions,
    caption_cot,
    lengths,
    w_qkv,
    w_out,
    w_up,
    w_down,
    gains,
    biases,
    b_up,
):
    owned = (w_qkv, w_out, w_up, w_down, gains, biases, b_up)
    image_seg = jnp.zeros((images.shape[0], images.shape[1]), jnp.int32)
    caption_seg = segment_ids(lengths, captions.shape[1])
    first_weights = fetch_weights(0, *owned)
    image_out = forward_layer(images, first_weights, image_seg)[-1].astype(jnp.bfloat16)
    second_weights = fetch_weights(1, *owned)
    caption_out = forward_layer(captions, second_weights, caption_seg)[-1].astype(jnp.bfloat16)
    second_back = fetch_again(1, *owned)
    _, caption_grad, caption_terms = backward_layer(captions, caption_cot, second_back, caption_seg)
    caption_shares = reduce_grads(caption_terms)
    first_back = fetch_again(0, *owned)
    _, image_grad, image_terms = backward_layer(images, image_cot, first_back, image_seg)
    image_shares = reduce_grads(image_terms)
    stacked = tuple((jnp.stack([image_shares[index], caption_shares[index]]) for index in range(7)))
    return (image_out, caption_out, image_grad, caption_grad) + stacked


def kernels_fit(mesh, w_qkv):
    return mesh.shape["dp"] == 4 and mesh.shape["fsdp"] % 2 == 0 and w_qkv.shape[1] % 32 == 0


def local(mesh, images, image_cot, captions, caption_cot, lengths, w_qkv, w_out, w_up, w_down, gains, biases, b_up):
    if not kernels_fit(mesh, w_qkv):
        return plain(
            images, image_cot, captions, caption_cot, lengths, w_qkv, w_out, w_up, w_down, gains, biases, b_up
        )
    return whole(
        mesh.shape["fsdp"] // 2, images, image_cot, captions, caption_cot, lengths,
        (w_qkv, w_out, w_up, w_down), gains, biases, b_up
    )


def solution(mesh):
    placed = (
        P(("dp", "fsdp"), None, None),
        P(("dp", "fsdp"), None, None),
        P(("dp", "fsdp"), None, None),
        P(("dp", "fsdp"), None, None),
        P(("dp", "fsdp"), None),
        P(None, "fsdp", None),
        P(None, "fsdp", None),
        P(None, "fsdp", None),
        P(None, "fsdp", None),
        P(None, None, "fsdp"),
        P(None, None, "fsdp"),
        P(None, "fsdp"),
    )
    return jax.shard_map(
        functools.partial(local, mesh),
        mesh=mesh,
        in_specs=placed,
        out_specs=(
            P(("dp", "fsdp"), None, None),
            P(("dp", "fsdp"), None, None),
            P(("dp", "fsdp"), None, None),
            P(("dp", "fsdp"), None, None),
            P(None, "fsdp", None),
            P(None, "fsdp", None),
            P(None, "fsdp", None),
            P(None, "fsdp", None),
            P(None, None, "fsdp"),
            P(None, None, "fsdp"),
            P(None, "fsdp"),
        ),
        check_vma=False,
    )
```

```python
import functools

import jax
import jax.numpy as jnp
from jax import lax
from jax.experimental import pallas as pl
from jax.experimental.pallas import tpu as pltpu
from jax.sharding import PartitionSpec as P

HEAD = 64

MESH = pl.DeviceIdType.MESH
NT = (((1,), (1,)), ((), ()))
TN = (((0,), (0,)), ((), ()))
TILE = 256
CHUNK = 64
ALL = slice(None)


def dot(a, b, dims=(((1,), (0,)), ((), ()))):
    return lax.dot_general(a, b, dims, preferred_element_type=jnp.float32)


def flat(value):
    return value.reshape(-1, value.shape[-1])


def at(t, size=TILE):
    return pl.ds(pl.multiple_of(t * size, size), size)


def remote(src, dst, send, recv, device):
    return pltpu.make_async_remote_copy(
        src_ref=src, dst_ref=dst, send_sem=send, recv_sem=recv, device_id=device, device_id_type=MESH
    )


class Place:
    def __init__(self, line):
        dp, fs = lax.axis_index("dp"), lax.axis_index("fsdp")
        self.line, self.dp, self.fs = line, dp, fs
        self.x, self.c = dp // 2, dp % 2
        self.z, self.y = fs // 2, fs % 2
        self.up, self.down = (dp, fs + 2), (dp, fs - 2)
        self.yway = (dp, self.z * 2 + 1 - self.y)
        self.xway = ((1 - self.x) * 2 + self.c, fs)
        self.core = (self.x * 2 + 1 - self.c, fs)
        self.has_up, self.has_down = self.z + 1 < line, self.z > 0

    def others(self):
        return [lax.rem(self.fs + step, 2 * self.line) for step in range(1, 2 * self.line)]

    def greet(self, meanwhile):
        barrier = pltpu.get_barrier_semaphore()
        known = [(self.dp, other) for other in self.others()] + [self.xway, self.core]
        for device in known:
            pl.semaphore_signal(barrier, inc=1, device_id=device, device_id_type=MESH)
        meanwhile()
        pl.semaphore_wait(barrier, len(known))


class Panel:
    def __init__(self, which, part, width):
        self.which, self.part, self.width = which, part, width

    def cols(self, cut):
        base = 0 if self.which == 3 else self.part * self.width
        if cut is None:
            return pl.ds(base, self.width)
        return pl.ds(pl.multiple_of(base + cut[0], 128), cut[1])

    def of(self, ref, *lead, cut=None):
        if self.which == 3:
            return ref.at[(*lead, self.part, ALL, self.cols(cut))]
        return ref.at[(*lead, ALL, self.cols(cut))]


class Cuts:
    def __init__(self, width, x, thirds):
        third = width // 3
        self.half = (x * (width // 2), width // 2)
        self.other_half = ((1 - x) * (width // 2), width // 2)
        self.wide, self.outer, self.other_outer = self.half, self.half, self.other_half
        if thirds:
            self.wide = (x * third, 2 * third)
            self.outer = (x * 2 * third, third)
            self.other_outer = ((1 - x) * 2 * third, third)


def ds(cut):
    return pl.ds(pl.multiple_of(cut[0], 128), cut[1])


def panels_of(layer_shapes, width, order):
    made = []
    for which in order:
        count = layer_shapes[which]
        made += [Panel(which, part, width) for part in range(count)]
    return made


class Gather:
    def __init__(self, at, place, own, panel, full, way, send, recv, near, trade):
        self.trade = trade
        self.at, self.place, self.own, self.panel, self.full = at, place, own, panel, full
        self.send, self.recv, self.near = send, recv, near
        self.split, self.older = way == SPLIT, None
        split = self.split
        cuts = Cuts(panel.width, place.x, way == THIRDS)
        self.lane, self.other_lane = (cuts.half, cuts.other_half) if split else (None, None)
        self.over_y = cuts.half if split else cuts.wide
        self.over_x, self.from_x = (cuts.half, cuts.other_half) if split else (cuts.outer, cuts.other_outer)

    def view(self, block, y, c, cut=None):
        return self.panel.of(self.full, block, y, c, cut=cut)

    def sent(self, slot):
        return self.send.at[self.at % AG_RING, slot]

    def got(self, slot):
        return self.recv.at[self.at, slot]

    def line_copy(self, way, block):
        p = self.place
        ref = self.view(block, p.y, p.c, self.lane)
        return remote(ref, ref, self.sent(block + way), self.got(block), (p.up, p.down)[way])

    def near_copy(self):
        p = self.place
        mine = self.panel.of(self.own, p.c)
        return pltpu.make_async_copy(mine, self.view(p.z, p.y, p.c), self.near.at[self.at % AG_RING])

    def far_copy(self, kind):
        p, line = self.place, self.place.line
        ref, device = {
            "y": (lambda: (self.view(ALL, p.y, p.c, self.over_y), p.yway)),
            "x": (lambda: (self.view(ALL, 1 - p.y, p.c, self.over_x), p.xway)),
            "core_own": (lambda: (self.view(ALL, p.y, p.c), p.core)),
            "core": (lambda: (self.view(ALL, 1 - p.y, p.c), p.core)),
        }[kind]()
        slot = FAR.index(kind)
        return remote(ref, ref, self.sent(line + 1 + slot), self.got(line + slot), device)

    def trade_copy(self, block, lane):
        p = self.place
        ref = self.view(block, p.y, p.c, lane)
        return remote(ref, ref, self.trade.at[0, block], self.trade.at[1, block], p.xway)

    def landed(self, kind):
        p, line = self.place, self.place.line
        ref = {
            "y": lambda: self.view(ALL, 1 - p.y, p.c, self.over_y),
            "x": lambda: self.view(ALL, 1 - p.y, p.c, self.from_x),
            "core_own": lambda: self.view(ALL, p.y, 1 - p.c),
            "core": lambda: self.view(ALL, 1 - p.y, 1 - p.c),
        }[kind]()
        slot = FAR.index(kind)
        return remote(ref, ref, self.sent(line + 1 + slot), self.got(line + slot), p.core)

    def kinds(self):
        return FAR

    def first(self):
        p = self.place
        if self.older is not None:
            self.older.drain()
        self.near_copy().start()
        mine = self.panel.of(self.own, p.c, cut=self.lane)
        there = self.view(p.z, p.y, p.c, self.lane)
        for way, able, device in ((0, p.has_up, p.up), (1, p.has_down, p.down)):
            copy = functools.partial(remote, mine, there, self.sent(p.z + way), self.got(p.z), device)
            pl.when(able)(lambda copy=copy: copy().start())

    def hop(self, k):
        p = self.place

        def pass_on(way, block, more):
            self.line_copy(way, block).wait_recv()
            pl.when(more)(lambda: self.line_copy(way, block).start())
            if self.split:
                self.trade_copy(block, self.lane).start()

        pl.when(p.z - k >= 0)(lambda: pass_on(0, p.z - k, p.has_up))
        pl.when(p.z + k < p.line)(lambda: pass_on(1, p.z + k, p.has_down))
        if k == p.line - 1:
            self.near_copy().wait()
            self.far_copy("y").start()
            if not self.split:
                self.far_copy("core_own").start()

    def cross(self):
        self.landed("y").wait_recv()
        self.far_copy("x").start()
        if self.split:
            self.trades(lambda block: self.trade_copy(block, self.other_lane).wait_recv())
            self.far_copy("core_own").start()

    def trades(self, body):
        for block in range(self.place.line):
            pl.when(block != self.place.z)(functools.partial(body, block))

    def share(self):
        self.landed("x").wait_recv()
        self.far_copy("core").start()

    def stages(self):
        hops = [functools.partial(self.hop, k) for k in range(1, self.place.line)]
        return [self.first, *hops, self.cross, self.share]

    def arrive(self):
        self.landed("core_own").wait_recv()
        self.landed("core").wait_recv()

    def drain(self):
        p = self.place

        def body(block, carry):
            pl.when(p.has_up & (block <= p.z))(lambda: self.line_copy(0, block).wait_send())
            pl.when(p.has_down & (block >= p.z))(lambda: self.line_copy(1, block).wait_send())
            return carry

        lax.fori_loop(0, p.line, body, 0)
        for kind in self.kinds():
            self.far_copy(kind).wait_send()
        if self.split:
            self.trades(lambda block: self.trade_copy(block, self.lane).wait_send())


FAR = ("y", "x", "core_own", "core")
HALVES, THIRDS, SPLIT, LINE_FIRST = range(4)
AG_RING = 12
GATHER_WAYS = (
    1, 2, 1, 1, 2, 0, 2, 1, 1, 2, 1, 2, 0, 0, 0, 0, 0, 0, 0, 0, 0, 0, 0, 0,
)
SUM_WAYS = (
    0, 1, 0, 0, 1, 1, 0, 1, 0, 1, 2, 1, 1, 0, 2, 0, 0, 1, 2, 1, 0, 1, 2, 0,
)
RINGS = dict(own=12, away=6, other=3, from_x=4, from_y=4, line_in=5, last=3, total=3, line_away=1)
LINE_FIRSTS = min(1, SUM_WAYS.count(LINE_FIRST))
SUM_SEMS = dict(
    core=(RINGS["away"], 1, RINGS["other"], 1),
    x=(RINGS["away"], 1, RINGS["from_x"], 1),
    y=(RINGS["away"], 1, RINGS["from_y"], 1),
    line=(RINGS["own"], 4, RINGS["line_in"], 5),
    line_away=(LINE_FIRSTS and RINGS["own"], 4, LINE_FIRSTS and RINGS["line_away"], 5),
    last=(RINGS["own"], 1, RINGS["last"], 1),
    out=(RINGS["total"], 1, 24, 1),
)


def starts_of(kinds):
    found, out_at, in_at = {}, 0, 0
    for name, (out_ring, out_each, in_ring, in_each) in kinds.items():
        found[name] = (out_at, in_at)
        out_at, in_at = out_at + out_ring * out_each, in_at + in_ring * in_each
    return found, out_at, in_at


SUM_STARTS, SUM_SENDS, SUM_ARRIVALS = starts_of(SUM_SEMS)
CREDITS, CREDIT_COUNT = {}, 0
for _name, _ring in (
    ("other", "other"),
    ("from_x", "from_x"),
    ("from_y", "from_y"),
    ("line_up", "line_in"),
    ("line_down", "line_in"),
    ("away_up", "line_away"),
    ("away_down", "line_away"),
    ("last", "last"),
):
    CREDITS[_name] = CREDIT_COUNT
    CREDIT_COUNT += RINGS[_ring]


class Reduce:
    def __init__(self, at, count, turn, place, panel, way, terms, out, bufs, credit, send, recv, near):
        self.at, self.count, self.place, self.panel, self.terms, self.out = at, count, place, panel, terms, out
        self.credit, self.send, self.recv, self.near = credit, send, recv, near
        self.older, self.flush = {}, None
        self.turn = turn
        self.b = {name: ref.at[self.slot(name)] for name, ref in bufs.items()}
        cuts = Cuts(panel.width, place.x, way == THIRDS)
        self.split, self.line_first = way == SPLIT, way == LINE_FIRST
        self.wide, self.outer, self.other_outer = ds(cuts.wide), ds(cuts.outer), ds(cuts.other_outer)
        self.lane = self.outer if self.split else pl.ds(0, panel.width)
        if self.split:
            self.wide = pl.ds(0, panel.width)
        self.lanes = panel.width // 2 if self.split else panel.width
        over_y = panel.width if self.split or self.line_first else cuts.wide[1]
        self.b["from_x"] = self.b["from_x"].at[:, :, 0 : cuts.outer[1]]
        self.b["from_y"] = self.b["from_y"].at[:, :, 0:over_y]
        self.b["last"] = self.b["last"].at[:, 0 : self.lanes]

    def turn_of(self, ring):
        return self.turn if ring == "line_away" else (self.at, self.count)

    def slot(self, ring):
        return self.turn_of(ring)[0] % RINGS[ring]

    def spend(self, name, ring):
        if self.turn_of(ring)[0] >= RINGS[ring]:
            pl.semaphore_wait(self.credit.at[CREDITS[name] + self.slot(ring)], 1)

    def grant(self, name, ring, device):
        turn, count = self.turn_of(ring)
        if turn + RINGS[ring] < count:
            credit = self.credit.at[CREDITS[name] + self.slot(ring)]
            pl.semaphore_signal(credit, inc=1, device_id=device, device_id_type=MESH)

    def sems(self, name, slot=(0, 0)):
        out_ring, out_each, in_ring, in_each = SUM_SEMS[name]
        out_at, in_at = SUM_STARTS[name]
        out_at += self.at % out_ring * out_each + slot[0]
        in_at += (self.slot(name) if name == "line_away" else self.at % in_ring) * in_each + slot[1]
        return self.send.at[out_at], self.recv.at[in_at]

    def core_copy(self):
        p = self.place
        return remote(self.panel.of(self.terms, ALL, ALL, 1 - p.c), self.b["other"], *self.sems("core"), p.core)

    def near_copy(self, away):
        p = self.place
        src = self.panel.of(self.terms, ALL, (1 - p.y) if away else p.y, p.c)
        return pltpu.make_async_copy(src, self.b["away" if away else "own"], self.near.at[self.at % RINGS["other"] * 2 + int(away)])

    def x_copy(self):
        p = self.place
        src = self.b["own" if self.split else "away"].at[:, :, self.other_outer]
        return remote(src, self.b["from_x"], *self.sems("x"), p.xway)

    def y_copy(self):
        p = self.place
        if self.line_first:
            return remote(self.b["away"].at[p.z], self.b["from_y"].at[0], *self.sems("y"), p.yway)
        return remote(self.b["away"].at[:, :, self.wide], self.b["from_y"], *self.sems("y"), p.yway)

    def came(self, way, block, away=False):
        return self.b["line_away" if away else "line_in"].at[block + 1 - way, :, 0 : self.lanes]

    def line_copy(self, way, block, away=False):
        p = self.place
        sems = self.sems("line_away" if away else "line", (block, block + 1 - way))
        src = self.b["away" if away else "own"].at[block, :, self.lane]
        return remote(src, self.came(way, block, away), *sems, (p.up, p.down)[way])

    def columns(self):
        return (False, True) if self.line_first else (False,)

    def last_copy(self):
        p = self.place
        return remote(self.b["own"].at[p.z, :, self.lane], self.b["last"], *self.sems("last"), p.xway)

    def out_copy(self):
        ref = self.panel.of(self.out, self.place.c)
        return remote(self.b["total"], ref, *self.sems("out"), self.place.core)

    def out_landed(self):
        ref = self.panel.of(self.out, 1 - self.place.c)
        return remote(self.b["total"], ref, *self.sems("out"), self.place.core)

    def out_near(self):
        return pltpu.make_async_copy(self.b["total"], self.panel.of(self.out, self.place.c), self.near.at[2 * RINGS["other"] + self.at % RINGS["total"]])

    def each(self, body):
        def step(block, carry):
            body(block)
            return carry

        lax.fori_loop(0, self.place.line, step, 0)

    def start(self):
        if self.flush is not None:
            self.flush()
        if "away" in self.older:
            self.older["away"].free_away()
        if "own" in self.older:
            self.older["own"].free_own()
        self.spend("other", "other")
        self.core_copy().start()
        self.near_copy(False).start()
        self.near_copy(True).start()

    def add_core(self):
        p, b = self.place, self.b
        self.near_copy(False).wait()
        self.near_copy(True).wait()
        self.core_copy().wait_recv()

        def body(block):
            b["away"][block] = b["away"][block] + b["other"][block, 1 - p.y]

        self.each(body)
        if self.split:
            self.spend("from_y", "from_y")
            self.y_copy().start()
        else:
            self.spend("from_x", "from_x")
            if self.line_first:
                self.grant("from_x", "from_x", p.xway)
            else:
                self.x_copy().start()

        def rest(block):
            b["own"][block] = b["own"][block] + b["other"][block, p.y]

        self.each(rest)
        self.grant("other", "other", p.core)

    def add_x(self):
        p, b = self.place, self.b
        self.x_copy().wait_recv()
        cols = self.outer

        def body(block):
            b["away"][block, :, cols] = b["away"][block, :, cols] + b["from_x"][block]

        self.each(body)
        self.spend("from_y", "from_y")
        self.y_copy().start()
        self.grant("from_x", "from_x", p.xway)

    def add_x_after(self):
        p, b = self.place, self.b
        self.x_copy().wait_recv()
        cols = self.outer

        def body(block):
            b["own"][block, :, cols] = b["own"][block, :, cols] + b["from_x"][block]

        self.each(body)
        self.grant("from_x", "from_x", p.xway)
        self.line_step(0)

    def add_y(self):
        p, b = self.place, self.b
        self.y_copy().wait_recv()
        cols = self.wide

        def body(block):
            b["own"][block, :, cols] = b["own"][block, :, cols] + b["from_y"][block]

        self.each(body)
        self.grant("from_y", "from_y", p.yway)
        if self.split:
            self.spend("from_x", "from_x")
            self.x_copy().start()
        else:
            self.line_step(0)

    def add_line(self, way, block):
        for away in self.columns():
            self.line_copy(way, block, away).wait_recv()
            sums, lane = self.b["away" if away else "own"], self.lane
            sums[block, :, lane] = sums[block, :, lane] + self.came(way, block, away)[...]

    def line_step(self, k):
        p, line = self.place, self.place.line
        if k == 0:
            pl.when(p.has_up)(lambda: self.spend("line_up", "line_in"))
            pl.when(p.has_down)(lambda: self.spend("line_down", "line_in"))
            if self.line_first:
                pl.when(p.has_up)(lambda: self.spend("away_up", "line_away"))
                pl.when(p.has_down)(lambda: self.spend("away_down", "line_away"))
        for way, steps_in, block, more in (
            (0, p.z, line - 1 - k + p.z, p.has_down),
            (1, line - 1 - p.z, k - (line - 1 - p.z), p.has_up),
        ):

            def body(way=way, block=block, more=more):
                pl.when(more)(lambda: self.add_line(way, block))
                for away in self.columns():
                    self.line_copy(way, block, away).start()

            pl.when(steps_in <= k)(body)

    def own_step(self):
        p = self.place
        pl.when(p.has_down)(lambda: self.add_line(0, p.z))
        pl.when(p.has_up)(lambda: self.add_line(1, p.z))
        if self.line_first:
            self.spend("from_y", "from_y")
            self.y_copy().start()
            pl.when(p.has_down)(lambda: self.grant("away_up", "line_away", p.down))
            pl.when(p.has_up)(lambda: self.grant("away_down", "line_away", p.up))
        else:
            self.spend("last", "last")
            self.last_copy().start()
        pl.when(p.has_down)(lambda: self.grant("line_up", "line_in", p.down))
        pl.when(p.has_up)(lambda: self.grant("line_down", "line_in", p.up))

    def add_y_last(self):
        p, b = self.place, self.b
        self.y_copy().wait_recv()
        b["own"][p.z] = b["own"][p.z] + b["from_y"][0]
        self.grant("from_y", "from_y", p.yway)
        self.spend("last", "last")
        self.last_copy().start()

    def finish(self):
        p, b = self.place, self.b
        if "total" in self.older:
            self.older["total"].free_total()
        self.last_copy().wait_recv()
        if self.split:
            b["total"][:, self.outer] = b["own"][p.z, :, self.outer].astype(jnp.float32)
            b["total"][:, self.other_outer] = b["last"][...].astype(jnp.float32)
        else:
            b["total"][...] = b["own"][p.z].astype(jnp.float32) + b["last"][...].astype(jnp.float32)
        self.grant("last", "last", p.xway)
        self.out_copy().start()
        self.out_near().start()

    def stages(self):
        if self.line_first:
            steps = [functools.partial(self.line_step, k) for k in range(self.place.line - 1)]
            return [self.start, self.add_core, *steps, self.own_step, self.add_y_last, self.finish]
        steps = [self.start, self.add_core]
        steps += [self.add_y, self.add_x_after] if self.split else [self.add_x, self.add_y]
        steps += [functools.partial(self.line_step, k) for k in range(1, self.place.line - 1)]
        return steps + [self.own_step, self.finish]

    def uses(self):
        if self.line_first:
            return dict(from_x=(1, 1), from_y=(5, 6), line_in=(2, 5), line_away=(2, 5), last=(6, 7))
        if self.split:
            return dict(from_y=(1, 2), from_x=(2, 3), line_in=(3, 6), last=(6, 7))
        return dict(from_x=(1, 2), from_y=(2, 3), line_in=(3, 6), last=(6, 7))

    def free_away(self):
        self.core_copy().wait_send()
        if not self.line_first:
            self.x_copy().wait_send()
        self.y_copy().wait_send()
        if self.line_first:
            self.free_line(True)

    def free_line(self, away):
        p = self.place
        for block in range(p.line):
            pl.when(block > p.z)(lambda block=block: self.line_copy(0, block, away).wait_send())
            pl.when(block < p.z)(lambda block=block: self.line_copy(1, block, away).wait_send())

    def free_own(self):
        self.free_line(False)
        self.last_copy().wait_send()

    def free_total(self):
        self.out_copy().wait_send()
        self.out_near().wait()


class Layer:
    def __init__(self, n, kept, weights, par, b_up, terms, g_par, g_bup):
        self.n, self.s = n, kept
        self.w_qkv, self.w_out, self.w_up, self.w_down = weights
        self.par, self.b_up = par, b_up
        self.g_qkv, self.g_out, self.g_up, self.g_down = terms
        self.g_par, self.g_bup = g_par, g_bup
        self.width, self.deep = self.w_out.shape[-1], self.w_up.shape[-1]
        self.pending = [None, None]

    def chunks(self, body):
        def step(i, carry):
            body(at(i, CHUNK))
            return carry

        lax.fori_loop(0, self.n // CHUNK, step, 0)

    def tiles(self, first, last, body):
        def step(i, carry):
            body(i)
            return carry

        lax.fori_loop(first, last, step, 0)

    def row(self, ref, i):
        return ref[i : i + 1, :]

    def tall_copy(self, ref, slot, t):
        stage = self.s["stage"].at[slot].reshape(*ref.shape[:4], self.width)
        cols = at(t, self.width)
        return pltpu.make_async_copy(stage, ref.at[:, :, :, :, cols], self.s["stage_sem"].at[slot])

    def wide_copy(self, ref, slot, t):
        stage = self.s["stage"].at[slot].reshape(*ref.shape[1:])
        return pltpu.make_async_copy(stage, ref.at[t], self.s["stage_sem"].at[slot])

    def put(self, make, slot, t, first, value):
        held = self.pending[slot]
        pl.when(t > first)(lambda: make(slot, t - 1).wait())
        if held is not None:
            pl.when(t == first)(lambda: held.wait())
        self.s["stage"][slot] = value.astype(jnp.bfloat16)
        make(slot, t).start()

    def put_all(self):
        for slot in range(2):
            if self.pending[slot] is not None:
                self.pending[slot].wait()
            self.pending[slot] = None

    def mask(self, ends):
        s = self.s

        def mask(rows):
            shape = (CHUNK, self.n)
            at_row = lax.broadcasted_iota(jnp.int32, shape, 0) + rows.start
            at_col = lax.broadcasted_iota(jnp.int32, shape, 1)
            one, other = jnp.zeros(shape, jnp.int32), jnp.zeros(shape, jnp.int32)
            for end in ends:
                one = one + (at_row >= end).astype(jnp.int32)
                other = other + (at_col >= end).astype(jnp.int32)
            s["bias"][rows, :] = jnp.where(one == other, 0.0, -1e30)

        self.chunks(mask)

    def prepare(self):
        s, width = self.s, self.width
        s["rows"][0:1, 0:width] = self.par[4:5, :]
        s["rows"][0:1, width : 2 * width] = jnp.zeros((1, width), jnp.float32)
        s["rows"][0:1, 2 * width :] = self.par[5:6, :]

    def norm_parts(self, values):
        center = values - jnp.mean(values, axis=-1, keepdims=True)
        scale = lax.rsqrt(jnp.mean(center * center, axis=-1, keepdims=True) + 1e-05)
        return center * scale, scale

    def norm(self, src, dst, which):
        def body(rows):
            unit, _ = self.norm_parts(src[rows, :].astype(jnp.float32))
            dst[rows, :] = (unit * self.row(self.par, which) + self.row(self.par, 2 + which)).astype(jnp.bfloat16)

        self.chunks(body)

    def norm_a(self):
        self.norm(self.s["x"], self.s["a"], 0)

    def project(self, first, last):
        s = self.s
        queries = self.width // TILE

        def body(t):
            scale = jnp.where(t < queries, HEAD ** (-0.5), 1.0)
            found = dot(s["a"][...], flat(self.w_qkv[:, :, :, :, at(t)])) + s["rows"][0:1, at(t)]
            s["qkv"][:, at(t)] = (found * scale).astype(jnp.bfloat16)

        self.tiles(first, last, body)

    def turn_a(self):
        self.s["a_t"][...] = self.s["a"][...].T

    def pair(self, i, which):
        start = which * self.width + i * 128
        return self.s["qkv"].at[:, pl.ds(pl.multiple_of(start, 128), 128)]

    def own_lanes(self, value, head):
        lanes = lax.broadcasted_iota(jnp.int32, value.shape, 1)
        return jnp.where((lanes < HEAD) == (head == 0), value, jnp.zeros_like(value))

    def attend(self, first, last):
        s = self.s

        def body(i):
            q, k, v = (self.pair(i, which) for which in range(3))
            keys = [self.own_lanes(k[...], head) for head in range(2)]
            vals = [self.own_lanes(v[...], head) for head in range(2)]
            for part in range(self.n // TILE):
                cols = slice(part * TILE, part * TILE + TILE)
                mixed = None
                for head in range(2):
                    scores = dot(keys[head], q[cols, :], NT) + s["bias"][:, cols]
                    raised = jnp.exp(scores - jnp.max(scores, axis=0, keepdims=True))
                    share = 1.0 / jnp.sum(raised, axis=0, keepdims=True)
                    weights = (raised * share).astype(jnp.bfloat16)
                    s["wt"][2 * i + head, :, cols] = weights
                    found = dot(vals[head], weights, TN)
                    mixed = found if mixed is None else mixed + found
                s["o"][cols, at(i, 128)] = mixed.T.astype(jnp.bfloat16)

        self.tiles(first, last, body)

    def branch(self):
        s = self.s

        def body(t):
            found = dot(s["o"][...], flat(self.w_out[:, :, :, :, at(t)])) + self.par[6:7, at(t)]
            s["h"][:, at(t)] = s["x"][:, at(t)].astype(jnp.float32) + found

        self.tiles(0, self.width // TILE, body)
        s["o_t"][...] = s["o"][...].T

    def norm_c(self):
        self.norm(self.s["h"], self.s["c"], 1)

    def up(self, first, last):
        s = self.s

        def body(t):
            before = dot(s["c"][...], flat(self.w_up[:, :, :, :, at(t)])) + self.b_up[0:1, at(t)]
            chance = 0.5 + 0.5 * lax.erf(before * 0.7071067811865476)
            s["g"][:, at(t)] = (before * chance).astype(jnp.bfloat16)
            slope = chance + before * (jnp.exp(before * before * -0.5) * 0.3989422804014327)
            s["du"][:, at(t)] = slope.astype(jnp.bfloat16)

        self.tiles(first, last, body)

    def turn_c(self):
        self.s["c_t"][...] = self.s["c"][...].T

    def down(self):
        s = self.s

        def body(t):
            found = dot(s["g"][...], flat(self.w_down[:, :, :, :, :, at(t)])) + self.par[7:8, at(t)]
            s["a"][:, at(t)] = (s["h"][:, at(t)] + found).astype(jnp.bfloat16)

        self.tiles(0, self.width // TILE, body)

    def feed_back(self, first, last):
        s, width = self.s, self.width
        tall = functools.partial(self.tall_copy, self.g_up)

        def body(t):
            cols = at(t, width)
            grad = dot(s["dy"][...], flat(self.w_down[t]), NT)
            low = (grad * s["du"][:, cols].astype(jnp.float32)).astype(jnp.bfloat16)
            s["du"][:, cols] = low
            self.g_bup[0:1, cols] = jnp.sum(low.astype(jnp.float32), axis=0, keepdims=True)
            self.put(tall, 1, t, first, dot(s["c_t"][...], low))

        self.tiles(first, last, body)
        self.pending[1] = tall(1, last - 1)

    def down_terms(self, first, last):
        s, width = self.s, self.width
        wide = functools.partial(self.wide_copy, self.g_down)

        def body(t):
            self.put(wide, 0, t, first, dot(s["g"][:, at(t, width)], s["dy"][...], TN))

        self.tiles(first, last, body)
        self.pending[0] = wide(0, last - 1)

    def up_back(self):
        self.s["sums"][...] = dot(self.s["du"][...], flat(self.w_up[...]), NT)

    def norm_back(self, src, which, grad, rest, body_out):
        def body(rows):
            unit, scale = self.norm_parts(src[rows, :].astype(jnp.float32))
            came = grad[rows, :]
            gained = came * self.row(self.par, which)
            self.g_par[which : which + 1, :] += jnp.sum(came * unit, axis=0, keepdims=True)
            self.g_par[2 + which : 3 + which, :] += jnp.sum(came, axis=0, keepdims=True)
            inner = gained - jnp.mean(gained, axis=-1, keepdims=True)
            inner = inner - unit * jnp.mean(gained * unit, axis=-1, keepdims=True)
            body_out(rows, rest[rows, :].astype(jnp.float32) + inner * scale)

        self.chunks(body)

    def norm_c_back(self):
        s = self.s

        def keep(rows, grad):
            s["h"][rows, :] = grad
            low = grad.astype(jnp.bfloat16)
            s["c"][rows, :] = low
            self.g_par[6:7, :] += jnp.sum(low.astype(jnp.float32), axis=0, keepdims=True)
            self.g_par[7:8, :] += jnp.sum(s["dy"][rows, :].astype(jnp.float32), axis=0, keepdims=True)

        self.norm_back(s["h"], 1, s["sums"], s["dy"], keep)

    def branch_back(self):
        s = self.s
        tall = functools.partial(self.tall_copy, self.g_out)
        self.put(tall, 0, 0, 0, dot(s["o_t"][...], s["c"][...]))
        self.pending[0] = tall(0, 0)
        s["a"][...] = dot(s["c"][...], flat(self.w_out[...]), NT).astype(jnp.bfloat16)

    def attend_back(self, first, last):
        s, width = self.s, self.width

        def body(i):
            q, k, v = (self.pair(i, which) for which in range(3))
            came = s["a"].at[:, at(i, 128)]
            dq = dk = dv = None
            for head in range(2):
                vals = self.own_lanes(v[...], head)
                for part in range(self.n // TILE):
                    cols = slice(part * TILE, part * TILE + TILE)
                    grad = dot(vals, came[cols, :], NT)
                    weights = s["wt"][2 * i + head, :, cols].astype(jnp.float32)
                    product = weights * grad
                    inner = jnp.sum(product, axis=0, keepdims=True)
                    s["ds"][:, cols] = (product - weights * inner).astype(jnp.bfloat16)
                one_q = dot(self.own_lanes(k[...], head), s["ds"][...], TN)
                one_k = dot(s["ds"][...], self.own_lanes(q[...], head))
                one_v = dot(s["wt"][2 * i + head], self.own_lanes(came[...], head))
                dq, dk, dv = (one_q, one_k, one_v) if head == 0 else (dq + one_q, dk + one_k, dv + one_v)
            s["g"][:, at(i, 128)] = dq.T.astype(jnp.bfloat16) * HEAD ** (-0.5)
            s["g"][:, pl.ds(pl.multiple_of(width + i * 128, 128), 128)] = dk.astype(jnp.bfloat16)
            s["g"][:, pl.ds(pl.multiple_of(2 * width + i * 128, 128), 128)] = dv.astype(jnp.bfloat16)

        self.tiles(first, last, body)

    def project_terms(self, first, last):
        s, width = self.s, self.width
        tall = functools.partial(self.tall_copy, self.g_qkv)
        for t in range(first, last):
            grad = s["g"][:, t * width : (t + 1) * width]
            if t != 1:
                row = 4 + t // 2
                self.g_par[row : row + 1, :] = jnp.sum(grad.astype(jnp.float32), axis=0, keepdims=True)
            slot = (t + 1) % 2
            self.put(tall, slot, t, t, dot(s["a_t"][...], grad))
            self.pending[slot] = tall(slot, t)

    def project_back(self):
        s = self.s
        s["sums"][...] = dot(s["g"][:, 0 : 3 * self.width], flat(self.w_qkv[...]), NT)

    def norm_a_back(self):
        s = self.s

        def keep(rows, grad):
            s["h"][rows, :] = grad

        self.norm_back(s["x"], 0, s["sums"], s["h"], keep)


def layer_scratch(n, width, deep):
    low, full = jnp.bfloat16, jnp.float32
    return dict(
        a=pltpu.VMEM((n, width), low),
        a_t=pltpu.VMEM((width, n), low),
        qkv=pltpu.VMEM((n, 3 * width), low),
        bias=pltpu.VMEM((n, n), full),
        wt=pltpu.VMEM((width // HEAD, n, n), low),
        ds=pltpu.VMEM((n, n), low),
        o=pltpu.VMEM((n, width), low),
        o_t=pltpu.VMEM((width, n), low),
        h=pltpu.VMEM((n, width), full),
        c=pltpu.VMEM((n, width), low),
        c_t=pltpu.VMEM((width, n), low),
        g=pltpu.VMEM((n, deep), low),
        du=pltpu.VMEM((n, deep), low),
        sums=pltpu.VMEM((n, width), full),
        rows=pltpu.VMEM((8, 3 * width), full),
        stage=pltpu.VMEM((2, width, width), low),
        stage_sem=pltpu.SemaphoreType.DMA((2,)),
    )


def cut(kept, n):
    cuts = dict(kept)
    for name in ("a", "qkv", "o", "h", "c", "g", "du", "sums"):
        cuts[name] = kept[name].at[0:n]
    for name in ("a_t", "o_t", "c_t"):
        cuts[name] = kept[name].at[:, 0:n]
    for name in ("bias", "ds"):
        cuts[name] = kept[name].at[0:n, 0:n]
    cuts["wt"] = kept["wt"].at[:, 0:n, 0:n]
    return cuts


ORDER = (0, 1, 2, 3)
BACK = (3, 2, 1, 0)


class SmallSum:
    def __init__(self, place, parts, land, line_land, out, send, recv):
        self.place, self.parts, self.land, self.line_land, self.out = place, parts, land, line_land, out
        self.send, self.recv = send, recv

    def near(self, step):
        p = self.place
        device = (p.core, p.xway, p.yway)[step]
        return remote(self.parts.at[step], self.land.at[step], self.send.at[step], self.recv.at[step], device)

    def far(self, step):
        p = self.place
        other = lax.rem(p.z + step, p.line)
        device = (p.dp, other * 2 + p.y)
        src = self.parts.at[3]
        return remote(src, self.line_land.at[p.z], self.send.at[3 + other], self.recv.at[3 + p.z], device)

    def from_far(self, step):
        p = self.place
        other = lax.rem(p.z + step, p.line)
        device = (p.dp, other * 2 + p.y)
        src = self.parts.at[3]
        return remote(src, self.line_land.at[other], self.send.at[3 + other], self.recv.at[3 + other], device)

    def stage(self, step):
        p = self.place
        if step:
            if step <= 3:
                self.near(step - 1).wait_recv()
                self.parts[step] = self.parts[step - 1] + self.land[step - 1]
        if step < 3:
            self.near(step).start()
        if step == 3:
            for other in range(1, p.line):
                self.far(other).start()
            self.line_land[p.z] = self.parts[3]
        if step == 4:
            for other in range(1, p.line):
                self.from_far(other).wait_recv()
            gains, biases, b_up = self.out
            piece, deep = gains.shape[-1], b_up.shape[-1]
            wide = self.line_land.shape[-1] // deep

            def mine(block):
                for block_at in range(p.line):
                    part = self.line_land[block_at, :, 0:8, block * piece : (block + 1) * piece]
                    row, start = 8 + block // wide, block % wide * deep
                    up = self.line_land[block_at, :, row, start : start + deep]
                    if block_at == 0:
                        total, total_up = part, up
                    else:
                        total, total_up = total + part, total_up + up
                gains[...] = total[:, 0:2]
                for row in range(biases.shape[0]):
                    biases[row] = total[:, 2 + row]
                b_up[...] = total_up

            for block in range(2 * p.line):
                pl.when(p.fs == block)(functools.partial(mine, block))
            for near in range(3):
                self.near(near).wait_send()
            for other in range(1, p.line):
                self.far(other).wait_send()


def whole_kernel(line, sizes, names, ring_names, *refs):
    take = list(refs)

    def some(count):
        found = take[:count]
        del take[:count]
        return found

    owned = some(4)
    gains, biases, own_up, lengths, x_t, dy_t, x_i, dy_i = some(8)
    y_i, y_t, gx_i, gx_t = some(4)
    shares, small_out = some(4), some(3)
    far_weights, terms_t, terms_i = some(4), some(4), some(4)
    weights = some(4)
    kept = dict(zip(names, some(len(names))))
    bufs = dict(zip(ring_names, some(len(ring_names))))
    pad_x, pad_dy, small, small_all, par, b_up, g_parts, g_land, g_line = some(9)
    ag_send, ag_recv, ag_near, ag_trade, rs_send, rs_recv, rs_near, credit = some(8)
    s_send, s_recv, g_send, g_recv, load_sem, io_sem = some(6)
    n_t, n_i, counts = sizes
    width = weights[1].shape[-1]
    place = Place(line)
    ahead, back = panels_of(counts, width, ORDER), panels_of(counts, width, BACK)
    base = len(ahead)
    units, sums = [], []
    for u in range(2 * base):
        panel, layer, into = ahead[u % base], u // base, (weights, far_weights)[u // base]
        own, full = owned[panel.which].at[layer], into[panel.which]
        trade = ag_trade.at[min(GATHER_WAYS[:u].count(SPLIT), ag_trade.shape[0] - 1)]
        units.append(Gather(u, place, own, panel, full, GATHER_WAYS[u], ag_send, ag_recv, ag_near, trade))
        units[u].older = units[u - AG_RING] if u >= AG_RING else None
    for u in range(2 * base):
        panel, layer, terms = back[u % base], u // base, (terms_i, terms_t)[u // base]
        share, term = shares[panel.which].at[layer], terms[panel.which]
        sems = credit, rs_send, rs_recv, rs_near
        turn = SUM_WAYS[:u].count(LINE_FIRST), SUM_WAYS.count(LINE_FIRST)
        sums.append(Reduce(u, 2 * base, turn, place, panel, SUM_WAYS[u], term, share, bufs, *sems))
        sums[u].older = {name: sums[u - RINGS[name]] for name in ("away", "own", "total") if u >= RINGS[name]}

    def layer_of(layer, n, view, terms):
        grads = g_parts.at[0, layer, 0:8], b_up.at[2 + layer]
        return Layer(n, view, weights, par.at[layer], b_up.at[layer], terms, *grads)

    text = layer_of(1, n_t, {**kept, "x": x_t.at[0], "dy": dy_t.at[0]}, terms_t)
    view = {**cut(kept, n_i), "x": pad_x, "dy": pad_dy}
    image = layer_of(0, n_i, view, terms_i)

    def prepare():
        small[...] = jnp.zeros_like(small)
        small[:, 0:2, 0 : gains.shape[2]] = gains[...].astype(jnp.float32)
        for row in range(biases.shape[0]):
            small[:, 2 + row, 0 : biases.shape[2]] = biases[row].astype(jnp.float32)
        for j in range(own_up.shape[1] // 128):
            small[:, 8 + j, :] = own_up[:, j * 128 : (j + 1) * 128].astype(jnp.float32)
        g_parts[0] = jnp.zeros(g_parts.shape[1:], jnp.float32)
        for src, dst in ((x_i, pad_x), (dy_i, pad_dy)):
            have = src.shape[1]
            if have < n_i:
                cut_at = have // 16 * 16
                dst[cut_at:, :] = jnp.zeros((n_i - cut_at, width), jnp.bfloat16)
            dst[0:have, :] = src[0]
        image.mask([x_i.shape[1]])

    place.greet(prepare)

    smalls = []
    for step, other in enumerate(place.others()):
        copy = remote(small, small_all.at[place.fs], s_send.at[step], s_recv.at[place.fs], (place.dp, other))
        copy.start()
        smalls.append(copy)
    for u, unit in enumerate(sums):
        unit.flush = image.put_all if u < base else text.put_all
    starts = [sum(counts[:which]) for which in range(5)]
    heads, tiles, panels = width // 128, width // TILE, counts[3]
    y_copy = pltpu.make_async_copy(kept["a"], y_t.at[0], io_sem.at[0])
    grad_copy = pltpu.make_async_copy(kept["h"], gx_t.at[0], io_sem.at[1])
    loads = [pltpu.make_async_copy(far_weights[i], weights[i], load_sem.at[i]) for i in range(4)]

    steps = []

    def add(body, *args, needs=()):
        def step():
            for unit in needs:
                units[unit].arrive()
            body(*args)

        step.needs = tuple(needs)
        steps.append(step)

    def first():
        small_all[place.fs] = small[...]
        for step, other in enumerate(place.others()):
            remote(small, small_all.at[other], s_send.at[step], s_recv.at[other], (place.dp, other)).wait_recv()
        piece, deep = width // (2 * line), b_up.shape[-1] // (2 * line)
        for layer in range(2):
            for block in range(2 * line):
                par[layer, :, block * piece : (block + 1) * piece] = small_all[block, layer, 0:8, 0:piece]
                for j in range(deep // 128):
                    start = block * deep + j * 128
                    b_up[layer, 0:1, start : start + 128] = small_all[block, layer, 8 + j : 9 + j, :]
        image.prepare()
        image.norm_a()

    def image_out():
        image.down()
        y_i[0] = view["a"][0 : y_i.shape[1], :]

    def image_last():
        image.norm_a_back()
        gx_i[0] = view["h"][0 : gx_i.shape[1], :]

    def text_first():
        ends = [lengths[0, 0]]
        for j in range(1, lengths.shape[1]):
            ends.append(ends[-1] + lengths[0, j])
        text.mask(ends)
        text.prepare()
        text.norm_a()

    def waiting(load, body):
        def step(*args):
            load.wait()
            body(*args)

        return step

    def text_out():
        loads[3].wait()
        text.down()
        y_copy.start()

    def text_branch_back():
        y_copy.wait()
        text.branch_back()

    def text_last():
        text.norm_a_back()
        grad_copy.start()
        for layer in range(2):
            for j in range(b_up.shape[-1] // width):
                g_parts[0, layer, 8 + j : 9 + j, :] = b_up[2 + layer, 0:1, j * width : (j + 1) * width]

    def load(which):
        add(loads[which].start, needs=range(base + starts[which], base + starts[which + 1]))

    add(first)
    for part in range(3):
        add(image.project, part * tiles, (part + 1) * tiles, needs=(part,))
    add(image.turn_a)
    for i in range(0, heads, 2):
        add(image.attend, i, i + 2)
    add(image.branch, needs=(starts[1],))
    add(image.norm_c)
    for part in range(panels):
        add(image.up, part * tiles, (part + 1) * tiles, needs=(starts[2] + part,))
        add(image.down_terms, part, part + 1)
    add(image.turn_c)
    add(image_out, needs=range(starts[3], starts[4]))
    for part in range(panels):
        add(image.feed_back, part, part + 1)
    add(image.up_back)
    add(image.norm_c_back)
    add(image.branch_back)
    for i in range(0, heads, 2):
        add(image.attend_back, i, i + 2)
    for part in range(3):
        add(image.project_terms, part, part + 1)
    add(image.project_back)
    add(image_last)
    load(0)
    add(text_first)
    for part in range(3):
        body = waiting(loads[0], text.project) if part == 0 else text.project
        add(body, part * tiles, (part + 1) * tiles)
    add(text.turn_a)
    load(1)
    for i in range(heads):
        add(text.attend, i, i + 1)
    add(waiting(loads[1], text.branch))
    load(2)
    add(text.norm_c)
    for part in range(panels):
        add(waiting(loads[2], text.up) if part == 0 else text.up, part * tiles, (part + 1) * tiles)
        add(text.down_terms, part, part + 1)
    load(3)
    add(text.turn_c)
    add(text_out)
    for part in range(panels):
        add(text.feed_back, part, part + 1)
    add(text.up_back)
    add(text.norm_c_back)
    add(text_branch_back)
    for i in range(heads):
        add(text.attend_back, i, i + 1)
    for part in range(3):
        add(text.project_terms, part, part + 1)
    add(text.project_back)
    add(text_last)
    small_sum = SmallSum(place, g_parts, g_land, g_line, small_out, g_send, g_recv)
    for stage in range(5):
        add(small_sum.stage, stage)

    drive(steps, [unit.stages() for unit in units], [unit.stages() for unit in sums])

    for unit in sums[-RINGS["away"] :]:
        unit.free_away()
    for unit in sums[-RINGS["own"] :]:
        unit.free_own()
    for unit in sums[-RINGS["total"] :]:
        unit.free_total()
    for unit in sums:
        unit.out_landed().wait_recv()
    for unit in units[-AG_RING:]:
        unit.drain()
    for copy in smalls:
        copy.wait_send()
    grad_copy.wait()


PLAN = (
    0, -1, 10, 1, 11, 20, 2, 12, 30, 21, 3, 13, 40, 31, 22, 41, 50, 4, 32, 60, 23, 42, 14, 5, -1, 51, 70, 33,
    61, 43, 15, 24, -1, 52, 80, 71, 62, 25, -1, 34, 53, 90, -1, -1, 44, 72, 81, -1, 35, 63, 100, 91, -1, 73, 54,
    -1, 45, 110, 82, -1, -1, 64, 92, 101, -1, 111, 120, 83, 55, -1, 102, 65, 74, 93, 112, -1, -1, 84, 121, 130,
    -1, 103, 113, 75, -1, 94, 122, -1, 131, 140, 85, -1, 1000, 123, 104, 132, 1001, 150, 95, 141, 114, 133, 151,
    1010, 142, 160, 124, 1002, 1011, 152, 105, 134, 115, 143, -1, 125, 153, 161, 170, 1003, 1020, -1, -1, 144,
    162, 1012, -1, 1021, 171, 180, -1, 135, -1, 1030, 154, 172, 1004, -1, 145, 181, 190, 163, -1, 173, 1013,
    1031, -1, 182, 1022, 1005, -1, 164, 191, 200, 1014, 1040, 155, 183, -1, 174, 1006, 1041, 1032, -1, 192, -1,
    -1, 201, 210, 1023, -1, 165, 193, 1015, 1050, -1, 184, 202, -1, -1, 1051, 175, 211, 220, 1007, 1024, -1,
    203, 1016, 1042, 1033, -1, 212, 1060, 194, -1, 185, 221, 230, -1, 1061, -1, 1025, 213, -1, 204, 1034, 1052,
    -1, 1017, 222, -1, 231, 1070, -1, -1, 1035, 223, 1043, 1071, 1026, -1, 214, 1080, 1062, 195, 232, -1, 1081,
    233, 1036, -1, -1, 1044, 1053, 1090, 205, -1, 224, 1027, 1045, 1091, 1100, 1072, -1, -1, 1063, -1, 1101,
    215, 1046, 1054, 1110, -1, 1082, -1, 1037, 1064, 234, 1111, -1, 1055, -1, 1065, 1073, 225, 1120, 1056, 1092,
    1121, 1066, 1047, 1130, 1074, 1102, 1131, 235, -1, 1140, -1, 1112, 1075, 1083, -1, 1093, 1057, 1084, 1122,
    1141, 1150, 1067, -1, 1103, 1113, 1151, -1, 1094, 1160, 1085, -1, 1104, 1132, 1161, 1114, 1076, -1, 1095,
    1123, -1, 1077, 1086, 1105, 1115, 1142, 1152, 1162, 1170, -1, 1096, 1124, 1133, -1, 1087, 1106, -1, 1116,
    1125, 1143, 1153, 1180, 1171, -1, 1097, 1107, 1134, 1163, 1181, -1, 1117, 1126, 1190, 1144, -1, 1154, 1172,
    -1, 1127, 1135, 1191, 1200, -1, 1164, 1182, -1, 1201, -1, 1136, 1210, 1192, 1145, 1155, -1, 1165, 1173, -1,
    1183, 1146, 1156, 1202, 1220, -1, 1137, 1174, 1193, 1147, -1, -1, 1157, 1166, 1184, 1230, 1203, -1, 1194,
    1175, 1185, 1211, 1221, 1231, -1, 1212, 1167, 1195, 1204, -1, 1222, 1232, 1176, 1186, 1196, 1205, 1213,
    1223, 1233, 1214, 1224, 1234, 1177, 1187, 1197, 1206, 1215, 1207, 1225, 1235, 1216, 1226, 1236, 1217, 1227,
    1237,
)


def drive(steps, gathers, sums):
    at_step = 0
    for code in PLAN:
        if code < 0:
            steps[at_step]()
            at_step += 1
        elif code < 1000:
            gathers[code // 10][code % 10]()
        else:
            sums[code // 10 - 100][code % 10]()


def padded(rows):
    return -(-rows // TILE) * TILE


def whole(line, x_i, dy_i, x_t, dy_t, lengths, owned, gains, biases, b_up):
    width, deep = owned[1].shape[2], owned[2].shape[2]
    rows = owned[1].shape[1] // 2
    counts = (3, 1, deep // width, deep // width)
    own = [w.reshape(2, 2, rows, w.shape[2]) for w in owned[:3]] + [owned[3].reshape(2, 2, counts[3], rows, width)]
    n_t, n_i = padded(x_t.shape[1]), padded(x_i.shape[1])
    low, full = jnp.bfloat16, jnp.float32
    turned = biases.transpose(1, 0, 2)
    kept = layer_scratch(n_t, width, deep)
    fulls = [(line, 2, *w.shape[1:]) for w in own]
    rings = dict(
        own=pltpu.VMEM((RINGS["own"], line, rows, width), low),
        away=pltpu.VMEM((RINGS["away"], line, rows, width), low),
        other=pltpu.VMEM((RINGS["other"], line, 2, rows, width), low),
        from_x=pltpu.VMEM((RINGS["from_x"], line, rows, width // 2), low),
        from_y=pltpu.VMEM((RINGS["from_y"], line, rows, width), low),
        line_in=pltpu.VMEM((RINGS["line_in"], line + 1, rows, width), low),
        last=pltpu.VMEM((RINGS["last"], rows, width), low),
        total=pltpu.VMEM((RINGS["total"], rows, width), full),
        line_away=pltpu.VMEM((RINGS["line_away"], line + 1, rows, width), low),
    )
    panels = 2 * sum(counts)
    small_rows = 8 + deep // width
    small_rows += -small_rows % 8
    own_rows = 8 + b_up.shape[1] // 128
    own_rows += -own_rows % 8
    anywhere, inside = pl.BlockSpec(memory_space=pl.ANY), pl.BlockSpec(memory_space=pltpu.VMEM)
    dma = pltpu.SemaphoreType.DMA
    outs = [
        jax.ShapeDtypeStruct(x_i.shape, low),
        jax.ShapeDtypeStruct(x_t.shape, low),
        jax.ShapeDtypeStruct(x_i.shape, full),
        jax.ShapeDtypeStruct(x_t.shape, full),
        *[jax.ShapeDtypeStruct(w.shape, full) for w in own],
        *[jax.ShapeDtypeStruct(v.shape, full) for v in (gains, turned, b_up)],
        *[jax.ShapeDtypeStruct(shape, low) for shape in fulls * 3],
    ]
    scratch = [
        *[pltpu.VMEM(shape, low) for shape in fulls],
        *kept.values(),
        *rings.values(),
        pltpu.VMEM((n_i, width), low),
        pltpu.VMEM((n_i, width), low),
        pltpu.VMEM((2, own_rows, 128), full),
        pltpu.VMEM((2 * line, 2, own_rows, 128), full),
        pltpu.VMEM((2, 8, width), full),
        pltpu.VMEM((4, 1, deep), full),
        pltpu.VMEM((4, 2, small_rows, width), full),
        pltpu.VMEM((3, 2, small_rows, width), full),
        pltpu.VMEM((line, 2, small_rows, width), full),
        dma((AG_RING, line + 5)),
        dma((panels, line + 4)),
        dma((AG_RING,)),
        dma((max(1, GATHER_WAYS.count(SPLIT)), 2, line)),
        dma((SUM_SENDS,)),
        dma((SUM_ARRIVALS,)),
        dma((2 * RINGS["other"] + RINGS["total"],)),
        pltpu.SemaphoreType.REGULAR((CREDIT_COUNT,)),
        dma((2 * line,)),
        dma((2 * line,)),
        dma((3 + line,)),
        dma((3 + line,)),
        dma((4,)),
        dma((2,)),
    ]
    found = pl.pallas_call(
        functools.partial(whole_kernel, line, (n_t, n_i, counts), list(kept), list(rings)),
        out_shape=outs,
        in_specs=[anywhere] * 4 + [inside] * 3 + [pl.BlockSpec(memory_space=pltpu.SMEM)] + [inside] * 4,
        out_specs=[inside, anywhere, inside, anywhere] + [anywhere] * 4 + [inside] * 3 + [anywhere] * 12,
        scratch_shapes=scratch,
        compiler_params=pltpu.CompilerParams(collective_id=0, has_side_effects=True, vmem_limit_bytes=63 * 2**20),
    )(*own, gains, turned, b_up, lengths, x_t, dy_t, x_i, dy_i)
    found = hand_over(found[:11])
    shares = [share.reshape(w.shape) for share, w in zip(found[4:8], owned)]
    image_grad = found[2].transpose(1, 0, 2)
    return (*found[:2], image_grad, found[3], *shares, found[8], found[9].transpose(1, 0, 2), found[10])


def hand_over(found):
    def kernel(*refs):
        count = len(found)
        held, (turned, there, back) = refs[2 * count : -3], refs[-3:]
        copies = [pltpu.make_async_copy(refs[i], held[i], there.at[i]) for i in range(count)]
        for copy in copies:
            copy.start()
        left = [turned if i == 2 else held[i] for i in range(count)]
        outs = [pltpu.make_async_copy(left[i], refs[count + i], back.at[i]) for i in range(count)]
        for i in range(count):
            copies[i].wait()
            if i == 2:
                turned[...] = held[i][...].reshape(turned.shape)
            outs[i].start()
        for out in outs:
            out.wait()

    anywhere = pl.BlockSpec(memory_space=pl.ANY)
    sems = pltpu.SemaphoreType.DMA((len(found),))
    kept = [jax.ShapeDtypeStruct(v.shape, v.dtype) for v in found]
    kept[2] = jax.ShapeDtypeStruct((found[2].shape[1], 1, found[2].shape[2]), found[2].dtype)
    return pl.pallas_call(
        kernel,
        out_shape=kept,
        in_specs=[anywhere] * len(found),
        out_specs=[anywhere] * len(found),
        scratch_shapes=[pltpu.VMEM(v.shape, v.dtype) for v in [*found, kept[2]]] + [sems, sems],
        compiler_params=pltpu.CompilerParams(vmem_limit_bytes=63 * 2**20),
    )(*found)


def normed(values, gain, shift):
    center = values - jnp.mean(values, axis=-1, keepdims=True)
    spread = jnp.mean(center * center, axis=-1, keepdims=True)
    return center * lax.rsqrt(spread + 1e-05) * gain + shift


def gelu_exact(values):
    return jax.nn.gelu(values, approximate=False)


def segment_ids(lengths, seq_len):
    bounds = jnp.cumsum(lengths, axis=-1)
    positions = jnp.arange(seq_len, dtype=jnp.int32)
    return jnp.sum((positions[None, :, None] >= bounds[:, None, :]).astype(jnp.int32), axis=-1)


def split_heads(values):
    batch, length, width = values.shape
    return values.reshape(batch, length, width // HEAD, HEAD)


def masked_scores(queries, keys_all, segment):
    scores = jnp.einsum(
        "bqhd,bkhd->bhqk",
        split_heads(queries),
        split_heads(keys_all),
        preferred_element_type=jnp.float32,
    )
    same = (segment[:, :, None] == segment[:, None, :])[:, None]
    return (jnp.where(same, scores, -1e30), same)


def attention(queries, keys_all, values_all, segment):
    scores, same = masked_scores(queries, keys_all, segment)
    largest = jnp.max(scores, axis=-1, keepdims=True)
    raised = jnp.exp(scores - largest)
    totals = jnp.sum(raised, axis=-1, keepdims=True)
    attn_weights = raised / totals
    log_total = largest + jnp.log(totals)
    mixed = jnp.einsum(
        "bhqk,bkhd->bqhd",
        attn_weights.astype(jnp.bfloat16),
        split_heads(values_all),
        preferred_element_type=jnp.float32,
    )
    return (mixed.reshape(queries.shape).astype(jnp.bfloat16), log_total)


def attention_back(queries, keys_all, values_all, segment, log_total, grad_mixed):
    scores, same = masked_scores(queries, keys_all, segment)
    attn_weights = jnp.where(same, jnp.exp(scores - log_total), 0.0)
    grad_heads = split_heads(grad_mixed)
    grad_weights = jnp.einsum(
        "bqhd,bkhd->bhqk", grad_heads, split_heads(values_all), preferred_element_type=jnp.float32
    )
    inner = jnp.sum(attn_weights * grad_weights, axis=-1, keepdims=True)
    grad_scores = (attn_weights * (grad_weights - inner)).astype(jnp.bfloat16)
    grad_queries = jnp.einsum(
        "bhqk,bkhd->bqhd", grad_scores, split_heads(keys_all), preferred_element_type=jnp.float32
    )
    grad_keys = jnp.einsum(
        "bhqk,bqhd->bkhd", grad_scores, split_heads(queries), preferred_element_type=jnp.float32
    )
    grad_values = jnp.einsum(
        "bhqk,bqhd->bkhd",
        attn_weights.astype(jnp.bfloat16),
        grad_heads,
        preferred_element_type=jnp.float32,
    )
    shape_rows = queries.shape
    return (
        grad_queries.reshape(shape_rows),
        grad_keys.reshape(shape_rows),
        grad_values.reshape(shape_rows),
    )


def forward_layer(inputs, weights, segment):
    qkv_weight, out_weight, up_weight, down_weight, gains, biases, up_bias = weights
    width = inputs.shape[-1]
    source = inputs.astype(jnp.float32)
    normed_a = normed(source, gains[0], biases[0]).astype(jnp.bfloat16)
    project = jnp.einsum("bld,de->ble", normed_a, qkv_weight, preferred_element_type=jnp.float32)
    queries = ((project[..., :width] + biases[2]) * HEAD ** (-0.5)).astype(jnp.bfloat16)
    keys_all = project[..., width : 2 * width].astype(jnp.bfloat16)
    values_all = (project[..., 2 * width :] + biases[3]).astype(jnp.bfloat16)
    mixed, log_total = attention(queries, keys_all, values_all, segment)
    hidden = (
        source
        + jnp.einsum("bld,de->ble", mixed, out_weight, preferred_element_type=jnp.float32)
        + biases[4]
    )
    normed_c = normed(hidden, gains[1], biases[1]).astype(jnp.bfloat16)
    before = (
        jnp.einsum("bld,df->blf", normed_c, up_weight, preferred_element_type=jnp.float32) + up_bias
    )
    activated = gelu_exact(before).astype(jnp.bfloat16)
    result = (
        hidden
        + jnp.einsum("blf,fd->bld", activated, down_weight, preferred_element_type=jnp.float32)
        + biases[5]
    )
    return (
        source,
        normed_a,
        queries,
        keys_all,
        values_all,
        log_total,
        mixed,
        hidden,
        normed_c,
        before,
        activated,
        result,
    )


def backward_layer(inputs, cotangent, weights, segment):
    qkv_weight, out_weight, up_weight, down_weight, gains, biases, up_bias = weights
    width = inputs.shape[-1]
    (
        source,
        normed_a,
        queries,
        keys_all,
        values_all,
        log_total,
        mixed,
        hidden,
        normed_c,
        before,
        activated,
        result,
    ) = forward_layer(inputs, weights, segment)
    grad_result = cotangent.astype(jnp.float32)
    grad_downw = jnp.einsum("blf,bld->fd", activated, cotangent, preferred_element_type=jnp.float32)
    grad_act = jnp.einsum("bld,fd->blf", cotangent, down_weight, preferred_element_type=jnp.float32)
    grad_before = jax.vjp(gelu_exact, before)[1](grad_act)[0].astype(jnp.bfloat16)
    grad_upw = jnp.einsum("bld,blf->df", normed_c, grad_before, preferred_element_type=jnp.float32)
    grad_upb = jnp.sum(grad_before.astype(jnp.float32), axis=(0, 1))
    grad_normc = jnp.einsum(
        "blf,df->bld", grad_before, up_weight, preferred_element_type=jnp.float32
    )
    hidden_back = jax.vjp(
        normed, hidden, gains[1].astype(jnp.float32), biases[1].astype(jnp.float32)
    )[1]
    grad_hidden_ln, grad_gain_two, grad_shift_two = hidden_back(grad_normc)
    grad_hidden = grad_result + grad_hidden_ln
    grad_branch = grad_hidden.astype(jnp.bfloat16)
    grad_outw = jnp.einsum("bld,ble->de", mixed, grad_branch, preferred_element_type=jnp.float32)
    grad_mixed = jnp.einsum(
        "ble,de->bld", grad_branch, out_weight, preferred_element_type=jnp.float32
    ).astype(jnp.bfloat16)
    grad_queries, grad_keys, grad_values = attention_back(
        queries, keys_all, values_all, segment, log_total, grad_mixed
    )
    grad_project = jnp.concatenate(
        [
            grad_queries.astype(jnp.bfloat16) * HEAD ** (-0.5),
            grad_keys.astype(jnp.bfloat16),
            grad_values.astype(jnp.bfloat16),
        ],
        axis=-1,
    )
    grad_qkvw = jnp.einsum(
        "bld,ble->de", normed_a, grad_project, preferred_element_type=jnp.float32
    )
    column_sums = jnp.sum(grad_project.astype(jnp.float32), axis=(0, 1))
    grad_norma = jnp.einsum(
        "ble,de->bld", grad_project, qkv_weight, preferred_element_type=jnp.float32
    )
    source_back = jax.vjp(
        normed, source, gains[0].astype(jnp.float32), biases[0].astype(jnp.float32)
    )[1]
    grad_source_ln, grad_gain_one, grad_shift_one = source_back(grad_norma)
    grad_inputs = grad_hidden + grad_source_ln
    grad_gains = jnp.stack([grad_gain_one, grad_gain_two])
    grad_biases = jnp.stack(
        [
            grad_shift_one,
            grad_shift_two,
            column_sums[:width],
            column_sums[2 * width :],
            jnp.sum(grad_branch.astype(jnp.float32), axis=(0, 1)),
            jnp.sum(grad_result, axis=(0, 1)),
        ]
    )
    return (
        result.astype(jnp.bfloat16),
        grad_inputs,
        (grad_qkvw, grad_outw, grad_upw, grad_downw, grad_gains, grad_biases, grad_upb),
    )


def fetch_weights(layer_index, w_qkv, w_out, w_up, w_down, gains, biases, b_up):
    return (
        lax.all_gather(w_qkv[layer_index], "fsdp", axis=0, tiled=True),
        lax.all_gather(w_out[layer_index], "fsdp", axis=0, tiled=True),
        lax.all_gather(w_up[layer_index], "fsdp", axis=0, tiled=True),
        lax.all_gather(w_down[layer_index], "fsdp", axis=0, tiled=True),
        lax.all_gather(gains[layer_index], "fsdp", axis=1, tiled=True),
        lax.all_gather(biases[layer_index], "fsdp", axis=1, tiled=True),
        lax.all_gather(b_up[layer_index], "fsdp", axis=0, tiled=True),
    )


def fetch_again(layer_index, w_qkv, w_out, w_up, w_down, gains, biases, b_up):
    return (
        lax.all_gather(w_qkv[layer_index], "fsdp", axis=0, tiled=True),
        lax.all_gather(w_out[layer_index], "fsdp", axis=0, tiled=True),
        lax.all_gather(w_up[layer_index], "fsdp", axis=0, tiled=True),
        lax.all_gather(w_down[layer_index], "fsdp", axis=0, tiled=True),
        lax.all_gather(gains[layer_index], "fsdp", axis=1, tiled=True),
        lax.all_gather(biases[layer_index], "fsdp", axis=1, tiled=True),
        lax.all_gather(b_up[layer_index], "fsdp", axis=0, tiled=True),
    )


def reduce_grads(gradients):
    shares = (
        lax.psum_scatter(gradients[0], "fsdp", scatter_dimension=0, tiled=True),
        lax.psum_scatter(gradients[1], "fsdp", scatter_dimension=0, tiled=True),
        lax.psum_scatter(gradients[2], "fsdp", scatter_dimension=0, tiled=True),
        lax.psum_scatter(gradients[3], "fsdp", scatter_dimension=0, tiled=True),
        lax.psum_scatter(gradients[4], "fsdp", scatter_dimension=1, tiled=True),
        lax.psum_scatter(gradients[5], "fsdp", scatter_dimension=1, tiled=True),
        lax.psum_scatter(gradients[6], "fsdp", scatter_dimension=0, tiled=True),
    )
    quarters = (
        lax.psum_scatter(
            shares[0].astype(jnp.bfloat16), "dp", scatter_dimension=0, tiled=True
        ).astype(jnp.float32),
        lax.psum_scatter(
            shares[1].astype(jnp.bfloat16), "dp", scatter_dimension=0, tiled=True
        ).astype(jnp.float32),
        lax.psum_scatter(
            shares[2].astype(jnp.bfloat16), "dp", scatter_dimension=0, tiled=True
        ).astype(jnp.float32),
        lax.psum_scatter(
            shares[3].astype(jnp.bfloat16), "dp", scatter_dimension=0, tiled=True
        ).astype(jnp.float32),
        lax.psum_scatter(
            shares[4].astype(jnp.bfloat16), "dp", scatter_dimension=1, tiled=True
        ).astype(jnp.float32),
        lax.psum_scatter(
            shares[5].astype(jnp.bfloat16), "dp", scatter_dimension=1, tiled=True
        ).astype(jnp.float32),
        lax.psum_scatter(
            shares[6].astype(jnp.bfloat16), "dp", scatter_dimension=0, tiled=True
        ).astype(jnp.float32),
    )
    return (
        lax.all_gather(quarters[0].astype(jnp.bfloat16), "dp", axis=0, tiled=True).astype(
            jnp.float32
        ),
        lax.all_gather(quarters[1].astype(jnp.bfloat16), "dp", axis=0, tiled=True).astype(
            jnp.float32
        ),
        lax.all_gather(quarters[2].astype(jnp.bfloat16), "dp", axis=0, tiled=True).astype(
            jnp.float32
        ),
        lax.all_gather(quarters[3].astype(jnp.bfloat16), "dp", axis=0, tiled=True).astype(
            jnp.float32
        ),
        lax.all_gather(quarters[4].astype(jnp.bfloat16), "dp", axis=1, tiled=True).astype(
            jnp.float32
        ),
        lax.all_gather(quarters[5].astype(jnp.bfloat16), "dp", axis=1, tiled=True).astype(
            jnp.float32
        ),
        lax.all_gather(quarters[6].astype(jnp.bfloat16), "dp", axis=0, tiled=True).astype(
            jnp.float32
        ),
    )


def plain(
    images,
    image_cot,
    captions,
    caption_cot,
    lengths,
    w_qkv,
    w_out,
    w_up,
    w_down,
    gains,
    biases,
    b_up,
):
    owned = (w_qkv, w_out, w_up, w_down, gains, biases, b_up)
    image_seg = jnp.zeros((images.shape[0], images.shape[1]), jnp.int32)
    caption_seg = segment_ids(lengths, captions.shape[1])
    first_weights = fetch_weights(0, *owned)
    image_out = forward_layer(images, first_weights, image_seg)[-1].astype(jnp.bfloat16)
    second_weights = fetch_weights(1, *owned)
    caption_out = forward_layer(captions, second_weights, caption_seg)[-1].astype(jnp.bfloat16)
    second_back = fetch_again(1, *owned)
    _, caption_grad, caption_terms = backward_layer(captions, caption_cot, second_back, caption_seg)
    caption_shares = reduce_grads(caption_terms)
    first_back = fetch_again(0, *owned)
    _, image_grad, image_terms = backward_layer(images, image_cot, first_back, image_seg)
    image_shares = reduce_grads(image_terms)
    stacked = tuple((jnp.stack([image_shares[index], caption_shares[index]]) for index in range(7)))
    return (image_out, caption_out, image_grad, caption_grad) + stacked


def kernels_fit(mesh, w_qkv):
    return mesh.shape["dp"] == 4 and mesh.shape["fsdp"] % 2 == 0 and w_qkv.shape[1] % 32 == 0


def local(mesh, images, image_cot, captions, caption_cot, lengths, w_qkv, w_out, w_up, w_down, gains, biases, b_up):
    if not kernels_fit(mesh, w_qkv):
        return plain(
            images, image_cot, captions, caption_cot, lengths, w_qkv, w_out, w_up, w_down, gains, biases, b_up
        )
    return whole(
        mesh.shape["fsdp"] // 2, images, image_cot, captions, caption_cot, lengths,
        (w_qkv, w_out, w_up, w_down), gains, biases, b_up
    )


def solution(mesh):
    placed = (
        P(("dp", "fsdp"), None, None),
        P(("dp", "fsdp"), None, None),
        P(("dp", "fsdp"), None, None),
        P(("dp", "fsdp"), None, None),
        P(("dp", "fsdp"), None),
        P(None, "fsdp", None),
        P(None, "fsdp", None),
        P(None, "fsdp", None),
        P(None, "fsdp", None),
        P(None, None, "fsdp"),
        P(None, None, "fsdp"),
        P(None, "fsdp"),
    )
    return jax.shard_map(
        functools.partial(local, mesh),
        mesh=mesh,
        in_specs=placed,
        out_specs=(
            P(("dp", "fsdp"), None, None),
            P(("dp", "fsdp"), None, None),
            P(("dp", "fsdp"), None, None),
            P(("dp", "fsdp"), None, None),
            P(None, "fsdp", None),
            P(None, "fsdp", None),
            P(None, "fsdp", None),
            P(None, "fsdp", None),
            P(None, None, "fsdp"),
            P(None, None, "fsdp"),
            P(None, "fsdp"),
        ),
        check_vma=False,
    )
```

```python
import functools

import jax
import jax.numpy as jnp
from jax import lax
from jax.experimental import pallas as pl
from jax.experimental.pallas import tpu as pltpu
from jax.sharding import PartitionSpec as P

HEAD = 64

MESH = pl.DeviceIdType.MESH
NT = (((1,), (1,)), ((), ()))
TN = (((0,), (0,)), ((), ()))
TILE = 256
CHUNK = 64
ALL = slice(None)


def dot(a, b, dims=(((1,), (0,)), ((), ()))):
    return lax.dot_general(a, b, dims, preferred_element_type=jnp.float32)


def flat(value):
    return value.reshape(-1, value.shape[-1])


def at(t, size=TILE):
    return pl.ds(pl.multiple_of(t * size, size), size)


def remote(src, dst, send, recv, device):
    return pltpu.make_async_remote_copy(
        src_ref=src, dst_ref=dst, send_sem=send, recv_sem=recv, device_id=device, device_id_type=MESH
    )


class Place:
    def __init__(self, line):
        dp, fs = lax.axis_index("dp"), lax.axis_index("fsdp")
        self.line, self.dp, self.fs = line, dp, fs
        self.x, self.c = dp // 2, dp % 2
        self.z, self.y = fs // 2, fs % 2
        self.up, self.down = (dp, fs + 2), (dp, fs - 2)
        self.yway = (dp, self.z * 2 + 1 - self.y)
        self.xway = ((1 - self.x) * 2 + self.c, fs)
        self.core = (self.x * 2 + 1 - self.c, fs)
        self.has_up, self.has_down = self.z + 1 < line, self.z > 0

    def others(self):
        return [lax.rem(self.fs + step, 2 * self.line) for step in range(1, 2 * self.line)]

    def greet(self, meanwhile):
        barrier = pltpu.get_barrier_semaphore()
        known = [(self.dp, other) for other in self.others()] + [self.xway, self.core]
        for device in known:
            pl.semaphore_signal(barrier, inc=1, device_id=device, device_id_type=MESH)
        meanwhile()
        pl.semaphore_wait(barrier, len(known))


class Panel:
    def __init__(self, which, part, width):
        self.which, self.part, self.width = which, part, width

    def cols(self, cut):
        base = 0 if self.which == 3 else self.part * self.width
        if cut is None:
            return pl.ds(base, self.width)
        return pl.ds(pl.multiple_of(base + cut[0], 128), cut[1])

    def of(self, ref, *lead, cut=None):
        if self.which == 3:
            return ref.at[(*lead, self.part, ALL, self.cols(cut))]
        return ref.at[(*lead, ALL, self.cols(cut))]


class Cuts:
    def __init__(self, width, x, thirds):
        third = width // 3
        self.half = (x * (width // 2), width // 2)
        self.other_half = ((1 - x) * (width // 2), width // 2)
        self.wide, self.outer, self.other_outer = self.half, self.half, self.other_half
        if thirds:
            self.wide = (x * third, 2 * third)
            self.outer = (x * 2 * third, third)
            self.other_outer = ((1 - x) * 2 * third, third)


def ds(cut):
    return pl.ds(pl.multiple_of(cut[0], 128), cut[1])


def panels_of(layer_shapes, width, order):
    made = []
    for which in order:
        count = layer_shapes[which]
        made += [Panel(which, part, width) for part in range(count)]
    return made


class Gather:
    def __init__(self, at, place, own, panel, full, way, send, recv, near, trade):
        self.trade = trade
        self.at, self.place, self.own, self.panel, self.full = at, place, own, panel, full
        self.send, self.recv, self.near = send, recv, near
        self.split, self.older = way == SPLIT, None
        split = self.split
        cuts = Cuts(panel.width, place.x, way == THIRDS)
        self.lane, self.other_lane = (cuts.half, cuts.other_half) if split else (None, None)
        self.over_y = cuts.half if split else cuts.wide
        self.over_x, self.from_x = (cuts.half, cuts.other_half) if split else (cuts.outer, cuts.other_outer)

    def view(self, block, y, c, cut=None):
        return self.panel.of(self.full, block, y, c, cut=cut)

    def sent(self, slot):
        return self.send.at[self.at % AG_RING, slot]

    def got(self, slot):
        return self.recv.at[self.at, slot]

    def line_copy(self, way, block):
        p = self.place
        ref = self.view(block, p.y, p.c, self.lane)
        return remote(ref, ref, self.sent(block + way), self.got(block), (p.up, p.down)[way])

    def near_copy(self):
        p = self.place
        mine = self.panel.of(self.own, p.c)
        return pltpu.make_async_copy(mine, self.view(p.z, p.y, p.c), self.near.at[self.at % AG_RING])

    def far_copy(self, kind):
        p, line = self.place, self.place.line
        ref, device = {
            "y": (lambda: (self.view(ALL, p.y, p.c, self.over_y), p.yway)),
            "x": (lambda: (self.view(ALL, 1 - p.y, p.c, self.over_x), p.xway)),
            "core_own": (lambda: (self.view(ALL, p.y, p.c), p.core)),
            "core": (lambda: (self.view(ALL, 1 - p.y, p.c), p.core)),
        }[kind]()
        slot = FAR.index(kind)
        return remote(ref, ref, self.sent(line + 1 + slot), self.got(line + slot), device)

    def trade_copy(self, block, lane):
        p = self.place
        ref = self.view(block, p.y, p.c, lane)
        return remote(ref, ref, self.trade.at[0, block], self.trade.at[1, block], p.xway)

    def landed(self, kind):
        p, line = self.place, self.place.line
        ref = {
            "y": lambda: self.view(ALL, 1 - p.y, p.c, self.over_y),
            "x": lambda: self.view(ALL, 1 - p.y, p.c, self.from_x),
            "core_own": lambda: self.view(ALL, p.y, 1 - p.c),
            "core": lambda: self.view(ALL, 1 - p.y, 1 - p.c),
        }[kind]()
        slot = FAR.index(kind)
        return remote(ref, ref, self.sent(line + 1 + slot), self.got(line + slot), p.core)

    def kinds(self):
        return FAR

    def first(self):
        p = self.place
        if self.older is not None:
            self.older.drain()
        self.near_copy().start()
        mine = self.panel.of(self.own, p.c, cut=self.lane)
        there = self.view(p.z, p.y, p.c, self.lane)
        for way, able, device in ((0, p.has_up, p.up), (1, p.has_down, p.down)):
            copy = functools.partial(remote, mine, there, self.sent(p.z + way), self.got(p.z), device)
            pl.when(able)(lambda copy=copy: copy().start())

    def hop(self, k):
        p = self.place

        def pass_on(way, block, more):
            self.line_copy(way, block).wait_recv()
            pl.when(more)(lambda: self.line_copy(way, block).start())
            if self.split:
                self.trade_copy(block, self.lane).start()

        pl.when(p.z - k >= 0)(lambda: pass_on(0, p.z - k, p.has_up))
        pl.when(p.z + k < p.line)(lambda: pass_on(1, p.z + k, p.has_down))
        if k == p.line - 1:
            self.near_copy().wait()
            self.far_copy("y").start()
            if not self.split:
                self.far_copy("core_own").start()

    def cross(self):
        self.landed("y").wait_recv()
        self.far_copy("x").start()
        if self.split:
            self.trades(lambda block: self.trade_copy(block, self.other_lane).wait_recv())
            self.far_copy("core_own").start()

    def trades(self, body):
        for block in range(self.place.line):
            pl.when(block != self.place.z)(functools.partial(body, block))

    def share(self):
        self.landed("x").wait_recv()
        self.far_copy("core").start()

    def stages(self):
        hops = [functools.partial(self.hop, k) for k in range(1, self.place.line)]
        return [self.first, *hops, self.cross, self.share]

    def arrive(self):
        self.landed("core_own").wait_recv()
        self.landed("core").wait_recv()

    def drain(self):
        p = self.place

        def body(block, carry):
            pl.when(p.has_up & (block <= p.z))(lambda: self.line_copy(0, block).wait_send())
            pl.when(p.has_down & (block >= p.z))(lambda: self.line_copy(1, block).wait_send())
            return carry

        lax.fori_loop(0, p.line, body, 0)
        for kind in self.kinds():
            self.far_copy(kind).wait_send()
        if self.split:
            self.trades(lambda block: self.trade_copy(block, self.lane).wait_send())


FAR = ("y", "x", "core_own", "core")
HALVES, THIRDS, SPLIT, LINE_FIRST = range(4)
AG_RING = 12
GATHER_WAYS = (
    1, 2, 1, 1, 2, 0, 2, 1, 1, 2, 1, 2, 0, 0, 0, 0, 0, 0, 0, 0, 0, 0, 0, 0,
)
SUM_WAYS = (
    0, 1, 0, 0, 1, 1, 0, 1, 0, 1, 2, 1, 1, 0, 2, 0, 0, 1, 2, 1, 0, 1, 2, 0,
)
RINGS = dict(own=12, away=6, other=3, from_x=4, from_y=4, line_in=5, last=3, total=3, line_away=1)
LINE_FIRSTS = min(1, SUM_WAYS.count(LINE_FIRST))
SUM_SEMS = dict(
    core=(RINGS["away"], 1, RINGS["other"], 1),
    x=(RINGS["away"], 1, RINGS["from_x"], 1),
    y=(RINGS["away"], 1, RINGS["from_y"], 1),
    line=(RINGS["own"], 4, RINGS["line_in"], 5),
    line_away=(LINE_FIRSTS and RINGS["own"], 4, LINE_FIRSTS and RINGS["line_away"], 5),
    last=(RINGS["own"], 1, RINGS["last"], 1),
    out=(RINGS["total"], 1, 24, 1),
)


def starts_of(kinds):
    found, out_at, in_at = {}, 0, 0
    for name, (out_ring, out_each, in_ring, in_each) in kinds.items():
        found[name] = (out_at, in_at)
        out_at, in_at = out_at + out_ring * out_each, in_at + in_ring * in_each
    return found, out_at, in_at


SUM_STARTS, SUM_SENDS, SUM_ARRIVALS = starts_of(SUM_SEMS)
CREDITS, CREDIT_COUNT = {}, 0
for _name, _ring in (
    ("other", "other"),
    ("from_x", "from_x"),
    ("from_y", "from_y"),
    ("line_up", "line_in"),
    ("line_down", "line_in"),
    ("away_up", "line_away"),
    ("away_down", "line_away"),
    ("last", "last"),
):
    CREDITS[_name] = CREDIT_COUNT
    CREDIT_COUNT += RINGS[_ring]


class Reduce:
    def __init__(self, at, count, turn, place, panel, way, terms, out, bufs, credit, send, recv, near):
        self.at, self.count, self.place, self.panel, self.terms, self.out = at, count, place, panel, terms, out
        self.credit, self.send, self.recv, self.near = credit, send, recv, near
        self.older, self.flush = {}, None
        self.turn = turn
        self.b = {name: ref.at[self.slot(name)] for name, ref in bufs.items()}
        cuts = Cuts(panel.width, place.x, way == THIRDS)
        self.split, self.line_first = way == SPLIT, way == LINE_FIRST
        self.wide, self.outer, self.other_outer = ds(cuts.wide), ds(cuts.outer), ds(cuts.other_outer)
        self.lane = self.outer if self.split else pl.ds(0, panel.width)
        if self.split:
            self.wide = pl.ds(0, panel.width)
        self.lanes = panel.width // 2 if self.split else panel.width
        over_y = panel.width if self.split or self.line_first else cuts.wide[1]
        self.b["from_x"] = self.b["from_x"].at[:, :, 0 : cuts.outer[1]]
        self.b["from_y"] = self.b["from_y"].at[:, :, 0:over_y]
        self.b["last"] = self.b["last"].at[:, 0 : self.lanes]

    def turn_of(self, ring):
        return self.turn if ring == "line_away" else (self.at, self.count)

    def slot(self, ring):
        return self.turn_of(ring)[0] % RINGS[ring]

    def spend(self, name, ring):
        if self.turn_of(ring)[0] >= RINGS[ring]:
            pl.semaphore_wait(self.credit.at[CREDITS[name] + self.slot(ring)], 1)

    def grant(self, name, ring, device):
        turn, count = self.turn_of(ring)
        if turn + RINGS[ring] < count:
            credit = self.credit.at[CREDITS[name] + self.slot(ring)]
            pl.semaphore_signal(credit, inc=1, device_id=device, device_id_type=MESH)

    def sems(self, name, slot=(0, 0)):
        out_ring, out_each, in_ring, in_each = SUM_SEMS[name]
        out_at, in_at = SUM_STARTS[name]
        out_at += self.at % out_ring * out_each + slot[0]
        in_at += (self.slot(name) if name == "line_away" else self.at % in_ring) * in_each + slot[1]
        return self.send.at[out_at], self.recv.at[in_at]

    def core_copy(self):
        p = self.place
        return remote(self.panel.of(self.terms, ALL, ALL, 1 - p.c), self.b["other"], *self.sems("core"), p.core)

    def near_copy(self, away):
        p = self.place
        src = self.panel.of(self.terms, ALL, (1 - p.y) if away else p.y, p.c)
        return pltpu.make_async_copy(src, self.b["away" if away else "own"], self.near.at[self.at % RINGS["other"] * 2 + int(away)])

    def x_copy(self):
        p = self.place
        src = self.b["own" if self.split else "away"].at[:, :, self.other_outer]
        return remote(src, self.b["from_x"], *self.sems("x"), p.xway)

    def y_copy(self):
        p = self.place
        if self.line_first:
            return remote(self.b["away"].at[p.z], self.b["from_y"].at[0], *self.sems("y"), p.yway)
        return remote(self.b["away"].at[:, :, self.wide], self.b["from_y"], *self.sems("y"), p.yway)

    def came(self, way, block, away=False):
        return self.b["line_away" if away else "line_in"].at[block + 1 - way, :, 0 : self.lanes]

    def line_copy(self, way, block, away=False):
        p = self.place
        sems = self.sems("line_away" if away else "line", (block, block + 1 - way))
        src = self.b["away" if away else "own"].at[block, :, self.lane]
        return remote(src, self.came(way, block, away), *sems, (p.up, p.down)[way])

    def columns(self):
        return (False, True) if self.line_first else (False,)

    def last_copy(self):
        p = self.place
        return remote(self.b["own"].at[p.z, :, self.lane], self.b["last"], *self.sems("last"), p.xway)

    def out_copy(self):
        ref = self.panel.of(self.out, self.place.c)
        return remote(self.b["total"], ref, *self.sems("out"), self.place.core)

    def out_landed(self):
        ref = self.panel.of(self.out, 1 - self.place.c)
        return remote(self.b["total"], ref, *self.sems("out"), self.place.core)

    def out_near(self):
        return pltpu.make_async_copy(self.b["total"], self.panel.of(self.out, self.place.c), self.near.at[2 * RINGS["other"] + self.at % RINGS["total"]])

    def each(self, body):
        def step(block, carry):
            body(block)
            return carry

        lax.fori_loop(0, self.place.line, step, 0)

    def start(self):
        if self.flush is not None:
            self.flush()
        if "away" in self.older:
            self.older["away"].free_away()
        if "own" in self.older:
            self.older["own"].free_own()
        self.spend("other", "other")
        self.core_copy().start()
        self.near_copy(False).start()
        self.near_copy(True).start()

    def add_core(self):
        p, b = self.place, self.b
        self.near_copy(False).wait()
        self.near_copy(True).wait()
        self.core_copy().wait_recv()

        def body(block):
            b["away"][block] = b["away"][block] + b["other"][block, 1 - p.y]

        self.each(body)
        if self.split:
            self.spend("from_y", "from_y")
            self.y_copy().start()
        else:
            self.spend("from_x", "from_x")
            if self.line_first:
                self.grant("from_x", "from_x", p.xway)
            else:
                self.x_copy().start()

        def rest(block):
            b["own"][block] = b["own"][block] + b["other"][block, p.y]

        self.each(rest)
        self.grant("other", "other", p.core)

    def add_x(self):
        p, b = self.place, self.b
        self.x_copy().wait_recv()
        cols = self.outer

        def body(block):
            b["away"][block, :, cols] = b["away"][block, :, cols] + b["from_x"][block]

        self.each(body)
        self.spend("from_y", "from_y")
        self.y_copy().start()
        self.grant("from_x", "from_x", p.xway)

    def add_x_after(self):
        p, b = self.place, self.b
        self.x_copy().wait_recv()
        cols = self.outer

        def body(block):
            b["own"][block, :, cols] = b["own"][block, :, cols] + b["from_x"][block]

        self.each(body)
        self.grant("from_x", "from_x", p.xway)
        self.line_step(0)

    def add_y(self):
        p, b = self.place, self.b
        self.y_copy().wait_recv()
        cols = self.wide

        def body(block):
            b["own"][block, :, cols] = b["own"][block, :, cols] + b["from_y"][block]

        self.each(body)
        self.grant("from_y", "from_y", p.yway)
        if self.split:
            self.spend("from_x", "from_x")
            self.x_copy().start()
        else:
            self.line_step(0)

    def add_line(self, way, block):
        for away in self.columns():
            self.line_copy(way, block, away).wait_recv()
            sums, lane = self.b["away" if away else "own"], self.lane
            sums[block, :, lane] = sums[block, :, lane] + self.came(way, block, away)[...]

    def line_step(self, k):
        p, line = self.place, self.place.line
        if k == 0:
            pl.when(p.has_up)(lambda: self.spend("line_up", "line_in"))
            pl.when(p.has_down)(lambda: self.spend("line_down", "line_in"))
            if self.line_first:
                pl.when(p.has_up)(lambda: self.spend("away_up", "line_away"))
                pl.when(p.has_down)(lambda: self.spend("away_down", "line_away"))
        for way, steps_in, block, more in (
            (0, p.z, line - 1 - k + p.z, p.has_down),
            (1, line - 1 - p.z, k - (line - 1 - p.z), p.has_up),
        ):

            def body(way=way, block=block, more=more):
                pl.when(more)(lambda: self.add_line(way, block))
                for away in self.columns():
                    self.line_copy(way, block, away).start()

            pl.when(steps_in <= k)(body)

    def own_step(self):
        p = self.place
        pl.when(p.has_down)(lambda: self.add_line(0, p.z))
        pl.when(p.has_up)(lambda: self.add_line(1, p.z))
        if self.line_first:
            self.spend("from_y", "from_y")
            self.y_copy().start()
            pl.when(p.has_down)(lambda: self.grant("away_up", "line_away", p.down))
            pl.when(p.has_up)(lambda: self.grant("away_down", "line_away", p.up))
        else:
            self.spend("last", "last")
            self.last_copy().start()
        pl.when(p.has_down)(lambda: self.grant("line_up", "line_in", p.down))
        pl.when(p.has_up)(lambda: self.grant("line_down", "line_in", p.up))

    def add_y_last(self):
        p, b = self.place, self.b
        self.y_copy().wait_recv()
        b["own"][p.z] = b["own"][p.z] + b["from_y"][0]
        self.grant("from_y", "from_y", p.yway)
        self.spend("last", "last")
        self.last_copy().start()

    def finish(self):
        p, b = self.place, self.b
        if "total" in self.older:
            self.older["total"].free_total()
        self.last_copy().wait_recv()
        if self.split:
            b["total"][:, self.outer] = b["own"][p.z, :, self.outer].astype(jnp.float32)
            b["total"][:, self.other_outer] = b["last"][...].astype(jnp.float32)
        else:
            b["total"][...] = b["own"][p.z].astype(jnp.float32) + b["last"][...].astype(jnp.float32)
        self.grant("last", "last", p.xway)
        self.out_copy().start()
        self.out_near().start()

    def stages(self):
        if self.line_first:
            steps = [functools.partial(self.line_step, k) for k in range(self.place.line - 1)]
            return [self.start, self.add_core, *steps, self.own_step, self.add_y_last, self.finish]
        steps = [self.start, self.add_core]
        steps += [self.add_y, self.add_x_after] if self.split else [self.add_x, self.add_y]
        steps += [functools.partial(self.line_step, k) for k in range(1, self.place.line - 1)]
        return steps + [self.own_step, self.finish]

    def uses(self):
        if self.line_first:
            return dict(from_x=(1, 1), from_y=(5, 6), line_in=(2, 5), line_away=(2, 5), last=(6, 7))
        if self.split:
            return dict(from_y=(1, 2), from_x=(2, 3), line_in=(3, 6), last=(6, 7))
        return dict(from_x=(1, 2), from_y=(2, 3), line_in=(3, 6), last=(6, 7))

    def free_away(self):
        self.core_copy().wait_send()
        if not self.line_first:
            self.x_copy().wait_send()
        self.y_copy().wait_send()
        if self.line_first:
            self.free_line(True)

    def free_line(self, away):
        p = self.place
        for block in range(p.line):
            pl.when(block > p.z)(lambda block=block: self.line_copy(0, block, away).wait_send())
            pl.when(block < p.z)(lambda block=block: self.line_copy(1, block, away).wait_send())

    def free_own(self):
        self.free_line(False)
        self.last_copy().wait_send()

    def free_total(self):
        self.out_copy().wait_send()
        self.out_near().wait()


class Layer:
    def __init__(self, n, kept, weights, par, b_up, terms, g_par, g_bup):
        self.n, self.s = n, kept
        self.w_qkv, self.w_out, self.w_up, self.w_down = weights
        self.par, self.b_up = par, b_up
        self.g_qkv, self.g_out, self.g_up, self.g_down = terms
        self.g_par, self.g_bup = g_par, g_bup
        self.width, self.deep = self.w_out.shape[-1], self.w_up.shape[-1]
        self.pending = [None, None]

    def chunks(self, body):
        def step(i, carry):
            body(at(i, CHUNK))
            return carry

        lax.fori_loop(0, self.n // CHUNK, step, 0)

    def tiles(self, first, last, body):
        def step(i, carry):
            body(i)
            return carry

        lax.fori_loop(first, last, step, 0)

    def row(self, ref, i):
        return ref[i : i + 1, :]

    def tall_copy(self, ref, slot, t):
        stage = self.s["stage"].at[slot].reshape(*ref.shape[:4], self.width)
        cols = at(t, self.width)
        return pltpu.make_async_copy(stage, ref.at[:, :, :, :, cols], self.s["stage_sem"].at[slot])

    def wide_copy(self, ref, slot, t):
        stage = self.s["stage"].at[slot].reshape(*ref.shape[1:])
        return pltpu.make_async_copy(stage, ref.at[t], self.s["stage_sem"].at[slot])

    def put(self, make, slot, t, first, value):
        held = self.pending[slot]
        pl.when(t > first)(lambda: make(slot, t - 1).wait())
        if held is not None:
            pl.when(t == first)(lambda: held.wait())
        self.s["stage"][slot] = value.astype(jnp.bfloat16)
        make(slot, t).start()

    def put_all(self):
        for slot in range(2):
            if self.pending[slot] is not None:
                self.pending[slot].wait()
            self.pending[slot] = None

    def mask(self, ends):
        s = self.s

        def mask(rows):
            shape = (CHUNK, self.n)
            at_row = lax.broadcasted_iota(jnp.int32, shape, 0) + rows.start
            at_col = lax.broadcasted_iota(jnp.int32, shape, 1)
            one, other = jnp.zeros(shape, jnp.int32), jnp.zeros(shape, jnp.int32)
            for end in ends:
                one = one + (at_row >= end).astype(jnp.int32)
                other = other + (at_col >= end).astype(jnp.int32)
            s["bias"][rows, :] = jnp.where(one == other, 0.0, -1e30)

        self.chunks(mask)

    def prepare(self):
        s, width = self.s, self.width
        s["rows"][0:1, 0:width] = self.par[4:5, :]
        s["rows"][0:1, width : 2 * width] = jnp.zeros((1, width), jnp.float32)
        s["rows"][0:1, 2 * width :] = self.par[5:6, :]

    def norm_parts(self, values):
        center = values - jnp.mean(values, axis=-1, keepdims=True)
        scale = lax.rsqrt(jnp.mean(center * center, axis=-1, keepdims=True) + 1e-05)
        return center * scale, scale

    def norm(self, src, dst, which):
        def body(rows):
            unit, _ = self.norm_parts(src[rows, :].astype(jnp.float32))
            dst[rows, :] = (unit * self.row(self.par, which) + self.row(self.par, 2 + which)).astype(jnp.bfloat16)

        self.chunks(body)

    def norm_a(self):
        self.norm(self.s["x"], self.s["a"], 0)

    def project(self, first, last):
        s = self.s
        queries = self.width // TILE

        def body(t):
            scale = jnp.where(t < queries, HEAD ** (-0.5), 1.0)
            found = dot(s["a"][...], flat(self.w_qkv[:, :, :, :, at(t)])) + s["rows"][0:1, at(t)]
            s["qkv"][:, at(t)] = (found * scale).astype(jnp.bfloat16)

        self.tiles(first, last, body)

    def turn_a(self):
        self.s["a_t"][...] = self.s["a"][...].T

    def pair(self, i, which):
        start = which * self.width + i * 128
        return self.s["qkv"].at[:, pl.ds(pl.multiple_of(start, 128), 128)]

    def own_lanes(self, value, head):
        lanes = lax.broadcasted_iota(jnp.int32, value.shape, 1)
        return jnp.where((lanes < HEAD) == (head == 0), value, jnp.zeros_like(value))

    def attend(self, first, last):
        s = self.s

        def body(i):
            q, k, v = (self.pair(i, which) for which in range(3))
            keys = [self.own_lanes(k[...], head) for head in range(2)]
            vals = [self.own_lanes(v[...], head) for head in range(2)]
            for part in range(self.n // TILE):
                cols = slice(part * TILE, part * TILE + TILE)
                mixed = None
                for head in range(2):
                    scores = dot(keys[head], q[cols, :], NT) + s["bias"][:, cols]
                    raised = jnp.exp(scores - jnp.max(scores, axis=0, keepdims=True))
                    share = 1.0 / jnp.sum(raised, axis=0, keepdims=True)
                    weights = (raised * share).astype(jnp.bfloat16)
                    s["wt"][2 * i + head, :, cols] = weights
                    found = dot(vals[head], weights, TN)
                    mixed = found if mixed is None else mixed + found
                s["o"][cols, at(i, 128)] = mixed.T.astype(jnp.bfloat16)

        self.tiles(first, last, body)

    def branch(self):
        s = self.s

        def body(t):
            found = dot(s["o"][...], flat(self.w_out[:, :, :, :, at(t)])) + self.par[6:7, at(t)]
            s["h"][:, at(t)] = s["x"][:, at(t)].astype(jnp.float32) + found

        self.tiles(0, self.width // TILE, body)
        s["o_t"][...] = s["o"][...].T

    def norm_c(self):
        self.norm(self.s["h"], self.s["c"], 1)

    def up(self, first, last):
        s = self.s

        def body(t):
            before = dot(s["c"][...], flat(self.w_up[:, :, :, :, at(t)])) + self.b_up[0:1, at(t)]
            chance = 0.5 + 0.5 * lax.erf(before * 0.7071067811865476)
            s["g"][:, at(t)] = (before * chance).astype(jnp.bfloat16)
            slope = chance + before * (jnp.exp(before * before * -0.5) * 0.3989422804014327)
            s["du"][:, at(t)] = slope.astype(jnp.bfloat16)

        self.tiles(first, last, body)

    def turn_c(self):
        self.s["c_t"][...] = self.s["c"][...].T

    def down(self):
        s = self.s

        def body(t):
            found = dot(s["g"][...], flat(self.w_down[:, :, :, :, :, at(t)])) + self.par[7:8, at(t)]
            s["a"][:, at(t)] = (s["h"][:, at(t)] + found).astype(jnp.bfloat16)

        self.tiles(0, self.width // TILE, body)

    def feed_back(self, first, last):
        s, width = self.s, self.width
        tall = functools.partial(self.tall_copy, self.g_up)

        def body(t):
            cols = at(t, width)
            grad = dot(s["dy"][...], flat(self.w_down[t]), NT)
            low = (grad * s["du"][:, cols].astype(jnp.float32)).astype(jnp.bfloat16)
            s["du"][:, cols] = low
            self.g_bup[0:1, cols] = jnp.sum(low.astype(jnp.float32), axis=0, keepdims=True)
            self.put(tall, 1, t, first, dot(s["c_t"][...], low))

        self.tiles(first, last, body)
        self.pending[1] = tall(1, last - 1)

    def down_terms(self, first, last):
        s, width = self.s, self.width
        wide = functools.partial(self.wide_copy, self.g_down)

        def body(t):
            self.put(wide, 0, t, first, dot(s["g"][:, at(t, width)], s["dy"][...], TN))

        self.tiles(first, last, body)
        self.pending[0] = wide(0, last - 1)

    def up_back(self):
        self.s["sums"][...] = dot(self.s["du"][...], flat(self.w_up[...]), NT)

    def norm_back(self, src, which, grad, rest, body_out):
        def body(rows):
            unit, scale = self.norm_parts(src[rows, :].astype(jnp.float32))
            came = grad[rows, :]
            gained = came * self.row(self.par, which)
            self.g_par[which : which + 1, :] += jnp.sum(came * unit, axis=0, keepdims=True)
            self.g_par[2 + which : 3 + which, :] += jnp.sum(came, axis=0, keepdims=True)
            inner = gained - jnp.mean(gained, axis=-1, keepdims=True)
            inner = inner - unit * jnp.mean(gained * unit, axis=-1, keepdims=True)
            body_out(rows, rest[rows, :].astype(jnp.float32) + inner * scale)

        self.chunks(body)

    def norm_c_back(self):
        s = self.s

        def keep(rows, grad):
            s["h"][rows, :] = grad
            low = grad.astype(jnp.bfloat16)
            s["c"][rows, :] = low
            self.g_par[6:7, :] += jnp.sum(low.astype(jnp.float32), axis=0, keepdims=True)
            self.g_par[7:8, :] += jnp.sum(s["dy"][rows, :].astype(jnp.float32), axis=0, keepdims=True)

        self.norm_back(s["h"], 1, s["sums"], s["dy"], keep)

    def branch_back(self):
        s = self.s
        tall = functools.partial(self.tall_copy, self.g_out)
        self.put(tall, 0, 0, 0, dot(s["o_t"][...], s["c"][...]))
        self.pending[0] = tall(0, 0)
        s["a"][...] = dot(s["c"][...], flat(self.w_out[...]), NT).astype(jnp.bfloat16)

    def attend_back(self, first, last):
        s, width = self.s, self.width

        def body(i):
            q, k, v = (self.pair(i, which) for which in range(3))
            came = s["a"].at[:, at(i, 128)]
            dq = dk = dv = None
            for head in range(2):
                vals = self.own_lanes(v[...], head)
                for part in range(self.n // TILE):
                    cols = slice(part * TILE, part * TILE + TILE)
                    grad = dot(vals, came[cols, :], NT)
                    weights = s["wt"][2 * i + head, :, cols].astype(jnp.float32)
                    product = weights * grad
                    inner = jnp.sum(product, axis=0, keepdims=True)
                    s["ds"][:, cols] = (product - weights * inner).astype(jnp.bfloat16)
                one_q = dot(self.own_lanes(k[...], head), s["ds"][...], TN)
                one_k = dot(s["ds"][...], self.own_lanes(q[...], head))
                one_v = dot(s["wt"][2 * i + head], self.own_lanes(came[...], head))
                dq, dk, dv = (one_q, one_k, one_v) if head == 0 else (dq + one_q, dk + one_k, dv + one_v)
            s["g"][:, at(i, 128)] = dq.T.astype(jnp.bfloat16) * HEAD ** (-0.5)
            s["g"][:, pl.ds(pl.multiple_of(width + i * 128, 128), 128)] = dk.astype(jnp.bfloat16)
            s["g"][:, pl.ds(pl.multiple_of(2 * width + i * 128, 128), 128)] = dv.astype(jnp.bfloat16)

        self.tiles(first, last, body)

    def project_terms(self, first, last):
        s, width = self.s, self.width
        tall = functools.partial(self.tall_copy, self.g_qkv)
        for t in range(first, last):
            grad = s["g"][:, t * width : (t + 1) * width]
            if t != 1:
                row = 4 + t // 2
                self.g_par[row : row + 1, :] = jnp.sum(grad.astype(jnp.float32), axis=0, keepdims=True)
            slot = (t + 1) % 2
            self.put(tall, slot, t, t, dot(s["a_t"][...], grad))
            self.pending[slot] = tall(slot, t)

    def project_back(self):
        s = self.s
        s["sums"][...] = dot(s["g"][:, 0 : 3 * self.width], flat(self.w_qkv[...]), NT)

    def norm_a_back(self):
        s = self.s

        def keep(rows, grad):
            s["h"][rows, :] = grad

        self.norm_back(s["x"], 0, s["sums"], s["h"], keep)


def layer_scratch(n, width, deep):
    low, full = jnp.bfloat16, jnp.float32
    return dict(
        a=pltpu.VMEM((n, width), low),
        a_t=pltpu.VMEM((width, n), low),
        qkv=pltpu.VMEM((n, 3 * width), low),
        bias=pltpu.VMEM((n, n), full),
        wt=pltpu.VMEM((width // HEAD, n, n), low),
        ds=pltpu.VMEM((n, n), low),
        o=pltpu.VMEM((n, width), low),
        o_t=pltpu.VMEM((width, n), low),
        h=pltpu.VMEM((n, width), full),
        c=pltpu.VMEM((n, width), low),
        c_t=pltpu.VMEM((width, n), low),
        g=pltpu.VMEM((n, deep), low),
        du=pltpu.VMEM((n, deep), low),
        sums=pltpu.VMEM((n, width), full),
        rows=pltpu.VMEM((8, 3 * width), full),
        stage=pltpu.VMEM((2, width, width), low),
        stage_sem=pltpu.SemaphoreType.DMA((2,)),
    )


def cut(kept, n):
    cuts = dict(kept)
    for name in ("a", "qkv", "o", "h", "c", "g", "du", "sums"):
        cuts[name] = kept[name].at[0:n]
    for name in ("a_t", "o_t", "c_t"):
        cuts[name] = kept[name].at[:, 0:n]
    for name in ("bias", "ds"):
        cuts[name] = kept[name].at[0:n, 0:n]
    cuts["wt"] = kept["wt"].at[:, 0:n, 0:n]
    return cuts


ORDER = (0, 1, 2, 3)
BACK = (3, 2, 1, 0)


class SmallSum:
    def __init__(self, place, parts, land, line_land, out, send, recv):
        self.place, self.parts, self.land, self.line_land, self.out = place, parts, land, line_land, out
        self.send, self.recv = send, recv

    def near(self, step):
        p = self.place
        device = (p.core, p.xway, p.yway)[step]
        return remote(self.parts.at[step], self.land.at[step], self.send.at[step], self.recv.at[step], device)

    def far(self, step):
        p = self.place
        other = lax.rem(p.z + step, p.line)
        device = (p.dp, other * 2 + p.y)
        src = self.parts.at[3]
        return remote(src, self.line_land.at[p.z], self.send.at[3 + other], self.recv.at[3 + p.z], device)

    def from_far(self, step):
        p = self.place
        other = lax.rem(p.z + step, p.line)
        device = (p.dp, other * 2 + p.y)
        src = self.parts.at[3]
        return remote(src, self.line_land.at[other], self.send.at[3 + other], self.recv.at[3 + other], device)

    def stage(self, step):
        p = self.place
        if step:
            if step <= 3:
                self.near(step - 1).wait_recv()
                self.parts[step] = self.parts[step - 1] + self.land[step - 1]
        if step < 3:
            self.near(step).start()
        if step == 3:
            for other in range(1, p.line):
                self.far(other).start()
            self.line_land[p.z] = self.parts[3]
        if step == 4:
            for other in range(1, p.line):
                self.from_far(other).wait_recv()
            gains, biases, b_up = self.out
            piece, deep = gains.shape[-1], b_up.shape[-1]
            wide = self.line_land.shape[-1] // deep

            def mine(block):
                for block_at in range(p.line):
                    part = self.line_land[block_at, :, 0:8, block * piece : (block + 1) * piece]
                    row, start = 8 + block // wide, block % wide * deep
                    up = self.line_land[block_at, :, row, start : start + deep]
                    if block_at == 0:
                        total, total_up = part, up
                    else:
                        total, total_up = total + part, total_up + up
                gains[...] = total[:, 0:2]
                for row in range(biases.shape[0]):
                    biases[row] = total[:, 2 + row]
                b_up[...] = total_up

            for block in range(2 * p.line):
                pl.when(p.fs == block)(functools.partial(mine, block))
            for near in range(3):
                self.near(near).wait_send()
            for other in range(1, p.line):
                self.far(other).wait_send()


def whole_kernel(line, sizes, names, ring_names, *refs):
    take = list(refs)

    def some(count):
        found = take[:count]
        del take[:count]
        return found

    owned = some(4)
    gains, biases, own_up, lengths, x_t, dy_t, x_i, dy_i = some(8)
    y_i, y_t, gx_i, gx_t = some(4)
    shares, small_out = some(4), some(3)
    far_weights, terms_t, terms_i = some(4), some(4), some(4)
    weights = some(4)
    kept = dict(zip(names, some(len(names))))
    bufs = dict(zip(ring_names, some(len(ring_names))))
    pad_x, pad_dy, held_x, held_dy, small, small_all, par, b_up, g_parts, g_land, g_line = some(11)
    ag_send, ag_recv, ag_near, ag_trade, rs_send, rs_recv, rs_near, credit = some(8)
    s_send, s_recv, g_send, g_recv, load_sem, io_sem = some(6)
    n_t, n_i, counts = sizes
    width = weights[1].shape[-1]
    place = Place(line)
    ahead, back = panels_of(counts, width, ORDER), panels_of(counts, width, BACK)
    base = len(ahead)
    units, sums = [], []
    for u in range(2 * base):
        panel, layer, into = ahead[u % base], u // base, (weights, far_weights)[u // base]
        own, full = owned[panel.which].at[layer], into[panel.which]
        trade = ag_trade.at[min(GATHER_WAYS[:u].count(SPLIT), ag_trade.shape[0] - 1)]
        units.append(Gather(u, place, own, panel, full, GATHER_WAYS[u], ag_send, ag_recv, ag_near, trade))
        units[u].older = units[u - AG_RING] if u >= AG_RING else None
    for u in range(2 * base):
        panel, layer, terms = back[u % base], u // base, (terms_i, terms_t)[u // base]
        share, term = shares[panel.which].at[layer], terms[panel.which]
        sems = credit, rs_send, rs_recv, rs_near
        turn = SUM_WAYS[:u].count(LINE_FIRST), SUM_WAYS.count(LINE_FIRST)
        sums.append(Reduce(u, 2 * base, turn, place, panel, SUM_WAYS[u], term, share, bufs, *sems))
        sums[u].older = {name: sums[u - RINGS[name]] for name in ("away", "own", "total") if u >= RINGS[name]}

    def layer_of(layer, n, view, terms):
        grads = g_parts.at[0, layer, 0:8], b_up.at[2 + layer]
        return Layer(n, view, weights, par.at[layer], b_up.at[layer], terms, *grads)

    text = layer_of(1, n_t, {**kept, "x": held_x, "dy": held_dy}, terms_t)
    view = {**cut(kept, n_i), "x": pad_x, "dy": pad_dy}
    image = layer_of(0, n_i, view, terms_i)

    comes = [
        pltpu.make_async_copy(src.at[0], dst, io_sem.at[2 + i])
        for i, (src, dst) in enumerate(((x_t, held_x), (dy_t, held_dy)))
    ]

    def prepare():
        for come in comes:
            come.start()
        small[...] = jnp.zeros_like(small)
        small[:, 0:2, 0 : gains.shape[2]] = gains[...].astype(jnp.float32)
        for row in range(biases.shape[0]):
            small[:, 2 + row, 0 : biases.shape[2]] = biases[row].astype(jnp.float32)
        for j in range(own_up.shape[1] // 128):
            small[:, 8 + j, :] = own_up[:, j * 128 : (j + 1) * 128].astype(jnp.float32)
        g_parts[0] = jnp.zeros(g_parts.shape[1:], jnp.float32)
        for src, dst in ((x_i, pad_x), (dy_i, pad_dy)):
            have = src.shape[1]
            if have < n_i:
                cut_at = have // 16 * 16
                dst[cut_at:, :] = jnp.zeros((n_i - cut_at, width), jnp.bfloat16)
            dst[0:have, :] = src[0]
        image.mask([x_i.shape[1]])

    place.greet(prepare)

    smalls = []
    for step, other in enumerate(place.others()):
        copy = remote(small, small_all.at[place.fs], s_send.at[step], s_recv.at[place.fs], (place.dp, other))
        copy.start()
        smalls.append(copy)
    for u, unit in enumerate(sums):
        unit.flush = image.put_all if u < base else text.put_all
    starts = [sum(counts[:which]) for which in range(5)]
    heads, tiles, panels = width // 128, width // TILE, counts[3]
    y_copy = pltpu.make_async_copy(kept["a"], y_t.at[0], io_sem.at[0])
    grad_copy = pltpu.make_async_copy(kept["h"], gx_t.at[0], io_sem.at[1])
    loads = [pltpu.make_async_copy(far_weights[i], weights[i], load_sem.at[i]) for i in range(4)]

    steps = []

    def add(body, *args, needs=()):
        def step():
            for unit in needs:
                units[unit].arrive()
            body(*args)

        step.needs = tuple(needs)
        steps.append(step)

    def first():
        small_all[place.fs] = small[...]
        for step, other in enumerate(place.others()):
            remote(small, small_all.at[other], s_send.at[step], s_recv.at[other], (place.dp, other)).wait_recv()
        piece, deep = width // (2 * line), b_up.shape[-1] // (2 * line)
        for layer in range(2):
            for block in range(2 * line):
                par[layer, :, block * piece : (block + 1) * piece] = small_all[block, layer, 0:8, 0:piece]
                for j in range(deep // 128):
                    start = block * deep + j * 128
                    b_up[layer, 0:1, start : start + 128] = small_all[block, layer, 8 + j : 9 + j, :]
        image.prepare()
        image.norm_a()

    def image_out():
        image.down()
        y_i[0] = view["a"][0 : y_i.shape[1], :]

    def image_last():
        image.norm_a_back()
        gx_i[0] = view["h"][0 : gx_i.shape[1], :]

    def text_first():
        for come in comes:
            come.wait()
        ends = [lengths[0, 0]]
        for j in range(1, lengths.shape[1]):
            ends.append(ends[-1] + lengths[0, j])
        text.mask(ends)
        text.prepare()
        text.norm_a()

    def waiting(load, body):
        def step(*args):
            load.wait()
            body(*args)

        return step

    def text_out():
        loads[3].wait()
        text.down()
        y_copy.start()

    def text_branch_back():
        y_copy.wait()
        text.branch_back()

    def text_last():
        text.norm_a_back()
        grad_copy.start()
        for layer in range(2):
            for j in range(b_up.shape[-1] // width):
                g_parts[0, layer, 8 + j : 9 + j, :] = b_up[2 + layer, 0:1, j * width : (j + 1) * width]

    def load(which):
        add(loads[which].start, needs=range(base + starts[which], base + starts[which + 1]))

    add(first)
    for part in range(3):
        add(image.project, part * tiles, (part + 1) * tiles, needs=(part,))
    add(image.turn_a)
    for i in range(0, heads, 2):
        add(image.attend, i, i + 2)
    add(image.branch, needs=(starts[1],))
    add(image.norm_c)
    for part in range(panels):
        add(image.up, part * tiles, (part + 1) * tiles, needs=(starts[2] + part,))
        add(image.down_terms, part, part + 1)
    add(image.turn_c)
    add(image_out, needs=range(starts[3], starts[4]))
    for part in range(panels):
        add(image.feed_back, part, part + 1)
    add(image.up_back)
    add(image.norm_c_back)
    add(image.branch_back)
    for i in range(0, heads, 2):
        add(image.attend_back, i, i + 2)
    for part in range(3):
        add(image.project_terms, part, part + 1)
    add(image.project_back)
    add(image_last)
    load(0)
    add(text_first)
    for part in range(3):
        body = waiting(loads[0], text.project) if part == 0 else text.project
        add(body, part * tiles, (part + 1) * tiles)
    add(text.turn_a)
    load(1)
    for i in range(heads):
        add(text.attend, i, i + 1)
    add(waiting(loads[1], text.branch))
    load(2)
    add(text.norm_c)
    for part in range(panels):
        add(waiting(loads[2], text.up) if part == 0 else text.up, part * tiles, (part + 1) * tiles)
        add(text.down_terms, part, part + 1)
    load(3)
    add(text.turn_c)
    add(text_out)
    for part in range(panels):
        add(text.feed_back, part, part + 1)
    add(text.up_back)
    add(text.norm_c_back)
    add(text_branch_back)
    for i in range(heads):
        add(text.attend_back, i, i + 1)
    for part in range(3):
        add(text.project_terms, part, part + 1)
    add(text.project_back)
    add(text_last)
    small_sum = SmallSum(place, g_parts, g_land, g_line, small_out, g_send, g_recv)
    for stage in range(5):
        add(small_sum.stage, stage)

    drive(steps, [unit.stages() for unit in units], [unit.stages() for unit in sums])

    for unit in sums[-RINGS["away"] :]:
        unit.free_away()
    for unit in sums[-RINGS["own"] :]:
        unit.free_own()
    for unit in sums[-RINGS["total"] :]:
        unit.free_total()
    for unit in sums:
        unit.out_landed().wait_recv()
    for unit in units[-AG_RING:]:
        unit.drain()
    for copy in smalls:
        copy.wait_send()
    grad_copy.wait()


PLAN = (
    0, -1, 10, 1, 11, 20, 2, 12, 30, 21, 3, 13, 40, 31, 22, 41, 50, 4, 32, 60, 23, 42, 14, 5, -1, 51, 70, 33,
    61, 43, 15, 24, -1, 52, 80, 71, 62, 25, -1, 34, 53, 90, -1, -1, 44, 72, 81, -1, 35, 63, 100, 91, -1, 73, 54,
    -1, 45, 110, 82, -1, -1, 64, 92, 101, -1, 111, 120, 83, 55, -1, 102, 65, 74, 93, 112, -1, -1, 84, 121, 130,
    -1, 103, 113, 75, -1, 94, 122, -1, 131, 140, 85, -1, 1000, 123, 104, 132, 1001, 150, 95, 141, 114, 133, 151,
    1010, 142, 160, 124, 1002, 1011, 152, 105, 134, 115, 143, -1, 125, 153, 161, 170, 1003, 1020, -1, -1, 144,
    162, 1012, -1, 1021, 171, 180, -1, 135, -1, 1030, 154, 172, 1004, -1, 145, 181, 190, 163, -1, 173, 1013,
    1031, -1, 182, 1022, 1005, -1, 164, 191, 200, 1014, 1040, 155, 183, -1, 174, 1006, 1041, 1032, -1, 192, -1,
    -1, 201, 210, 1023, -1, 165, 193, 1015, 1050, -1, 184, 202, -1, -1, 1051, 175, 211, 220, 1007, 1024, -1,
    203, 1016, 1042, 1033, -1, 212, 1060, 194, -1, 185, 221, 230, -1, 1061, -1, 1025, 213, -1, 204, 1034, 1052,
    -1, 1017, 222, -1, 231, 1070, -1, -1, 1035, 223, 1043, 1071, 1026, -1, 214, 1080, 1062, 195, 232, -1, 1081,
    233, 1036, -1, -1, 1044, 1053, 1090, 205, -1, 224, 1027, 1045, 1091, 1100, 1072, -1, -1, 1063, -1, 1101,
    215, 1046, 1054, 1110, -1, 1082, -1, 1037, 1064, 234, 1111, -1, 1055, -1, 1065, 1073, 225, 1120, 1056, 1092,
    1121, 1066, 1047, 1130, 1074, 1102, 1131, 235, -1, 1140, -1, 1112, 1075, 1083, -1, 1093, 1057, 1084, 1122,
    1141, 1150, 1067, -1, 1103, 1113, 1151, -1, 1094, 1160, 1085, -1, 1104, 1132, 1161, 1114, 1076, -1, 1095,
    1123, -1, 1077, 1086, 1105, 1115, 1142, 1152, 1162, 1170, -1, 1096, 1124, 1133, -1, 1087, 1106, -1, 1116,
    1125, 1143, 1153, 1180, 1171, -1, 1097, 1107, 1134, 1163, 1181, -1, 1117, 1126, 1190, 1144, -1, 1154, 1172,
    -1, 1127, 1135, 1191, 1200, -1, 1164, 1182, -1, 1201, -1, 1136, 1210, 1192, 1145, 1155, -1, 1165, 1173, -1,
    1183, 1146, 1156, 1202, 1220, -1, 1137, 1174, 1193, 1147, -1, -1, 1157, 1166, 1184, 1230, 1203, -1, 1194,
    1175, 1185, 1211, 1221, 1231, -1, 1212, 1167, 1195, 1204, -1, 1222, 1232, 1176, 1186, 1196, 1205, 1213,
    1223, 1233, 1214, 1224, 1234, 1177, 1187, 1197, 1206, 1215, 1207, 1225, 1235, 1216, 1226, 1236, 1217, 1227,
    1237,
)


def drive(steps, gathers, sums):
    at_step = 0
    for code in PLAN:
        if code < 0:
            steps[at_step]()
            at_step += 1
        elif code < 1000:
            gathers[code // 10][code % 10]()
        else:
            sums[code // 10 - 100][code % 10]()


def padded(rows):
    return -(-rows // TILE) * TILE


def whole(line, x_i, dy_i, x_t, dy_t, lengths, owned, gains, biases, b_up):
    width, deep = owned[1].shape[2], owned[2].shape[2]
    rows = owned[1].shape[1] // 2
    counts = (3, 1, deep // width, deep // width)
    own = [w.reshape(2, 2, rows, w.shape[2]) for w in owned[:3]] + [owned[3].reshape(2, 2, counts[3], rows, width)]
    n_t, n_i = padded(x_t.shape[1]), padded(x_i.shape[1])
    low, full = jnp.bfloat16, jnp.float32
    turned = biases.transpose(1, 0, 2)
    kept = layer_scratch(n_t, width, deep)
    fulls = [(line, 2, *w.shape[1:]) for w in own]
    rings = dict(
        own=pltpu.VMEM((RINGS["own"], line, rows, width), low),
        away=pltpu.VMEM((RINGS["away"], line, rows, width), low),
        other=pltpu.VMEM((RINGS["other"], line, 2, rows, width), low),
        from_x=pltpu.VMEM((RINGS["from_x"], line, rows, width // 2), low),
        from_y=pltpu.VMEM((RINGS["from_y"], line, rows, width), low),
        line_in=pltpu.VMEM((RINGS["line_in"], line + 1, rows, width), low),
        last=pltpu.VMEM((RINGS["last"], rows, width), low),
        total=pltpu.VMEM((RINGS["total"], rows, width), full),
        line_away=pltpu.VMEM((RINGS["line_away"], line + 1, rows, width), low),
    )
    panels = 2 * sum(counts)
    small_rows = 8 + deep // width
    small_rows += -small_rows % 8
    own_rows = 8 + b_up.shape[1] // 128
    own_rows += -own_rows % 8
    anywhere, inside = pl.BlockSpec(memory_space=pl.ANY), pl.BlockSpec(memory_space=pltpu.VMEM)
    dma = pltpu.SemaphoreType.DMA
    outs = [
        jax.ShapeDtypeStruct(x_i.shape, low),
        jax.ShapeDtypeStruct(x_t.shape, low),
        jax.ShapeDtypeStruct(x_i.shape, full),
        jax.ShapeDtypeStruct(x_t.shape, full),
        *[jax.ShapeDtypeStruct(w.shape, full) for w in own],
        *[jax.ShapeDtypeStruct(v.shape, full) for v in (gains, turned, b_up)],
        *[jax.ShapeDtypeStruct(shape, low) for shape in fulls * 3],
    ]
    scratch = [
        *[pltpu.VMEM(shape, low) for shape in fulls],
        *kept.values(),
        *rings.values(),
        pltpu.VMEM((n_i, width), low),
        pltpu.VMEM((n_i, width), low),
        pltpu.VMEM((n_t, width), low),
        pltpu.VMEM((n_t, width), low),
        pltpu.VMEM((2, own_rows, 128), full),
        pltpu.VMEM((2 * line, 2, own_rows, 128), full),
        pltpu.VMEM((2, 8, width), full),
        pltpu.VMEM((4, 1, deep), full),
        pltpu.VMEM((4, 2, small_rows, width), full),
        pltpu.VMEM((3, 2, small_rows, width), full),
        pltpu.VMEM((line, 2, small_rows, width), full),
        dma((AG_RING, line + 5)),
        dma((panels, line + 4)),
        dma((AG_RING,)),
        dma((max(1, GATHER_WAYS.count(SPLIT)), 2, line)),
        dma((SUM_SENDS,)),
        dma((SUM_ARRIVALS,)),
        dma((2 * RINGS["other"] + RINGS["total"],)),
        pltpu.SemaphoreType.REGULAR((CREDIT_COUNT,)),
        dma((2 * line,)),
        dma((2 * line,)),
        dma((3 + line,)),
        dma((3 + line,)),
        dma((4,)),
        dma((4,)),
    ]
    found = pl.pallas_call(
        functools.partial(whole_kernel, line, (n_t, n_i, counts), list(kept), list(rings)),
        out_shape=outs,
        in_specs=[anywhere] * 4 + [inside] * 3 + [pl.BlockSpec(memory_space=pltpu.SMEM)] + [anywhere] * 2 + [inside] * 2,
        out_specs=[inside, anywhere, inside, anywhere] + [anywhere] * 4 + [inside] * 3 + [anywhere] * 12,
        scratch_shapes=scratch,
        compiler_params=pltpu.CompilerParams(collective_id=0, has_side_effects=True, vmem_limit_bytes=63 * 2**20),
    )(*own, gains, turned, b_up, lengths, x_t, dy_t, x_i, dy_i)
    found = hand_over(found[:11])
    shares = [share.reshape(w.shape) for share, w in zip(found[4:8], owned)]
    image_grad = found[2].transpose(1, 0, 2)
    return (*found[:2], image_grad, found[3], *shares, found[8], found[9].transpose(1, 0, 2), found[10])


def hand_over(found):
    def kernel(*refs):
        count = len(found)
        held, (turned, there, back) = refs[2 * count : -3], refs[-3:]
        copies = [pltpu.make_async_copy(refs[i], held[i], there.at[i]) for i in range(count)]
        for copy in copies:
            copy.start()
        left = [turned if i == 2 else held[i] for i in range(count)]
        outs = [pltpu.make_async_copy(left[i], refs[count + i], back.at[i]) for i in range(count)]
        for i in range(count):
            copies[i].wait()
            if i == 2:
                turned[...] = held[i][...].reshape(turned.shape)
            outs[i].start()
        for out in outs:
            out.wait()

    anywhere = pl.BlockSpec(memory_space=pl.ANY)
    sems = pltpu.SemaphoreType.DMA((len(found),))
    kept = [jax.ShapeDtypeStruct(v.shape, v.dtype) for v in found]
    kept[2] = jax.ShapeDtypeStruct((found[2].shape[1], 1, found[2].shape[2]), found[2].dtype)
    return pl.pallas_call(
        kernel,
        out_shape=kept,
        in_specs=[anywhere] * len(found),
        out_specs=[anywhere] * len(found),
        scratch_shapes=[pltpu.VMEM(v.shape, v.dtype) for v in [*found, kept[2]]] + [sems, sems],
        compiler_params=pltpu.CompilerParams(vmem_limit_bytes=63 * 2**20),
    )(*found)


def normed(values, gain, shift):
    center = values - jnp.mean(values, axis=-1, keepdims=True)
    spread = jnp.mean(center * center, axis=-1, keepdims=True)
    return center * lax.rsqrt(spread + 1e-05) * gain + shift


def gelu_exact(values):
    return jax.nn.gelu(values, approximate=False)


def segment_ids(lengths, seq_len):
    bounds = jnp.cumsum(lengths, axis=-1)
    positions = jnp.arange(seq_len, dtype=jnp.int32)
    return jnp.sum((positions[None, :, None] >= bounds[:, None, :]).astype(jnp.int32), axis=-1)


def split_heads(values):
    batch, length, width = values.shape
    return values.reshape(batch, length, width // HEAD, HEAD)


def masked_scores(queries, keys_all, segment):
    scores = jnp.einsum(
        "bqhd,bkhd->bhqk",
        split_heads(queries),
        split_heads(keys_all),
        preferred_element_type=jnp.float32,
    )
    same = (segment[:, :, None] == segment[:, None, :])[:, None]
    return (jnp.where(same, scores, -1e30), same)


def attention(queries, keys_all, values_all, segment):
    scores, same = masked_scores(queries, keys_all, segment)
    largest = jnp.max(scores, axis=-1, keepdims=True)
    raised = jnp.exp(scores - largest)
    totals = jnp.sum(raised, axis=-1, keepdims=True)
    attn_weights = raised / totals
    log_total = largest + jnp.log(totals)
    mixed = jnp.einsum(
        "bhqk,bkhd->bqhd",
        attn_weights.astype(jnp.bfloat16),
        split_heads(values_all),
        preferred_element_type=jnp.float32,
    )
    return (mixed.reshape(queries.shape).astype(jnp.bfloat16), log_total)


def attention_back(queries, keys_all, values_all, segment, log_total, grad_mixed):
    scores, same = masked_scores(queries, keys_all, segment)
    attn_weights = jnp.where(same, jnp.exp(scores - log_total), 0.0)
    grad_heads = split_heads(grad_mixed)
    grad_weights = jnp.einsum(
        "bqhd,bkhd->bhqk", grad_heads, split_heads(values_all), preferred_element_type=jnp.float32
    )
    inner = jnp.sum(attn_weights * grad_weights, axis=-1, keepdims=True)
    grad_scores = (attn_weights * (grad_weights - inner)).astype(jnp.bfloat16)
    grad_queries = jnp.einsum(
        "bhqk,bkhd->bqhd", grad_scores, split_heads(keys_all), preferred_element_type=jnp.float32
    )
    grad_keys = jnp.einsum(
        "bhqk,bqhd->bkhd", grad_scores, split_heads(queries), preferred_element_type=jnp.float32
    )
    grad_values = jnp.einsum(
        "bhqk,bqhd->bkhd",
        attn_weights.astype(jnp.bfloat16),
        grad_heads,
        preferred_element_type=jnp.float32,
    )
    shape_rows = queries.shape
    return (
        grad_queries.reshape(shape_rows),
        grad_keys.reshape(shape_rows),
        grad_values.reshape(shape_rows),
    )


def forward_layer(inputs, weights, segment):
    qkv_weight, out_weight, up_weight, down_weight, gains, biases, up_bias = weights
    width = inputs.shape[-1]
    source = inputs.astype(jnp.float32)
    normed_a = normed(source, gains[0], biases[0]).astype(jnp.bfloat16)
    project = jnp.einsum("bld,de->ble", normed_a, qkv_weight, preferred_element_type=jnp.float32)
    queries = ((project[..., :width] + biases[2]) * HEAD ** (-0.5)).astype(jnp.bfloat16)
    keys_all = project[..., width : 2 * width].astype(jnp.bfloat16)
    values_all = (project[..., 2 * width :] + biases[3]).astype(jnp.bfloat16)
    mixed, log_total = attention(queries, keys_all, values_all, segment)
    hidden = (
        source
        + jnp.einsum("bld,de->ble", mixed, out_weight, preferred_element_type=jnp.float32)
        + biases[4]
    )
    normed_c = normed(hidden, gains[1], biases[1]).astype(jnp.bfloat16)
    before = (
        jnp.einsum("bld,df->blf", normed_c, up_weight, preferred_element_type=jnp.float32) + up_bias
    )
    activated = gelu_exact(before).astype(jnp.bfloat16)
    result = (
        hidden
        + jnp.einsum("blf,fd->bld", activated, down_weight, preferred_element_type=jnp.float32)
        + biases[5]
    )
    return (
        source,
        normed_a,
        queries,
        keys_all,
        values_all,
        log_total,
        mixed,
        hidden,
        normed_c,
        before,
        activated,
        result,
    )


def backward_layer(inputs, cotangent, weights, segment):
    qkv_weight, out_weight, up_weight, down_weight, gains, biases, up_bias = weights
    width = inputs.shape[-1]
    (
        source,
        normed_a,
        queries,
        keys_all,
        values_all,
        log_total,
        mixed,
        hidden,
        normed_c,
        before,
        activated,
        result,
    ) = forward_layer(inputs, weights, segment)
    grad_result = cotangent.astype(jnp.float32)
    grad_downw = jnp.einsum("blf,bld->fd", activated, cotangent, preferred_element_type=jnp.float32)
    grad_act = jnp.einsum("bld,fd->blf", cotangent, down_weight, preferred_element_type=jnp.float32)
    grad_before = jax.vjp(gelu_exact, before)[1](grad_act)[0].astype(jnp.bfloat16)
    grad_upw = jnp.einsum("bld,blf->df", normed_c, grad_before, preferred_element_type=jnp.float32)
    grad_upb = jnp.sum(grad_before.astype(jnp.float32), axis=(0, 1))
    grad_normc = jnp.einsum(
        "blf,df->bld", grad_before, up_weight, preferred_element_type=jnp.float32
    )
    hidden_back = jax.vjp(
        normed, hidden, gains[1].astype(jnp.float32), biases[1].astype(jnp.float32)
    )[1]
    grad_hidden_ln, grad_gain_two, grad_shift_two = hidden_back(grad_normc)
    grad_hidden = grad_result + grad_hidden_ln
    grad_branch = grad_hidden.astype(jnp.bfloat16)
    grad_outw = jnp.einsum("bld,ble->de", mixed, grad_branch, preferred_element_type=jnp.float32)
    grad_mixed = jnp.einsum(
        "ble,de->bld", grad_branch, out_weight, preferred_element_type=jnp.float32
    ).astype(jnp.bfloat16)
    grad_queries, grad_keys, grad_values = attention_back(
        queries, keys_all, values_all, segment, log_total, grad_mixed
    )
    grad_project = jnp.concatenate(
        [
            grad_queries.astype(jnp.bfloat16) * HEAD ** (-0.5),
            grad_keys.astype(jnp.bfloat16),
            grad_values.astype(jnp.bfloat16),
        ],
        axis=-1,
    )
    grad_qkvw = jnp.einsum(
        "bld,ble->de", normed_a, grad_project, preferred_element_type=jnp.float32
    )
    column_sums = jnp.sum(grad_project.astype(jnp.float32), axis=(0, 1))
    grad_norma = jnp.einsum(
        "ble,de->bld", grad_project, qkv_weight, preferred_element_type=jnp.float32
    )
    source_back = jax.vjp(
        normed, source, gains[0].astype(jnp.float32), biases[0].astype(jnp.float32)
    )[1]
    grad_source_ln, grad_gain_one, grad_shift_one = source_back(grad_norma)
    grad_inputs = grad_hidden + grad_source_ln
    grad_gains = jnp.stack([grad_gain_one, grad_gain_two])
    grad_biases = jnp.stack(
        [
            grad_shift_one,
            grad_shift_two,
            column_sums[:width],
            column_sums[2 * width :],
            jnp.sum(grad_branch.astype(jnp.float32), axis=(0, 1)),
            jnp.sum(grad_result, axis=(0, 1)),
        ]
    )
    return (
        result.astype(jnp.bfloat16),
        grad_inputs,
        (grad_qkvw, grad_outw, grad_upw, grad_downw, grad_gains, grad_biases, grad_upb),
    )


def fetch_weights(layer_index, w_qkv, w_out, w_up, w_down, gains, biases, b_up):
    return (
        lax.all_gather(w_qkv[layer_index], "fsdp", axis=0, tiled=True),
        lax.all_gather(w_out[layer_index], "fsdp", axis=0, tiled=True),
        lax.all_gather(w_up[layer_index], "fsdp", axis=0, tiled=True),
        lax.all_gather(w_down[layer_index], "fsdp", axis=0, tiled=True),
        lax.all_gather(gains[layer_index], "fsdp", axis=1, tiled=True),
        lax.all_gather(biases[layer_index], "fsdp", axis=1, tiled=True),
        lax.all_gather(b_up[layer_index], "fsdp", axis=0, tiled=True),
    )


def fetch_again(layer_index, w_qkv, w_out, w_up, w_down, gains, biases, b_up):
    return (
        lax.all_gather(w_qkv[layer_index], "fsdp", axis=0, tiled=True),
        lax.all_gather(w_out[layer_index], "fsdp", axis=0, tiled=True),
        lax.all_gather(w_up[layer_index], "fsdp", axis=0, tiled=True),
        lax.all_gather(w_down[layer_index], "fsdp", axis=0, tiled=True),
        lax.all_gather(gains[layer_index], "fsdp", axis=1, tiled=True),
        lax.all_gather(biases[layer_index], "fsdp", axis=1, tiled=True),
        lax.all_gather(b_up[layer_index], "fsdp", axis=0, tiled=True),
    )


def reduce_grads(gradients):
    shares = (
        lax.psum_scatter(gradients[0], "fsdp", scatter_dimension=0, tiled=True),
        lax.psum_scatter(gradients[1], "fsdp", scatter_dimension=0, tiled=True),
        lax.psum_scatter(gradients[2], "fsdp", scatter_dimension=0, tiled=True),
        lax.psum_scatter(gradients[3], "fsdp", scatter_dimension=0, tiled=True),
        lax.psum_scatter(gradients[4], "fsdp", scatter_dimension=1, tiled=True),
        lax.psum_scatter(gradients[5], "fsdp", scatter_dimension=1, tiled=True),
        lax.psum_scatter(gradients[6], "fsdp", scatter_dimension=0, tiled=True),
    )
    quarters = (
        lax.psum_scatter(
            shares[0].astype(jnp.bfloat16), "dp", scatter_dimension=0, tiled=True
        ).astype(jnp.float32),
        lax.psum_scatter(
            shares[1].astype(jnp.bfloat16), "dp", scatter_dimension=0, tiled=True
        ).astype(jnp.float32),
        lax.psum_scatter(
            shares[2].astype(jnp.bfloat16), "dp", scatter_dimension=0, tiled=True
        ).astype(jnp.float32),
        lax.psum_scatter(
            shares[3].astype(jnp.bfloat16), "dp", scatter_dimension=0, tiled=True
        ).astype(jnp.float32),
        lax.psum_scatter(
            shares[4].astype(jnp.bfloat16), "dp", scatter_dimension=1, tiled=True
        ).astype(jnp.float32),
        lax.psum_scatter(
            shares[5].astype(jnp.bfloat16), "dp", scatter_dimension=1, tiled=True
        ).astype(jnp.float32),
        lax.psum_scatter(
            shares[6].astype(jnp.bfloat16), "dp", scatter_dimension=0, tiled=True
        ).astype(jnp.float32),
    )
    return (
        lax.all_gather(quarters[0].astype(jnp.bfloat16), "dp", axis=0, tiled=True).astype(
            jnp.float32
        ),
        lax.all_gather(quarters[1].astype(jnp.bfloat16), "dp", axis=0, tiled=True).astype(
            jnp.float32
        ),
        lax.all_gather(quarters[2].astype(jnp.bfloat16), "dp", axis=0, tiled=True).astype(
            jnp.float32
        ),
        lax.all_gather(quarters[3].astype(jnp.bfloat16), "dp", axis=0, tiled=True).astype(
            jnp.float32
        ),
        lax.all_gather(quarters[4].astype(jnp.bfloat16), "dp", axis=1, tiled=True).astype(
            jnp.float32
        ),
        lax.all_gather(quarters[5].astype(jnp.bfloat16), "dp", axis=1, tiled=True).astype(
            jnp.float32
        ),
        lax.all_gather(quarters[6].astype(jnp.bfloat16), "dp", axis=0, tiled=True).astype(
            jnp.float32
        ),
    )


def plain(
    images,
    image_cot,
    captions,
    caption_cot,
    lengths,
    w_qkv,
    w_out,
    w_up,
    w_down,
    gains,
    biases,
    b_up,
):
    owned = (w_qkv, w_out, w_up, w_down, gains, biases, b_up)
    image_seg = jnp.zeros((images.shape[0], images.shape[1]), jnp.int32)
    caption_seg = segment_ids(lengths, captions.shape[1])
    first_weights = fetch_weights(0, *owned)
    image_out = forward_layer(images, first_weights, image_seg)[-1].astype(jnp.bfloat16)
    second_weights = fetch_weights(1, *owned)
    caption_out = forward_layer(captions, second_weights, caption_seg)[-1].astype(jnp.bfloat16)
    second_back = fetch_again(1, *owned)
    _, caption_grad, caption_terms = backward_layer(captions, caption_cot, second_back, caption_seg)
    caption_shares = reduce_grads(caption_terms)
    first_back = fetch_again(0, *owned)
    _, image_grad, image_terms = backward_layer(images, image_cot, first_back, image_seg)
    image_shares = reduce_grads(image_terms)
    stacked = tuple((jnp.stack([image_shares[index], caption_shares[index]]) for index in range(7)))
    return (image_out, caption_out, image_grad, caption_grad) + stacked


def kernels_fit(mesh, w_qkv):
    return mesh.shape["dp"] == 4 and mesh.shape["fsdp"] % 2 == 0 and w_qkv.shape[1] % 32 == 0


def local(mesh, images, image_cot, captions, caption_cot, lengths, w_qkv, w_out, w_up, w_down, gains, biases, b_up):
    if not kernels_fit(mesh, w_qkv):
        return plain(
            images, image_cot, captions, caption_cot, lengths, w_qkv, w_out, w_up, w_down, gains, biases, b_up
        )
    return whole(
        mesh.shape["fsdp"] // 2, images, image_cot, captions, caption_cot, lengths,
        (w_qkv, w_out, w_up, w_down), gains, biases, b_up
    )


def solution(mesh):
    placed = (
        P(("dp", "fsdp"), None, None),
        P(("dp", "fsdp"), None, None),
        P(("dp", "fsdp"), None, None),
        P(("dp", "fsdp"), None, None),
        P(("dp", "fsdp"), None),
        P(None, "fsdp", None),
        P(None, "fsdp", None),
        P(None, "fsdp", None),
        P(None, "fsdp", None),
        P(None, None, "fsdp"),
        P(None, None, "fsdp"),
        P(None, "fsdp"),
    )
    return jax.shard_map(
        functools.partial(local, mesh),
        mesh=mesh,
        in_specs=placed,
        out_specs=(
            P(("dp", "fsdp"), None, None),
            P(("dp", "fsdp"), None, None),
            P(("dp", "fsdp"), None, None),
            P(("dp", "fsdp"), None, None),
            P(None, "fsdp", None),
            P(None, "fsdp", None),
            P(None, "fsdp", None),
            P(None, "fsdp", None),
            P(None, None, "fsdp"),
            P(None, None, "fsdp"),
            P(None, "fsdp"),
        ),
        check_vma=False,
    )
```
